32 devices in a mesh: dp: 8 (over z, y), tensor: 4 (over x, core).
Axes of the slice: x: 2, y: 2, z: 4, core: 2. Of those that a mesh axis runs over, the one named last changes fastest.
Arguments:
- tokens: bfloat16 [3072, 8, 768], P(None, 'dp'), may hold values from -6 to 6
- cotangent: bfloat16 [3072, 8, 768], P(None, 'dp'), may hold values from -6 to 6
- lengths: int32 [16], replicated, may hold values from 1024 to 2048, as said below
- dealing: int32 [16], replicated, may hold values from 0 to 15, as said below
- w_qkv: bfloat16 [768, 3, 768], P(None, None, 'tensor'), may hold values from -0.3125 to 0.3125
- w_out: bfloat16 [768, 768], P(None, 'tensor'), may hold values from -0.875 to 0.875
- w_gu: bfloat16 [768, 2, 3072], P(None, None, 'tensor'), may hold values from -0.21875 to 0.21875
- w_down: bfloat16 [768, 3072], P(None, 'tensor'), may hold values from -0.15625 to 0.15625
- gains: float32 [768, 2], replicated, may hold values from 0.25 to 1.75
- shifts: float32 [768, 2], replicated, may hold values from -1.8 to 1.8
Outputs:
- result: bfloat16 [3072, 8, 768], P(None, 'dp')
- input_grad: bfloat16 [3072, 8, 768], P(None, 'dp')
- grad_qkv: float32 [768, 3, 768], P('dp', None, 'tensor')
- grad_out: float32 [768, 768], P('dp', 'tensor')
- grad_gu: float32 [768, 2, 3072], P('dp', None, 'tensor')
- grad_down: float32 [768, 3072], P('dp', 'tensor')
- grad_gains: float32 [768, 2], P(('dp', 'tensor'))
- grad_shifts: float32 [768, 2], P(('dp', 'tensor'))
The draws below stay inside these ranges and needn't reach their ends.
Inputs may be any that keep to these rules, and one draw needn't show every extreme that they name: Group g's two sequences, dealing[2g] and dealing[2g+1], have lengths adding to 3072; some group holds one of 2048 and one of 1024. `dealing`: a permutation of the sequences.
All inputs are finite; a program needn't handle non-finite values.
Results may differ from the reference program's by a relative error of at most 0.025.
The reference program's roundings to bfloat16 on the way count: a program that leaves them out, or rounds other values in their place, can miss the bound.
Values may be sent and summed in bfloat16 or wider, within the bound.
A program may use at most 192 MiB of HBM per device.

```python
import jax
import jax.numpy as jnp
from jax import lax

D = 768
HEADS = 12
HEAD = 64
FF = 3072
MINLEN = 1024
MAXLEN = 2048
GROUP_TOK = 3072
NSEQ = 16
TOKENS = 24576
N_DP = 8


def dealt_pairs(key):
    key_len, key_most, key_order = jax.random.split(key, 3)
    first_len = jax.random.randint(key_len, (N_DP,), MINLEN, MAXLEN + 1)
    longest = jax.random.randint(key_most, (), 0, N_DP)
    first_len = jnp.where(jnp.arange(N_DP) == longest, MAXLEN, first_len)
    flat_len = jnp.stack([first_len, GROUP_TOK - first_len], 1).reshape(-1).astype(jnp.int32)
    dealing_order = jax.random.permutation(key_order, NSEQ).astype(jnp.int32)
    seq_len = jnp.zeros((NSEQ,), jnp.int32).at[dealing_order].set(flat_len)
    return (seq_len, dealing_order)


def draw_lengths(key, part):
    seq_len, dealing_order = dealt_pairs(key)
    return seq_len


def draw_dealing(key, part):
    seq_len, dealing_order = dealt_pairs(key)
    return dealing_order


def shard_levels(own_key, shape, pieces, smallest, largest):
    def one(position, parts):
        draws = jax.random.uniform(jax.random.fold_in(jax.random.fold_in(own_key, 6), position), (parts,), jnp.float32, smallest / len(pieces), largest / len(pieces))
        return jnp.repeat(jnp.exp(draws), shape[position] // parts).reshape((-1,) + (1,) * (len(shape) - position - 1))

    loudness = one(*pieces[0])
    for cut in pieces[1:]:
        loudness = loudness * one(*cut)
    return loudness


def bell_draw(key, extent, scale, limit, pieces=(), held_as=jnp.bfloat16):
    loudness = shard_levels(key, extent, pieces, -0.22, 0.18) if pieces else 1.0
    array = jax.random.normal(key, extent, jnp.float32) * scale * loudness
    return jnp.minimum(jnp.maximum(array, -limit), limit).astype(held_as)


def setup_inputs(seed: int = 0) -> dict:
    keys = jax.random.split(jax.random.key(seed), 11)
    tokens = bell_draw(keys[0], (GROUP_TOK, N_DP, D), 1.0, 6.0, ((1, 8),))
    cotangent = bell_draw(keys[1], (GROUP_TOK, N_DP, D), 1.0, 6.0, ((1, 8),))
    lengths = draw_lengths(jax.random.fold_in(keys[10], 71), 0)
    dealing = draw_dealing(jax.random.fold_in(keys[10], 71), 0)
    w_qkv = bell_draw(keys[4], (D, 3, D), (D // 2) ** -0.5, 0.3125, ((2, 4),))
    w_out = bell_draw(keys[5], (D, D), (D // 16) ** -0.5, 0.875, ((1, 4),))
    w_gu = bell_draw(keys[6], (D, 2, FF), D ** -0.5, 0.21875, ((2, 4),))
    w_down = bell_draw(keys[7], (D, FF), (FF // 2) ** -0.5, 0.15625, ((1, 4),))
    gains = jnp.clip(1.0 + 0.15 * jax.random.normal(keys[8], (D, 2), jnp.float32), 0.25, 1.75)
    shifts = bell_draw(keys[9], (D, 2), 0.3, 1.8, (), jnp.float32)
    return dict(tokens=tokens, cotangent=cotangent, lengths=lengths, dealing=dealing, w_qkv=w_qkv, w_out=w_out, w_gu=w_gu, w_down=w_down, gains=gains, shifts=shifts)


@jax.custom_vjp
def low(v):
    return lax.optimization_barrier(v.astype(jnp.bfloat16)).astype(jnp.float32)

@jax.custom_vjp
def low_back(v):
    return v

def low_keep(v):
    return (low(v), None)

def low_pass(kept, grad):
    return (grad,)

def back_keep(v):
    return (v, None)

def back_low(kept, grad):
    return (low(grad),)
low.defvjp(low_keep, low_pass)
low_back.defvjp(back_keep, back_low)
EPSILON = 1e-05
NEGATIVE = -1000000000.0
HIGH = lax.Precision.HIGHEST

def rope_tables(positions):
    half_width = HEAD // 2
    frequency = 1000.0 ** (-(jnp.arange(half_width, dtype=jnp.float32) * 2.0) / HEAD)
    angles = positions.astype(jnp.float32)[:, None] * frequency[None, :]
    return (jnp.cos(angles)[:, None, :], jnp.sin(angles)[:, None, :])

def rotate(head_rows, cosine_table, sine_table):
    half_width = head_rows.shape[-1] // 2
    first_half = head_rows[..., :half_width]
    second_half = head_rows[..., half_width:]
    return jnp.concatenate([first_half * cosine_table - second_half * sine_table, second_half * cosine_table + first_half * sine_table], -1)

def layer_norm(resid_rows, gain_vec, shift_vec):
    row_mean = lax.optimization_barrier(jnp.mean(resid_rows, -1, keepdims=True))
    centred = resid_rows - row_mean
    inverse = lax.rsqrt(lax.optimization_barrier(jnp.mean(centred * centred, -1, keepdims=True)) + EPSILON)
    return centred * inverse * gain_vec + shift_vec

def layer_forward(inputs, w_qkv, w_out, w_gu, w_down, gains, shifts, segment, cosine_table, sine_table):
    row_count = inputs.shape[0]
    projected = low_back(jnp.einsum('rd,dcn->rcn', inputs, w_qkv, precision=HIGH))
    query_rot = low(rotate(projected[:, 0].reshape(row_count, HEADS, HEAD), cosine_table, sine_table))
    keys_rot = low(rotate(projected[:, 1].reshape(row_count, HEADS, HEAD), cosine_table, sine_table))
    values_all = low(projected[:, 2].reshape(row_count, HEADS, HEAD))
    block_rows = 512 if row_count % 512 == 0 else row_count
    score_scale = HEAD ** (-0.5)

    def attend(block_pair):
        query_block, segment_block = block_pair
        scores = low_back(jnp.einsum('qhe,khe->hqk', query_block, keys_rot, precision=HIGH) * score_scale)
        same_seq = (segment_block[:, None] == segment[None, :])[None]
        scores = jnp.where(same_seq, scores, NEGATIVE)
        soft_weights = low(jax.nn.softmax(scores, axis=-1))
        return jnp.einsum('hqk,khe->qhe', soft_weights, values_all, precision=HIGH)
    mixed_heads = lax.map(jax.checkpoint(attend), (query_rot.reshape(row_count // block_rows, block_rows, HEADS, HEAD), segment.reshape(row_count // block_rows, block_rows)))
    mixed_heads = low_back(low(mixed_heads.reshape(row_count, HEADS * HEAD)))
    attn_branch = low_back(jnp.dot(mixed_heads, w_out.T, precision=HIGH))
    normed_one = layer_norm(inputs + attn_branch, gains[:, 0], shifts[:, 0])
    gate_up = low_back(jnp.einsum('rd,dcf->rcf', low(normed_one), w_gu, precision=HIGH))
    hidden = low(jax.nn.silu(gate_up[:, 0]) * gate_up[:, 1])
    mlp_branch = low_back(jnp.dot(hidden, w_down.T, precision=HIGH))
    return layer_norm(normed_one + mlp_branch, gains[:, 1], shifts[:, 1])

def reference(tokens, cotangent, lengths, dealing, w_qkv, w_out, w_gu, w_down, gains, shifts):
    model_width = tokens.shape[2]
    flat_in = tokens.reshape(TOKENS, model_width).astype(jnp.float32)
    flat_cot = cotangent.reshape(TOKENS, model_width).astype(jnp.float32)
    offsets = (jnp.cumsum(lengths) - lengths).astype(jnp.int32)
    params = (w_qkv.astype(jnp.float32), w_out.astype(jnp.float32), w_gu.astype(jnp.float32), w_down.astype(jnp.float32), gains.astype(jnp.float32), shifts.astype(jnp.float32))
    row_ids = jnp.arange(GROUP_TOK, dtype=jnp.int32)

    def one_group(totals, group_id):
        first_seq = dealing[2 * group_id]
        second_seq = dealing[2 * group_id + 1]
        split_row = lengths[first_seq]
        in_second = row_ids >= split_row
        token_ids = jnp.where(in_second, offsets[second_seq] + row_ids - split_row, offsets[first_seq] + row_ids).astype(jnp.int32)
        positions = jnp.where(in_second, row_ids - split_row, row_ids).astype(jnp.int32)
        segment = in_second.astype(jnp.int32)
        cosine_table, sine_table = rope_tables(positions)
        group_in = flat_in[token_ids]
        group_cot = flat_cot[token_ids]

        def forward_fn(inputs, *weights):
            return layer_forward(inputs, *weights, segment, cosine_table, sine_table)
        outcome, pull_back = jax.vjp(forward_fn, group_in, *params)
        gradients = pull_back(group_cot)
        totals = jax.tree.map(jnp.add, totals, tuple(gradients[1:]))
        return (totals, (outcome.astype(jnp.bfloat16), gradients[0].astype(jnp.bfloat16), token_ids))
    zero_init = tuple((jnp.zeros_like(weight_arr) for weight_arr in params))
    totals, (outcomes, in_grads, all_ids) = lax.scan(one_group, zero_init, jnp.arange(N_DP, dtype=jnp.int32))
    flat_ids = all_ids.reshape(-1)
    result = jnp.zeros((TOKENS, model_width), jnp.bfloat16).at[flat_ids].set(outcomes.reshape(-1, model_width)).reshape(GROUP_TOK, N_DP, model_width)
    input_grad = jnp.zeros((TOKENS, model_width), jnp.bfloat16).at[flat_ids].set(in_grads.reshape(-1, model_width)).reshape(GROUP_TOK, N_DP, model_width)
    return (result, input_grad, totals[0], totals[1], totals[2], totals[3], totals[4], totals[5])
```

```python
import functools

import jax
import jax.numpy as jnp
from jax import lax
from jax.experimental import pallas as pl
from jax.experimental.pallas import tpu as pltpu
from jax.sharding import PartitionSpec as P

HEAD = 64
HALF = HEAD // 2
BLOCK = 256
EPSILON = 1e-05
NEGATIVE = -1000000000.0
START = -1e30
BF = jnp.bfloat16
F32 = jnp.float32
VMEM_LIMIT = 56 * 1024 * 1024


def mm(a, b, ca, cb):
    return lax.dot_general(a, b, (((ca,), (cb,)), ((), ())), preferred_element_type=F32)


def project_kernel(me_ref, x_ref, w_ref, cos_ref, sin_ref, q_ref, k_ref, v_ref, krow_ref, vrow_ref):
    cols = x_ref.shape[1]
    heads = q_ref.shape[0] // HEAD
    width = heads * HEAD
    projected = mm(w_ref[...], x_ref[0], 1, 1)
    cosine = cos_ref[...]
    sine = sin_ref[...]
    for part, out_ref, scale in ((0, q_ref, HEAD ** (-0.5)), (1, k_ref, 1.0)):
        for head in range(heads):
            base = part * width + head * HEAD
            first = projected[base : base + HALF]
            second = projected[base + HALF : base + HEAD]
            turned = jnp.concatenate(
                [first * cosine - second * sine, second * cosine + first * sine], 0
            )
            out_ref[head * HEAD : (head + 1) * HEAD, :] = (turned.astype(BF) * scale).astype(BF)
            if part == 1:
                krow_ref[head] = turned.T.astype(BF)
    for head in range(heads):
        base = 2 * width + head * HEAD
        value = projected[base : base + HEAD]
        v_ref[head * HEAD : (head + 1) * HEAD, :] = value.astype(BF)
        vrow_ref[head] = value.T.astype(BF)


def project(x_rel, w_t, cosine, sine, me):
    parts, share, width = x_rel.shape
    rows = parts * share
    local = w_t.shape[0] // 3
    heads = local // HEAD
    flat = jax.ShapeDtypeStruct((local, rows), BF)
    tall = jax.ShapeDtypeStruct((heads, rows, HEAD), BF)
    wide_spec = pl.BlockSpec((local, share), lambda i, me: (0, i))
    tall_spec = pl.BlockSpec((heads, share, HEAD), lambda i, me: (0, i, 0))
    table_spec = pl.BlockSpec((HALF, share), lambda i, me: (0, i))
    return pl.pallas_call(
        project_kernel,
        grid_spec=pltpu.PrefetchScalarGridSpec(
            num_scalar_prefetch=1,
            grid=(parts,),
            in_specs=[
                pl.BlockSpec((1, share, width), lambda i, me: (jnp.bitwise_xor(i, me[0]), 0, 0)),
                pl.BlockSpec((3 * local, width), lambda i, me: (0, 0)),
                table_spec,
                table_spec,
            ],
            out_specs=[wide_spec, wide_spec, wide_spec, tall_spec, tall_spec],
        ),
        out_shape=[flat, flat, flat, tall, tall],
        compiler_params=pltpu.CompilerParams(vmem_limit_bytes=VMEM_LIMIT),
        cost_estimate=pl.CostEstimate(
            flops=2 * rows * width * 3 * local, bytes_accessed=8 << 20, transcendentals=0
        ),
        name="project",
    )(me, x_rel, w_t, cosine, sine)


def visit(mixed, index, blocks, body, carry):
    low = jnp.where(index > mixed, mixed + 1, 0)
    high = jnp.where(index > mixed, blocks, jnp.where(index < mixed, mixed, 0))
    carry = lax.fori_loop(low, high, lambda j, c: body(j, False, c), carry)
    low = jnp.where(index == mixed, 0, mixed)
    high = jnp.where(index == mixed, blocks, mixed + 1)
    return lax.fori_loop(low, high, lambda j, c: body(j, True, c), carry)


def attend_kernel(info, q_ref, k_ref, v_ref, segrow_ref, segcol_ref, o_ref, lse_ref, acc_ref):
    index = pl.program_id(0)
    blocks = pl.num_programs(0)
    heads = k_ref.shape[0]
    acc_ref[...] = jnp.zeros_like(acc_ref)
    segrow = segrow_ref[...]

    def body(j, masked, carry):
        keys = pl.ds(pl.multiple_of(j * BLOCK, BLOCK), BLOCK)
        if masked:
            same = segcol_ref[keys, :] == segrow
        out = []
        for head in range(heads):
            top, total = carry[head]
            part = slice(head * HEAD, (head + 1) * HEAD)
            scores = mm(k_ref[head, keys, :], q_ref[part, :], 1, 0)
            if masked:
                scores = jnp.where(same, scores, NEGATIVE)
            new_top = jnp.maximum(top, jnp.max(scores, 0, keepdims=True))
            shrink = jnp.exp(top - new_top)
            weights = jnp.exp(scores - new_top)
            total = total * shrink + jnp.sum(weights, 0, keepdims=True)
            acc_ref[part, :] = acc_ref[part, :] * shrink + mm(
                v_ref[part, keys], weights.astype(BF), 1, 0
            )
            out.append((new_top, total))
        return tuple(out)

    width = q_ref.shape[1]
    start = (jnp.full((1, width), START, F32), jnp.zeros((1, width), F32))
    carry = visit(info[0], index, blocks, body, (start,) * heads)
    for head in range(heads):
        top, total = carry[head]
        part = slice(head * HEAD, (head + 1) * HEAD)
        o_ref[0, part, :] = (acc_ref[part, :] / total).astype(BF)
        lse_ref[head : head + 1, :] = top + jnp.log(total)


def attend(info, q, k_rows, v, seg_row, seg_col, parts):
    local, rows = q.shape
    heads = local // HEAD
    blocks = rows // BLOCK
    each = blocks // parts
    return pl.pallas_call(
        attend_kernel,
        grid_spec=pltpu.PrefetchScalarGridSpec(
            num_scalar_prefetch=1,
            grid=(blocks,),
            in_specs=[
                pl.BlockSpec((local, BLOCK), lambda i, info: (0, i)),
                pl.BlockSpec((heads, rows, HEAD), lambda i, info: (0, 0, 0)),
                pl.BlockSpec((local, rows), lambda i, info: (0, 0)),
                pl.BlockSpec((1, BLOCK), lambda i, info: (0, i)),
                pl.BlockSpec((rows, 1), lambda i, info: (0, 0)),
            ],
            out_specs=[
                pl.BlockSpec(
                    (1, local, BLOCK),
                    lambda i, info: (jnp.bitwise_xor(i // each, info[1]), 0, i % each),
                ),
                pl.BlockSpec((heads, BLOCK), lambda i, info: (0, i)),
            ],
            scratch_shapes=[pltpu.VMEM((local, BLOCK), F32)],
        ),
        out_shape=[
            jax.ShapeDtypeStruct((parts, local, rows // parts), BF),
            jax.ShapeDtypeStruct((heads, rows), F32),
        ],
        compiler_params=pltpu.CompilerParams(vmem_limit_bytes=VMEM_LIMIT),
        cost_estimate=pl.CostEstimate(
            flops=2 * 2 * rows * rows * 256 * heads // 2,
            bytes_accessed=8 << 20,
            transcendentals=heads * rows * rows // 2,
        ),
        name="attend",
    )(info, q, k_rows, v, seg_row, seg_col)


def unturn(first, second, cosine, sine):
    return first * cosine + second * sine, second * cosine - first * sine


def attend_back_kernel(
    info,
    q_ref,
    krow_ref,
    k_ref,
    vrow_ref,
    o_ref,
    do_ref,
    lse_ref,
    segrow_ref,
    segcol_ref,
    cos_ref,
    sin_ref,
    out_ref,
    dq_ref,
    dk_ref,
    dv_ref,
):
    index = pl.program_id(0)
    blocks = pl.num_programs(0)
    heads = krow_ref.shape[0]
    width = heads * HEAD

    @pl.when(index == 0)
    def _():
        dk_ref[...] = jnp.zeros_like(dk_ref)
        dv_ref[...] = jnp.zeros_like(dv_ref)

    dq_ref[...] = jnp.zeros_like(dq_ref)
    segrow = segrow_ref[...]
    deltas = []
    for head in range(heads):
        part = slice(head * HEAD, (head + 1) * HEAD)
        deltas.append(
            jnp.sum(do_ref[0, part, :].astype(F32) * o_ref[0, part, :].astype(F32), 0, keepdims=True)
        )

    def body(j, masked, carry):
        keys = pl.ds(pl.multiple_of(j * BLOCK, BLOCK), BLOCK)
        if masked:
            same = segcol_ref[keys, :] == segrow
        for head in range(heads):
            part = slice(head * HEAD, (head + 1) * HEAD)
            queries = q_ref[part, :]
            upstream = do_ref[0, part, :]
            scores = mm(krow_ref[head, keys, :], queries, 1, 0)
            if masked:
                scores = jnp.where(same, scores, NEGATIVE)
            soft = jnp.exp(scores - lse_ref[head : head + 1, :])
            grad_soft = mm(vrow_ref[head, keys, :], upstream, 1, 0)
            grad_scores = (soft * (grad_soft - deltas[head])).astype(BF)
            dv_ref[head, keys, :] += mm(soft.astype(BF), upstream, 1, 1)
            dk_ref[head, keys, :] += mm(grad_scores, queries, 1, 1)
            dq_ref[part, :] += mm(k_ref[part, keys], grad_scores, 1, 0)
        return carry

    visit(info[0], index, blocks, body, 0)

    columns = pl.ds(pl.multiple_of(index * BLOCK, BLOCK), BLOCK)
    for head in range(heads):
        base = head * HEAD
        grad = dq_ref[base : base + HEAD, :] * HEAD ** (-0.5)
        low, high = unturn(grad[:HALF], grad[HALF:], cos_ref[:, columns], sin_ref[:, columns])
        out_ref[base : base + HALF, columns] = low.astype(BF)
        out_ref[base + HALF : base + HEAD, columns] = high.astype(BF)

    @pl.when(index == blocks - 1)
    def _():
        @pl.loop(0, blocks)
        def _(j):
            rows = pl.ds(pl.multiple_of(j * BLOCK, BLOCK), BLOCK)
            for head in range(heads):
                base = width + head * HEAD
                grad = dk_ref[head, rows, :].T
                low, high = unturn(grad[:HALF], grad[HALF:], cos_ref[:, rows], sin_ref[:, rows])
                out_ref[base : base + HALF, rows] = low.astype(BF)
                out_ref[base + HALF : base + HEAD, rows] = high.astype(BF)
                base = 2 * width + head * HEAD
                out_ref[base : base + HEAD, rows] = dv_ref[head, rows, :].T.astype(BF)


def attend_back(info, q, k_rows, k, v_rows, o, do, lse, seg_row, seg_col, cosine, sine):
    parts = o.shape[0]
    local, rows = q.shape
    heads = local // HEAD
    blocks = rows // BLOCK
    each = blocks // parts
    whole = lambda *shape: pl.BlockSpec(shape, lambda i, info: (0,) * len(shape))
    member = pl.BlockSpec(
        (1, local, BLOCK), lambda i, info: (jnp.bitwise_xor(i // each, info[1]), 0, i % each)
    )
    return pl.pallas_call(
        attend_back_kernel,
        grid_spec=pltpu.PrefetchScalarGridSpec(
            num_scalar_prefetch=1,
            grid=(blocks,),
            in_specs=[
                pl.BlockSpec((local, BLOCK), lambda i, info: (0, i)),
                whole(heads, rows, HEAD),
                whole(local, rows),
                whole(heads, rows, HEAD),
                member,
                member,
                pl.BlockSpec((heads, BLOCK), lambda i, info: (0, i)),
                pl.BlockSpec((1, BLOCK), lambda i, info: (0, i)),
                whole(rows, 1),
                whole(HALF, rows),
                whole(HALF, rows),
            ],
            out_specs=whole(3 * local, rows),
            scratch_shapes=[
                pltpu.VMEM((local, BLOCK), F32),
                pltpu.VMEM((heads, rows, HEAD), F32),
                pltpu.VMEM((heads, rows, HEAD), F32),
            ],
        ),
        out_shape=jax.ShapeDtypeStruct((3 * local, rows), BF),
        compiler_params=pltpu.CompilerParams(vmem_limit_bytes=VMEM_LIMIT),
        cost_estimate=pl.CostEstimate(
            flops=2 * 5 * rows * rows * 256 * heads // 2,
            bytes_accessed=16 << 20,
            transcendentals=heads * rows * rows // 2,
        ),
        name="attend_back",
    )(info, q, k_rows, k, v_rows, o, do, lse, seg_row, seg_col, cosine, sine)


def norm_forward(resid_rows, gain_vec, shift_vec):
    row_mean = jnp.mean(resid_rows, -1, keepdims=True)
    centred = resid_rows - row_mean
    inverse = lax.rsqrt(jnp.mean(centred * centred, -1, keepdims=True) + EPSILON)
    unit_rows = centred * inverse
    return (unit_rows * gain_vec + shift_vec, unit_rows, inverse)


def norm_backward(upstream, unit_rows, inverse, gain_vec):
    scaled = upstream * gain_vec
    inner_term = (
        scaled
        - jnp.mean(scaled, -1, keepdims=True)
        - unit_rows * jnp.mean(scaled * unit_rows, -1, keepdims=True)
    )
    return (inner_term * inverse, jnp.sum(upstream * unit_rows, 0), jnp.sum(upstream, 0))


def swap(array, size, step):
    return lax.ppermute(array, "tensor", [(i, i ^ step) for i in range(size)])


def gather_members(own):
    size = lax.axis_size("tensor")
    across = swap(own, size, 2)
    return [own, swap(own, size, 1), across, swap(across, size, 1)]


def exchange_members(pieces):
    size = lax.axis_size("tensor")
    return [pieces[0]] + [swap(pieces[r], size, r) for r in range(1, size)]


def reduce_members(pieces):
    size = lax.axis_size("tensor")
    near = swap(pieces[1], size, 1)
    far = swap(pieces[3], size, 1)
    other = (pieces[2].astype(F32) + far.astype(F32)).astype(BF)
    across = swap(other, size, 2)
    return pieces[0].astype(F32) + near.astype(F32) + across.astype(F32)


def spans(offset, length, source, groups):
    low = (offset - source + groups - 1) // groups
    high = (offset + length - source + groups - 1) // groups
    return low, high - low


def local(tokens, cotangent, lengths, dealing, w_qkv, w_out, w_gu, w_down, gains, shifts):
    groups = lax.axis_size("dp")
    member = lax.axis_index("dp")
    size = lax.axis_size("tensor")
    me = lax.axis_index("tensor")
    rows = tokens.shape[0]
    width = tokens.shape[2]
    slots = rows // groups
    share = slots // size
    own_rows = rows // size
    subs = own_rows // BLOCK
    sub = share // subs
    extra = 8
    packed = share + extra
    i32 = jnp.int32

    seq_count = lengths.shape[0]
    count_up = jnp.arange(seq_count, dtype=i32)
    offsets = jnp.sum(jnp.where(count_up[None, :] < count_up[:, None], lengths[None, :], 0), 1)
    chosen = dealing[:, None] == count_up[None, :]
    dealt_len = jnp.sum(jnp.where(chosen, lengths[None, :], 0), 1).reshape(groups, 2)
    dealt_off = jnp.sum(jnp.where(chosen, offsets[None, :], 0), 1).reshape(groups, 2)
    group_ids = jnp.arange(groups, dtype=i32)

    low_a, count_a = spans(dealt_off[:, 0], dealt_len[:, 0], member, groups)
    low_b, count_b = spans(dealt_off[:, 1], dealt_len[:, 1], member, groups)
    place = jnp.arange(packed, dtype=i32)[None, :]
    slot = jnp.where(place < share, me * share + place, slots)
    picked = jnp.where(
        slot < count_a[:, None], low_a[:, None] + slot, (low_b - count_a)[:, None] + slot
    )
    picked = jnp.clip(picked, 0, rows - 1).reshape(-1)
    send_x = jnp.take(tokens.reshape(rows, width), picked, axis=0).reshape(groups, packed, width)
    send_c = jnp.take(cotangent.reshape(rows, width), picked, axis=0).reshape(
        groups, packed, width
    )
    recv_x = lax.all_to_all(send_x, "dp", split_axis=0, concat_axis=0, tiled=True)
    recv_c = lax.all_to_all(send_c, "dp", split_axis=0, concat_axis=0, tiled=True)

    mine = group_ids == member
    pick_group = lambda table: jnp.sum(jnp.where(mine[:, None], table, 0), 0)
    my_len = pick_group(dealt_len)
    my_off = pick_group(dealt_off)
    glow_a, gcount_a = spans(my_off[0], my_len[0], group_ids, groups)
    glow_b, gcount_b = spans(my_off[1], my_len[1], group_ids, groups)
    filled = gcount_a + gcount_b
    hole = filled < slots
    over = filled > slots
    before = group_ids[None, :] < group_ids[:, None]
    hole_rank = jnp.sum(jnp.where(before & hole[None, :], 1, 0), 1)
    over_rank = jnp.sum(jnp.where(before & over[None, :], 1, 0), 1)
    match = hole[:, None] & over[None, :] & (hole_rank[:, None] == over_rank[None, :])
    last_token = (glow_b - gcount_a + slots) * groups + group_ids
    hole_token = jnp.sum(jnp.where(match, last_token[None, :], 0), 1)
    match_bf = match.astype(BF)
    is_last = me == size - 1

    def fill(received):
        body = received[:, :share]
        spare = jnp.dot(match_bf, received[:, share], preferred_element_type=F32).astype(BF)
        fix = (hole & is_last)[:, None, None] & (jnp.arange(share) == share - 1)[None, :, None]
        body = jnp.where(fix, spare[:, None, :], body)
        body = body.reshape(groups, subs, sub, width).transpose(1, 0, 2, 3)
        return body.reshape(own_rows, width)

    shape = (size * subs, groups, sub)
    block_id = lax.broadcasted_iota(i32, shape, 0)
    source_id = lax.broadcasted_iota(i32, shape, 1)
    slot_id = block_id * sub + lax.broadcasted_iota(i32, shape, 2)
    spread = lambda vec: vec[None, :, None]
    in_a = slot_id < spread(gcount_a)
    token_id = (
        jnp.where(in_a, spread(glow_a), spread(glow_b - gcount_a)) + slot_id
    ) * groups + source_id
    token_id = jnp.where(spread(hole) & (slot_id == slots - 1), spread(hole_token), token_id)
    positions = (token_id - jnp.where(in_a, my_off[0], my_off[1])).reshape(rows)
    segment = jnp.where(in_a, 0, 1).astype(F32).reshape(rows)
    frequency = 1000.0 ** (-(jnp.arange(HALF, dtype=F32) * 2.0) / HEAD)
    angles = frequency[:, None] * positions.astype(F32)[None, :]
    cosine = jnp.cos(angles)
    sine = jnp.sin(angles)
    seg_row = segment[None, :]
    seg_col = segment[:, None]
    info = jnp.stack([my_len[0] // BLOCK, me]).astype(i32)

    x_own = fill(recv_x)
    x_rel = jnp.stack(gather_members(x_own))
    local_width = w_qkv.shape[2]
    w_qkv_t = w_qkv.transpose(1, 2, 0).reshape(3 * local_width, width)
    q, k, v, k_rows, v_rows = project(x_rel, w_qkv_t, cosine, sine, me[None])
    o_rel, lse = attend(info, q, k_rows, v, seg_row, seg_col, size)

    w_out_t = jnp.concatenate(gather_members(w_out.T), 0)
    gu_parts = gather_members(w_gu.reshape(width, -1))
    down_parts = gather_members(w_down)

    heads_out = jnp.concatenate(exchange_members([o_rel[r] for r in range(size)]), 0)
    x_share = x_own.astype(F32)
    attn = mm(heads_out, w_out_t, 0, 0)
    normed_one, unit_one, inverse_one = norm_forward(x_share + attn, gains[:, 0], shifts[:, 0])
    normed = normed_one.astype(BF)
    hidden_width = w_down.shape[1]
    branch = jnp.zeros((own_rows, width), F32)
    kept = []
    for r in range(size):
        both = mm(normed, gu_parts[r], 1, 0)
        gate = both[:, :hidden_width]
        up = both[:, hidden_width:]
        sig = jax.nn.sigmoid(gate)
        hidden = (gate * sig * up).astype(BF)
        branch = branch + mm(hidden, down_parts[r], 1, 1)
        kept.append((gate, up, sig, hidden))
    result_own, unit_two, inverse_two = norm_forward(
        normed_one + branch, gains[:, 1], shifts[:, 1]
    )
    cot_share = fill(recv_c).astype(F32)
    grad_two, gain_two, shift_two = norm_backward(cot_share, unit_two, inverse_two, gains[:, 1])
    d_branch = grad_two.astype(BF)
    back_normed = jnp.zeros((own_rows, width), F32)
    pieces = []
    for r in range(size):
        gate, up, sig, hidden = kept[r]
        grad_hidden = mm(d_branch, down_parts[r], 1, 0)
        grad_gate = grad_hidden * up * sig * (1.0 + gate * (1.0 - sig))
        grad_up = grad_hidden * gate * sig
        grad_gu = jnp.concatenate([grad_gate, grad_up], 1).astype(BF)
        back_normed = back_normed + mm(grad_gu, gu_parts[r], 1, 1)
        pieces.append([mm(normed, grad_gu, 0, 0), mm(d_branch, hidden, 0, 0)])
    grad_one, gain_one, shift_one = norm_backward(
        grad_two + back_normed, unit_one, inverse_one, gains[:, 0]
    )
    d_attn = grad_one.astype(BF)
    d_heads = mm(w_out_t, d_attn, 1, 1).astype(BF).reshape(size, local_width, own_rows)
    d_out = mm(d_attn, heads_out, 0, 1)
    norm_grads = jnp.stack([gain_one, gain_two, shift_one, shift_two], 1)
    wide = 2 * hidden_width + hidden_width + local_width + 4
    pad = (-wide) % 128
    for r in range(size):
        pieces[r] = jnp.concatenate(
            pieces[r]
            + [
                d_out[:, r * local_width : (r + 1) * local_width],
                norm_grads,
                jnp.zeros((width, pad), F32),
            ],
            1,
        ).astype(BF)

    do_rel = jnp.stack(exchange_members([d_heads[r] for r in range(size)]))
    d_qkv_t = attend_back(
        info, q, k_rows, k, v_rows, o_rel, do_rel, lse, seg_row, seg_col, cosine, sine
    )
    grad_qkv_t = jnp.concatenate(
        [
            mm(d_qkv_t.reshape(3 * local_width, size, own_rows)[:, i], _member(x_rel, i, me), 1, 0)[
                None
            ]
            for i in range(size)
        ],
        0,
    ).sum(0)
    back_parts = []
    for r in range(size):
        columns = lax.dynamic_slice_in_dim(
            d_qkv_t, jnp.bitwise_xor(me, r) * own_rows, own_rows, 1
        )
        back_parts.append(mm(columns, w_qkv_t, 0, 0).astype(BF))
    input_own = (grad_one + reduce_members(back_parts)).astype(BF)

    wide_own = reduce_members(pieces).astype(BF)
    both_grads = jnp.concatenate([wide_own, grad_qkv_t.T.astype(BF)], 1)
    summed = lax.psum_scatter(both_grads, "dp", scatter_dimension=0, tiled=True).astype(F32)
    gu_sum = summed[:, : 2 * hidden_width].reshape(-1, 2, hidden_width)
    down_sum = summed[:, 2 * hidden_width : 3 * hidden_width]
    out_sum = summed[:, 3 * hidden_width : 3 * hidden_width + local_width]
    norm_sum = summed[:, 3 * hidden_width + local_width : wide]
    norm_sum = lax.dynamic_slice_in_dim(
        norm_sum, me * (norm_sum.shape[0] // size), norm_sum.shape[0] // size, 0
    )
    qkv_sum = summed[:, wide + pad :].reshape(-1, 3, local_width)

    row_ids = jnp.arange(rows, dtype=i32)[None, :]
    home_low_a = low_a[:, None]
    home_low_b = low_b[:, None]
    here_a = (row_ids >= home_low_a) & (row_ids < home_low_a + count_a[:, None])
    here_b = (row_ids >= home_low_b) & (row_ids < home_low_b + count_b[:, None])
    home_slot = jnp.where(
        here_a, row_ids - home_low_a, row_ids - home_low_b + count_a[:, None]
    )
    spilled = home_slot >= slots
    home_part = jnp.where(spilled, size - 1, home_slot // share)
    home_place = jnp.where(spilled, share, home_slot - home_part * share)
    home_flat = (
        jnp.bitwise_xor(home_part, me) * groups + group_ids[:, None]
    ) * packed + home_place
    home_flat = jnp.sum(jnp.where(here_a | here_b, home_flat, 0), 0)

    def go_home(own):
        body = own.reshape(subs, groups, sub, width).transpose(1, 0, 2, 3)
        body = body.reshape(groups, share, width)
        spare = lax.dot_general(
            match_bf, body[:, share - 1], (((0,), (0,)), ((), ())), preferred_element_type=F32
        ).astype(BF)
        spare = jnp.broadcast_to(spare[:, None, :], (groups, extra, width))
        sent = jnp.concatenate([body, spare], 1)
        home = lax.all_to_all(sent, "dp", split_axis=0, concat_axis=0, tiled=True)
        every = jnp.concatenate(gather_members(home.reshape(groups * packed, width)), 0)
        return jnp.take(every, home_flat, axis=0).reshape(rows, 1, width)

    result = go_home(result_own.astype(BF))
    input_grad = go_home(input_own)
    return (
        result,
        input_grad,
        qkv_sum,
        out_sum,
        gu_sum,
        down_sum,
        norm_sum[:, :2],
        norm_sum[:, 2:],
    )


def _member(x_rel, absolute, me):
    return lax.dynamic_index_in_dim(x_rel, jnp.bitwise_xor(absolute, me), 0, keepdims=False)


def solution(mesh):
    placed = (
        P(None, "dp", None),
        P(None, "dp", None),
        P(),
        P(),
        P(None, None, "tensor"),
        P(None, "tensor"),
        P(None, None, "tensor"),
        P(None, "tensor"),
        P(),
        P(),
    )
    return jax.shard_map(
        local,
        mesh=mesh,
        in_specs=placed,
        out_specs=(
            P(None, "dp", None),
            P(None, "dp", None),
            P("dp", None, "tensor"),
            P("dp", "tensor"),
            P("dp", None, "tensor"),
            P("dp", "tensor"),
            P(("dp", "tensor"), None),
            P(("dp", "tensor"), None),
        ),
        check_vma=False,
    )
```

```python
import functools

import jax
import jax.numpy as jnp
from jax import lax
from jax.experimental import pallas as pl
from jax.experimental.pallas import tpu as pltpu
from jax.sharding import PartitionSpec as P

HEAD = 64
HALF = HEAD // 2
BLOCK = 256
QUERIES = 512
PADDED = HEAD + 16
KEYS = 512
LOG_2 = 0.6931471805599453
EPSILON = 1e-05
NEGATIVE = -1000000000.0
START = -1e30
BF = jnp.bfloat16
F32 = jnp.float32
VMEM_LIMIT = 56 * 1024 * 1024


def mm(a, b, ca, cb):
    return lax.dot_general(a, b, (((ca,), (cb,)), ((), ())), preferred_element_type=F32)


def project_kernel(me_ref, x_ref, w_ref, cos_ref, sin_ref, q_ref, k_ref, v_ref, krow_ref, vrow_ref):
    cols = x_ref.shape[1]
    heads = q_ref.shape[0] // HEAD
    width = heads * HEAD
    projected = mm(w_ref[...], x_ref[0], 1, 1)
    cosine = cos_ref[...]
    sine = sin_ref[...]
    for part, out_ref, scale in ((0, q_ref, HEAD ** (-0.5) / LOG_2), (1, k_ref, 1.0)):
        for head in range(heads):
            base = part * width + head * HEAD
            first = projected[base : base + HALF]
            second = projected[base + HALF : base + HEAD]
            turned = jnp.concatenate(
                [first * cosine - second * sine, second * cosine + first * sine], 0
            )
            out_ref[head * HEAD : (head + 1) * HEAD, :] = (turned * scale).astype(BF)
            if part == 1:
                krow_ref[head] = turned.T.astype(BF)
    for head in range(heads):
        base = 2 * width + head * HEAD
        value = projected[base : base + HEAD]
        rest = lax.broadcasted_iota(jnp.int32, (PADDED - HEAD, cols), 0) == 0
        v_ref[head * PADDED : (head + 1) * PADDED, :] = jnp.concatenate(
            [value, jnp.where(rest, 1.0, 0.0)], 0
        ).astype(BF)
        vrow_ref[head] = value.T.astype(BF)


def project(x_rel, w_t, cosine, sine, me):
    parts, share, width = x_rel.shape
    rows = parts * share
    local = w_t.shape[0] // 3
    heads = local // HEAD
    flat = jax.ShapeDtypeStruct((local, rows), BF)
    tall = jax.ShapeDtypeStruct((heads, rows, HEAD), BF)
    wide_spec = pl.BlockSpec((local, share), lambda i, me: (0, i))
    tall_spec = pl.BlockSpec((heads, share, HEAD), lambda i, me: (0, i, 0))
    table_spec = pl.BlockSpec((HALF, share), lambda i, me: (0, i))
    return pl.pallas_call(
        project_kernel,
        grid_spec=pltpu.PrefetchScalarGridSpec(
            num_scalar_prefetch=1,
            grid=(parts,),
            in_specs=[
                pl.BlockSpec((1, share, width), lambda i, me: (jnp.bitwise_xor(i, me[0]), 0, 0)),
                pl.BlockSpec((3 * local, width), lambda i, me: (0, 0)),
                table_spec,
                table_spec,
            ],
            out_specs=[
                wide_spec,
                wide_spec,
                pl.BlockSpec((heads * PADDED, share), lambda i, me: (0, i)),
                tall_spec,
                tall_spec,
            ],
        ),
        out_shape=[
            flat,
            flat,
            jax.ShapeDtypeStruct((heads * PADDED, rows), BF),
            tall,
            tall,
        ],
        compiler_params=pltpu.CompilerParams(vmem_limit_bytes=VMEM_LIMIT),
        cost_estimate=pl.CostEstimate(
            flops=2 * rows * width * 3 * local, bytes_accessed=8 << 20, transcendentals=0
        ),
        name="project",
    )(me, x_rel, w_t, cosine, sine)


def visible(info, index, q_blocks, k_blocks, count):
    is_a = (index + 1) * q_blocks <= info[0]
    is_b = index * q_blocks >= info[1]
    pure = is_a | is_b
    end_a = info[0] // k_blocks
    start_b = (info[1] + k_blocks - 1) // k_blocks
    plain_low = jnp.where(is_b, start_b, 0)
    plain_high = jnp.where(is_b, count, jnp.where(is_a, end_a, 0))
    return plain_low, plain_high, jnp.where(pure, end_a, 0), jnp.where(pure, start_b, count)


def attend_kernel(info, q_ref, k_ref, v_ref, segrow_ref, segcol_ref, o_ref, lse_ref, acc_ref):
    index = pl.program_id(0)
    heads, rows, _ = k_ref.shape
    width = q_ref.shape[1]
    tall = v_ref.shape[0] // heads
    spans_ = visible(info, index, width // BLOCK, KEYS // BLOCK, rows // KEYS)
    acc_ref[...] = jnp.zeros_like(acc_ref)
    segrow = segrow_ref[...]
    ids = range(heads)

    def step(masked, j, tops):
        keys = pl.ds(pl.multiple_of(j * KEYS, KEYS), KEYS)
        scores = [mm(k_ref[h, keys, :], q_ref[h * HEAD : (h + 1) * HEAD, :], 1, 0) for h in ids]
        if masked:
            same = segcol_ref[keys, :] == segrow
            scores = [jnp.where(same, s, NEGATIVE) for s in scores]
        new = [jnp.maximum(tops[h], jnp.max(scores[h], 0, keepdims=True)) for h in ids]
        weights = [jnp.exp2(scores[h] - new[h]).astype(BF) for h in ids]
        shrink = [jnp.exp2(tops[h] - new[h]) for h in ids]
        sums = [mm(v_ref[h * tall : (h + 1) * tall, keys], weights[h], 1, 0) for h in ids]
        for h in ids:
            part = slice(h * tall, (h + 1) * tall)
            acc_ref[part, :] = acc_ref[part, :] * shrink[h] + sums[h]
        return tuple(new)

    tops = (jnp.full((1, width), START, F32),) * heads
    tops = lax.fori_loop(spans_[0], spans_[1], functools.partial(step, False), tops)
    tops = lax.fori_loop(spans_[2], spans_[3], functools.partial(step, True), tops)
    for h in ids:
        total = acc_ref[h * tall + HEAD : h * tall + HEAD + 1, :]
        out = (acc_ref[h * tall : h * tall + HEAD, :] / total).astype(BF)
        each = o_ref.shape[2]
        for i in range(width // each):
            o_ref[i, h * HEAD : (h + 1) * HEAD, :] = out[:, i * each : (i + 1) * each]
        lse_ref[h : h + 1, :] = tops[h] + jnp.log2(total)


def attend(info, q, k_rows, v, seg_row, seg_col):
    local, rows = q.shape
    heads = local // HEAD
    return pl.pallas_call(
        attend_kernel,
        grid_spec=pltpu.PrefetchScalarGridSpec(
            num_scalar_prefetch=1,
            grid=(rows // QUERIES,),
            in_specs=[
                pl.BlockSpec((local, QUERIES), lambda i, info: (0, i)),
                pl.BlockSpec((heads, rows, HEAD), lambda i, info: (0, 0, 0)),
                pl.BlockSpec(v.shape, lambda i, info: (0, 0)),
                pl.BlockSpec((1, QUERIES), lambda i, info: (0, i)),
                pl.BlockSpec((rows, 1), lambda i, info: (0, 0)),
            ],
            out_specs=[
                pl.BlockSpec((QUERIES // BLOCK, local, BLOCK), lambda i, info: (i, 0, 0)),
                pl.BlockSpec((heads, QUERIES), lambda i, info: (0, i)),
            ],
            scratch_shapes=[pltpu.VMEM((v.shape[0], QUERIES), F32)],
        ),
        out_shape=[
            jax.ShapeDtypeStruct((rows // BLOCK, local, BLOCK), BF),
            jax.ShapeDtypeStruct((heads, rows), F32),
        ],
        compiler_params=pltpu.CompilerParams(vmem_limit_bytes=VMEM_LIMIT),
        cost_estimate=pl.CostEstimate(
            flops=2 * 2 * rows * rows * 256 * heads // 2,
            bytes_accessed=8 << 20,
            transcendentals=heads * rows * rows // 2,
        ),
        name="attend",
    )(info, q, k_rows, v, seg_row, seg_col)


def unturn(grad, cosine, sine):
    first = grad[:HALF]
    second = grad[HALF:]
    return jnp.concatenate(
        [first * cosine + second * sine, second * cosine - first * sine], 0
    ).astype(BF)


def attend_back_kernel(
    info,
    q_ref,
    krow_ref,
    k_ref,
    vrow_ref,
    o_ref,
    do_ref,
    lse_ref,
    segrow_ref,
    segcol_ref,
    cos_ref,
    sin_ref,
    out_ref,
    dq_ref,
    dk_ref,
    dv_ref,
):
    index = pl.program_id(0)
    heads, rows, _ = krow_ref.shape
    width = heads * HEAD
    parts, _, share = out_ref.shape
    each = share // BLOCK
    ids = range(heads)
    part = [slice(h * HEAD, (h + 1) * HEAD) for h in ids]

    @pl.when(index == 0)
    def _():
        dk_ref[...] = jnp.zeros_like(dk_ref)
        dv_ref[...] = jnp.zeros_like(dv_ref)

    dq_ref[...] = jnp.zeros_like(dq_ref)
    segrow = segrow_ref[...]
    delta = [
        jnp.sum(do_ref[0, p, :].astype(F32) * o_ref[0, p, :].astype(F32), 0, keepdims=True)
        for p in part
    ]
    spans_ = visible(info, index, 1, KEYS // BLOCK, rows // KEYS)

    def step(masked, j, carry):
        keys = pl.ds(pl.multiple_of(j * KEYS, KEYS), KEYS)
        scores = [mm(krow_ref[h, keys, :], q_ref[part[h], :], 1, 0) for h in ids]
        grad_soft = [mm(vrow_ref[h, keys, :], do_ref[0, part[h], :], 1, 0) for h in ids]
        if masked:
            same = segcol_ref[keys, :] == segrow
            scores = [jnp.where(same, s, NEGATIVE) for s in scores]
        soft = [jnp.exp2(scores[h] - lse_ref[h : h + 1, :]) for h in ids]
        grad_scores = [(soft[h] * (grad_soft[h] - delta[h])).astype(BF) for h in ids]
        soft = [s.astype(BF) for s in soft]
        dv = [mm(do_ref[0, part[h], :], soft[h], 1, 1) for h in ids]
        dk = [mm(q_ref[part[h], :], grad_scores[h], 1, 1) for h in ids]
        dq = [mm(k_ref[part[h], keys], grad_scores[h], 1, 0) for h in ids]
        for h in ids:
            dv_ref[part[h], keys] += dv[h]
            dk_ref[part[h], keys] += dk[h]
            dq_ref[part[h], :] += dq[h]
        return carry

    lax.fori_loop(spans_[0], spans_[1], functools.partial(step, False), 0)
    lax.fori_loop(spans_[2], spans_[3], functools.partial(step, True), 0)

    owner = index // each
    columns = pl.ds(pl.multiple_of(index * BLOCK, BLOCK), BLOCK)
    inside = pl.ds(pl.multiple_of(index % each * BLOCK, BLOCK), BLOCK)
    for h in ids:
        out_ref[owner, part[h], inside] = unturn(
            dq_ref[part[h], :] * HEAD ** (-0.5), cos_ref[:, columns], sin_ref[:, columns]
        )

    @pl.when(index == pl.num_programs(0) - 1)
    def _():
        @pl.loop(0, parts)
        def _(j):
            columns = pl.ds(pl.multiple_of(j * share, share), share)
            for h in ids:
                base = width + h * HEAD
                out_ref[j, base : base + HEAD, :] = unturn(
                    dk_ref[part[h], columns] * LOG_2, cos_ref[:, columns], sin_ref[:, columns]
                )
                base = 2 * width + h * HEAD
                out_ref[j, base : base + HEAD, :] = dv_ref[part[h], columns].astype(BF)


def attend_back(info, q, k_rows, k, v_rows, o, do, lse, seg_row, seg_col, cosine, sine):
    parts = do.shape[0]
    local, rows = q.shape
    heads = local // HEAD
    blocks = rows // BLOCK
    each = blocks // parts
    whole = lambda *shape: pl.BlockSpec(shape, lambda i, info: (0,) * len(shape))
    return pl.pallas_call(
        attend_back_kernel,
        grid_spec=pltpu.PrefetchScalarGridSpec(
            num_scalar_prefetch=1,
            grid=(blocks,),
            in_specs=[
                pl.BlockSpec((local, BLOCK), lambda i, info: (0, i)),
                whole(heads, rows, HEAD),
                whole(local, rows),
                whole(heads, rows, HEAD),
                pl.BlockSpec((1, local, BLOCK), lambda i, info: (i, 0, 0)),
                pl.BlockSpec(
                    (1, local, BLOCK),
                    lambda i, info: (jnp.bitwise_xor(i // each, info[2]), 0, i % each),
                ),
                pl.BlockSpec((heads, BLOCK), lambda i, info: (0, i)),
                pl.BlockSpec((1, BLOCK), lambda i, info: (0, i)),
                whole(rows, 1),
                whole(HALF, rows),
                whole(HALF, rows),
            ],
            out_specs=whole(parts, 3 * local, rows // parts),
            scratch_shapes=[
                pltpu.VMEM((local, BLOCK), F32),
                pltpu.VMEM((local, rows), F32),
                pltpu.VMEM((local, rows), F32),
            ],
        ),
        out_shape=jax.ShapeDtypeStruct((parts, 3 * local, rows // parts), BF),
        compiler_params=pltpu.CompilerParams(vmem_limit_bytes=VMEM_LIMIT),
        cost_estimate=pl.CostEstimate(
            flops=2 * 5 * rows * rows * 256 * heads // 2,
            bytes_accessed=16 << 20,
            transcendentals=heads * rows * rows // 2,
        ),
        name="attend_back",
    )(info, q, k_rows, k, v_rows, o, do, lse, seg_row, seg_col, cosine, sine)


def project_back_kernel(me_ref, d_ref, x_ref, w_ref, back_ref, grad_ref, acc_ref):
    index = pl.program_id(0)

    @pl.when(index == 0)
    def _():
        acc_ref[...] = jnp.zeros_like(acc_ref)

    d_t = d_ref[0]
    back_ref[0] = mm(d_t, w_ref[...], 0, 0).astype(BF)
    acc_ref[...] += mm(d_t, x_ref[0], 1, 0)

    @pl.when(index == pl.num_programs(0) - 1)
    def _():
        grad_ref[...] = acc_ref[...].T.astype(BF)


def project_back(d_qkv_t, x_rel, w_t, me):
    parts, local, share = d_qkv_t.shape
    width = w_t.shape[1]
    relative = lambda i, me: (jnp.bitwise_xor(i, me[0]), 0, 0)
    return pl.pallas_call(
        project_back_kernel,
        grid_spec=pltpu.PrefetchScalarGridSpec(
            num_scalar_prefetch=1,
            grid=(parts,),
            in_specs=[
                pl.BlockSpec((1, local, share), lambda i, me: (i, 0, 0)),
                pl.BlockSpec((1, share, width), relative),
                pl.BlockSpec((local, width), lambda i, me: (0, 0)),
            ],
            out_specs=[
                pl.BlockSpec((1, share, width), relative),
                pl.BlockSpec((width, local), lambda i, me: (0, 0)),
            ],
            scratch_shapes=[pltpu.VMEM((local, width), F32)],
        ),
        out_shape=[
            jax.ShapeDtypeStruct((parts, share, width), BF),
            jax.ShapeDtypeStruct((width, local), BF),
        ],
        compiler_params=pltpu.CompilerParams(vmem_limit_bytes=VMEM_LIMIT),
        cost_estimate=pl.CostEstimate(
            flops=4 * parts * share * local * width, bytes_accessed=15 << 20, transcendentals=0
        ),
        name="project_back",
    )(me, d_qkv_t, x_rel, w_t)


MESH = pl.DeviceIdType.MESH


def greet(groups, steps, d, t):
    barrier = pltpu.get_barrier_semaphore()
    for k in range(1, groups):
        pl.semaphore_signal(
            barrier, inc=1, device_id=(lax.rem(d + k, groups), t), device_id_type=MESH
        )
    for step in steps:
        pl.semaphore_signal(
            barrier, inc=1, device_id=(d, jnp.bitwise_xor(t, step)), device_id_type=MESH
        )
    pl.semaphore_wait(barrier, groups - 1 + len(steps))


def remote(src, dst, send, recv, device):
    return pltpu.make_async_remote_copy(
        src_ref=src,
        dst_ref=dst,
        send_sem=send,
        recv_sem=recv,
        device_id=device,
        device_id_type=MESH,
    )


class Spread:
    def __init__(self, out, sems, groups, d, t):
        self.out, self.sems, self.groups, self.d, self.t = out, sems, groups, d, t

    def at(self, r, k, rest):
        return self.out.at[(r, lax.rem(self.d - k + self.groups, self.groups)) + rest]

    def arrival(self, source, k, rest, where):
        send, recv = self.sems
        to = lax.rem(self.d + k, self.groups)
        return remote(
            source, self.at(0, 0, rest), send.at[(0, k) + where], recv.at[(0, k) + where], (to, self.t)
        )

    def across(self, k, rest, where):
        send, recv = self.sems
        return remote(
            self.at(0, k, rest),
            self.at(2, k, rest),
            send.at[(2, k) + where],
            recv.at[(2, k) + where],
            (self.d, jnp.bitwise_xor(self.t, 2)),
        )

    def beside(self, r, k, rest, where):
        send, recv = self.sems
        return remote(
            self.at(r, k, rest),
            self.at(r + 1, k, rest),
            send.at[(r + 1, k) + where],
            recv.at[(r + 1, k) + where],
            (self.d, jnp.bitwise_xor(self.t, 1)),
        )


def norm_forward(resid_rows, gain_vec, shift_vec):
    row_mean = jnp.mean(resid_rows, -1, keepdims=True)
    centred = resid_rows - row_mean
    inverse = lax.rsqrt(jnp.mean(centred * centred, -1, keepdims=True) + EPSILON)
    unit_rows = centred * inverse
    return (unit_rows * gain_vec + shift_vec, unit_rows, inverse)


def norm_backward(upstream, unit_rows, inverse, gain_vec):
    scaled = upstream * gain_vec
    inner_term = (
        scaled
        - jnp.mean(scaled, -1, keepdims=True)
        - unit_rows * jnp.mean(scaled * unit_rows, -1, keepdims=True)
    )
    return (
        inner_term * inverse,
        jnp.sum(upstream * unit_rows, 0, keepdims=True),
        jnp.sum(upstream, 0, keepdims=True),
    )


def middle_kernel(size, *refs):
    x_ref, cot_ref, norm_ref = refs[:3]
    blocks_ref = refs[3]
    out_hbm, gu_hbm, down_hbm = (refs[4 + i * size : 4 + (i + 1) * size] for i in range(3))
    (
        result_ref,
        grad_one_ref,
        d_heads_ref,
        heads_ref,
        normed_t_ref,
        d_branch_t_ref,
        d_attn_t_ref,
        hidden_ref,
        d_gu_ref,
        norm_grad_ref,
        w_out_ref,
        w_gu_ref,
        w_down_ref,
        slope_ref,
        swish_ref,
        arrived_ref,
        sems,
        sends,
        recvs,
        keep,
    ) = refs[4 + 3 * size :]
    index = pl.program_id(0)
    first = index == 0
    d = lax.axis_index("dp")
    t = lax.axis_index("tensor")
    subs, local, _ = arrived_ref.shape[1:]
    inner = down_hbm[0].shape[1]
    ids = range(size)
    part = [slice(r * local, (r + 1) * local) for r in ids]
    copies_out = [
        pltpu.make_async_copy(out_hbm[r], w_out_ref.at[part[r]], sems.at[0, r]) for r in ids
    ]
    copies_gu = [pltpu.make_async_copy(gu_hbm[r], w_gu_ref.at[r], sems.at[1, r]) for r in ids]
    copies_down = [
        pltpu.make_async_copy(down_hbm[r], w_down_ref.at[r], sems.at[2, r]) for r in ids
    ]

    def heads_copy(r, i):
        other = jnp.bitwise_xor(t, r)
        return remote(
            blocks_ref.at[other * subs + i],
            arrived_ref.at[r, i],
            sends.at[r, i],
            recvs.at[r, i],
            (d, other),
        )

    own_copy = pltpu.make_async_copy(blocks_ref.at[pl.ds(t * subs, subs)], arrived_ref.at[0], keep)

    @pl.when(first)
    def _():
        own_copy.start()
        for copy in copies_out:
            copy.start()
        greet(1, (1, 2, 3), d, t)
        for i in range(subs):
            for r in (2, 3, 1):
                heads_copy(r, i).start()
        own_copy.wait()
        for r in ids:
            copies_gu[r].start()
            copies_down[r].start()
        for copy in copies_out:
            copy.wait()

    for r in ids[1:]:
        heads_copy(r, index).wait_recv()
        heads_copy(r, index).wait_send()
    for r in ids:
        heads_ref[r] = arrived_ref[r, index]
    heads_out = jnp.concatenate([arrived_ref[r, index] for r in ids], 0)
    attn = mm(heads_out, w_out_ref[...], 0, 0)
    gain_one, gain_two, shift_one, shift_two = (norm_ref[i : i + 1, :] for i in range(4))
    normed_one, unit_one, inverse_one = norm_forward(
        x_ref[...].astype(F32) + attn, gain_one, shift_one
    )
    normed = normed_one.astype(BF)
    normed_t_ref[...] = normed_one.T.astype(BF)
    branch = jnp.zeros(normed_one.shape, F32)
    for r in ids:

        @pl.when(first)
        def _():
            copies_gu[r].wait()
            copies_down[r].wait()

        both = mm(normed, w_gu_ref[r], 1, 0)
        gate = both[:, :inner]
        up = both[:, inner:]
        sig = jax.nn.sigmoid(gate)
        swish = gate * sig
        hidden = (swish * up).astype(BF)
        swish_ref[r] = swish
        slope_ref[r] = up * sig * (1.0 + gate * (1.0 - sig))
        hidden_ref[r] = hidden
        branch = branch + mm(hidden, w_down_ref[r], 1, 1)
    result, unit_two, inverse_two = norm_forward(normed_one + branch, gain_two, shift_two)
    result_ref[...] = result.astype(BF)
    grad_two, d_gain_two, d_shift_two = norm_backward(
        cot_ref[...].astype(F32), unit_two, inverse_two, gain_two
    )
    d_branch = grad_two.astype(BF)
    d_branch_t_ref[...] = grad_two.T.astype(BF)
    back = grad_two
    for r in ids:
        grad_hidden = mm(d_branch, w_down_ref[r], 1, 0)
        d_gate = (grad_hidden * slope_ref[r]).astype(BF)
        d_up = (grad_hidden * swish_ref[r]).astype(BF)
        d_gu_ref[r, :, :inner] = d_gate
        d_gu_ref[r, :, inner:] = d_up
        back = back + mm(jnp.concatenate([d_gate, d_up], 1), w_gu_ref[r], 1, 1)
    grad_one, d_gain_one, d_shift_one = norm_backward(back, unit_one, inverse_one, gain_one)
    grad_one_ref[...] = grad_one
    d_attn_t = grad_one.T.astype(BF)
    d_attn_t_ref[...] = d_attn_t
    d_heads = mm(w_out_ref[...], d_attn_t, 1, 0).astype(BF)
    for r in ids:
        d_heads_ref[r] = d_heads[part[r]]

    @pl.when(first)
    def _():
        norm_grad_ref[...] = jnp.zeros_like(norm_grad_ref)

    for i, grad in enumerate((d_gain_one, d_gain_two, d_shift_one, d_shift_two)):
        norm_grad_ref[i : i + 1, :] += grad


def middle(x_own, cot_own, norms, o_blocks, w_out_parts, gu_parts, down_parts):
    rows, width = x_own.shape
    size = len(gu_parts)
    local = o_blocks.shape[1]
    inner = down_parts[0].shape[1]
    block = pl.BlockSpec((BLOCK, width), lambda i: (i, 0))
    turned = pl.BlockSpec((width, BLOCK), lambda i: (0, i))
    anywhere = pl.BlockSpec(memory_space=pl.ANY)
    shape = jax.ShapeDtypeStruct
    return pl.pallas_call(
        functools.partial(middle_kernel, size),
        grid=(rows // BLOCK,),
        in_specs=[block, block, pl.BlockSpec(norms.shape, lambda i: (0, 0))]
        + [anywhere] * (1 + 3 * size),
        out_specs=[
            block,
            block,
            pl.BlockSpec((size, local, BLOCK), lambda i: (0, 0, i)),
            pl.BlockSpec((size, local, BLOCK), lambda i: (0, 0, i)),
            turned,
            turned,
            turned,
            pl.BlockSpec((size, BLOCK, inner), lambda i: (0, i, 0)),
            pl.BlockSpec((size, BLOCK, 2 * inner), lambda i: (0, i, 0)),
            pl.BlockSpec((8, width), lambda i: (0, 0)),
        ],
        out_shape=[
            shape((rows, width), BF),
            shape((rows, width), F32),
            shape((size, local, rows), BF),
            shape((size, local, rows), BF),
            shape((width, rows), BF),
            shape((width, rows), BF),
            shape((width, rows), BF),
            shape((size, rows, inner), BF),
            shape((size, rows, 2 * inner), BF),
            shape((8, width), F32),
        ],
        scratch_shapes=[
            pltpu.VMEM((size * local, width), BF),
            pltpu.VMEM((size, width, 2 * inner), BF),
            pltpu.VMEM((size, width, inner), BF),
            pltpu.VMEM((size, BLOCK, inner), F32),
            pltpu.VMEM((size, BLOCK, inner), F32),
            pltpu.VMEM((size, rows // BLOCK, local, BLOCK), BF),
            pltpu.SemaphoreType.DMA((3, size)),
            pltpu.SemaphoreType.DMA((size, rows // BLOCK)),
            pltpu.SemaphoreType.DMA((size, rows // BLOCK)),
            pltpu.SemaphoreType.DMA,
        ],
        compiler_params=pltpu.CompilerParams(
            collective_id=2, has_side_effects=True, vmem_limit_bytes=VMEM_LIMIT
        ),
        cost_estimate=pl.CostEstimate(
            flops=2 * rows * width * (6 * size * inner + 2 * size * local),
            bytes_accessed=40 << 20,
            transcendentals=rows * size * inner,
        ),
        name="middle",
    )(x_own, cot_own, norms, o_blocks, *w_out_parts, *gu_parts, *down_parts)


def weight_grads_tile(
    normed_t_ref, d_branch_t_ref, d_attn_t_ref, hidden_ref, d_gu_ref, heads_ref, norm_ref, store
):
    inner = hidden_ref.shape[2]
    local = heads_ref.shape[1]
    width = normed_t_ref.shape[0]
    store(0, 2 * inner, mm(normed_t_ref[...], d_gu_ref[0], 1, 0))
    store(2 * inner, 3 * inner, mm(d_branch_t_ref[...], hidden_ref[0], 1, 0))
    d_out = mm(d_attn_t_ref[...], heads_ref[0], 1, 1)
    norm = norm_ref[...].T
    spare = -(local + norm.shape[1]) % 128
    tail = jnp.concatenate([d_out, norm, jnp.zeros((width, spare), F32)], 1)
    store(3 * inner, 3 * inner + tail.shape[1], tail)


def weight_grads_kernel(*refs):
    out_ref = refs[-1]

    def store(low, high, value):
        out_ref[0, :, low:high] = value.astype(BF)

    weight_grads_tile(*refs[:-1], store)


def weight_grads(odd, normed_t, d_branch_t, d_attn_t, hidden, d_gu, heads, norm_grads):
    size, rows, inner = hidden.shape
    local = heads.shape[1]
    width = normed_t.shape[0]
    wide = 3 * inner + local + norm_grads.shape[0]
    wide = (wide + 127) // 128 * 128
    flat = pl.BlockSpec((width, rows), lambda i: (0, 0))
    pick = lambda i: (2 * i + odd, 0, 0)
    return pl.pallas_call(
        weight_grads_kernel,
        grid=(size // 2,),
        in_specs=[
            flat,
            flat,
            flat,
            pl.BlockSpec((1, rows, inner), pick),
            pl.BlockSpec((1, rows, 2 * inner), pick),
            pl.BlockSpec((1, local, rows), pick),
            pl.BlockSpec(norm_grads.shape, lambda i: (0, 0)),
        ],
        out_specs=pl.BlockSpec((1, width, wide), lambda i: (i, 0, 0)),
        out_shape=jax.ShapeDtypeStruct((size // 2, width, wide), BF),
        compiler_params=pltpu.CompilerParams(vmem_limit_bytes=VMEM_LIMIT),
        cost_estimate=pl.CostEstimate(
            flops=size * rows * width * (3 * inner + local), bytes_accessed=20 << 20, transcendentals=0
        ),
        name="weight_grads",
    )(normed_t, d_branch_t, d_attn_t, hidden, d_gu, heads, norm_grads)


def grads_kernel(groups, size, match_ref, *refs):
    tile_refs = refs[:7]
    (
        d_heads_ref,
        result_ref,
        pair_ref,
        do_ref,
        home_ref,
        over_ref,
        sent_ref,
        got_ref,
        own_ref,
        spare_ref,
        s_grad,
        r_grad,
        s_heads,
        r_heads,
        sends,
        recvs,
        s_over,
        r_over,
        keep,
    ) = refs[7:]
    step = pl.program_id(0)
    d = lax.axis_index("dp")
    t = lax.axis_index("tensor")
    chunks, _, sub, width = own_ref.shape
    core = (d, jnp.bitwise_xor(t, 1))
    body = Spread(home_ref, (sends, recvs), groups, d, t)
    extra = Spread(over_ref, (s_over, r_over), groups, d, t)

    def heads_copy(r):
        return remote(
            d_heads_ref.at[r],
            do_ref.at[r],
            s_heads.at[r],
            r_heads.at[r],
            (d, jnp.bitwise_xor(t, r)),
        )

    def grad_copy(i):
        return remote(sent_ref.at[i], got_ref.at[i], s_grad.at[i], r_grad.at[i], core)

    def own_copy(c):
        return pltpu.make_async_copy(own_ref.at[c, d], home_ref.at[0, d, c], keep.at[c])

    load = pltpu.make_async_copy(result_ref, own_ref, keep.at[chunks])
    own_heads = pltpu.make_async_copy(d_heads_ref.at[0], do_ref.at[0], keep.at[chunks + 1])
    own_over = pltpu.make_async_copy(spare_ref.at[d], over_ref.at[0, d], keep.at[chunks + 2])

    def pass_on(c):
        own_copy(c).wait()
        for k in range(groups):
            if k > 0:
                body.arrival(own_ref.at[c, 0], k, (c,), (c,)).wait_recv()
            body.across(k, (c,), (c,)).start()
            body.beside(0, k, (c,), (c,)).start()

    def pass_far(c):
        for k in range(groups):
            body.across(k, (c,), (c,)).wait_recv()
            body.beside(2, k, (c,), (c,)).start()

    @pl.when(step == 0)
    def _():
        load.start()
        own_heads.start()
        greet(groups, (1, 2, 3), d, t)
        for r in (2, 3, 1):
            heads_copy(r).start()
        load.wait()
        for c in range(chunks):
            own_copy(c).start()
            for k in range(1, groups):
                body.arrival(own_ref.at[c, lax.rem(d + k, groups)], k, (c,), (c,)).start()
        last = [own_ref[chunks - 1, g, sub - 16 :, :].astype(F32)[15:16] for g in range(groups)]
        for to in range(groups):
            spare = last[0] * match_ref[to]
            for g in range(1, groups):
                spare = spare + last[g] * match_ref[g * groups + to]
            spare_ref[to] = spare.astype(BF)
        own_over.start()
        for k in range(1, groups):
            extra.arrival(spare_ref.at[lax.rem(d + k, groups)], k, (), ()).start()

    for c in range(2):

        @pl.when(step == c + 2)
        def _():
            pass_on(c)

    @pl.when(step < 2)
    def _():
        def store(low, high, value):
            sent_ref[step, :, low:high] = value.astype(BF)

        weight_grads_tile(*tile_refs, store)
        grad_copy(step).start()

    @pl.when(step >= 2)
    def _():
        grad_copy(step - 2).wait_recv()

        def store(low, high, value):
            other = got_ref[step - 2, :, low:high].astype(F32)
            pair_ref[0, :, low:high] = (value + other).astype(BF)

        weight_grads_tile(*tile_refs, store)

    @pl.when(step == size - 1)
    def _():
        for c in range(2, chunks):
            pass_on(c)
        own_over.wait()
        for k in range(groups):
            if k > 0:
                extra.arrival(spare_ref.at[0], k, (), ()).wait_recv()
            extra.across(k, (), ()).start()
            extra.beside(0, k, (), ()).start()
        for c in range(chunks):
            pass_far(c)
        for k in range(groups):
            extra.across(k, (), ()).wait_recv()
            extra.beside(2, k, (), ()).start()
        own_heads.wait()
        for r in range(1, size):
            heads_copy(r).wait_recv()
            heads_copy(r).wait_send()
        for i in range(2):
            grad_copy(i).wait_send()
        for k in range(groups):
            for c in range(chunks):
                body.beside(0, k, (c,), (c,)).wait_recv()
                body.beside(2, k, (c,), (c,)).wait_recv()
                if k > 0:
                    body.arrival(own_ref.at[c, 0], k, (c,), (c,)).wait_send()
                body.across(k, (c,), (c,)).wait_send()
                body.beside(0, k, (c,), (c,)).wait_send()
                body.beside(2, k, (c,), (c,)).wait_send()
            extra.beside(0, k, (), ()).wait_recv()
            extra.beside(2, k, (), ()).wait_recv()
            if k > 0:
                extra.arrival(spare_ref.at[0], k, (), ()).wait_send()
            extra.across(k, (), ()).wait_send()
            extra.beside(0, k, (), ()).wait_send()
            extra.beside(2, k, (), ()).wait_send()


def grads(
    match, groups, normed_t, d_branch_t, d_attn_t, hidden, d_gu, heads, norm_grads, d_heads, result
):
    size, rows, inner = hidden.shape
    local = heads.shape[1]
    width = normed_t.shape[0]
    chunks = rows // BLOCK
    sub = BLOCK // groups
    wide = 3 * inner + (local + norm_grads.shape[0] + 127) // 128 * 128
    flat = pl.BlockSpec((width, rows), lambda i: (0, 0))
    pick = lambda i: (jnp.where(i < 2, 2 * i + 1, 2 * i - 4), 0, 0)
    anywhere = pl.BlockSpec(memory_space=pl.ANY)
    dma = pltpu.SemaphoreType.DMA
    return pl.pallas_call(
        functools.partial(grads_kernel, groups, size),
        grid=(size,),
        in_specs=[
            pl.BlockSpec(memory_space=pltpu.SMEM),
            flat,
            flat,
            flat,
            pl.BlockSpec((1, rows, inner), pick),
            pl.BlockSpec((1, rows, 2 * inner), pick),
            pl.BlockSpec((1, local, rows), pick),
            pl.BlockSpec(norm_grads.shape, lambda i: (0, 0)),
            anywhere,
            anywhere,
        ],
        out_specs=[
            pl.BlockSpec((1, width, wide), lambda i: (jnp.maximum(i - 2, 0), 0, 0)),
            anywhere,
            anywhere,
            anywhere,
        ],
        out_shape=[
            jax.ShapeDtypeStruct((2, width, wide), BF),
            jax.ShapeDtypeStruct(d_heads.shape, BF),
            jax.ShapeDtypeStruct((size, groups, chunks, sub, width), BF),
            jax.ShapeDtypeStruct((size, groups, 1, width), BF),
        ],
        scratch_shapes=[
            pltpu.VMEM((2, width, wide), BF),
            pltpu.VMEM((2, width, wide), BF),
            pltpu.VMEM((chunks, groups, sub, width), BF),
            pltpu.VMEM((groups, 1, width), BF),
            dma((2,)),
            dma((2,)),
            dma((size,)),
            dma((size,)),
            dma((4, groups, chunks)),
            dma((4, groups, chunks)),
            dma((4, groups)),
            dma((4, groups)),
            dma((chunks + 3,)),
        ],
        compiler_params=pltpu.CompilerParams(
            collective_id=3, has_side_effects=True, vmem_limit_bytes=VMEM_LIMIT
        ),
        cost_estimate=pl.CostEstimate(
            flops=2 * size * rows * width * (3 * inner + local),
            bytes_accessed=80 << 20,
            transcendentals=0,
        ),
        name="grads",
    )(
        match,
        normed_t,
        d_branch_t,
        d_attn_t,
        hidden,
        d_gu,
        heads,
        norm_grads,
        d_heads,
        result.reshape(chunks, groups, sub, width),
    )


def swap(array, size, step):
    return lax.ppermute(array, "tensor", [(i, i ^ step) for i in range(size)])


def gather_members(own):
    size = lax.axis_size("tensor")
    across = swap(own, size, 2)
    return [own, swap(own, size, 1), across, swap(across, size, 1)]


def exchange_members(pieces):
    size = lax.axis_size("tensor")
    return [pieces[0]] + [swap(pieces[r], size, r) for r in range(1, size)]


def reduce_members(pieces):
    size = lax.axis_size("tensor")
    near = swap(pieces[1], size, 1)
    far = swap(pieces[3], size, 1)
    other = (pieces[2].astype(F32) + far.astype(F32)).astype(BF)
    across = swap(other, size, 2)
    return pieces[0].astype(F32) + near.astype(F32) + across.astype(F32)


def route_kernel(groups, size, send_ref, over_ref, out_ref, over_out_ref, sends, recvs, keep):
    d = lax.axis_index("dp")
    t = lax.axis_index("tensor")
    greet(groups, (1, 2), d, t)
    spread = Spread(out_ref, (sends, recvs), groups, d, t)
    own = pltpu.make_async_copy(send_ref.at[d], out_ref.at[0, d], keep.at[0])
    own_over = pltpu.make_async_copy(over_ref.at[d], over_out_ref.at[d], keep.at[1])
    own.start()
    own_over.start()

    def over_copy(k):
        to = lax.rem(d + k, groups)
        return remote(
            over_ref.at[to], over_out_ref.at[d], sends.at[4, k], recvs.at[4, k], (to, t)
        )

    for k in range(1, groups):
        spread.arrival(send_ref.at[lax.rem(d + k, groups)], k, (), ()).start()
    for k in range(1, groups):
        over_copy(k).start()
    own.wait()
    for k in range(groups):
        if k > 0:
            spread.arrival(send_ref.at[0], k, (), ()).wait_recv()
        spread.across(k, (), ()).start()
        spread.beside(0, k, (), ()).start()
        if k > 0:
            spread.across(k - 1, (), ()).wait_recv()
            spread.beside(2, k - 1, (), ()).start()
    spread.across(groups - 1, (), ()).wait_recv()
    spread.beside(2, groups - 1, (), ()).start()
    own_over.wait()
    for k in range(groups):
        spread.beside(0, k, (), ()).wait_recv()
        spread.beside(2, k, (), ()).wait_recv()
        if k > 0:
            over_copy(k).wait_recv()
            over_copy(k).wait_send()
            spread.arrival(send_ref.at[0], k, (), ()).wait_send()
        spread.across(k, (), ()).wait_send()
        spread.beside(0, k, (), ()).wait_send()
        spread.beside(2, k, (), ()).wait_send()


def route(send, over, size):
    groups = send.shape[0]
    anywhere = pl.BlockSpec(memory_space=pl.ANY)
    return pl.pallas_call(
        functools.partial(route_kernel, groups, size),
        in_specs=[anywhere, anywhere],
        out_specs=[anywhere, anywhere],
        out_shape=[
            jax.ShapeDtypeStruct((size,) + send.shape, BF),
            jax.ShapeDtypeStruct(over.shape, BF),
        ],
        scratch_shapes=[
            pltpu.SemaphoreType.DMA((5, groups)),
            pltpu.SemaphoreType.DMA((5, groups)),
            pltpu.SemaphoreType.DMA((2,)),
        ],
        compiler_params=pltpu.CompilerParams(collective_id=0, has_side_effects=True),
        cost_estimate=pl.CostEstimate(flops=0, bytes_accessed=60 << 20, transcendentals=0),
        name="route",
    )(send, over)


def settle_kernel(
    groups,
    size,
    match_ref,
    back_ref,
    one_ref,
    gq_ref,
    home_ref,
    over_ref,
    sum_ref,
    far_ref,
    near_ref,
    pair_ref,
    other_ref,
    own_ref,
    spare_ref,
    gqr_ref,
    sends,
    recvs,
    s_over,
    r_over,
    s_sum,
    r_sum,
    s_gq,
    r_gq,
    keep,
):
    d = lax.axis_index("dp")
    t = lax.axis_index("tensor")
    chunks, _, sub, width = own_ref.shape
    greet(groups, (1, 2), d, t)
    core = (d, jnp.bitwise_xor(t, 1))
    chip = (d, jnp.bitwise_xor(t, 2))

    def rows(c):
        return pl.ds(c * BLOCK, BLOCK)

    def far(c):
        return remote(back_ref.at[3, rows(c)], far_ref.at[c], s_sum.at[0, c], r_sum.at[0, c], core)

    def near(c):
        return remote(back_ref.at[1, rows(c)], near_ref.at[c], s_sum.at[1, c], r_sum.at[1, c], core)

    def other(c):
        return remote(pair_ref.at[c], other_ref.at[c], s_sum.at[2, c], r_sum.at[2, c], chip)

    def gq(k):
        to = lax.rem(d + k, groups)
        return remote(gq_ref.at[to], gqr_ref.at[d], s_gq.at[k], r_gq.at[k], (to, t))

    for c in range(chunks):
        far(c).start()
    for c in range(chunks):
        near(c).start()
    for c in range(chunks):
        far(c).wait_recv()
        pair = back_ref[2, rows(c), :].astype(F32) + far_ref[c].astype(F32)
        pair_ref[c] = pair.astype(BF)
        other(c).start()
    own_gq = pltpu.make_async_copy(gq_ref.at[d], gqr_ref.at[d], keep.at[chunks])
    own_gq.start()

    body = Spread(home_ref, (sends, recvs), groups, d, t)
    extra = Spread(over_ref, (s_over, r_over), groups, d, t)

    def own_copy(c):
        return pltpu.make_async_copy(own_ref.at[c, d], home_ref.at[0, d, c], keep.at[c])

    own_over = pltpu.make_async_copy(spare_ref.at[d], over_ref.at[0, d], keep.at[chunks + 1])

    def pass_on(c):
        own_copy(c).wait()
        for k in range(groups):
            if k > 0:
                body.arrival(own_ref.at[c, 0], k, (c,), (c,)).wait_recv()
            body.across(k, (c,), (c,)).start()
            body.beside(0, k, (c,), (c,)).start()

    def pass_far(c):
        for k in range(groups):
            body.across(k, (c,), (c,)).wait_recv()
            body.beside(2, k, (c,), (c,)).start()

    for c in range(chunks):
        near(c).wait_recv()
        partial = (
            one_ref[rows(c), :] + back_ref[0, rows(c), :].astype(F32) + near_ref[c].astype(F32)
        )
        other(c).wait_recv()
        done = (partial + other_ref[c].astype(F32)).astype(BF)
        for g in range(groups):
            own_ref[c, g] = done[g * sub : (g + 1) * sub]
        own_copy(c).start()
        for k in range(1, groups):
            body.arrival(own_ref.at[c, lax.rem(d + k, groups)], k, (c,), (c,)).start()
        if c == chunks - 1:
            last = [
                own_ref[c, g, sub - 16 :, :].astype(F32)[15:16] for g in range(groups)
            ]
            for to in range(groups):
                spare = last[0] * match_ref[to]
                for g in range(1, groups):
                    spare = spare + last[g] * match_ref[g * groups + to]
                spare_ref[to] = spare.astype(BF)
            own_over.start()
            for k in range(1, groups):
                extra.arrival(spare_ref.at[lax.rem(d + k, groups)], k, (), ()).start()
        if c == 0:
            for k in range(1, groups):
                gq(k).start()
        else:
            pass_on(c - 1)
    pass_on(chunks - 1)
    own_over.wait()
    for k in range(groups):
        if k > 0:
            extra.arrival(spare_ref.at[0], k, (), ()).wait_recv()
        extra.across(k, (), ()).start()
        extra.beside(0, k, (), ()).start()
    own_gq.wait()
    total = gqr_ref[d].astype(F32)
    for k in range(1, groups):
        gq(k).wait_recv()
        total = total + gqr_ref[lax.rem(d - k + groups, groups)].astype(F32)
    sum_ref[...] = total
    for c in range(chunks):
        pass_far(c)
    for k in range(groups):
        extra.across(k, (), ()).wait_recv()
        extra.beside(2, k, (), ()).start()
    for c in range(chunks):
        far(c).wait_send()
        near(c).wait_send()
        other(c).wait_send()
    for k in range(groups):
        for c in range(chunks):
            body.beside(0, k, (c,), (c,)).wait_recv()
            body.beside(2, k, (c,), (c,)).wait_recv()
            if k > 0:
                body.arrival(own_ref.at[c, 0], k, (c,), (c,)).wait_send()
            body.across(k, (c,), (c,)).wait_send()
            body.beside(0, k, (c,), (c,)).wait_send()
            body.beside(2, k, (c,), (c,)).wait_send()
        extra.beside(0, k, (), ()).wait_recv()
        extra.beside(2, k, (), ()).wait_recv()
        if k > 0:
            gq(k).wait_send()
            extra.arrival(spare_ref.at[0], k, (), ()).wait_send()
        extra.across(k, (), ()).wait_send()
        extra.beside(0, k, (), ()).wait_send()
        extra.beside(2, k, (), ()).wait_send()


def settle(match, back_rel, grad_one, grad_qkv):
    size, rows, width = back_rel.shape
    groups, part, local = grad_qkv.shape
    chunks = rows // BLOCK
    sub = BLOCK // groups
    anywhere = pl.BlockSpec(memory_space=pl.ANY)
    vmem = pl.BlockSpec(memory_space=pltpu.VMEM)
    dma = pltpu.SemaphoreType.DMA
    buffer = pltpu.VMEM((chunks, BLOCK, width), BF)
    return pl.pallas_call(
        functools.partial(settle_kernel, groups, size),
        in_specs=[pl.BlockSpec(memory_space=pltpu.SMEM), vmem, vmem, anywhere],
        out_specs=[anywhere, anywhere, vmem],
        out_shape=[
            jax.ShapeDtypeStruct((size, groups, chunks, sub, width), BF),
            jax.ShapeDtypeStruct((size, groups, 1, width), BF),
            jax.ShapeDtypeStruct((part, local), F32),
        ],
        scratch_shapes=[
            buffer,
            buffer,
            buffer,
            buffer,
            pltpu.VMEM((chunks, groups, sub, width), BF),
            pltpu.VMEM((groups, 1, width), BF),
            pltpu.VMEM((groups, part, local), BF),
            dma((4, groups, chunks)),
            dma((4, groups, chunks)),
            dma((4, groups)),
            dma((4, groups)),
            dma((3, chunks)),
            dma((3, chunks)),
            dma((groups,)),
            dma((groups,)),
            dma((chunks + 2,)),
        ],
        compiler_params=pltpu.CompilerParams(
            collective_id=1, has_side_effects=True, vmem_limit_bytes=VMEM_LIMIT
        ),
        cost_estimate=pl.CostEstimate(flops=0, bytes_accessed=150 << 20, transcendentals=0),
        name="settle",
    )(match, back_rel, grad_one, grad_qkv)


ROWS = 32


def unpack_kernel(info, home_ref, over_ref, out_ref, src_ref, dst_ref):
    size, groups, share, _ = home_ref.shape
    rows = out_ref.shape[0]
    slots = size * share
    me = info[0, 0]

    @pl.loop(0, size)
    def _(part):
        source = jnp.bitwise_xor(part, me)
        at = pl.ds(pl.multiple_of(ROWS + part * share, 8), share)
        for g in range(groups):
            src_ref[g, at, :] = home_ref[source, g].astype(F32)

    last = jnp.bitwise_xor(size - 1, me)
    for g in range(groups):
        src_ref[g, ROWS + slots : ROWS + slots + 1, :] = over_ref[last, g].astype(F32)
    row_ids = lax.broadcasted_iota(jnp.int32, (ROWS, 1), 0)

    @pl.loop(0, info.shape[1] - 1)
    def _(j):
        low = info[0, 1 + j]
        count = info[1, 1 + j]
        group = info[2, 1 + j]
        first = info[3, 1 + j]

        @pl.loop(low // ROWS, (low + count + ROWS - 1) // ROWS)
        def _(i):
            start = i * ROWS + first - low + ROWS
            offset = jnp.bitwise_and(start, 7)
            loaded = src_ref[group, pl.ds(pl.multiple_of(start - offset, 8), ROWS + 8), :]
            moved = pltpu.roll(loaded, ROWS + 8 - offset, 0)[:ROWS]
            at = pl.ds(pl.multiple_of(i * ROWS, ROWS), ROWS)
            dst_ref[at, :] = jnp.where(row_ids >= low - i * ROWS, moved, dst_ref[at, :])

    out_ref[...] = dst_ref[:rows, :].astype(BF)


def unpack(info, home, over):
    size, groups, share, width = home.shape
    rows = size * groups * share
    whole = lambda *shape: pl.BlockSpec(shape, lambda i, info: (0,) * len(shape))
    return pl.pallas_call(
        unpack_kernel,
        grid_spec=pltpu.PrefetchScalarGridSpec(
            num_scalar_prefetch=1,
            grid=(1,),
            in_specs=[whole(*home.shape), whole(*over.shape)],
            out_specs=whole(rows, width),
            scratch_shapes=[
                pltpu.VMEM((groups, size * share + 4 * ROWS, width), F32),
                pltpu.VMEM((rows + ROWS, width), F32),
            ],
        ),
        out_shape=jax.ShapeDtypeStruct((rows, width), BF),
        compiler_params=pltpu.CompilerParams(vmem_limit_bytes=VMEM_LIMIT),
        cost_estimate=pl.CostEstimate(flops=0, bytes_accessed=30 << 20, transcendentals=0),
        name="unpack",
    )(info, home, over)


def spans(offset, length, source, groups):
    low = (offset - source + groups - 1) // groups
    high = (offset + length - source + groups - 1) // groups
    return low, high - low


def local(tokens, cotangent, lengths, dealing, w_qkv, w_out, w_gu, w_down, gains, shifts):
    groups = lax.axis_size("dp")
    member = lax.axis_index("dp")
    size = lax.axis_size("tensor")
    me = lax.axis_index("tensor")
    rows = tokens.shape[0]
    width = tokens.shape[2]
    slots = rows // groups
    share = slots // size
    own_rows = rows // size
    subs = own_rows // BLOCK
    sub = share // subs
    i32 = jnp.int32

    seq_count = lengths.shape[0]
    count_up = jnp.arange(seq_count, dtype=i32)
    offsets = jnp.sum(jnp.where(count_up[None, :] < count_up[:, None], lengths[None, :], 0), 1)
    chosen = dealing[:, None] == count_up[None, :]
    dealt_len = jnp.sum(jnp.where(chosen, lengths[None, :], 0), 1).reshape(groups, 2)
    dealt_off = jnp.sum(jnp.where(chosen, offsets[None, :], 0), 1).reshape(groups, 2)
    group_ids = jnp.arange(groups, dtype=i32)

    low_a, count_a = spans(dealt_off[:, 0], dealt_len[:, 0], member, groups)
    low_b, count_b = spans(dealt_off[:, 1], dealt_len[:, 1], member, groups)
    fused = sub % 16 == 0
    body_slots = me * share + jnp.arange(share, dtype=i32)[None, :]

    def pick(slot):
        found = jnp.where(
            slot < count_a[:, None], low_a[:, None] + slot, (low_b - count_a)[:, None] + slot
        )
        return jnp.clip(found, 0, rows - 1).reshape(-1)

    picked = jnp.concatenate([pick(body_slots), pick(jnp.full((1, 1), slots, i32))])

    def pack(array):
        taken = jnp.take(array.reshape(rows, width), picked, axis=0)
        return (
            taken[: groups * share].reshape(groups, share, width),
            taken[groups * share :].reshape(groups, 1, width),
        )

    def over_dp(pair):
        return tuple(
            lax.all_to_all(a, "dp", split_axis=0, concat_axis=0, tiled=True) for a in pair
        )

    send_x = pack(tokens)
    send_c = pack(cotangent)
    far_out, far_down = swap(w_out.T, size, 2), swap(w_down, size, 2)
    if fused:
        recv_x, over_x = route(*send_x, size)
    else:
        recv_x, over_x = over_dp(send_x)
        recv_x = jnp.stack(gather_members(recv_x))
    send_c, recv_x, far_out, far_down = lax.optimization_barrier(
        (send_c, recv_x, far_out, far_down)
    )
    recv_c, over_c = over_dp(send_c)

    mine = group_ids == member
    pick_group = lambda table: jnp.sum(jnp.where(mine[:, None], table, 0), 0)
    my_len = pick_group(dealt_len)
    my_off = pick_group(dealt_off)
    glow_a, gcount_a = spans(my_off[0], my_len[0], group_ids, groups)
    glow_b, gcount_b = spans(my_off[1], my_len[1], group_ids, groups)
    filled = gcount_a + gcount_b
    hole = filled < slots
    over = filled > slots
    before = group_ids[None, :] < group_ids[:, None]
    hole_rank = jnp.sum(jnp.where(before & hole[None, :], 1, 0), 1)
    over_rank = jnp.sum(jnp.where(before & over[None, :], 1, 0), 1)
    match = hole[:, None] & over[None, :] & (hole_rank[:, None] == over_rank[None, :])
    last_token = (glow_b - gcount_a + slots) * groups + group_ids
    hole_token = jnp.sum(jnp.where(match, last_token[None, :], 0), 1)
    match_bf = match.astype(BF)
    relative = jnp.bitwise_xor(jnp.arange(size, dtype=i32), me)

    place_ids = jnp.arange(share, dtype=i32)

    def fill(received, over, last):
        spare = jnp.dot(match_bf, over[:, 0], preferred_element_type=F32).astype(BF)
        fix = last[:, None, None] & (hole[:, None] & (place_ids == share - 1)[None, :])[None]
        body = jnp.where(fix[..., None], spare[None, :, None, :], received)
        body = body.reshape(-1, groups, subs, sub, width).transpose(0, 2, 1, 3, 4)
        return body.reshape(-1, own_rows, width)

    shape = (size * subs, groups, sub)
    block_id = lax.broadcasted_iota(i32, shape, 0)
    source_id = lax.broadcasted_iota(i32, shape, 1)
    slot_id = block_id * sub + lax.broadcasted_iota(i32, shape, 2)
    spread = lambda vec: vec[None, :, None]
    in_a = slot_id < spread(gcount_a)
    token_id = (
        jnp.where(in_a, spread(glow_a), spread(glow_b - gcount_a)) + slot_id
    ) * groups + source_id
    token_id = jnp.where(spread(hole) & (slot_id == slots - 1), spread(hole_token), token_id)
    positions = (token_id - jnp.where(in_a, my_off[0], my_off[1])).reshape(rows)
    segment = jnp.where(in_a, 0, 1).astype(F32).reshape(rows)
    frequency = 1000.0 ** (-(jnp.arange(HALF, dtype=F32) * 2.0) / HEAD)
    angles = frequency[:, None] * positions.astype(F32)[None, :]
    cosine = jnp.cos(angles)
    sine = jnp.sin(angles)
    seg_row = segment[None, :]
    seg_col = segment[:, None]
    first_b = (my_len[0] + BLOCK - 1) // BLOCK
    info = jnp.stack([my_len[0] // BLOCK, first_b, me]).astype(i32)

    x_rel = fill(recv_x, over_x, relative == size - 1)
    x_own = x_rel[0]
    local_width = w_qkv.shape[2]
    w_qkv_t = w_qkv.transpose(1, 2, 0).reshape(3 * local_width, width)
    x_rel, near_gu = lax.optimization_barrier((x_rel, w_gu.reshape(width, -1)))
    far_gu = swap(near_gu, size, 2)
    q, k, v, k_rows, v_rows = project(x_rel, w_qkv_t, cosine, sine, me[None])
    o_blocks, lse = attend(info, q, k_rows, v, seg_row, seg_col)
    o_blocks, far_gu, recv_c = lax.optimization_barrier((o_blocks, far_gu, recv_c))

    spread_parts = lambda near, far: [near, swap(near, size, 1), far, swap(far, size, 1)]
    w_out_parts = spread_parts(w_out.T, far_out)
    down_parts = spread_parts(w_down, far_down)
    gu_parts = spread_parts(near_gu, far_gu)
    cot_own = fill(recv_c[None], over_c, (me == size - 1)[None])[0]
    norms = jnp.concatenate([gains.T, shifts.T], 0)
    (
        result_own,
        grad_one,
        d_heads,
        heads_own,
        normed_t,
        d_branch_t,
        d_attn_t,
        hidden,
        d_gu,
        norm_grads,
    ) = middle(x_own, cot_own, norms, o_blocks, w_out_parts, gu_parts, down_parts)
    grad_args = (normed_t, d_branch_t, d_attn_t, hidden, d_gu, heads_own, norm_grads)
    match_all = match.astype(F32).reshape(-1)
    if fused:
        pair, do_rel, home_result, over_result = grads(
            match_all, groups, *grad_args, d_heads, result_own
        )
        home_result = (home_result.reshape(size, groups, share, width), over_result)
    else:
        sent_grads = weight_grads(1, *grad_args)
        kept_grads = weight_grads(0, *grad_args)
        pair = (kept_grads.astype(F32) + swap(sent_grads, size, 1).astype(F32)).astype(BF)
        do_rel = jnp.stack(exchange_members([d_heads[r] for r in range(size)]))

    d_qkv_t = attend_back(
        info, q, k_rows, k, v_rows, o_blocks, do_rel, lse, seg_row, seg_col, cosine, sine
    )
    back_rel, grad_qkv = project_back(d_qkv_t, x_rel, w_qkv_t, me[None])
    grad_qkv = grad_qkv.reshape(groups, width // groups, 3 * local_width)

    pair = lax.psum_scatter(pair, "dp", scatter_dimension=1, tiled=True)
    spot_low = jnp.stack([low_a, low_b], 1).reshape(-1)
    spot_count = jnp.stack([count_a, count_b], 1).reshape(-1)
    spot_first = jnp.stack([jnp.zeros_like(count_a), count_a], 1).reshape(-1)
    spot_group = jnp.arange(seq_count, dtype=i32) // 2
    table = jnp.stack([spot_low, spot_count, spot_group, spot_first])
    table = jnp.sum(jnp.where(chosen[None], table[:, :, None], 0), 1)
    table = jnp.concatenate([jnp.full((4, 1), me, i32), table], 1)

    def send_back(own):
        body = own.reshape(subs, groups, sub, width).transpose(1, 0, 2, 3)
        body = body.reshape(groups, share, width)
        spare = lax.dot_general(
            match_bf, body[:, share - 1], (((0,), (0,)), ((), ())), preferred_element_type=F32
        ).astype(BF)
        pair = over_dp((body, spare.reshape(groups, 1, width)))
        return tuple(jnp.stack(gather_members(a)) for a in pair)

    if fused:
        home_input, home_over, qkv_sum = settle(
            match_all, back_rel, grad_one, grad_qkv
        )
        home_input = (home_input.reshape(size, groups, share, width), home_over)
        pair, home_input = lax.optimization_barrier((pair, home_input))
    else:
        home_result = send_back(result_own)
        input_own = grad_one + reduce_members([back_rel[r] for r in range(size)])
        home_input = send_back(input_own.astype(BF))
        grad_qkv = lax.all_to_all(grad_qkv, "dp", split_axis=0, concat_axis=0, tiled=True)
        qkv_sum = jnp.sum(grad_qkv.astype(F32), 0)
    qkv_sum = qkv_sum.reshape(-1, 3, local_width)
    summed = pair[0].astype(F32) + swap(pair[1], size, 2).astype(F32)
    inner = w_down.shape[1]
    gu_sum = summed[:, : 2 * inner].reshape(-1, 2, inner)
    down_sum = summed[:, 2 * inner : 3 * inner]
    out_sum = summed[:, 3 * inner : 3 * inner + local_width]
    norm_sum = summed[:, 3 * inner + local_width : 3 * inner + local_width + 4]
    norm_sum = lax.dynamic_slice_in_dim(
        norm_sum, me * (norm_sum.shape[0] // size), norm_sum.shape[0] // size, 0
    )
    if fused:
        arrange = functools.partial(unpack, table)
    else:
        row_ids = jnp.arange(rows, dtype=i32)[None, :]
        here = (row_ids >= spot_low[:, None]) & (row_ids < (spot_low + spot_count)[:, None])
        slot = row_ids + (spot_first - spot_low)[:, None]
        home_part = jnp.minimum(slot // share, size - 1)
        flat = (jnp.bitwise_xor(home_part, me) * groups + spot_group[:, None]) * (share + 1)
        flat = jnp.sum(jnp.where(here, flat + slot - home_part * share, 0), 0)

        def arrange(home, over):
            every = jnp.concatenate([home, over], 2).reshape(-1, width)
            return jnp.take(every, flat, axis=0)

    result = arrange(*home_result).reshape(rows, 1, width)
    input_grad = arrange(*home_input).reshape(rows, 1, width)
    return (
        result,
        input_grad,
        qkv_sum,
        out_sum,
        gu_sum,
        down_sum,
        norm_sum[:, :2],
        norm_sum[:, 2:],
    )


def solution(mesh):
    placed = (
        P(None, "dp", None),
        P(None, "dp", None),
        P(),
        P(),
        P(None, None, "tensor"),
        P(None, "tensor"),
        P(None, None, "tensor"),
        P(None, "tensor"),
        P(),
        P(),
    )
    return jax.shard_map(
        local,
        mesh=mesh,
        in_specs=placed,
        out_specs=(
            P(None, "dp", None),
            P(None, "dp", None),
            P("dp", None, "tensor"),
            P("dp", "tensor"),
            P("dp", None, "tensor"),
            P("dp", "tensor"),
            P(("dp", "tensor"), None),
            P(("dp", "tensor"), None),
        ),
        check_vma=False,
    )
```

```python
import functools

import jax
import jax.numpy as jnp
from jax import lax
from jax.experimental import pallas as pl
from jax.experimental.pallas import tpu as pltpu
from jax.sharding import PartitionSpec as P

HEAD = 64
HALF = HEAD // 2
BLOCK = 256
QUERIES = 512
PADDED = HEAD + 16
KEYS = 512
LOG_2 = 0.6931471805599453
EPSILON = 1e-05
NEGATIVE = -1000000000.0
START = -1e30
BF = jnp.bfloat16
F32 = jnp.float32
VMEM_LIMIT = 56 * 1024 * 1024


def mm(a, b, ca, cb):
    return lax.dot_general(a, b, (((ca,), (cb,)), ((), ())), preferred_element_type=F32)


HOLES = 8


def extra_of(source, offset, length, groups):
    turned = lax.rem(source - offset + groups, groups)
    return turned, jnp.where(turned < lax.rem(length, groups), 1, 0)


def pack_kernel(
    groups,
    size,
    lengths,
    dealing,
    ids,
    x_ref,
    c_ref,
    send_x_ref,
    over_x_ref,
    send_c_ref,
    meta_ref,
    table_ref,
    match_ref,
):
    d = ids[0]
    t = ids[1]
    rows = x_ref.shape[0]
    slots = rows // groups
    share = slots // size
    window = (share + 31) // 16 * 16

    def lookup(q):
        seq = dealing[q]
        offset = lax.fori_loop(0, seq, lambda j, total: total + lengths[j], jnp.int32(0))
        return seq, offset, lengths[seq]

    def span(offset, length):
        low = lax.div(offset - d + groups - 1, groups)
        return low, lax.div(offset + length - d + groups - 1, groups) - low

    def load(ref, row, count):
        start = jnp.clip(jnp.bitwise_and(row, -16), 0, rows - window)
        shift = jnp.clip(row - start, 1 - window, window - 1)
        loaded = ref[pl.ds(pl.multiple_of(start, 16), window), :].astype(F32)
        return pltpu.roll(loaded, lax.rem(window - shift, window), 0)[:count]

    table_ref[0, 0] = t
    slot_ids = lax.broadcasted_iota(jnp.int32, (share, 1), 0) + t * share

    @pl.loop(0, groups)
    def _(g):
        seq_a, off_a, len_a = lookup(2 * g)
        seq_b, off_b, len_b = lookup(2 * g + 1)
        low_a, count_a = span(off_a, len_a)
        low_b, count_b = span(off_b, len_b)
        for seq, entries in ((seq_a, (low_a, count_a, g, 0)), (seq_b, (low_b, count_b, g, count_a))):
            for i, entry in enumerate(entries):
                table_ref[i, 1 + seq] = jnp.int32(entry)
        shifted = low_b - count_a
        for ref, out_ref in ((x_ref, send_x_ref), (c_ref, send_c_ref)):
            first = load(ref, low_a + t * share, share)
            second = load(ref, shifted + t * share, share)
            out_ref[g, :share] = jnp.where(slot_ids < count_a, first, second).astype(BF)
        over_x_ref[g] = load(x_ref, shifted + slots, 1).astype(BF)
        spare = send_c_ref.shape[1] - share
        send_c_ref[g, share:] = load(c_ref, shifted + slots, spare).astype(BF)

    _, off_a, len_a = lookup(2 * d)
    _, off_b, len_b = lookup(2 * d + 1)
    off_a = lax.rem(off_a, groups)
    off_b = lax.rem(off_b, groups)
    meta_ref[0] = lax.div(len_a, BLOCK)
    meta_ref[1] = lax.div(len_a + BLOCK - 1, BLOCK)
    meta_ref[2] = t
    meta_ref[3] = off_a
    meta_ref[4] = off_b
    meta_ref[5] = len_a
    meta_ref[6] = jnp.int32(0)
    meta_ref[7] = jnp.int32(0)

    def counts(source):
        first = lax.div(len_a, groups) + extra_of(source, off_a, len_a, groups)[1]
        second = lax.div(len_b, groups) + extra_of(source, off_b, len_b, groups)[1]
        return first, first + second

    @pl.loop(0, groups)
    def _(hole):
        lacks = lambda source: jnp.where(counts(source)[1] < slots, 1, 0)
        rank = lax.fori_loop(0, hole, lambda j, total: total + lacks(j), jnp.int32(0))
        rank = jnp.where(lacks(hole) == 1, rank, -1)

        def scan(source, carry):
            seen, found = carry
            over = jnp.where(counts(source)[1] > slots, 1, 0)
            hit = (over == 1) & (seen == rank)
            match_ref[hole * groups + source] = jnp.where(hit, jnp.float32(1.0), jnp.float32(0.0))
            return seen + over, jnp.where(hit, source, found)

        _, found = lax.fori_loop(0, groups, scan, (jnp.int32(0), jnp.int32(-1)))
        source = jnp.maximum(found, 0)
        position = (slots - counts(source)[0]) * groups + extra_of(source, off_b, len_b, groups)[0]
        meta_ref[HOLES + hole] = jnp.where(found >= 0, position, -1)


def pack(lengths, dealing, ids, x, cotangent, groups, size):
    rows, width = x.shape
    share = rows // groups // size
    whole = lambda *shape: pl.BlockSpec(shape, lambda i, *refs: (0,) * len(shape))
    smem = pl.BlockSpec(memory_space=pltpu.SMEM)
    shapes = [(groups, share, width), (groups, 1, width), (groups, share + 16, width)]
    return pl.pallas_call(
        functools.partial(pack_kernel, groups, size),
        grid_spec=pltpu.PrefetchScalarGridSpec(
            num_scalar_prefetch=3,
            grid=(1,),
            in_specs=[whole(rows, width)] * 2,
            out_specs=[whole(*shape) for shape in shapes] + [smem] * 3,
        ),
        out_shape=[jax.ShapeDtypeStruct(shape, BF) for shape in shapes]
        + [
            jax.ShapeDtypeStruct((HOLES + groups,), jnp.int32),
            jax.ShapeDtypeStruct((4, 1 + lengths.shape[0]), jnp.int32),
            jax.ShapeDtypeStruct((groups * groups,), F32),
        ],
        compiler_params=pltpu.CompilerParams(vmem_limit_bytes=VMEM_LIMIT),
        cost_estimate=pl.CostEstimate(flops=0, bytes_accessed=20 << 20, transcendentals=0),
        name="pack",
    )(lengths, dealing, ids, x, cotangent)


def place(row, groups):
    sub = BLOCK // groups
    inside = lax.rem(row, BLOCK)
    return lax.div(inside, sub), lax.div(row, BLOCK) * sub + lax.rem(inside, sub)


def count_first(meta, source, groups):
    turned, extra = extra_of(source, meta[3], meta[5], groups)
    return turned, lax.div(meta[5], groups) + extra


def in_second(meta, row, groups):
    source, slot = place(row, groups)
    return jnp.where(slot < count_first(meta, source, groups)[1], 0, 1)


def positions_of(meta, row, groups, slots):
    source, slot = place(row, groups)
    turned, count = count_first(meta, source, groups)
    turned_b = lax.rem(source - meta[4] + groups, groups)
    position = jnp.where(slot < count, slot * groups + turned, (slot - count) * groups + turned_b)
    for g in range(groups):
        fills = meta[HOLES + g]
        here = (slot == slots - 1) & (source == g) & (fills >= 0)
        position = jnp.where(here, fills, position)
    return position


def spare_row(match_ref, groups, hole, rows):
    total = rows[0] * match_ref[hole * groups]
    flag = match_ref[hole * groups]
    for source in range(1, groups):
        weight = match_ref[hole * groups + source]
        total = total + rows[source] * weight
        flag = flag + weight
    return total, flag


def project_kernel(
    groups,
    packed,
    meta,
    match_ref,
    x_in_ref,
    over_ref,
    w_ref,
    freq_ref,
    q_ref,
    k_ref,
    v_ref,
    krow_ref,
    vrow_ref,
    cos_ref,
    sin_ref,
    x_ref,
    own_ref,
):
    index = pl.program_id(0)
    parts = pl.num_programs(0)
    share, width = x_ref.shape[1:]
    heads = q_ref.shape[0] // HEAD
    local = heads * HEAD
    sub = BLOCK // groups
    if packed:
        for i in range(share // BLOCK):
            for g in range(groups):
                base = i * BLOCK + g * sub
                x_ref[0, base : base + sub, :] = x_in_ref[0, g, i * sub : (i + 1) * sub, :]

        @pl.when(index == parts - 1)
        def _():
            rows = [over_ref[g].astype(F32) for g in range(groups)]
            at_end = lax.broadcasted_iota(jnp.int32, (16, 1), 0) == 15
            for g in range(groups):
                end = share - BLOCK + (g + 1) * sub
                spare, _ = spare_row(match_ref, groups, g, rows)
                old = x_ref[0, end - 16 : end, :].astype(F32)
                new = jnp.where(at_end & (meta[HOLES + g] >= 0), spare, old)
                x_ref[0, end - 16 : end, :] = new.astype(BF)
    else:
        x_ref[...] = x_in_ref[...]

    @pl.when(index == meta[2])
    def _():
        own_ref[...] = x_ref[0]

    row = lax.broadcasted_iota(jnp.int32, (1, share), 1) + index * share
    position = positions_of(meta, row, groups, parts * share // groups)
    angles = freq_ref[...] * position.astype(F32)
    cosine = jnp.cos(angles)
    sine = jnp.sin(angles)
    cos_ref[...] = cosine
    sin_ref[...] = sine
    projected = mm(w_ref[...], x_ref[0], 1, 1)
    for part, out_ref, scale in ((0, q_ref, HEAD ** (-0.5) / LOG_2), (1, k_ref, 1.0)):
        for head in range(heads):
            base = part * local + head * HEAD
            first = projected[base : base + HALF]
            second = projected[base + HALF : base + HEAD]
            turned = jnp.concatenate(
                [first * cosine - second * sine, second * cosine + first * sine], 0
            )
            out_ref[head * HEAD : (head + 1) * HEAD, :] = (turned * scale).astype(BF)
            if part == 1:
                krow_ref[head] = turned.T.astype(BF)
    for head in range(heads):
        base = 2 * local + head * HEAD
        value = projected[base : base + HEAD]
        rest = lax.broadcasted_iota(jnp.int32, (PADDED - HEAD, share), 0) == 0
        v_ref[head * PADDED : (head + 1) * PADDED, :] = jnp.concatenate(
            [value, jnp.where(rest, 1.0, 0.0)], 0
        ).astype(BF)
        vrow_ref[head] = value.T.astype(BF)


def project(meta, match, x_rel, over, w_t, freq, groups, packed):
    parts = x_rel.shape[0]
    width = x_rel.shape[-1]
    share = x_rel.size // parts // width
    rows = parts * share
    local = w_t.shape[0] // 3
    heads = local // HEAD
    shape = jax.ShapeDtypeStruct
    columns = lambda *lead: pl.BlockSpec(lead + (share,), lambda i, meta: (0,) * len(lead) + (i,))
    tall_spec = pl.BlockSpec((heads, share, HEAD), lambda i, meta: (0, i, 0))
    whole = lambda *shape: pl.BlockSpec(shape, lambda i, meta: (0,) * len(shape))
    lead = x_rel.shape[1:]
    return pl.pallas_call(
        functools.partial(project_kernel, groups, packed),
        grid_spec=pltpu.PrefetchScalarGridSpec(
            num_scalar_prefetch=1,
            grid=(parts,),
            in_specs=[
                pl.BlockSpec(memory_space=pltpu.SMEM),
                pl.BlockSpec(
                    (1,) + lead, lambda i, meta: (jnp.bitwise_xor(i, meta[2]),) + (0,) * len(lead)
                ),
                whole(*over.shape),
                whole(3 * local, width),
                whole(HALF, 1),
            ],
            out_specs=[
                columns(local),
                columns(local),
                columns(heads * PADDED),
                tall_spec,
                tall_spec,
                columns(HALF),
                columns(HALF),
                pl.BlockSpec((1, share, width), lambda i, meta: (i, 0, 0)),
                whole(share, width),
            ],
        ),
        out_shape=[
            shape((local, rows), BF),
            shape((local, rows), BF),
            shape((heads * PADDED, rows), BF),
            shape((heads, rows, HEAD), BF),
            shape((heads, rows, HEAD), BF),
            shape((HALF, rows), F32),
            shape((HALF, rows), F32),
            shape((parts, share, width), BF),
            shape((share, width), BF),
        ],
        compiler_params=pltpu.CompilerParams(vmem_limit_bytes=VMEM_LIMIT),
        cost_estimate=pl.CostEstimate(
            flops=2 * rows * width * 3 * local, bytes_accessed=16 << 20, transcendentals=0
        ),
        name="project",
    )(meta, match, x_rel, over, w_t, freq)


def visible(info, index, q_blocks, k_blocks, count):
    is_a = (index + 1) * q_blocks <= info[0]
    is_b = index * q_blocks >= info[1]
    pure = is_a | is_b
    end_a = info[0] // k_blocks
    start_b = (info[1] + k_blocks - 1) // k_blocks
    plain_low = jnp.where(is_b, start_b, 0)
    plain_high = jnp.where(is_b, count, jnp.where(is_a, end_a, 0))
    return plain_low, plain_high, jnp.where(pure, end_a, 0), jnp.where(pure, start_b, count)


def attend_kernel(groups, info, q_ref, k_ref, v_ref, o_ref, lse_ref, acc_ref):
    index = pl.program_id(0)
    heads, rows, _ = k_ref.shape
    width = q_ref.shape[1]
    tall = v_ref.shape[0] // heads
    spans_ = visible(info, index, width // BLOCK, KEYS // BLOCK, rows // KEYS)
    acc_ref[...] = jnp.zeros_like(acc_ref)
    query_ids = lax.broadcasted_iota(jnp.int32, (1, width), 1) + index * width
    key_ids = lax.broadcasted_iota(jnp.int32, (KEYS, 1), 0)
    ids = range(heads)

    def step(masked, j, tops):
        keys = pl.ds(pl.multiple_of(j * KEYS, KEYS), KEYS)
        scores = [mm(k_ref[h, keys, :], q_ref[h * HEAD : (h + 1) * HEAD, :], 1, 0) for h in ids]
        if masked:
            same = in_second(info, key_ids + j * KEYS, groups) == in_second(info, query_ids, groups)
            scores = [jnp.where(same, s, NEGATIVE) for s in scores]
        new = [jnp.maximum(tops[h], jnp.max(scores[h], 0, keepdims=True)) for h in ids]
        weights = [jnp.exp2(scores[h] - new[h]).astype(BF) for h in ids]
        shrink = [jnp.exp2(tops[h] - new[h]) for h in ids]
        sums = [mm(v_ref[h * tall : (h + 1) * tall, keys], weights[h], 1, 0) for h in ids]
        for h in ids:
            part = slice(h * tall, (h + 1) * tall)
            acc_ref[part, :] = acc_ref[part, :] * shrink[h] + sums[h]
        return tuple(new)

    tops = (jnp.full((1, width), START, F32),) * heads
    tops = lax.fori_loop(spans_[0], spans_[1], functools.partial(step, False), tops)
    tops = lax.fori_loop(spans_[2], spans_[3], functools.partial(step, True), tops)
    for h in ids:
        total = acc_ref[h * tall + HEAD : h * tall + HEAD + 1, :]
        out = (acc_ref[h * tall : h * tall + HEAD, :] / total).astype(BF)
        each = o_ref.shape[2]
        for i in range(width // each):
            o_ref[i, h * HEAD : (h + 1) * HEAD, :] = out[:, i * each : (i + 1) * each]
        lse_ref[h : h + 1, :] = tops[h] + jnp.log2(total)


def attend(info, q, k_rows, v, groups):
    local, rows = q.shape
    heads = local // HEAD
    return pl.pallas_call(
        functools.partial(attend_kernel, groups),
        grid_spec=pltpu.PrefetchScalarGridSpec(
            num_scalar_prefetch=1,
            grid=(rows // QUERIES,),
            in_specs=[
                pl.BlockSpec((local, QUERIES), lambda i, info: (0, i)),
                pl.BlockSpec((heads, rows, HEAD), lambda i, info: (0, 0, 0)),
                pl.BlockSpec(v.shape, lambda i, info: (0, 0)),
            ],
            out_specs=[
                pl.BlockSpec((QUERIES // BLOCK, local, BLOCK), lambda i, info: (i, 0, 0)),
                pl.BlockSpec((heads, QUERIES), lambda i, info: (0, i)),
            ],
            scratch_shapes=[pltpu.VMEM((v.shape[0], QUERIES), F32)],
        ),
        out_shape=[
            jax.ShapeDtypeStruct((rows // BLOCK, local, BLOCK), BF),
            jax.ShapeDtypeStruct((heads, rows), F32),
        ],
        compiler_params=pltpu.CompilerParams(vmem_limit_bytes=VMEM_LIMIT),
        cost_estimate=pl.CostEstimate(
            flops=2 * 2 * rows * rows * 256 * heads // 2,
            bytes_accessed=8 << 20,
            transcendentals=heads * rows * rows // 2,
        ),
        name="attend",
    )(info, q, k_rows, v)


def unturn(grad, cosine, sine):
    first = grad[:HALF]
    second = grad[HALF:]
    return jnp.concatenate(
        [first * cosine + second * sine, second * cosine - first * sine], 0
    ).astype(BF)


def attend_back_kernel(
    groups,
    info,
    q_ref,
    krow_ref,
    k_ref,
    vrow_ref,
    o_ref,
    do_ref,
    lse_ref,
    cos_ref,
    sin_ref,
    out_ref,
    dq_ref,
    dk_ref,
    dv_ref,
):
    index = pl.program_id(0)
    heads, rows, _ = krow_ref.shape
    width = heads * HEAD
    parts, _, share = out_ref.shape
    each = share // BLOCK
    ids = range(heads)
    part = [slice(h * HEAD, (h + 1) * HEAD) for h in ids]

    @pl.when(index == 0)
    def _():
        dk_ref[...] = jnp.zeros_like(dk_ref)
        dv_ref[...] = jnp.zeros_like(dv_ref)

    dq_ref[...] = jnp.zeros_like(dq_ref)
    query_ids = lax.broadcasted_iota(jnp.int32, (1, BLOCK), 1) + index * BLOCK
    key_ids = lax.broadcasted_iota(jnp.int32, (KEYS, 1), 0)
    delta = [
        jnp.sum(do_ref[0, p, :].astype(F32) * o_ref[0, p, :].astype(F32), 0, keepdims=True)
        for p in part
    ]
    spans_ = visible(info, index, 1, KEYS // BLOCK, rows // KEYS)

    def step(masked, j, carry):
        keys = pl.ds(pl.multiple_of(j * KEYS, KEYS), KEYS)
        scores = [mm(krow_ref[h, keys, :], q_ref[part[h], :], 1, 0) for h in ids]
        grad_soft = [mm(vrow_ref[h, keys, :], do_ref[0, part[h], :], 1, 0) for h in ids]
        if masked:
            same = in_second(info, key_ids + j * KEYS, groups) == in_second(info, query_ids, groups)
            scores = [jnp.where(same, s, NEGATIVE) for s in scores]
        soft = [jnp.exp2(scores[h] - lse_ref[h : h + 1, :]) for h in ids]
        grad_scores = [(soft[h] * (grad_soft[h] - delta[h])).astype(BF) for h in ids]
        soft = [s.astype(BF) for s in soft]
        dv = [mm(do_ref[0, part[h], :], soft[h], 1, 1) for h in ids]
        dk = [mm(q_ref[part[h], :], grad_scores[h], 1, 1) for h in ids]
        dq = [mm(k_ref[part[h], keys], grad_scores[h], 1, 0) for h in ids]
        for h in ids:
            dv_ref[part[h], keys] += dv[h]
            dk_ref[part[h], keys] += dk[h]
            dq_ref[part[h], :] += dq[h]
        return carry

    lax.fori_loop(spans_[0], spans_[1], functools.partial(step, False), 0)
    lax.fori_loop(spans_[2], spans_[3], functools.partial(step, True), 0)

    owner = index // each
    columns = pl.ds(pl.multiple_of(index * BLOCK, BLOCK), BLOCK)
    inside = pl.ds(pl.multiple_of(index % each * BLOCK, BLOCK), BLOCK)
    for h in ids:
        out_ref[owner, part[h], inside] = unturn(
            dq_ref[part[h], :] * HEAD ** (-0.5), cos_ref[:, columns], sin_ref[:, columns]
        )

    @pl.when(index == pl.num_programs(0) - 1)
    def _():
        @pl.loop(0, parts)
        def _(j):
            columns = pl.ds(pl.multiple_of(j * share, share), share)
            for h in ids:
                base = width + h * HEAD
                out_ref[j, base : base + HEAD, :] = unturn(
                    dk_ref[part[h], columns] * LOG_2, cos_ref[:, columns], sin_ref[:, columns]
                )
                base = 2 * width + h * HEAD
                out_ref[j, base : base + HEAD, :] = dv_ref[part[h], columns].astype(BF)


def attend_back(info, q, k_rows, k, v_rows, o, do, lse, cosine, sine, groups):
    parts = do.shape[0]
    local, rows = q.shape
    heads = local // HEAD
    blocks = rows // BLOCK
    each = blocks // parts
    whole = lambda *shape: pl.BlockSpec(shape, lambda i, info: (0,) * len(shape))
    return pl.pallas_call(
        functools.partial(attend_back_kernel, groups),
        grid_spec=pltpu.PrefetchScalarGridSpec(
            num_scalar_prefetch=1,
            grid=(blocks,),
            in_specs=[
                pl.BlockSpec((local, BLOCK), lambda i, info: (0, i)),
                whole(heads, rows, HEAD),
                whole(local, rows),
                whole(heads, rows, HEAD),
                pl.BlockSpec((1, local, BLOCK), lambda i, info: (i, 0, 0)),
                pl.BlockSpec(
                    (1, local, BLOCK),
                    lambda i, info: (jnp.bitwise_xor(i // each, info[2]), 0, i % each),
                ),
                pl.BlockSpec((heads, BLOCK), lambda i, info: (0, i)),
                whole(HALF, rows),
                whole(HALF, rows),
            ],
            out_specs=whole(parts, 3 * local, rows // parts),
            scratch_shapes=[
                pltpu.VMEM((local, BLOCK), F32),
                pltpu.VMEM((local, rows), F32),
                pltpu.VMEM((local, rows), F32),
            ],
        ),
        out_shape=jax.ShapeDtypeStruct((parts, 3 * local, rows // parts), BF),
        compiler_params=pltpu.CompilerParams(vmem_limit_bytes=VMEM_LIMIT),
        cost_estimate=pl.CostEstimate(
            flops=2 * 5 * rows * rows * 256 * heads // 2,
            bytes_accessed=16 << 20,
            transcendentals=heads * rows * rows // 2,
        ),
        name="attend_back",
    )(info, q, k_rows, k, v_rows, o, do, lse, cosine, sine)


def project_back_kernel(meta, d_ref, x_ref, w_ref, back_ref, grad_ref, acc_ref):
    index = pl.program_id(0)

    @pl.when(index == 0)
    def _():
        acc_ref[...] = jnp.zeros_like(acc_ref)

    d_t = d_ref[0]
    back_ref[0] = mm(d_t, w_ref[...], 0, 0).astype(BF)
    acc_ref[...] += mm(d_t, x_ref[0], 1, 0)

    @pl.when(index == pl.num_programs(0) - 1)
    def _():
        grad_ref[...] = acc_ref[...].T.astype(BF)


def project_back(meta, d_qkv_t, x_all, w_t):
    parts, local, share = d_qkv_t.shape
    width = w_t.shape[1]
    relative = lambda i, meta: (jnp.bitwise_xor(i, meta[2]), 0, 0)
    whole = lambda *shape: pl.BlockSpec(shape, lambda i, meta: (0,) * len(shape))
    return pl.pallas_call(
        project_back_kernel,
        grid_spec=pltpu.PrefetchScalarGridSpec(
            num_scalar_prefetch=1,
            grid=(parts,),
            in_specs=[
                pl.BlockSpec((1, local, share), lambda i, meta: (i, 0, 0)),
                pl.BlockSpec((1, share, width), lambda i, meta: (i, 0, 0)),
                whole(local, width),
            ],
            out_specs=[
                pl.BlockSpec((1, share, width), relative),
                whole(width, local),
            ],
            scratch_shapes=[pltpu.VMEM((local, width), F32)],
        ),
        out_shape=[
            jax.ShapeDtypeStruct((parts, share, width), BF),
            jax.ShapeDtypeStruct((width, local), BF),
        ],
        compiler_params=pltpu.CompilerParams(vmem_limit_bytes=VMEM_LIMIT),
        cost_estimate=pl.CostEstimate(
            flops=4 * parts * share * local * width, bytes_accessed=15 << 20, transcendentals=0
        ),
        name="project_back",
    )(meta, d_qkv_t, x_all, w_t)


MESH = pl.DeviceIdType.MESH


def greet(groups, steps, d, t):
    barrier = pltpu.get_barrier_semaphore()
    for k in range(1, groups):
        pl.semaphore_signal(
            barrier, inc=1, device_id=(lax.rem(d + k, groups), t), device_id_type=MESH
        )
    for step in steps:
        pl.semaphore_signal(
            barrier, inc=1, device_id=(d, jnp.bitwise_xor(t, step)), device_id_type=MESH
        )
    pl.semaphore_wait(barrier, groups - 1 + len(steps))


def remote(src, dst, send, recv, device):
    return pltpu.make_async_remote_copy(
        src_ref=src,
        dst_ref=dst,
        send_sem=send,
        recv_sem=recv,
        device_id=device,
        device_id_type=MESH,
    )


class Spread:
    def __init__(self, out, sems, groups, d, t):
        self.out, self.sems, self.groups, self.d, self.t = out, sems, groups, d, t

    def at(self, r, k, rest):
        return self.out.at[(r, lax.rem(self.d - k + self.groups, self.groups)) + rest]

    def arrival(self, source, k, rest, where):
        send, recv = self.sems
        to = lax.rem(self.d + k, self.groups)
        return remote(
            source, self.at(0, 0, rest), send.at[(0, k) + where], recv.at[(0, k) + where], (to, self.t)
        )

    def across(self, k, rest, where):
        send, recv = self.sems
        return remote(
            self.at(0, k, rest),
            self.at(2, k, rest),
            send.at[(2, k) + where],
            recv.at[(2, k) + where],
            (self.d, jnp.bitwise_xor(self.t, 2)),
        )

    def beside(self, r, k, rest, where):
        send, recv = self.sems
        return remote(
            self.at(r, k, rest),
            self.at(r + 1, k, rest),
            send.at[(r + 1, k) + where],
            recv.at[(r + 1, k) + where],
            (self.d, jnp.bitwise_xor(self.t, 1)),
        )


def norm_forward(resid_rows, gain_vec, shift_vec):
    row_mean = jnp.mean(resid_rows, -1, keepdims=True)
    centred = resid_rows - row_mean
    inverse = lax.rsqrt(jnp.mean(centred * centred, -1, keepdims=True) + EPSILON)
    unit_rows = centred * inverse
    return (unit_rows * gain_vec + shift_vec, unit_rows, inverse)


def norm_backward(upstream, unit_rows, inverse, gain_vec):
    scaled = upstream * gain_vec
    inner_term = (
        scaled
        - jnp.mean(scaled, -1, keepdims=True)
        - unit_rows * jnp.mean(scaled * unit_rows, -1, keepdims=True)
    )
    return (
        inner_term * inverse,
        jnp.sum(upstream * unit_rows, 0, keepdims=True),
        jnp.sum(upstream, 0, keepdims=True),
    )


def middle_kernel(size, groups, *refs):
    x_ref, match_ref, cot_ref, over_ref, norm_ref, blocks_ref = refs[:6]
    out_hbm, gu_hbm, down_hbm = (refs[6 + i * size : 6 + (i + 1) * size] for i in range(3))
    (
        result_ref,
        grad_one_ref,
        d_heads_ref,
        heads_ref,
        normed_t_ref,
        d_branch_t_ref,
        d_attn_t_ref,
        hidden_ref,
        d_gu_ref,
        norm_grad_ref,
        w_out_ref,
        w_gu_ref,
        w_down_ref,
        slope_ref,
        swish_ref,
        arrived_ref,
        sems,
        sends,
        recvs,
        keep,
    ) = refs[6 + 3 * size :]
    index = pl.program_id(0)
    first = index == 0
    d = lax.axis_index("dp")
    t = lax.axis_index("tensor")
    subs, local, _ = arrived_ref.shape[1:]
    inner = down_hbm[0].shape[1]
    ids = range(size)
    part = [slice(r * local, (r + 1) * local) for r in ids]
    copies_out = [
        pltpu.make_async_copy(out_hbm[r], w_out_ref.at[part[r]], sems.at[0, r]) for r in ids
    ]
    copies_gu = [pltpu.make_async_copy(gu_hbm[r], w_gu_ref.at[r], sems.at[1, r]) for r in ids]
    copies_down = [
        pltpu.make_async_copy(down_hbm[r], w_down_ref.at[r], sems.at[2, r]) for r in ids
    ]

    def heads_copy(r, i):
        other = jnp.bitwise_xor(t, r)
        return remote(
            blocks_ref.at[other * subs + i],
            arrived_ref.at[r, i],
            sends.at[r, i],
            recvs.at[r, i],
            (d, other),
        )

    own_copy = pltpu.make_async_copy(blocks_ref.at[pl.ds(t * subs, subs)], arrived_ref.at[0], keep)

    @pl.when(first)
    def _():
        own_copy.start()
        for copy in copies_out:
            copy.start()
        greet(1, (1, 2, 3), d, t)
        for i in range(subs):
            for r in (2, 3, 1):
                heads_copy(r, i).start()
        own_copy.wait()
        for r in ids:
            copies_gu[r].start()
            copies_down[r].start()
        for copy in copies_out:
            copy.wait()

    for r in ids[1:]:
        heads_copy(r, index).wait_recv()
        heads_copy(r, index).wait_send()
    for r in ids:
        heads_ref[r] = arrived_ref[r, index]
    heads_out = jnp.concatenate([arrived_ref[r, index] for r in ids], 0)
    attn = mm(heads_out, w_out_ref[...], 0, 0)
    gain_one, gain_two, shift_one, shift_two = (norm_ref[i : i + 1, :] for i in range(4))
    normed_one, unit_one, inverse_one = norm_forward(
        x_ref[...].astype(F32) + attn, gain_one, shift_one
    )
    normed = normed_one.astype(BF)
    normed_t_ref[...] = normed_one.T.astype(BF)
    branch = jnp.zeros(normed_one.shape, F32)
    for r in ids:

        @pl.when(first)
        def _():
            copies_gu[r].wait()
            copies_down[r].wait()

        both = mm(normed, w_gu_ref[r], 1, 0)
        gate = both[:, :inner]
        up = both[:, inner:]
        sig = jax.nn.sigmoid(gate)
        swish = gate * sig
        hidden = (swish * up).astype(BF)
        swish_ref[r] = swish
        slope_ref[r] = up * sig * (1.0 + gate * (1.0 - sig))
        hidden_ref[r] = hidden
        branch = branch + mm(hidden, w_down_ref[r], 1, 1)
    result, unit_two, inverse_two = norm_forward(normed_one + branch, gain_two, shift_two)
    result_ref[...] = result.astype(BF)
    if groups:
        sub = BLOCK // groups
        spares = [over_ref[g, 0:1, :].astype(F32) for g in range(groups)]
        in_last = jnp.where((index == subs - 1) & (t == size - 1), 1.0, 0.0)
        ends = lax.broadcasted_iota(jnp.int32, (sub, 1), 0) == sub - 1
        pieces = []
        for g in range(groups):
            piece = cot_ref[g].astype(F32)
            spare, flag = spare_row(match_ref, groups, g, spares)
            fix = jnp.where(ends, flag * in_last, 0.0)
            pieces.append(piece * (1.0 - fix) + spare * fix)
        cot = jnp.concatenate(pieces, 0)
    else:
        cot = cot_ref[...].astype(F32)
    grad_two, d_gain_two, d_shift_two = norm_backward(cot, unit_two, inverse_two, gain_two)
    d_branch = grad_two.astype(BF)
    d_branch_t_ref[...] = grad_two.T.astype(BF)
    back = grad_two
    for r in ids:
        grad_hidden = mm(d_branch, w_down_ref[r], 1, 0)
        d_gate = (grad_hidden * slope_ref[r]).astype(BF)
        d_up = (grad_hidden * swish_ref[r]).astype(BF)
        d_gu_ref[r, :, :inner] = d_gate
        d_gu_ref[r, :, inner:] = d_up
        back = back + mm(jnp.concatenate([d_gate, d_up], 1), w_gu_ref[r], 1, 1)
    grad_one, d_gain_one, d_shift_one = norm_backward(back, unit_one, inverse_one, gain_one)
    grad_one_ref[...] = grad_one
    d_attn_t = grad_one.T.astype(BF)
    d_attn_t_ref[...] = d_attn_t
    d_heads = mm(w_out_ref[...], d_attn_t, 1, 0).astype(BF)
    for r in ids:
        d_heads_ref[r] = d_heads[part[r]]

    @pl.when(first)
    def _():
        norm_grad_ref[...] = jnp.zeros_like(norm_grad_ref)

    for i, grad in enumerate((d_gain_one, d_gain_two, d_shift_one, d_shift_two)):
        norm_grad_ref[i : i + 1, :] += grad


def middle(x_own, match, cot, norms, o_blocks, w_out_parts, gu_parts, down_parts):
    rows, width = x_own.shape
    size = len(gu_parts)
    local = o_blocks.shape[1]
    inner = down_parts[0].shape[1]
    block = pl.BlockSpec((BLOCK, width), lambda i: (i, 0))
    turned = pl.BlockSpec((width, BLOCK), lambda i: (0, i))
    anywhere = pl.BlockSpec(memory_space=pl.ANY)
    shape = jax.ShapeDtypeStruct
    groups = cot.shape[0] if cot.ndim == 3 else 0
    if groups:
        sub = BLOCK // groups
        last = cot.shape[1] // 16 - 1
        cot_specs = [
            pl.BlockSpec((groups, sub, width), lambda i: (0, i, 0)),
            pl.BlockSpec((groups, 16, width), lambda i: (0, last, 0)),
        ]
    else:
        cot_specs = [block, pl.BlockSpec((16, width), lambda i: (0, 0))]
    return pl.pallas_call(
        functools.partial(middle_kernel, size, groups),
        grid=(rows // BLOCK,),
        in_specs=[block, pl.BlockSpec(memory_space=pltpu.SMEM)]
        + cot_specs
        + [pl.BlockSpec(norms.shape, lambda i: (0, 0))]
        + [anywhere] * (1 + 3 * size),
        out_specs=[
            block,
            block,
            pl.BlockSpec((size, local, BLOCK), lambda i: (0, 0, i)),
            pl.BlockSpec((size, local, BLOCK), lambda i: (0, 0, i)),
            turned,
            turned,
            turned,
            pl.BlockSpec((size, BLOCK, inner), lambda i: (0, i, 0)),
            pl.BlockSpec((size, BLOCK, 2 * inner), lambda i: (0, i, 0)),
            pl.BlockSpec((8, width), lambda i: (0, 0)),
        ],
        out_shape=[
            shape((rows, width), BF),
            shape((rows, width), F32),
            shape((size, local, rows), BF),
            shape((size, local, rows), BF),
            shape((width, rows), BF),
            shape((width, rows), BF),
            shape((width, rows), BF),
            shape((size, rows, inner), BF),
            shape((size, rows, 2 * inner), BF),
            shape((8, width), F32),
        ],
        scratch_shapes=[
            pltpu.VMEM((size * local, width), BF),
            pltpu.VMEM((size, width, 2 * inner), BF),
            pltpu.VMEM((size, width, inner), BF),
            pltpu.VMEM((size, BLOCK, inner), F32),
            pltpu.VMEM((size, BLOCK, inner), F32),
            pltpu.VMEM((size, rows // BLOCK, local, BLOCK), BF),
            pltpu.SemaphoreType.DMA((3, size)),
            pltpu.SemaphoreType.DMA((size, rows // BLOCK)),
            pltpu.SemaphoreType.DMA((size, rows // BLOCK)),
            pltpu.SemaphoreType.DMA,
        ],
        compiler_params=pltpu.CompilerParams(
            collective_id=2, has_side_effects=True, vmem_limit_bytes=VMEM_LIMIT
        ),
        cost_estimate=pl.CostEstimate(
            flops=2 * rows * width * (6 * size * inner + 2 * size * local),
            bytes_accessed=40 << 20,
            transcendentals=rows * size * inner,
        ),
        name="middle",
    )(x_own, match, cot, cot, norms, o_blocks, *w_out_parts, *gu_parts, *down_parts)


def weight_grads_tile(
    normed_t_ref, d_branch_t_ref, d_attn_t_ref, hidden_ref, d_gu_ref, heads_ref, norm_ref, store
):
    inner = hidden_ref.shape[2]
    local = heads_ref.shape[1]
    width = normed_t_ref.shape[0]
    store(0, 2 * inner, mm(normed_t_ref[...], d_gu_ref[0], 1, 0))
    store(2 * inner, 3 * inner, mm(d_branch_t_ref[...], hidden_ref[0], 1, 0))
    d_out = mm(d_attn_t_ref[...], heads_ref[0], 1, 1)
    norm = norm_ref[...].T
    spare = -(local + norm.shape[1]) % 128
    tail = jnp.concatenate([d_out, norm, jnp.zeros((width, spare), F32)], 1)
    store(3 * inner, 3 * inner + tail.shape[1], tail)


def weight_grads_kernel(*refs):
    out_ref = refs[-1]

    def store(low, high, value):
        out_ref[0, :, low:high] = value.astype(BF)

    weight_grads_tile(*refs[:-1], store)


def weight_grads(odd, normed_t, d_branch_t, d_attn_t, hidden, d_gu, heads, norm_grads):
    size, rows, inner = hidden.shape
    local = heads.shape[1]
    width = normed_t.shape[0]
    wide = 3 * inner + local + norm_grads.shape[0]
    wide = (wide + 127) // 128 * 128
    flat = pl.BlockSpec((width, rows), lambda i: (0, 0))
    pick = lambda i: (2 * i + odd, 0, 0)
    return pl.pallas_call(
        weight_grads_kernel,
        grid=(size // 2,),
        in_specs=[
            flat,
            flat,
            flat,
            pl.BlockSpec((1, rows, inner), pick),
            pl.BlockSpec((1, rows, 2 * inner), pick),
            pl.BlockSpec((1, local, rows), pick),
            pl.BlockSpec(norm_grads.shape, lambda i: (0, 0)),
        ],
        out_specs=pl.BlockSpec((1, width, wide), lambda i: (i, 0, 0)),
        out_shape=jax.ShapeDtypeStruct((size // 2, width, wide), BF),
        compiler_params=pltpu.CompilerParams(vmem_limit_bytes=VMEM_LIMIT),
        cost_estimate=pl.CostEstimate(
            flops=size * rows * width * (3 * inner + local), bytes_accessed=20 << 20, transcendentals=0
        ),
        name="weight_grads",
    )(normed_t, d_branch_t, d_attn_t, hidden, d_gu, heads, norm_grads)


def grads_kernel(groups, size, match_ref, *refs):
    tile_refs = refs[:7]
    (
        d_heads_ref,
        result_ref,
        pair_ref,
        do_ref,
        home_ref,
        over_ref,
        sent_ref,
        got_ref,
        own_ref,
        spare_ref,
        s_grad,
        r_grad,
        s_heads,
        r_heads,
        sends,
        recvs,
        s_over,
        r_over,
        keep,
    ) = refs[7:]
    step = pl.program_id(0)
    d = lax.axis_index("dp")
    t = lax.axis_index("tensor")
    chunks, _, sub, width = own_ref.shape
    core = (d, jnp.bitwise_xor(t, 1))
    body = Spread(home_ref, (sends, recvs), groups, d, t)
    extra = Spread(over_ref, (s_over, r_over), groups, d, t)

    def heads_copy(r):
        return remote(
            d_heads_ref.at[r],
            do_ref.at[r],
            s_heads.at[r],
            r_heads.at[r],
            (d, jnp.bitwise_xor(t, r)),
        )

    def grad_copy(i):
        return remote(sent_ref.at[i], got_ref.at[i], s_grad.at[i], r_grad.at[i], core)

    def own_copy(c):
        return pltpu.make_async_copy(own_ref.at[c, d], home_ref.at[0, d, c], keep.at[c])

    load = pltpu.make_async_copy(result_ref, own_ref, keep.at[chunks])
    own_heads = pltpu.make_async_copy(d_heads_ref.at[0], do_ref.at[0], keep.at[chunks + 1])
    own_over = pltpu.make_async_copy(spare_ref.at[d], over_ref.at[0, d], keep.at[chunks + 2])

    def pass_on(c):
        own_copy(c).wait()
        for k in range(groups):
            if k > 0:
                body.arrival(own_ref.at[c, 0], k, (c,), (c,)).wait_recv()
            body.across(k, (c,), (c,)).start()
            body.beside(0, k, (c,), (c,)).start()

    def pass_far(c):
        for k in range(groups):
            body.across(k, (c,), (c,)).wait_recv()
            body.beside(2, k, (c,), (c,)).start()

    @pl.when(step == 0)
    def _():
        load.start()
        own_heads.start()
        greet(groups, (1, 2, 3), d, t)
        for r in (2, 3, 1):
            heads_copy(r).start()
        load.wait()
        for c in range(chunks):
            own_copy(c).start()
            for k in range(1, groups):
                body.arrival(own_ref.at[c, lax.rem(d + k, groups)], k, (c,), (c,)).start()
        last = [own_ref[chunks - 1, g, sub - 16 :, :].astype(F32)[15:16] for g in range(groups)]
        for to in range(groups):
            spare = last[0] * match_ref[to]
            for g in range(1, groups):
                spare = spare + last[g] * match_ref[g * groups + to]
            spare_ref[to] = spare.astype(BF)
        own_over.start()
        for k in range(1, groups):
            extra.arrival(spare_ref.at[lax.rem(d + k, groups)], k, (), ()).start()

    for c in range(2):

        @pl.when(step == c + 2)
        def _():
            pass_on(c)

    @pl.when(step < 2)
    def _():
        def store(low, high, value):
            sent_ref[step, :, low:high] = value.astype(BF)

        weight_grads_tile(*tile_refs, store)
        grad_copy(step).start()

    @pl.when(step >= 2)
    def _():
        grad_copy(step - 2).wait_recv()

        def store(low, high, value):
            other = got_ref[step - 2, :, low:high].astype(F32)
            pair_ref[0, :, low:high] = (value + other).astype(BF)

        weight_grads_tile(*tile_refs, store)

    @pl.when(step == size - 1)
    def _():
        for c in range(2, chunks):
            pass_on(c)
        own_over.wait()
        for k in range(groups):
            if k > 0:
                extra.arrival(spare_ref.at[0], k, (), ()).wait_recv()
            extra.across(k, (), ()).start()
            extra.beside(0, k, (), ()).start()
        for c in range(chunks):
            pass_far(c)
        for k in range(groups):
            extra.across(k, (), ()).wait_recv()
            extra.beside(2, k, (), ()).start()
        own_heads.wait()
        for r in range(1, size):
            heads_copy(r).wait_recv()
            heads_copy(r).wait_send()
        for i in range(2):
            grad_copy(i).wait_send()
        for k in range(groups):
            for c in range(chunks):
                body.beside(0, k, (c,), (c,)).wait_recv()
                body.beside(2, k, (c,), (c,)).wait_recv()
                if k > 0:
                    body.arrival(own_ref.at[c, 0], k, (c,), (c,)).wait_send()
                body.across(k, (c,), (c,)).wait_send()
                body.beside(0, k, (c,), (c,)).wait_send()
                body.beside(2, k, (c,), (c,)).wait_send()
            extra.beside(0, k, (), ()).wait_recv()
            extra.beside(2, k, (), ()).wait_recv()
            if k > 0:
                extra.arrival(spare_ref.at[0], k, (), ()).wait_send()
            extra.across(k, (), ()).wait_send()
            extra.beside(0, k, (), ()).wait_send()
            extra.beside(2, k, (), ()).wait_send()


def grads(
    match, groups, normed_t, d_branch_t, d_attn_t, hidden, d_gu, heads, norm_grads, d_heads, result
):
    size, rows, inner = hidden.shape
    local = heads.shape[1]
    width = normed_t.shape[0]
    chunks = rows // BLOCK
    sub = BLOCK // groups
    wide = 3 * inner + (local + norm_grads.shape[0] + 127) // 128 * 128
    flat = pl.BlockSpec((width, rows), lambda i: (0, 0))
    pick = lambda i: (jnp.where(i < 2, 2 * i + 1, 2 * i - 4), 0, 0)
    anywhere = pl.BlockSpec(memory_space=pl.ANY)
    dma = pltpu.SemaphoreType.DMA
    return pl.pallas_call(
        functools.partial(grads_kernel, groups, size),
        grid=(size,),
        in_specs=[
            pl.BlockSpec(memory_space=pltpu.SMEM),
            flat,
            flat,
            flat,
            pl.BlockSpec((1, rows, inner), pick),
            pl.BlockSpec((1, rows, 2 * inner), pick),
            pl.BlockSpec((1, local, rows), pick),
            pl.BlockSpec(norm_grads.shape, lambda i: (0, 0)),
            anywhere,
            anywhere,
        ],
        out_specs=[
            pl.BlockSpec((1, width, wide), lambda i: (jnp.maximum(i - 2, 0), 0, 0)),
            anywhere,
            anywhere,
            anywhere,
        ],
        out_shape=[
            jax.ShapeDtypeStruct((2, width, wide), BF),
            jax.ShapeDtypeStruct(d_heads.shape, BF),
            jax.ShapeDtypeStruct((size, groups, chunks, sub, width), BF),
            jax.ShapeDtypeStruct((size, groups, 1, width), BF),
        ],
        scratch_shapes=[
            pltpu.VMEM((2, width, wide), BF),
            pltpu.VMEM((2, width, wide), BF),
            pltpu.VMEM((chunks, groups, sub, width), BF),
            pltpu.VMEM((groups, 1, width), BF),
            dma((2,)),
            dma((2,)),
            dma((size,)),
            dma((size,)),
            dma((4, groups, chunks)),
            dma((4, groups, chunks)),
            dma((4, groups)),
            dma((4, groups)),
            dma((chunks + 3,)),
        ],
        compiler_params=pltpu.CompilerParams(
            collective_id=3, has_side_effects=True, vmem_limit_bytes=VMEM_LIMIT
        ),
        cost_estimate=pl.CostEstimate(
            flops=2 * size * rows * width * (3 * inner + local),
            bytes_accessed=80 << 20,
            transcendentals=0,
        ),
        name="grads",
    )(
        match,
        normed_t,
        d_branch_t,
        d_attn_t,
        hidden,
        d_gu,
        heads,
        norm_grads,
        d_heads,
        result.reshape(chunks, groups, sub, width),
    )


def swap(array, size, step):
    return lax.ppermute(array, "tensor", [(i, i ^ step) for i in range(size)])


def gather_members(own):
    size = lax.axis_size("tensor")
    across = swap(own, size, 2)
    return [own, swap(own, size, 1), across, swap(across, size, 1)]


def exchange_members(pieces):
    size = lax.axis_size("tensor")
    return [pieces[0]] + [swap(pieces[r], size, r) for r in range(1, size)]


def reduce_members(pieces):
    size = lax.axis_size("tensor")
    near = swap(pieces[1], size, 1)
    far = swap(pieces[3], size, 1)
    other = (pieces[2].astype(F32) + far.astype(F32)).astype(BF)
    across = swap(other, size, 2)
    return pieces[0].astype(F32) + near.astype(F32) + across.astype(F32)


def route_kernel(groups, size, send_ref, over_ref, out_ref, over_out_ref, sends, recvs, keep):
    d = lax.axis_index("dp")
    t = lax.axis_index("tensor")
    greet(groups, (1, 2), d, t)
    spread = Spread(out_ref, (sends, recvs), groups, d, t)
    own = pltpu.make_async_copy(send_ref.at[d], out_ref.at[0, d], keep.at[0])
    own_over = pltpu.make_async_copy(over_ref.at[d], over_out_ref.at[d], keep.at[1])
    own.start()
    own_over.start()

    def over_copy(k):
        to = lax.rem(d + k, groups)
        return remote(
            over_ref.at[to], over_out_ref.at[d], sends.at[4, k], recvs.at[4, k], (to, t)
        )

    for k in range(1, groups):
        spread.arrival(send_ref.at[lax.rem(d + k, groups)], k, (), ()).start()
    for k in range(1, groups):
        over_copy(k).start()
    own.wait()
    for k in range(groups):
        if k > 0:
            spread.arrival(send_ref.at[0], k, (), ()).wait_recv()
        spread.across(k, (), ()).start()
        spread.beside(0, k, (), ()).start()
        if k > 0:
            spread.across(k - 1, (), ()).wait_recv()
            spread.beside(2, k - 1, (), ()).start()
    spread.across(groups - 1, (), ()).wait_recv()
    spread.beside(2, groups - 1, (), ()).start()
    own_over.wait()
    for k in range(groups):
        spread.beside(0, k, (), ()).wait_recv()
        spread.beside(2, k, (), ()).wait_recv()
        if k > 0:
            over_copy(k).wait_recv()
            over_copy(k).wait_send()
            spread.arrival(send_ref.at[0], k, (), ()).wait_send()
        spread.across(k, (), ()).wait_send()
        spread.beside(0, k, (), ()).wait_send()
        spread.beside(2, k, (), ()).wait_send()


def route(send, over, size):
    groups = send.shape[0]
    anywhere = pl.BlockSpec(memory_space=pl.ANY)
    return pl.pallas_call(
        functools.partial(route_kernel, groups, size),
        in_specs=[anywhere, anywhere],
        out_specs=[anywhere, anywhere],
        out_shape=[
            jax.ShapeDtypeStruct((size,) + send.shape, BF),
            jax.ShapeDtypeStruct(over.shape, BF),
        ],
        scratch_shapes=[
            pltpu.SemaphoreType.DMA((5, groups)),
            pltpu.SemaphoreType.DMA((5, groups)),
            pltpu.SemaphoreType.DMA((2,)),
        ],
        compiler_params=pltpu.CompilerParams(collective_id=0, has_side_effects=True),
        cost_estimate=pl.CostEstimate(flops=0, bytes_accessed=60 << 20, transcendentals=0),
        name="route",
    )(send, over)


def settle_kernel(
    groups,
    size,
    match_ref,
    back_ref,
    one_ref,
    gq_ref,
    home_ref,
    over_ref,
    sum_ref,
    far_ref,
    near_ref,
    pair_ref,
    other_ref,
    own_ref,
    spare_ref,
    gqr_ref,
    sends,
    recvs,
    s_over,
    r_over,
    s_sum,
    r_sum,
    s_gq,
    r_gq,
    keep,
):
    d = lax.axis_index("dp")
    t = lax.axis_index("tensor")
    chunks, _, sub, width = own_ref.shape
    greet(groups, (1, 2), d, t)
    core = (d, jnp.bitwise_xor(t, 1))
    chip = (d, jnp.bitwise_xor(t, 2))

    def rows(c):
        return pl.ds(c * BLOCK, BLOCK)

    def far(c):
        return remote(back_ref.at[3, rows(c)], far_ref.at[c], s_sum.at[0, c], r_sum.at[0, c], core)

    def near(c):
        return remote(back_ref.at[1, rows(c)], near_ref.at[c], s_sum.at[1, c], r_sum.at[1, c], core)

    def other(c):
        return remote(pair_ref.at[c], other_ref.at[c], s_sum.at[2, c], r_sum.at[2, c], chip)

    def gq(k):
        to = lax.rem(d + k, groups)
        return remote(gq_ref.at[to], gqr_ref.at[d], s_gq.at[k], r_gq.at[k], (to, t))

    for c in range(chunks):
        far(c).start()
    for c in range(chunks):
        near(c).start()
    for c in range(chunks):
        far(c).wait_recv()
        pair = back_ref[2, rows(c), :].astype(F32) + far_ref[c].astype(F32)
        pair_ref[c] = pair.astype(BF)
        other(c).start()
    own_gq = pltpu.make_async_copy(gq_ref.at[d], gqr_ref.at[d], keep.at[chunks])
    own_gq.start()

    body = Spread(home_ref, (sends, recvs), groups, d, t)
    extra = Spread(over_ref, (s_over, r_over), groups, d, t)

    def own_copy(c):
        return pltpu.make_async_copy(own_ref.at[c, d], home_ref.at[0, d, c], keep.at[c])

    own_over = pltpu.make_async_copy(spare_ref.at[d], over_ref.at[0, d], keep.at[chunks + 1])

    def pass_on(c):
        own_copy(c).wait()
        for k in range(groups):
            if k > 0:
                body.arrival(own_ref.at[c, 0], k, (c,), (c,)).wait_recv()
            body.across(k, (c,), (c,)).start()
            body.beside(0, k, (c,), (c,)).start()

    def pass_far(c):
        for k in range(groups):
            body.across(k, (c,), (c,)).wait_recv()
            body.beside(2, k, (c,), (c,)).start()

    for c in range(chunks):
        near(c).wait_recv()
        partial = (
            one_ref[rows(c), :] + back_ref[0, rows(c), :].astype(F32) + near_ref[c].astype(F32)
        )
        other(c).wait_recv()
        done = (partial + other_ref[c].astype(F32)).astype(BF)
        for g in range(groups):
            own_ref[c, g] = done[g * sub : (g + 1) * sub]
        own_copy(c).start()
        for k in range(1, groups):
            body.arrival(own_ref.at[c, lax.rem(d + k, groups)], k, (c,), (c,)).start()
        if c == chunks - 1:
            last = [
                own_ref[c, g, sub - 16 :, :].astype(F32)[15:16] for g in range(groups)
            ]
            for to in range(groups):
                spare = last[0] * match_ref[to]
                for g in range(1, groups):
                    spare = spare + last[g] * match_ref[g * groups + to]
                spare_ref[to] = spare.astype(BF)
            own_over.start()
            for k in range(1, groups):
                extra.arrival(spare_ref.at[lax.rem(d + k, groups)], k, (), ()).start()
        if c == 0:
            for k in range(1, groups):
                gq(k).start()
        else:
            pass_on(c - 1)
    pass_on(chunks - 1)
    own_over.wait()
    for k in range(groups):
        if k > 0:
            extra.arrival(spare_ref.at[0], k, (), ()).wait_recv()
        extra.across(k, (), ()).start()
        extra.beside(0, k, (), ()).start()
    own_gq.wait()
    total = gqr_ref[d].astype(F32)
    for k in range(1, groups):
        gq(k).wait_recv()
        total = total + gqr_ref[lax.rem(d - k + groups, groups)].astype(F32)
    sum_ref[...] = total
    for c in range(chunks):
        pass_far(c)
    for k in range(groups):
        extra.across(k, (), ()).wait_recv()
        extra.beside(2, k, (), ()).start()
    for c in range(chunks):
        far(c).wait_send()
        near(c).wait_send()
        other(c).wait_send()
    for k in range(groups):
        for c in range(chunks):
            body.beside(0, k, (c,), (c,)).wait_recv()
            body.beside(2, k, (c,), (c,)).wait_recv()
            if k > 0:
                body.arrival(own_ref.at[c, 0], k, (c,), (c,)).wait_send()
            body.across(k, (c,), (c,)).wait_send()
            body.beside(0, k, (c,), (c,)).wait_send()
            body.beside(2, k, (c,), (c,)).wait_send()
        extra.beside(0, k, (), ()).wait_recv()
        extra.beside(2, k, (), ()).wait_recv()
        if k > 0:
            gq(k).wait_send()
            extra.arrival(spare_ref.at[0], k, (), ()).wait_send()
        extra.across(k, (), ()).wait_send()
        extra.beside(0, k, (), ()).wait_send()
        extra.beside(2, k, (), ()).wait_send()


def settle(match, back_rel, grad_one, grad_qkv):
    size, rows, width = back_rel.shape
    groups, part, local = grad_qkv.shape
    chunks = rows // BLOCK
    sub = BLOCK // groups
    anywhere = pl.BlockSpec(memory_space=pl.ANY)
    vmem = pl.BlockSpec(memory_space=pltpu.VMEM)
    dma = pltpu.SemaphoreType.DMA
    buffer = pltpu.VMEM((chunks, BLOCK, width), BF)
    return pl.pallas_call(
        functools.partial(settle_kernel, groups, size),
        in_specs=[pl.BlockSpec(memory_space=pltpu.SMEM), vmem, vmem, anywhere],
        out_specs=[anywhere, anywhere, vmem],
        out_shape=[
            jax.ShapeDtypeStruct((size, groups, chunks, sub, width), BF),
            jax.ShapeDtypeStruct((size, groups, 1, width), BF),
            jax.ShapeDtypeStruct((part, local), F32),
        ],
        scratch_shapes=[
            buffer,
            buffer,
            buffer,
            buffer,
            pltpu.VMEM((chunks, groups, sub, width), BF),
            pltpu.VMEM((groups, 1, width), BF),
            pltpu.VMEM((groups, part, local), BF),
            dma((4, groups, chunks)),
            dma((4, groups, chunks)),
            dma((4, groups)),
            dma((4, groups)),
            dma((3, chunks)),
            dma((3, chunks)),
            dma((groups,)),
            dma((groups,)),
            dma((chunks + 2,)),
        ],
        compiler_params=pltpu.CompilerParams(
            collective_id=1, has_side_effects=True, vmem_limit_bytes=VMEM_LIMIT
        ),
        cost_estimate=pl.CostEstimate(flops=0, bytes_accessed=150 << 20, transcendentals=0),
        name="settle",
    )(match, back_rel, grad_one, grad_qkv)


ROWS = 32


def unpack_kernel(info, home_ref, over_ref, out_ref, src_ref, dst_ref):
    size, groups, share, _ = home_ref.shape
    rows = out_ref.shape[0]
    slots = size * share
    me = info[0, 0]

    @pl.loop(0, size)
    def _(part):
        source = jnp.bitwise_xor(part, me)
        at = pl.ds(pl.multiple_of(ROWS + part * share, 8), share)
        for g in range(groups):
            src_ref[g, at, :] = home_ref[source, g].astype(F32)

    last = jnp.bitwise_xor(size - 1, me)
    for g in range(groups):
        src_ref[g, ROWS + slots : ROWS + slots + 1, :] = over_ref[last, g].astype(F32)
    row_ids = lax.broadcasted_iota(jnp.int32, (ROWS, 1), 0)

    @pl.loop(0, info.shape[1] - 1)
    def _(j):
        low = info[0, 1 + j]
        count = info[1, 1 + j]
        group = info[2, 1 + j]
        first = info[3, 1 + j]

        @pl.loop(low // ROWS, (low + count + ROWS - 1) // ROWS)
        def _(i):
            start = i * ROWS + first - low + ROWS
            offset = jnp.bitwise_and(start, 7)
            loaded = src_ref[group, pl.ds(pl.multiple_of(start - offset, 8), ROWS + 8), :]
            moved = pltpu.roll(loaded, ROWS + 8 - offset, 0)[:ROWS]
            at = pl.ds(pl.multiple_of(i * ROWS, ROWS), ROWS)
            dst_ref[at, :] = jnp.where(row_ids >= low - i * ROWS, moved, dst_ref[at, :])

    out_ref[...] = dst_ref[:rows, :].astype(BF)


def unpack(info, home, over):
    size, groups, share, width = home.shape
    rows = size * groups * share
    whole = lambda *shape: pl.BlockSpec(shape, lambda i, info: (0,) * len(shape))
    return pl.pallas_call(
        unpack_kernel,
        grid_spec=pltpu.PrefetchScalarGridSpec(
            num_scalar_prefetch=1,
            grid=(1,),
            in_specs=[whole(*home.shape), whole(*over.shape)],
            out_specs=whole(rows, width),
            scratch_shapes=[
                pltpu.VMEM((groups, size * share + 4 * ROWS, width), F32),
                pltpu.VMEM((rows + ROWS, width), F32),
            ],
        ),
        out_shape=jax.ShapeDtypeStruct((rows, width), BF),
        compiler_params=pltpu.CompilerParams(vmem_limit_bytes=VMEM_LIMIT),
        cost_estimate=pl.CostEstimate(flops=0, bytes_accessed=30 << 20, transcendentals=0),
        name="unpack",
    )(info, home, over)


def local(tokens, cotangent, lengths, dealing, w_qkv, w_out, w_gu, w_down, gains, shifts):
    groups = lax.axis_size("dp")
    size = lax.axis_size("tensor")
    me = lax.axis_index("tensor")
    rows = tokens.shape[0]
    width = tokens.shape[2]
    slots = rows // groups
    share = slots // size
    own_rows = rows // size
    subs = own_rows // BLOCK
    sub = share // subs
    fused = sub % 16 == 0
    i32 = jnp.int32

    ids = jnp.stack([lax.axis_index("dp"), me]).astype(i32)
    send_x, over_x, send_c, meta, table, match = pack(
        lengths,
        dealing,
        ids,
        tokens.reshape(rows, width),
        cotangent.reshape(rows, width),
        groups,
        size,
    )

    def over_dp(array):
        return lax.all_to_all(array, "dp", split_axis=0, concat_axis=0, tiled=True)

    far_out, far_down = swap(w_out.T, size, 2), swap(w_down, size, 2)
    match_square = match.reshape(groups, groups)

    def fill(received, over, last):
        spare = jnp.dot(match_square.astype(BF), over, preferred_element_type=F32).astype(BF)
        hole = (jnp.sum(match_square, 1) > 0)[:, None] & (jnp.arange(share) == share - 1)[None, :]
        fix = last[:, None, None] & hole[None]
        body = jnp.where(fix[..., None], spare[None, :, None, :], received)
        body = body.reshape(-1, groups, subs, sub, width).transpose(0, 2, 1, 3, 4)
        return body.reshape(-1, own_rows, width)

    if fused:
        x_rel, over_x = route(send_x, over_x, size)
        send_c, x_rel, far_out, far_down = lax.optimization_barrier(
            (send_c, x_rel, far_out, far_down)
        )
    else:
        x_rel = jnp.stack(gather_members(over_dp(send_x)))
        relative = jnp.bitwise_xor(jnp.arange(size, dtype=i32), me)
        x_rel = fill(x_rel, over_dp(over_x)[:, 0], relative == size - 1)
    cot = over_dp(send_c)
    if not fused:
        cot = fill(cot[None, :, :share], cot[:, share], (me == size - 1)[None])[0]

    local_width = w_qkv.shape[2]
    w_qkv_t = w_qkv.transpose(1, 2, 0).reshape(3 * local_width, width)
    x_rel, near_gu = lax.optimization_barrier((x_rel, w_gu.reshape(width, -1)))
    far_gu = swap(near_gu, size, 2)
    frequency = 1000.0 ** (-(jnp.arange(HALF, dtype=F32) * 2.0) / HEAD)
    q, k, v, k_rows, v_rows, cosine, sine, x_all, x_own = project(
        meta, match, x_rel, over_x, w_qkv_t, frequency[:, None], groups, fused
    )
    o_blocks, lse = attend(meta, q, k_rows, v, groups)
    o_blocks, far_gu, cot = lax.optimization_barrier((o_blocks, far_gu, cot))

    spread_parts = lambda near, far: [near, swap(near, size, 1), far, swap(far, size, 1)]
    w_out_parts = spread_parts(w_out.T, far_out)
    down_parts = spread_parts(w_down, far_down)
    gu_parts = spread_parts(near_gu, far_gu)
    norms = jnp.concatenate([gains.T, shifts.T], 0)
    (
        result_own,
        grad_one,
        d_heads,
        heads_own,
        normed_t,
        d_branch_t,
        d_attn_t,
        hidden,
        d_gu,
        norm_grads,
    ) = middle(x_own, match, cot, norms, o_blocks, w_out_parts, gu_parts, down_parts)
    grad_args = (normed_t, d_branch_t, d_attn_t, hidden, d_gu, heads_own, norm_grads)
    if fused:
        pair, do_rel, home_result, over_result = grads(
            match, groups, *grad_args, d_heads, result_own
        )
        home_result = (home_result.reshape(size, groups, share, width), over_result)
    else:
        sent_grads = weight_grads(1, *grad_args)
        kept_grads = weight_grads(0, *grad_args)
        pair = (kept_grads.astype(F32) + swap(sent_grads, size, 1).astype(F32)).astype(BF)
        do_rel = jnp.stack(exchange_members([d_heads[r] for r in range(size)]))

    d_qkv_t = attend_back(
        meta, q, k_rows, k, v_rows, o_blocks, do_rel, lse, cosine, sine, groups
    )
    back_rel, grad_qkv = project_back(meta, d_qkv_t, x_all, w_qkv_t)
    grad_qkv = grad_qkv.reshape(groups, width // groups, 3 * local_width)

    pair = lax.psum_scatter(pair, "dp", scatter_dimension=1, tiled=True)
    def send_back(own):
        body = own.reshape(subs, groups, sub, width).transpose(1, 0, 2, 3)
        body = body.reshape(groups, share, width)
        spare = lax.dot_general(
            match_square.astype(BF),
            body[:, share - 1],
            (((0,), (0,)), ((), ())),
            preferred_element_type=F32,
        ).astype(BF)
        pair = (over_dp(body), over_dp(spare.reshape(groups, 1, width)))
        return tuple(jnp.stack(gather_members(a)) for a in pair)

    if fused:
        home_input, home_over, qkv_sum = settle(
            match, back_rel, grad_one, grad_qkv
        )
        home_input = (home_input.reshape(size, groups, share, width), home_over)
        pair, home_input = lax.optimization_barrier((pair, home_input))
    else:
        home_result = send_back(result_own)
        input_own = grad_one + reduce_members([back_rel[r] for r in range(size)])
        home_input = send_back(input_own.astype(BF))
        grad_qkv = lax.all_to_all(grad_qkv, "dp", split_axis=0, concat_axis=0, tiled=True)
        qkv_sum = jnp.sum(grad_qkv.astype(F32), 0)
    qkv_sum = qkv_sum.reshape(-1, 3, local_width)
    summed = pair[0].astype(F32) + swap(pair[1], size, 2).astype(F32)
    inner = w_down.shape[1]
    gu_sum = summed[:, : 2 * inner].reshape(-1, 2, inner)
    down_sum = summed[:, 2 * inner : 3 * inner]
    out_sum = summed[:, 3 * inner : 3 * inner + local_width]
    norm_sum = summed[:, 3 * inner + local_width : 3 * inner + local_width + 4]
    norm_sum = lax.dynamic_slice_in_dim(
        norm_sum, me * (norm_sum.shape[0] // size), norm_sum.shape[0] // size, 0
    )
    if fused:
        arrange = functools.partial(unpack, table)
    else:
        row_ids = jnp.arange(rows, dtype=i32)[None, :]
        low, count, group, first = (table[i, 1:][:, None] for i in range(4))
        here = (row_ids >= low) & (row_ids < low + count)
        slot = row_ids + first - low
        home_part = jnp.minimum(slot // share, size - 1)
        flat = (jnp.bitwise_xor(home_part, me) * groups + group) * (share + 1)
        flat = jnp.sum(jnp.where(here, flat + slot - home_part * share, 0), 0)

        def arrange(home, over):
            every = jnp.concatenate([home, over], 2).reshape(-1, width)
            return jnp.take(every, flat, axis=0)

    result = arrange(*home_result).reshape(rows, 1, width)
    input_grad = arrange(*home_input).reshape(rows, 1, width)
    return (
        result,
        input_grad,
        qkv_sum,
        out_sum,
        gu_sum,
        down_sum,
        norm_sum[:, :2],
        norm_sum[:, 2:],
    )


def solution(mesh):
    placed = (
        P(None, "dp", None),
        P(None, "dp", None),
        P(),
        P(),
        P(None, None, "tensor"),
        P(None, "tensor"),
        P(None, None, "tensor"),
        P(None, "tensor"),
        P(),
        P(),
    )
    return jax.shard_map(
        local,
        mesh=mesh,
        in_specs=placed,
        out_specs=(
            P(None, "dp", None),
            P(None, "dp", None),
            P("dp", None, "tensor"),
            P("dp", "tensor"),
            P("dp", None, "tensor"),
            P("dp", "tensor"),
            P(("dp", "tensor"), None),
            P(("dp", "tensor"), None),
        ),
        check_vma=False,
    )
```

```python
import functools

import jax
import jax.numpy as jnp
from jax import lax
from jax.experimental import pallas as pl
from jax.experimental.pallas import tpu as pltpu
from jax.sharding import PartitionSpec as P

HEAD = 64
HALF = HEAD // 2
BLOCK = 256
QUERIES = 512
PADDED = HEAD + 16
KEYS = 512
LOG_2 = 0.6931471805599453
EPSILON = 1e-05
NEGATIVE = -1000000000.0
START = -1e30
BF = jnp.bfloat16
F32 = jnp.float32
VMEM_LIMIT = 56 * 1024 * 1024


def mm(a, b, ca, cb):
    return lax.dot_general(a, b, (((ca,), (cb,)), ((), ())), preferred_element_type=F32)


HOLES = 8
ROWS = 128


def div(value, size):
    if size & (size - 1) == 0:
        return lax.shift_right_arithmetic(value, jnp.int32(size.bit_length() - 1))
    return lax.div(value, size)


def rem(value, size):
    if size & (size - 1) == 0:
        return lax.bitwise_and(value, jnp.int32(size - 1))
    return lax.rem(value, size)


def extra_of(source, offset, length, groups):
    turned = rem(source - offset + groups, groups)
    return turned, jnp.where(turned < rem(length, groups), 1, 0)


def pack_kernel(
    groups,
    size,
    lengths,
    dealing,
    ids,
    x_ref,
    c_ref,
    send_x_ref,
    over_x_ref,
    send_c_ref,
    meta_ref,
    table_ref,
    match_ref,
    spots_ref,
):
    d = ids[0]
    t = ids[1]
    rows = x_ref.shape[0]
    slots = rows // groups
    share = slots // size
    window = (share + 31) // 16 * 16

    def lookup(q):
        seq = dealing[q]
        offset = lax.fori_loop(0, seq, lambda j, total: total + lengths[j], jnp.int32(0))
        return seq, offset, lengths[seq]

    def span(offset, length):
        low = div(offset - d + groups - 1, groups)
        return low, div(offset + length - d + groups - 1, groups) - low

    def window_at(row):
        start = jnp.clip(jnp.bitwise_and(row, -16), 0, rows - window)
        return pl.ds(pl.multiple_of(start, 16), window), row - start

    def one_hot(steps, shift, wanted):
        return jnp.where((steps == shift) & wanted, 1.0, 0.0).astype(BF)

    def steps_of(count):
        shape = (count, window)
        return lax.broadcasted_iota(jnp.int32, shape, 1) - lax.broadcasted_iota(jnp.int32, shape, 0)

    steps = steps_of(share)
    spare_steps = steps_of(16)
    top = lax.broadcasted_iota(jnp.int32, (16, 1), 0) == 0
    table_ref[0, 0] = t
    slot_ids = lax.broadcasted_iota(jnp.int32, (share, 1), 0) + t * share

    @pl.loop(0, groups)
    def _(g):
        seq_a, off_a, len_a = lookup(2 * g)
        seq_b, off_b, len_b = lookup(2 * g + 1)
        low_a, count_a = span(off_a, len_a)
        low_b, count_b = span(off_b, len_b)
        for seq, entries in ((seq_a, (low_a, count_a, g, 0)), (seq_b, (low_b, count_b, g, count_a))):
            for i, entry in enumerate(entries):
                table_ref[i, 1 + seq] = jnp.int32(entry)
        shifted = low_b - count_a
        at_a, shift_a = window_at(low_a + t * share)
        at_b, shift_b = window_at(shifted + t * share)
        at_over, shift_over = window_at(shifted + slots)
        hot_a = one_hot(steps, shift_a, slot_ids < count_a)
        hot_b = one_hot(steps, shift_b, slot_ids >= count_a)
        hot_over = one_hot(spare_steps, shift_over, top)
        for ref, out_ref in ((x_ref, send_x_ref), (c_ref, send_c_ref)):
            picked = mm(hot_a, ref[at_a, :], 1, 0) + mm(hot_b, ref[at_b, :], 1, 0)
            out_ref[g, :share] = picked.astype(BF)
        over_x_ref[g] = mm(hot_over, x_ref[at_over, :], 1, 0)[:1].astype(BF)
        send_c_ref[g, share:] = mm(hot_over, c_ref[at_over, :], 1, 0).astype(BF)

    count = lengths.shape[0]

    @pl.loop(0, rows // ROWS)
    def _(i):
        row = i * ROWS
        begun = lambda j, total: total + jnp.where(table_ref[0, 1 + j] <= row, 1, 0)
        here = lax.fori_loop(0, count, begun, jnp.int32(0)) - 1
        after = jnp.minimum(here + 1, count - 1)
        for k, j in enumerate((here, after)):
            slot = row + table_ref[3, 1 + j] - table_ref[0, 1 + j]
            start = jnp.clip(jnp.bitwise_and(slot, -16), 0, slots - ROWS)
            spots_ref[8 * i + 3 * k] = table_ref[2, 1 + j]
            spots_ref[8 * i + 3 * k + 1] = div(start, 16)
            spots_ref[8 * i + 3 * k + 2] = slot - start
        spots_ref[8 * i + 6] = jnp.where(here + 1 < count, table_ref[0, 1 + after] - row, ROWS)
        spots_ref[8 * i + 7] = jnp.int32(0)

    _, off_a, len_a = lookup(2 * d)
    _, off_b, len_b = lookup(2 * d + 1)
    off_a = rem(off_a, groups)
    off_b = rem(off_b, groups)
    meta_ref[0] = div(len_a, BLOCK)
    meta_ref[1] = div(len_a + BLOCK - 1, BLOCK)
    meta_ref[2] = t
    meta_ref[3] = off_a
    meta_ref[4] = off_b
    meta_ref[5] = len_a
    meta_ref[6] = jnp.int32(0)
    meta_ref[7] = jnp.int32(0)

    def counts(source):
        first = div(len_a, groups) + extra_of(source, off_a, len_a, groups)[1]
        second = div(len_b, groups) + extra_of(source, off_b, len_b, groups)[1]
        return first, first + second

    @pl.loop(0, groups)
    def _(hole):
        lacks = lambda source: jnp.where(counts(source)[1] < slots, 1, 0)
        rank = lax.fori_loop(0, hole, lambda j, total: total + lacks(j), jnp.int32(0))
        rank = jnp.where(lacks(hole) == 1, rank, -1)

        def scan(source, carry):
            seen, found = carry
            over = jnp.where(counts(source)[1] > slots, 1, 0)
            hit = (over == 1) & (seen == rank)
            match_ref[hole * groups + source] = jnp.where(hit, jnp.float32(1.0), jnp.float32(0.0))
            return seen + over, jnp.where(hit, source, found)

        _, found = lax.fori_loop(0, groups, scan, (jnp.int32(0), jnp.int32(-1)))
        source = jnp.maximum(found, 0)
        position = (slots - counts(source)[0]) * groups + extra_of(source, off_b, len_b, groups)[0]
        meta_ref[HOLES + hole] = jnp.where(found >= 0, position, -1)


def pack(lengths, dealing, ids, x, cotangent, groups, size):
    rows, width = x.shape
    share = rows // groups // size
    whole = lambda *shape: pl.BlockSpec(shape, lambda i, *refs: (0,) * len(shape))
    smem = pl.BlockSpec(memory_space=pltpu.SMEM)
    shapes = [(groups, share, width), (groups, 1, width), (groups, share + 16, width)]
    return pl.pallas_call(
        functools.partial(pack_kernel, groups, size),
        grid_spec=pltpu.PrefetchScalarGridSpec(
            num_scalar_prefetch=3,
            grid=(1,),
            in_specs=[whole(rows, width)] * 2,
            out_specs=[whole(*shape) for shape in shapes] + [smem] * 4,
        ),
        out_shape=[jax.ShapeDtypeStruct(shape, BF) for shape in shapes]
        + [
            jax.ShapeDtypeStruct((HOLES + groups,), jnp.int32),
            jax.ShapeDtypeStruct((4, 1 + lengths.shape[0]), jnp.int32),
            jax.ShapeDtypeStruct((groups * groups,), F32),
            jax.ShapeDtypeStruct((rows // ROWS * 8,), jnp.int32),
        ],
        compiler_params=pltpu.CompilerParams(vmem_limit_bytes=VMEM_LIMIT),
        cost_estimate=pl.CostEstimate(flops=0, bytes_accessed=20 << 20, transcendentals=0),
        name="pack",
    )(lengths, dealing, ids, x, cotangent)


def place(row, groups):
    sub = BLOCK // groups
    inside = rem(row, BLOCK)
    return div(inside, sub), div(row, BLOCK) * sub + rem(inside, sub)


def count_first(meta, source, groups):
    turned, extra = extra_of(source, meta[3], meta[5], groups)
    return turned, div(meta[5], groups) + extra


def in_second(meta, row, groups):
    source, slot = place(row, groups)
    return jnp.where(slot < count_first(meta, source, groups)[1], 0, 1)


def positions_of(meta, row, groups, slots):
    source, slot = place(row, groups)
    turned, count = count_first(meta, source, groups)
    turned_b = rem(source - meta[4] + groups, groups)
    position = jnp.where(slot < count, slot * groups + turned, (slot - count) * groups + turned_b)
    for g in range(groups):
        fills = meta[HOLES + g]
        here = (slot == slots - 1) & (source == g) & (fills >= 0)
        position = jnp.where(here, fills, position)
    return position


def spare_row(match_ref, groups, hole, rows):
    total = rows[0] * match_ref[hole * groups]
    flag = match_ref[hole * groups]
    for source in range(1, groups):
        weight = match_ref[hole * groups + source]
        total = total + rows[source] * weight
        flag = flag + weight
    return total, flag


def project_kernel(
    groups,
    packed,
    meta,
    match_ref,
    x_in_ref,
    over_ref,
    w_ref,
    freq_ref,
    q_ref,
    k_ref,
    v_ref,
    krow_ref,
    vrow_ref,
    cos_ref,
    sin_ref,
    x_ref,
    own_ref,
):
    index = pl.program_id(0)
    parts = pl.num_programs(0)
    share, width = x_ref.shape[1:]
    heads = q_ref.shape[0] // HEAD
    local = heads * HEAD
    sub = BLOCK // groups
    if packed:
        for i in range(share // BLOCK):
            for g in range(groups):
                base = i * BLOCK + g * sub
                x_ref[0, base : base + sub, :] = x_in_ref[0, g, i * sub : (i + 1) * sub, :]

        @pl.when(index == parts - 1)
        def _():
            rows = [over_ref[g].astype(F32) for g in range(groups)]
            at_end = lax.broadcasted_iota(jnp.int32, (16, 1), 0) == 15
            for g in range(groups):
                end = share - BLOCK + (g + 1) * sub
                spare, _ = spare_row(match_ref, groups, g, rows)
                old = x_ref[0, end - 16 : end, :].astype(F32)
                new = jnp.where(at_end & (meta[HOLES + g] >= 0), spare, old)
                x_ref[0, end - 16 : end, :] = new.astype(BF)
    else:
        x_ref[...] = x_in_ref[...]

    @pl.when(index == meta[2])
    def _():
        own_ref[...] = x_ref[0]

    row = lax.broadcasted_iota(jnp.int32, (1, share), 1) + index * share
    position = positions_of(meta, row, groups, parts * share // groups)
    angles = freq_ref[...] * position.astype(F32)
    cosine = jnp.cos(angles)
    sine = jnp.sin(angles)
    cos_ref[...] = cosine
    sin_ref[...] = sine
    projected = mm(w_ref[...], x_ref[0], 1, 1)
    for part, out_ref, scale in ((0, q_ref, HEAD ** (-0.5) / LOG_2), (1, k_ref, 1.0)):
        for head in range(heads):
            base = part * local + head * HEAD
            first = projected[base : base + HALF]
            second = projected[base + HALF : base + HEAD]
            turned = jnp.concatenate(
                [first * cosine - second * sine, second * cosine + first * sine], 0
            )
            out_ref[head * HEAD : (head + 1) * HEAD, :] = (turned * scale).astype(BF)
            if part == 1:
                krow_ref[head] = turned.T.astype(BF)
    for head in range(heads):
        base = 2 * local + head * HEAD
        value = projected[base : base + HEAD]
        rest = lax.broadcasted_iota(jnp.int32, (PADDED - HEAD, share), 0) == 0
        v_ref[head * PADDED : (head + 1) * PADDED, :] = jnp.concatenate(
            [value, jnp.where(rest, 1.0, 0.0)], 0
        ).astype(BF)
        vrow_ref[head] = value.T.astype(BF)


def project(meta, match, x_rel, over, w_t, freq, groups, packed):
    parts = x_rel.shape[0]
    width = x_rel.shape[-1]
    share = x_rel.size // parts // width
    rows = parts * share
    local = w_t.shape[0] // 3
    heads = local // HEAD
    shape = jax.ShapeDtypeStruct
    columns = lambda *lead: pl.BlockSpec(lead + (share,), lambda i, meta: (0,) * len(lead) + (i,))
    tall_spec = pl.BlockSpec((heads, share, HEAD), lambda i, meta: (0, i, 0))
    whole = lambda *shape: pl.BlockSpec(shape, lambda i, meta: (0,) * len(shape))
    lead = x_rel.shape[1:]
    return pl.pallas_call(
        functools.partial(project_kernel, groups, packed),
        grid_spec=pltpu.PrefetchScalarGridSpec(
            num_scalar_prefetch=1,
            grid=(parts,),
            in_specs=[
                pl.BlockSpec(memory_space=pltpu.SMEM),
                pl.BlockSpec(
                    (1,) + lead, lambda i, meta: (jnp.bitwise_xor(i, meta[2]),) + (0,) * len(lead)
                ),
                whole(*over.shape),
                whole(3 * local, width),
                whole(HALF, 1),
            ],
            out_specs=[
                columns(local),
                columns(local),
                columns(heads * PADDED),
                tall_spec,
                tall_spec,
                columns(HALF),
                columns(HALF),
                pl.BlockSpec((1, share, width), lambda i, meta: (i, 0, 0)),
                whole(share, width),
            ],
        ),
        out_shape=[
            shape((local, rows), BF),
            shape((local, rows), BF),
            shape((heads * PADDED, rows), BF),
            shape((heads, rows, HEAD), BF),
            shape((heads, rows, HEAD), BF),
            shape((HALF, rows), F32),
            shape((HALF, rows), F32),
            shape((parts, share, width), BF),
            shape((share, width), BF),
        ],
        compiler_params=pltpu.CompilerParams(vmem_limit_bytes=VMEM_LIMIT),
        cost_estimate=pl.CostEstimate(
            flops=2 * rows * width * 3 * local, bytes_accessed=16 << 20, transcendentals=0
        ),
        name="project",
    )(meta, match, x_rel, over, w_t, freq)


def visible(info, index, q_blocks, k_blocks, count):
    is_a = (index + 1) * q_blocks <= info[0]
    is_b = index * q_blocks >= info[1]
    pure = is_a | is_b
    end_a = info[0] // k_blocks
    start_b = (info[1] + k_blocks - 1) // k_blocks
    plain_low = jnp.where(is_b, start_b, 0)
    plain_high = jnp.where(is_b, count, jnp.where(is_a, end_a, 0))
    return plain_low, plain_high, jnp.where(pure, end_a, 0), jnp.where(pure, start_b, count)


def attend_kernel(groups, info, q_ref, k_ref, v_ref, o_ref, lse_ref, acc_ref):
    index = pl.program_id(0)
    heads, rows, _ = k_ref.shape
    width = q_ref.shape[1]
    tall = v_ref.shape[0] // heads
    spans_ = visible(info, index, width // BLOCK, KEYS // BLOCK, rows // KEYS)
    acc_ref[...] = jnp.zeros_like(acc_ref)
    query_ids = lax.broadcasted_iota(jnp.int32, (1, width), 1) + index * width
    key_ids = lax.broadcasted_iota(jnp.int32, (KEYS, 1), 0)
    ids = range(heads)

    def step(masked, j, tops):
        keys = pl.ds(pl.multiple_of(j * KEYS, KEYS), KEYS)
        scores = [mm(k_ref[h, keys, :], q_ref[h * HEAD : (h + 1) * HEAD, :], 1, 0) for h in ids]
        if masked:
            same = in_second(info, key_ids + j * KEYS, groups) == in_second(info, query_ids, groups)
            scores = [jnp.where(same, s, NEGATIVE) for s in scores]
        new = [jnp.maximum(tops[h], jnp.max(scores[h], 0, keepdims=True)) for h in ids]
        weights = [jnp.exp2(scores[h] - new[h]).astype(BF) for h in ids]
        shrink = [jnp.exp2(tops[h] - new[h]) for h in ids]
        sums = [mm(v_ref[h * tall : (h + 1) * tall, keys], weights[h], 1, 0) for h in ids]
        for h in ids:
            part = slice(h * tall, (h + 1) * tall)
            acc_ref[part, :] = acc_ref[part, :] * shrink[h] + sums[h]
        return tuple(new)

    tops = (jnp.full((1, width), START, F32),) * heads
    tops = lax.fori_loop(spans_[0], spans_[1], functools.partial(step, False), tops)
    tops = lax.fori_loop(spans_[2], spans_[3], functools.partial(step, True), tops)
    for h in ids:
        total = acc_ref[h * tall + HEAD : h * tall + HEAD + 1, :]
        out = (acc_ref[h * tall : h * tall + HEAD, :] / total).astype(BF)
        each = o_ref.shape[2]
        for i in range(width // each):
            o_ref[i, h * HEAD : (h + 1) * HEAD, :] = out[:, i * each : (i + 1) * each]
        lse_ref[h : h + 1, :] = tops[h] + jnp.log2(total)


def attend(info, q, k_rows, v, groups):
    local, rows = q.shape
    heads = local // HEAD
    return pl.pallas_call(
        functools.partial(attend_kernel, groups),
        grid_spec=pltpu.PrefetchScalarGridSpec(
            num_scalar_prefetch=1,
            grid=(rows // QUERIES,),
            in_specs=[
                pl.BlockSpec((local, QUERIES), lambda i, info: (0, i)),
                pl.BlockSpec((heads, rows, HEAD), lambda i, info: (0, 0, 0)),
                pl.BlockSpec(v.shape, lambda i, info: (0, 0)),
            ],
            out_specs=[
                pl.BlockSpec((QUERIES // BLOCK, local, BLOCK), lambda i, info: (i, 0, 0)),
                pl.BlockSpec((heads, QUERIES), lambda i, info: (0, i)),
            ],
            scratch_shapes=[pltpu.VMEM((v.shape[0], QUERIES), F32)],
        ),
        out_shape=[
            jax.ShapeDtypeStruct((rows // BLOCK, local, BLOCK), BF),
            jax.ShapeDtypeStruct((heads, rows), F32),
        ],
        compiler_params=pltpu.CompilerParams(vmem_limit_bytes=VMEM_LIMIT),
        cost_estimate=pl.CostEstimate(
            flops=2 * 2 * rows * rows * 256 * heads // 2,
            bytes_accessed=8 << 20,
            transcendentals=heads * rows * rows // 2,
        ),
        name="attend",
    )(info, q, k_rows, v)


def unturn(grad, cosine, sine):
    first = grad[:HALF]
    second = grad[HALF:]
    return jnp.concatenate(
        [first * cosine + second * sine, second * cosine - first * sine], 0
    ).astype(BF)


def attend_back_kernel(
    groups,
    info,
    q_ref,
    krow_ref,
    k_ref,
    vrow_ref,
    o_ref,
    do_ref,
    lse_ref,
    cos_ref,
    sin_ref,
    out_ref,
    dq_ref,
    dk_ref,
    dv_ref,
):
    index = pl.program_id(0)
    heads, rows, _ = krow_ref.shape
    width = heads * HEAD
    parts, _, share = out_ref.shape
    each = share // BLOCK
    ids = range(heads)
    part = [slice(h * HEAD, (h + 1) * HEAD) for h in ids]

    @pl.when(index == 0)
    def _():
        dk_ref[...] = jnp.zeros_like(dk_ref)
        dv_ref[...] = jnp.zeros_like(dv_ref)

    dq_ref[...] = jnp.zeros_like(dq_ref)
    query_ids = lax.broadcasted_iota(jnp.int32, (1, BLOCK), 1) + index * BLOCK
    key_ids = lax.broadcasted_iota(jnp.int32, (KEYS, 1), 0)
    delta = [
        jnp.sum(do_ref[0, p, :].astype(F32) * o_ref[0, p, :].astype(F32), 0, keepdims=True)
        for p in part
    ]
    spans_ = visible(info, index, 1, KEYS // BLOCK, rows // KEYS)

    def step(masked, j, carry):
        keys = pl.ds(pl.multiple_of(j * KEYS, KEYS), KEYS)
        scores = [mm(krow_ref[h, keys, :], q_ref[part[h], :], 1, 0) for h in ids]
        grad_soft = [mm(vrow_ref[h, keys, :], do_ref[0, part[h], :], 1, 0) for h in ids]
        if masked:
            same = in_second(info, key_ids + j * KEYS, groups) == in_second(info, query_ids, groups)
            scores = [jnp.where(same, s, NEGATIVE) for s in scores]
        soft = [jnp.exp2(scores[h] - lse_ref[h : h + 1, :]) for h in ids]
        grad_scores = [(soft[h] * (grad_soft[h] - delta[h])).astype(BF) for h in ids]
        soft = [s.astype(BF) for s in soft]
        dv = [mm(do_ref[0, part[h], :], soft[h], 1, 1) for h in ids]
        dk = [mm(q_ref[part[h], :], grad_scores[h], 1, 1) for h in ids]
        dq = [mm(k_ref[part[h], keys], grad_scores[h], 1, 0) for h in ids]
        for h in ids:
            dv_ref[part[h], keys] += dv[h]
            dk_ref[part[h], keys] += dk[h]
            dq_ref[part[h], :] += dq[h]
        return carry

    lax.fori_loop(spans_[0], spans_[1], functools.partial(step, False), 0)
    lax.fori_loop(spans_[2], spans_[3], functools.partial(step, True), 0)

    owner = index // each
    columns = pl.ds(pl.multiple_of(index * BLOCK, BLOCK), BLOCK)
    inside = pl.ds(pl.multiple_of(index % each * BLOCK, BLOCK), BLOCK)
    for h in ids:
        out_ref[owner, part[h], inside] = unturn(
            dq_ref[part[h], :] * HEAD ** (-0.5), cos_ref[:, columns], sin_ref[:, columns]
        )

    @pl.when(index == pl.num_programs(0) - 1)
    def _():
        @pl.loop(0, parts)
        def _(j):
            columns = pl.ds(pl.multiple_of(j * share, share), share)
            for h in ids:
                base = width + h * HEAD
                out_ref[j, base : base + HEAD, :] = unturn(
                    dk_ref[part[h], columns] * LOG_2, cos_ref[:, columns], sin_ref[:, columns]
                )
                base = 2 * width + h * HEAD
                out_ref[j, base : base + HEAD, :] = dv_ref[part[h], columns].astype(BF)


def attend_back(info, q, k_rows, k, v_rows, o, do, lse, cosine, sine, groups):
    parts = do.shape[0]
    local, rows = q.shape
    heads = local // HEAD
    blocks = rows // BLOCK
    each = blocks // parts
    whole = lambda *shape: pl.BlockSpec(shape, lambda i, info: (0,) * len(shape))
    return pl.pallas_call(
        functools.partial(attend_back_kernel, groups),
        grid_spec=pltpu.PrefetchScalarGridSpec(
            num_scalar_prefetch=1,
            grid=(blocks,),
            in_specs=[
                pl.BlockSpec((local, BLOCK), lambda i, info: (0, i)),
                whole(heads, rows, HEAD),
                whole(local, rows),
                whole(heads, rows, HEAD),
                pl.BlockSpec((1, local, BLOCK), lambda i, info: (i, 0, 0)),
                pl.BlockSpec(
                    (1, local, BLOCK),
                    lambda i, info: (jnp.bitwise_xor(i // each, info[2]), 0, i % each),
                ),
                pl.BlockSpec((heads, BLOCK), lambda i, info: (0, i)),
                whole(HALF, rows),
                whole(HALF, rows),
            ],
            out_specs=whole(parts, 3 * local, rows // parts),
            scratch_shapes=[
                pltpu.VMEM((local, BLOCK), F32),
                pltpu.VMEM((local, rows), F32),
                pltpu.VMEM((local, rows), F32),
            ],
        ),
        out_shape=jax.ShapeDtypeStruct((parts, 3 * local, rows // parts), BF),
        compiler_params=pltpu.CompilerParams(vmem_limit_bytes=VMEM_LIMIT),
        cost_estimate=pl.CostEstimate(
            flops=2 * 5 * rows * rows * 256 * heads // 2,
            bytes_accessed=16 << 20,
            transcendentals=heads * rows * rows // 2,
        ),
        name="attend_back",
    )(info, q, k_rows, k, v_rows, o, do, lse, cosine, sine)


def project_back_kernel(meta, d_ref, x_ref, w_ref, back_ref, grad_ref, acc_ref):
    index = pl.program_id(0)

    @pl.when(index == 0)
    def _():
        acc_ref[...] = jnp.zeros_like(acc_ref)

    d_t = d_ref[0]
    back_ref[0] = mm(d_t, w_ref[...], 0, 0).astype(BF)
    acc_ref[...] += mm(d_t, x_ref[0], 1, 0)

    @pl.when(index == pl.num_programs(0) - 1)
    def _():
        grad_ref[...] = acc_ref[...].T.astype(BF)


def project_back(meta, d_qkv_t, x_all, w_t):
    parts, local, share = d_qkv_t.shape
    width = w_t.shape[1]
    relative = lambda i, meta: (jnp.bitwise_xor(i, meta[2]), 0, 0)
    whole = lambda *shape: pl.BlockSpec(shape, lambda i, meta: (0,) * len(shape))
    return pl.pallas_call(
        project_back_kernel,
        grid_spec=pltpu.PrefetchScalarGridSpec(
            num_scalar_prefetch=1,
            grid=(parts,),
            in_specs=[
                pl.BlockSpec((1, local, share), lambda i, meta: (i, 0, 0)),
                pl.BlockSpec((1, share, width), lambda i, meta: (i, 0, 0)),
                whole(local, width),
            ],
            out_specs=[
                pl.BlockSpec((1, share, width), relative),
                whole(width, local),
            ],
            scratch_shapes=[pltpu.VMEM((local, width), F32)],
        ),
        out_shape=[
            jax.ShapeDtypeStruct((parts, share, width), BF),
            jax.ShapeDtypeStruct((width, local), BF),
        ],
        compiler_params=pltpu.CompilerParams(vmem_limit_bytes=VMEM_LIMIT),
        cost_estimate=pl.CostEstimate(
            flops=4 * parts * share * local * width, bytes_accessed=15 << 20, transcendentals=0
        ),
        name="project_back",
    )(meta, d_qkv_t, x_all, w_t)


MESH = pl.DeviceIdType.MESH


def greet(groups, steps, d, t):
    barrier = pltpu.get_barrier_semaphore()
    for k in range(1, groups):
        pl.semaphore_signal(
            barrier, inc=1, device_id=(lax.rem(d + k, groups), t), device_id_type=MESH
        )
    for step in steps:
        pl.semaphore_signal(
            barrier, inc=1, device_id=(d, jnp.bitwise_xor(t, step)), device_id_type=MESH
        )
    pl.semaphore_wait(barrier, groups - 1 + len(steps))


def remote(src, dst, send, recv, device):
    return pltpu.make_async_remote_copy(
        src_ref=src,
        dst_ref=dst,
        send_sem=send,
        recv_sem=recv,
        device_id=device,
        device_id_type=MESH,
    )


class Spread:
    def __init__(self, out, sems, groups, d, t):
        self.out, self.sems, self.groups, self.d, self.t = out, sems, groups, d, t

    def at(self, r, k, rest):
        return self.out.at[(r, lax.rem(self.d - k + self.groups, self.groups)) + rest]

    def arrival(self, source, k, rest, where):
        send, recv = self.sems
        to = lax.rem(self.d + k, self.groups)
        return remote(
            source, self.at(0, 0, rest), send.at[(0, k) + where], recv.at[(0, k) + where], (to, self.t)
        )

    def across(self, k, rest, where):
        send, recv = self.sems
        return remote(
            self.at(0, k, rest),
            self.at(2, k, rest),
            send.at[(2, k) + where],
            recv.at[(2, k) + where],
            (self.d, jnp.bitwise_xor(self.t, 2)),
        )

    def beside(self, r, k, rest, where):
        send, recv = self.sems
        return remote(
            self.at(r, k, rest),
            self.at(r + 1, k, rest),
            send.at[(r + 1, k) + where],
            recv.at[(r + 1, k) + where],
            (self.d, jnp.bitwise_xor(self.t, 1)),
        )


def norm_forward(resid_rows, gain_vec, shift_vec):
    row_mean = jnp.mean(resid_rows, -1, keepdims=True)
    centred = resid_rows - row_mean
    inverse = lax.rsqrt(jnp.mean(centred * centred, -1, keepdims=True) + EPSILON)
    unit_rows = centred * inverse
    return (unit_rows * gain_vec + shift_vec, unit_rows, inverse)


def norm_backward(upstream, unit_rows, inverse, gain_vec):
    scaled = upstream * gain_vec
    inner_term = (
        scaled
        - jnp.mean(scaled, -1, keepdims=True)
        - unit_rows * jnp.mean(scaled * unit_rows, -1, keepdims=True)
    )
    return (
        inner_term * inverse,
        jnp.sum(upstream * unit_rows, 0, keepdims=True),
        jnp.sum(upstream, 0, keepdims=True),
    )


def middle_kernel(size, groups, *refs):
    x_ref, match_ref, cot_ref, over_ref, norm_ref, blocks_ref = refs[:6]
    weights_hbm = refs[6:12]
    (
        result_ref,
        grad_one_ref,
        d_heads_ref,
        heads_ref,
        normed_t_ref,
        d_branch_t_ref,
        d_attn_t_ref,
        hidden_ref,
        d_gu_ref,
        norm_grad_ref,
        w_out_ref,
        w_gu_ref,
        w_down_ref,
        slope_ref,
        swish_ref,
        arrived_ref,
        sems,
        sends,
        recvs,
        keep,
    ) = refs[12:]
    index = pl.program_id(0)
    first = index == 0
    d = lax.axis_index("dp")
    t = lax.axis_index("tensor")
    subs, local, _ = arrived_ref.shape[1:]
    inner = w_down_ref.shape[2]
    ids = (0, 2, 1, 3)
    part = [slice(r * local, (r + 1) * local) for r in range(size)]
    core = (d, jnp.bitwise_xor(t, 1))
    targets = (lambda r: w_out_ref.at[part[r]], lambda r: w_gu_ref.at[r], lambda r: w_down_ref.at[r])

    def weight_copy(kind, r):
        source = weights_hbm[2 * kind + r // 2]
        if r % 2 == 0:
            return pltpu.make_async_copy(source, targets[kind](r), sems.at[kind, r])
        return remote(source, targets[kind](r), sems.at[kind, r - 1 + size], sems.at[kind, r], core)

    def weight_wait(kind, r):
        if r % 2 == 0:
            weight_copy(kind, r).wait()
        else:
            weight_copy(kind, r).wait_recv()

    def heads_copy(r, i):
        other = jnp.bitwise_xor(t, r)
        return remote(
            blocks_ref.at[other * subs + i],
            arrived_ref.at[r, i],
            sends.at[r, i],
            recvs.at[r, i],
            (d, other),
        )

    own_copy = pltpu.make_async_copy(blocks_ref.at[pl.ds(t * subs, subs)], arrived_ref.at[0], keep)

    @pl.when(first)
    def _():
        own_copy.start()
        for r in (0, 2):
            weight_copy(0, r).start()
        greet(1, (1, 2, 3), d, t)
        for i in range(subs):
            for r in (2, 3, 1):
                heads_copy(r, i).start()
            if i == 0:
                for r in (1, 3):
                    weight_copy(0, r).start()
        for r in ids:
            for kind in (1, 2):
                weight_copy(kind, r).start()
        own_copy.wait()
        for r in ids:
            weight_wait(0, r)

    for r in ids[1:]:
        heads_copy(r, index).wait_recv()
        heads_copy(r, index).wait_send()
    for r in ids:
        heads_ref[r] = arrived_ref[r, index]
    heads_out = jnp.concatenate([arrived_ref[r, index] for r in range(size)], 0)
    attn = mm(heads_out, w_out_ref[...], 0, 0)
    gain_one, gain_two, shift_one, shift_two = (norm_ref[i : i + 1, :] for i in range(4))
    normed_one, unit_one, inverse_one = norm_forward(
        x_ref[...].astype(F32) + attn, gain_one, shift_one
    )
    normed = normed_one.astype(BF)
    normed_t_ref[...] = normed_one.T.astype(BF)
    branch = jnp.zeros(normed_one.shape, F32)
    for r in ids:

        @pl.when(first)
        def _():
            weight_wait(1, r)
            weight_wait(2, r)

        both = mm(normed, w_gu_ref[r], 1, 0)
        gate = both[:, :inner]
        up = both[:, inner:]
        sig = jax.nn.sigmoid(gate)
        swish = gate * sig
        hidden = (swish * up).astype(BF)
        swish_ref[r] = swish
        slope_ref[r] = up * sig * (1.0 + gate * (1.0 - sig))
        hidden_ref[r] = hidden
        branch = branch + mm(hidden, w_down_ref[r], 1, 1)
    result, unit_two, inverse_two = norm_forward(normed_one + branch, gain_two, shift_two)
    result_ref[...] = result.astype(BF)
    if groups:
        sub = BLOCK // groups
        spares = [over_ref[g, 0:1, :].astype(F32) for g in range(groups)]
        in_last = jnp.where((index == subs - 1) & (t == size - 1), 1.0, 0.0)
        ends = lax.broadcasted_iota(jnp.int32, (sub, 1), 0) == sub - 1
        pieces = []
        for g in range(groups):
            piece = cot_ref[g].astype(F32)
            spare, flag = spare_row(match_ref, groups, g, spares)
            fix = jnp.where(ends, flag * in_last, 0.0)
            pieces.append(piece * (1.0 - fix) + spare * fix)
        cot = jnp.concatenate(pieces, 0)
    else:
        cot = cot_ref[...].astype(F32)
    grad_two, d_gain_two, d_shift_two = norm_backward(cot, unit_two, inverse_two, gain_two)
    d_branch = grad_two.astype(BF)
    d_branch_t_ref[...] = grad_two.T.astype(BF)
    back = grad_two
    for r in ids:
        grad_hidden = mm(d_branch, w_down_ref[r], 1, 0)
        d_gate = (grad_hidden * slope_ref[r]).astype(BF)
        d_up = (grad_hidden * swish_ref[r]).astype(BF)
        d_gu_ref[r, :, :inner] = d_gate
        d_gu_ref[r, :, inner:] = d_up
        back = back + mm(jnp.concatenate([d_gate, d_up], 1), w_gu_ref[r], 1, 1)
    grad_one, d_gain_one, d_shift_one = norm_backward(back, unit_one, inverse_one, gain_one)
    grad_one_ref[...] = grad_one
    d_attn_t = grad_one.T.astype(BF)
    d_attn_t_ref[...] = d_attn_t
    d_heads = mm(w_out_ref[...], d_attn_t, 1, 0).astype(BF)
    for r in ids:
        d_heads_ref[r] = d_heads[part[r]]

    @pl.when(first)
    def _():
        norm_grad_ref[...] = jnp.zeros_like(norm_grad_ref)

    @pl.when(index == subs - 1)
    def _():
        for kind in range(3):
            for r in (1, 3):
                weight_copy(kind, r).wait_send()

    for i, grad in enumerate((d_gain_one, d_gain_two, d_shift_one, d_shift_two)):
        norm_grad_ref[i : i + 1, :] += grad


def middle(x_own, match, cot, norms, o_blocks, size, *weights):
    rows, width = x_own.shape
    local = o_blocks.shape[1]
    inner = weights[-1].shape[1]
    block = pl.BlockSpec((BLOCK, width), lambda i: (i, 0))
    turned = pl.BlockSpec((width, BLOCK), lambda i: (0, i))
    anywhere = pl.BlockSpec(memory_space=pl.ANY)
    shape = jax.ShapeDtypeStruct
    groups = cot.shape[0] if cot.ndim == 3 else 0
    if groups:
        sub = BLOCK // groups
        last = cot.shape[1] // 16 - 1
        cot_specs = [
            pl.BlockSpec((groups, sub, width), lambda i: (0, i, 0)),
            pl.BlockSpec((groups, 16, width), lambda i: (0, last, 0)),
        ]
    else:
        cot_specs = [block, pl.BlockSpec((16, width), lambda i: (0, 0))]
    return pl.pallas_call(
        functools.partial(middle_kernel, size, groups),
        grid=(rows // BLOCK,),
        in_specs=[block, pl.BlockSpec(memory_space=pltpu.SMEM)]
        + cot_specs
        + [pl.BlockSpec(norms.shape, lambda i: (0, 0))]
        + [anywhere] * (1 + len(weights)),
        out_specs=[
            block,
            block,
            pl.BlockSpec((size, local, BLOCK), lambda i: (0, 0, i)),
            pl.BlockSpec((size, local, BLOCK), lambda i: (0, 0, i)),
            turned,
            turned,
            turned,
            pl.BlockSpec((size, BLOCK, inner), lambda i: (0, i, 0)),
            pl.BlockSpec((size, BLOCK, 2 * inner), lambda i: (0, i, 0)),
            pl.BlockSpec((8, width), lambda i: (0, 0)),
        ],
        out_shape=[
            shape((rows, width), BF),
            shape((rows, width), F32),
            shape((size, local, rows), BF),
            shape((size, local, rows), BF),
            shape((width, rows), BF),
            shape((width, rows), BF),
            shape((width, rows), BF),
            shape((size, rows, inner), BF),
            shape((size, rows, 2 * inner), BF),
            shape((8, width), F32),
        ],
        scratch_shapes=[
            pltpu.VMEM((size * local, width), BF),
            pltpu.VMEM((size, width, 2 * inner), BF),
            pltpu.VMEM((size, width, inner), BF),
            pltpu.VMEM((size, BLOCK, inner), F32),
            pltpu.VMEM((size, BLOCK, inner), F32),
            pltpu.VMEM((size, rows // BLOCK, local, BLOCK), BF),
            pltpu.SemaphoreType.DMA((3, 2 * size)),
            pltpu.SemaphoreType.DMA((size, rows // BLOCK)),
            pltpu.SemaphoreType.DMA((size, rows // BLOCK)),
            pltpu.SemaphoreType.DMA,
        ],
        compiler_params=pltpu.CompilerParams(
            collective_id=2, has_side_effects=True, vmem_limit_bytes=VMEM_LIMIT
        ),
        cost_estimate=pl.CostEstimate(
            flops=2 * rows * width * (6 * size * inner + 2 * size * local),
            bytes_accessed=40 << 20,
            transcendentals=rows * size * inner,
        ),
        name="middle",
    )(x_own, match, cot, cot, norms, o_blocks, *weights)


def weight_grads_tile(
    normed_t_ref, d_branch_t_ref, d_attn_t_ref, hidden_ref, d_gu_ref, heads_ref, norm_ref, store
):
    inner = hidden_ref.shape[2]
    local = heads_ref.shape[1]
    width = normed_t_ref.shape[0]
    store(0, 2 * inner, mm(normed_t_ref[...], d_gu_ref[0], 1, 0))
    store(2 * inner, 3 * inner, mm(d_branch_t_ref[...], hidden_ref[0], 1, 0))
    d_out = mm(d_attn_t_ref[...], heads_ref[0], 1, 1)
    norm = norm_ref[...].T
    spare = -(local + norm.shape[1]) % 128
    tail = jnp.concatenate([d_out, norm, jnp.zeros((width, spare), F32)], 1)
    store(3 * inner, 3 * inner + tail.shape[1], tail)


def weight_grads_kernel(*refs):
    out_ref = refs[-1]

    def store(low, high, value):
        out_ref[0, :, low:high] = value.astype(BF)

    weight_grads_tile(*refs[:-1], store)


def weight_grads(odd, normed_t, d_branch_t, d_attn_t, hidden, d_gu, heads, norm_grads):
    size, rows, inner = hidden.shape
    local = heads.shape[1]
    width = normed_t.shape[0]
    wide = 3 * inner + local + norm_grads.shape[0]
    wide = (wide + 127) // 128 * 128
    flat = pl.BlockSpec((width, rows), lambda i: (0, 0))
    pick = lambda i: (2 * i + odd, 0, 0)
    return pl.pallas_call(
        weight_grads_kernel,
        grid=(size // 2,),
        in_specs=[
            flat,
            flat,
            flat,
            pl.BlockSpec((1, rows, inner), pick),
            pl.BlockSpec((1, rows, 2 * inner), pick),
            pl.BlockSpec((1, local, rows), pick),
            pl.BlockSpec(norm_grads.shape, lambda i: (0, 0)),
        ],
        out_specs=pl.BlockSpec((1, width, wide), lambda i: (i, 0, 0)),
        out_shape=jax.ShapeDtypeStruct((size // 2, width, wide), BF),
        compiler_params=pltpu.CompilerParams(vmem_limit_bytes=VMEM_LIMIT),
        cost_estimate=pl.CostEstimate(
            flops=size * rows * width * (3 * inner + local), bytes_accessed=20 << 20, transcendentals=0
        ),
        name="weight_grads",
    )(normed_t, d_branch_t, d_attn_t, hidden, d_gu, heads, norm_grads)


def grads_kernel(groups, size, match_ref, *refs):
    tile_refs = refs[:7]
    (
        d_heads_ref,
        result_ref,
        gu_own_ref,
        gu_other_ref,
        pair_ref,
        do_ref,
        home_ref,
        over_ref,
        sent_ref,
        got_ref,
        own_ref,
        spare_ref,
        s_grad,
        r_grad,
        s_heads,
        r_heads,
        sends,
        recvs,
        s_over,
        r_over,
        keep,
    ) = refs[7:]
    step = pl.program_id(0)
    d = lax.axis_index("dp")
    t = lax.axis_index("tensor")
    chunks, _, sub, width = own_ref.shape
    core = (d, jnp.bitwise_xor(t, 1))
    body = Spread(home_ref, (sends, recvs), groups, d, t)
    extra = Spread(over_ref, (s_over, r_over), groups, d, t)

    def heads_copy(r):
        return remote(
            d_heads_ref.at[r],
            do_ref.at[r],
            s_heads.at[r],
            r_heads.at[r],
            (d, jnp.bitwise_xor(t, r)),
        )

    def grad_copy(i):
        return remote(sent_ref.at[i], got_ref.at[i], s_grad.at[i], r_grad.at[i], core)

    def own_copy(c):
        return pltpu.make_async_copy(own_ref.at[c, d], home_ref.at[0, d, c], keep.at[c])

    def pass_on(c):
        own_copy(c).wait()
        for k in range(groups):
            if k > 0:
                body.arrival(own_ref.at[c, 0], k, (c,), (c,)).wait_recv()
            body.across(k, (c,), (c,)).start()

    load = pltpu.make_async_copy(result_ref, own_ref, keep.at[chunks])
    own_heads = pltpu.make_async_copy(d_heads_ref.at[0], do_ref.at[0], keep.at[chunks + 1])
    own_over = pltpu.make_async_copy(spare_ref.at[d], over_ref.at[0, d], keep.at[chunks + 2])

    @pl.when(step == 0)
    def _():
        load.start()
        own_heads.start()
        greet(groups, (1, 2, 3), d, t)
        for r in (2, 3, 1):
            heads_copy(r).start()
        load.wait()
        for c in range(chunks):
            own_copy(c).start()
            for k in range(1, groups):
                body.arrival(own_ref.at[c, lax.rem(d + k, groups)], k, (c,), (c,)).start()
        last = [own_ref[chunks - 1, g, sub - 16 :, :].astype(F32)[15:16] for g in range(groups)]
        for to in range(groups):
            spare = last[0] * match_ref[to]
            for g in range(1, groups):
                spare = spare + last[g] * match_ref[g * groups + to]
            spare_ref[to] = spare.astype(BF)
        own_over.start()
        for k in range(1, groups):
            extra.arrival(spare_ref.at[lax.rem(d + k, groups)], k, (), ()).start()

    for c in range(chunks - 1):

        @pl.when(step == c + 2)
        def _():
            pass_on(c)

    @pl.when(step < 2)
    def _():
        def store(low, high, value):
            sent_ref[step, :, low:high] = value.astype(BF)

        weight_grads_tile(*tile_refs, store)
        grad_copy(step).start()

    gu_wide = gu_own_ref.shape[1]
    for i, gu_ref in ((0, gu_own_ref), (1, gu_other_ref)):

        @pl.when(step == 2 + i)
        def _():
            grad_copy(i).wait_recv()

            def store(low, high, value):
                total = (value + got_ref[i, :, low:high].astype(F32)).astype(BF)
                if high <= gu_wide:
                    gu_ref[:, low:high] = total
                else:
                    pair_ref[0, :, low - gu_wide : high - gu_wide] = total

            weight_grads_tile(*tile_refs, store)

    @pl.when(step == size - 1)
    def _():
        own_over.wait()
        for k in range(groups):
            if k > 0:
                extra.arrival(spare_ref.at[0], k, (), ()).wait_recv()
            extra.across(k, (), ()).start()
            extra.beside(0, k, (), ()).start()
        for k in range(groups):
            extra.across(k, (), ()).wait_recv()
            extra.beside(2, k, (), ()).start()
        own_heads.wait()
        for r in range(1, size):
            heads_copy(r).wait_recv()
            heads_copy(r).wait_send()
        for i in range(2):
            grad_copy(i).wait_send()
        own_copy(chunks - 1).wait()
        for c in range(chunks):
            for k in range(groups):
                if k > 0 and c == chunks - 1:
                    body.arrival(own_ref.at[c, 0], k, (c,), (c,)).wait_recv()
                if k > 0:
                    body.arrival(own_ref.at[c, 0], k, (c,), (c,)).wait_send()
                if c < chunks - 1:
                    body.across(k, (c,), (c,)).wait_recv()
                    body.across(k, (c,), (c,)).wait_send()
        for k in range(groups):
            extra.beside(0, k, (), ()).wait_recv()
            extra.beside(2, k, (), ()).wait_recv()
            if k > 0:
                extra.arrival(spare_ref.at[0], k, (), ()).wait_send()
            extra.across(k, (), ()).wait_send()
            extra.beside(0, k, (), ()).wait_send()
            extra.beside(2, k, (), ()).wait_send()


def grads(
    match, groups, normed_t, d_branch_t, d_attn_t, hidden, d_gu, heads, norm_grads, d_heads, result
):
    size, rows, inner = hidden.shape
    local = heads.shape[1]
    width = normed_t.shape[0]
    chunks = rows // BLOCK
    sub = BLOCK // groups
    wide = 3 * inner + (local + norm_grads.shape[0] + 127) // 128 * 128
    flat = pl.BlockSpec((width, rows), lambda i: (0, 0))
    pick = lambda i: (jnp.where(i < 2, 2 * i + 1, 2 * i - 4), 0, 0)
    anywhere = pl.BlockSpec(memory_space=pl.ANY)
    dma = pltpu.SemaphoreType.DMA
    return pl.pallas_call(
        functools.partial(grads_kernel, groups, size),
        grid=(size,),
        in_specs=[
            pl.BlockSpec(memory_space=pltpu.SMEM),
            flat,
            flat,
            flat,
            pl.BlockSpec((1, rows, inner), pick),
            pl.BlockSpec((1, rows, 2 * inner), pick),
            pl.BlockSpec((1, local, rows), pick),
            pl.BlockSpec(norm_grads.shape, lambda i: (0, 0)),
            anywhere,
            anywhere,
        ],
        out_specs=[
            pl.BlockSpec((width, 2 * inner), lambda i: (0, 0)),
            pl.BlockSpec((width, 2 * inner), lambda i: (0, 0)),
            pl.BlockSpec((1, width, wide - 2 * inner), lambda i: (jnp.maximum(i - 2, 0), 0, 0)),
            anywhere,
            anywhere,
            anywhere,
        ],
        out_shape=[
            jax.ShapeDtypeStruct((width, 2 * inner), BF),
            jax.ShapeDtypeStruct((width, 2 * inner), BF),
            jax.ShapeDtypeStruct((2, width, wide - 2 * inner), BF),
            jax.ShapeDtypeStruct(d_heads.shape, BF),
            jax.ShapeDtypeStruct((3, groups, chunks, sub, width), BF),
            jax.ShapeDtypeStruct((size, groups, 1, width), BF),
        ],
        scratch_shapes=[
            pltpu.VMEM((2, width, wide), BF),
            pltpu.VMEM((2, width, wide), BF),
            pltpu.VMEM((chunks, groups, sub, width), BF),
            pltpu.VMEM((groups, 1, width), BF),
            dma((2,)),
            dma((2,)),
            dma((size,)),
            dma((size,)),
            dma((3, groups, chunks)),
            dma((3, groups, chunks)),
            dma((4, groups)),
            dma((4, groups)),
            dma((chunks + 3,)),
        ],
        compiler_params=pltpu.CompilerParams(
            collective_id=3, has_side_effects=True, vmem_limit_bytes=VMEM_LIMIT
        ),
        cost_estimate=pl.CostEstimate(
            flops=2 * size * rows * width * (3 * inner + local),
            bytes_accessed=80 << 20,
            transcendentals=0,
        ),
        name="grads",
    )(
        match,
        normed_t,
        d_branch_t,
        d_attn_t,
        hidden,
        d_gu,
        heads,
        norm_grads,
        d_heads,
        result.reshape(chunks, groups, sub, width),
    )


def swap(array, size, step):
    return lax.ppermute(array, "tensor", [(i, i ^ step) for i in range(size)])


def gather_members(own):
    size = lax.axis_size("tensor")
    across = swap(own, size, 2)
    return [own, swap(own, size, 1), across, swap(across, size, 1)]


def exchange_members(pieces):
    size = lax.axis_size("tensor")
    return [pieces[0]] + [swap(pieces[r], size, r) for r in range(1, size)]


def reduce_members(pieces):
    size = lax.axis_size("tensor")
    near = swap(pieces[1], size, 1)
    far = swap(pieces[3], size, 1)
    other = (pieces[2].astype(F32) + far.astype(F32)).astype(BF)
    across = swap(other, size, 2)
    return pieces[0].astype(F32) + near.astype(F32) + across.astype(F32)


def unpack_block(spots_ref, src_ref, i):
    window = ROWS + 16
    shape = (ROWS, window)
    rows = lax.broadcasted_iota(jnp.int32, shape, 0)
    steps = lax.broadcasted_iota(jnp.int32, shape, 1) - rows
    bound = spots_ref[8 * i + 6]
    total = None
    for k in range(2):
        group, start, shift = (spots_ref[8 * i + 3 * k + j] for j in range(3))
        wanted = rows < bound if k == 0 else rows >= bound
        hot = jnp.where((steps == shift) & wanted, 1.0, 0.0).astype(BF)
        tiles = [src_ref[group, start + j] for j in range(window // 16)]
        part = mm(hot, jnp.concatenate(tiles, 0), 1, 0)
        total = part if k == 0 else total + part
    return total.astype(BF)


def store_over(src_ref, over_ref, last):
    top = lax.broadcasted_iota(jnp.int32, (16, 1), 0) == 0
    end = src_ref.shape[1] - 1
    for g in range(src_ref.shape[0]):
        src_ref[g, end] = jnp.where(top, over_ref[last, g].astype(F32), 0.0).astype(BF)


def unpack_kernel(size, spots, me, home_ref, over_ref, out_ref, src_ref, sems):
    tiles = home_ref.shape[2]

    def load(r):
        at = pl.ds(jnp.bitwise_xor(me[0], r) * tiles, tiles)
        return pltpu.make_async_copy(home_ref.at[r], src_ref.at[:, at], sems.at[r])

    for r in range(size):
        load(r).start()
    store_over(src_ref, over_ref, jnp.bitwise_xor(size - 1, me[0]))
    for r in range(size):
        load(r).wait()
    for i in range(out_ref.shape[0] // ROWS):
        out_ref[i * ROWS : (i + 1) * ROWS, :] = unpack_block(spots, src_ref, i)


def unpack(spots, me, home, over):
    size, groups, share, width = home.shape
    rows = size * groups * share
    home = home.reshape(size, groups, share // 16, 16, width)
    whole = lambda *shape: pl.BlockSpec(shape, lambda i, *refs: (0,) * len(shape))
    return pl.pallas_call(
        functools.partial(unpack_kernel, size),
        grid_spec=pltpu.PrefetchScalarGridSpec(
            num_scalar_prefetch=2,
            grid=(1,),
            in_specs=[pl.BlockSpec(memory_space=pl.ANY), whole(*over.shape)],
            out_specs=whole(rows, width),
            scratch_shapes=[
                pltpu.VMEM((groups, size * share // 16 + 1, 16, width), BF),
                pltpu.SemaphoreType.DMA((size,)),
            ],
        ),
        out_shape=jax.ShapeDtypeStruct((rows, width), BF),
        compiler_params=pltpu.CompilerParams(vmem_limit_bytes=VMEM_LIMIT),
        cost_estimate=pl.CostEstimate(flops=0, bytes_accessed=30 << 20, transcendentals=0),
        name="unpack",
    )(spots, me, home, over)


def route_kernel(groups, size, send_ref, over_ref, out_ref, over_out_ref, sends, recvs, keep):
    d = lax.axis_index("dp")
    t = lax.axis_index("tensor")
    greet(groups, (1, 2), d, t)
    spread = Spread(out_ref, (sends, recvs), groups, d, t)
    own = pltpu.make_async_copy(send_ref.at[d], out_ref.at[0, d], keep.at[0])
    own_over = pltpu.make_async_copy(over_ref.at[d], over_out_ref.at[d], keep.at[1])
    own.start()
    own_over.start()

    def over_copy(k):
        to = lax.rem(d + k, groups)
        return remote(
            over_ref.at[to], over_out_ref.at[d], sends.at[4, k], recvs.at[4, k], (to, t)
        )

    for k in range(1, groups):
        spread.arrival(send_ref.at[lax.rem(d + k, groups)], k, (), ()).start()
    for k in range(1, groups):
        over_copy(k).start()
    own.wait()
    for k in range(groups):
        if k > 0:
            spread.arrival(send_ref.at[0], k, (), ()).wait_recv()
        spread.across(k, (), ()).start()
        spread.beside(0, k, (), ()).start()
        if k > 0:
            spread.across(k - 1, (), ()).wait_recv()
            spread.beside(2, k - 1, (), ()).start()
    spread.across(groups - 1, (), ()).wait_recv()
    spread.beside(2, groups - 1, (), ()).start()
    own_over.wait()
    for k in range(groups):
        spread.beside(0, k, (), ()).wait_recv()
        spread.beside(2, k, (), ()).wait_recv()
        if k > 0:
            over_copy(k).wait_recv()
            over_copy(k).wait_send()
            spread.arrival(send_ref.at[0], k, (), ()).wait_send()
        spread.across(k, (), ()).wait_send()
        spread.beside(0, k, (), ()).wait_send()
        spread.beside(2, k, (), ()).wait_send()


def route(send, over, size):
    groups = send.shape[0]
    anywhere = pl.BlockSpec(memory_space=pl.ANY)
    return pl.pallas_call(
        functools.partial(route_kernel, groups, size),
        in_specs=[anywhere, anywhere],
        out_specs=[anywhere, anywhere],
        out_shape=[
            jax.ShapeDtypeStruct((size,) + send.shape, BF),
            jax.ShapeDtypeStruct(over.shape, BF),
        ],
        scratch_shapes=[
            pltpu.SemaphoreType.DMA((5, groups)),
            pltpu.SemaphoreType.DMA((5, groups)),
            pltpu.SemaphoreType.DMA((2,)),
        ],
        compiler_params=pltpu.CompilerParams(collective_id=0, has_side_effects=True),
        cost_estimate=pl.CostEstimate(flops=0, bytes_accessed=60 << 20, transcendentals=0),
        name="route",
    )(send, over)


class Halving:
    def __init__(self, fetch, bits, refs, sems, d, t):
        self.fetch, self.bits, self.d, self.t = fetch, bits, d, t
        self.out, self.got, self.held = refs
        self.send, self.recv = sems

    def mine(self, step):
        return lax.rem(lax.div(self.d, self.bits[step]), 2)

    def block(self, first, i):
        one, two, three = self.bits
        return first * one + lax.rem(i, 2) * two + lax.div(i, 2) * three

    def copy(self, i):
        step = 0 if i < 4 else 1 if i < 6 else 2
        return remote(
            self.out.at[i],
            self.got.at[i],
            self.send.at[i],
            self.recv.at[i],
            (jnp.bitwise_xor(self.d, self.bits[step]), self.t),
        )

    def start(self):
        for i in range(4):
            self.out[i] = self.fetch(self.block(1 - self.mine(0), jnp.int32(i))).astype(BF)
            self.copy(i).start()

    def second(self):
        for i in range(4):
            self.copy(i).wait_recv()
        own = self.mine(1)
        for keep in (False, True):
            for j in range(2):
                i = (own if keep else 1 - own) + 2 * j
                value = self.fetch(self.block(self.mine(0), i)) + self.got[i].astype(F32)
                if keep:
                    self.held[j] = value
                else:
                    self.out[4 + j] = value.astype(BF)
                    self.copy(4 + j).start()

    def third(self):
        for j in range(2):
            self.copy(4 + j).wait_recv()
        other = 1 - self.mine(2)
        self.out[6] = (self.held[other] + self.got[4 + other].astype(F32)).astype(BF)
        self.copy(6).start()

    def total(self):
        self.copy(6).wait_recv()
        own = self.mine(2)
        return self.held[own] + self.got[4 + own].astype(F32) + self.got[6].astype(F32)

    def finish(self):
        for i in range(7):
            self.copy(i).wait_send()


def settle_kernel(
    groups,
    size,
    match_ref,
    spots_ref,
    res_over_ref,
    d_hbm,
    x_hbm,
    w_hbm,
    one_hbm,
    gu_own_hbm,
    gu_other_hbm,
    res_hbm,
    home_ref,
    over_ref,
    result_hbm,
    gq_sum_ref,
    gu_sum_ref,
    d_ref,
    x_ref,
    w_ref,
    one_ref,
    gu_own_ref,
    gu_other_ref,
    src_ref,
    out_ref,
    to_core_ref,
    from_core_ref,
    pair_ref,
    other_ref,
    own_ref,
    spare_ref,
    gq_ref,
    *refs,
):
    halving_refs = (refs[:3], refs[3:6], refs[6:9])
    (
        loads,
        s_res,
        r_res,
        s_half,
        r_half,
        sends,
        recvs,
        s_over,
        r_over,
        s_sum,
        r_sum,
        keep,
    ) = refs[9:]
    d = lax.axis_index("dp")
    t = lax.axis_index("tensor")
    chunks, _, sub, width = own_ref.shape
    tiles = res_hbm.shape[2]
    sent = (chunks - 1) * tiles // chunks
    rest = tiles - sent
    core = (d, jnp.bitwise_xor(t, 1))
    chip = (d, jnp.bitwise_xor(t, 2))

    def load(source, target, i):
        return pltpu.make_async_copy(source, target, loads.at[i])

    def load_d(r):
        part = jnp.bitwise_xor(t, r)
        return load(d_hbm.at[part], d_ref.at[part], r)

    load_w = load(w_hbm, w_ref, 4)
    load_x = load(x_hbm, x_ref, 5)
    load_one = load(one_hbm, one_ref, 6)
    load_gu = (load(gu_own_hbm, gu_own_ref, 7), load(gu_other_hbm, gu_other_ref, 8))

    def slots_of(r, low, count):
        return pl.ds(jnp.bitwise_xor(t, r) * tiles + low, count)

    def source_of(r, low, count):
        return res_hbm.at[r, :, pl.ds(low, count)]

    def in_src(r, low, count):
        return src_ref.at[:, slots_of(r, low, count)]

    load_res = (
        load(source_of(0, 0, tiles), in_src(0, 0, tiles), 9),
        load(source_of(2, 0, sent), in_src(2, 0, sent), 10),
    )
    beside_res = (
        remote(source_of(0, 0, tiles), in_src(0, 0, tiles), s_res.at[0], r_res.at[0], core),
        remote(source_of(2, 0, sent), in_src(2, 0, sent), s_res.at[1], r_res.at[1], core),
        remote(in_src(2, sent, rest), in_src(2, sent, rest), s_res.at[2], r_res.at[2], core),
    )
    across_res = remote(
        source_of(0, sent, rest), in_src(0, sent, rest), s_res.at[3], r_res.at[3], chip
    )

    load_w.start()
    for r in (3, 2, 1, 0):
        load_d(r).start()
    load_gu[0].start()
    load_gu[1].start()
    load_x.start()
    load_one.start()
    load_res[0].start()
    load_res[1].start()
    greet(groups, (1, 2), d, t)
    across_res.start()

    def rows(c):
        return slice(c * BLOCK, (c + 1) * BLOCK)

    def piece(r, c):
        return mm(d_ref[jnp.bitwise_xor(t, r), :, rows(c)], w_ref[...], 0, 0)

    def to_core(i, c):
        return remote(
            to_core_ref.at[i, c], from_core_ref.at[i, c], s_sum.at[i, c], r_sum.at[i, c], core
        )

    def other(c):
        return remote(pair_ref.at[c], other_ref.at[c], s_sum.at[2, c], r_sum.at[2, c], chip)

    load_w.wait()
    load_d(3).wait()
    for c in range(chunks):
        to_core_ref[0, c] = piece(3, c).astype(BF)
        to_core(0, c).start()
    load_d(2).wait()
    for c in range(chunks):
        value = piece(2, c)
        to_core(0, c).wait_recv()
        pair_ref[c] = (value + from_core_ref[0, c].astype(F32)).astype(BF)
        other(c).start()
    block_rows = gu_sum_ref.shape[0]

    wide = gu_sum_ref.shape[1] // 2

    def gu_rows(low, block):
        at = pl.ds(pl.multiple_of(block * block_rows, block_rows), block_rows)
        columns = slice(low, low + wide)
        return gu_own_ref[at, columns].astype(F32) + gu_other_ref[at, columns].astype(F32)

    sums = [
        Halving(fetch, bits, halving_refs[i], (s_half.at[i], r_half.at[i]), d, t)
        for i, (fetch, bits) in enumerate(
            (
                (functools.partial(gu_rows, 0), (1, 2, 4)),
                (functools.partial(gu_rows, wide), (2, 1, 4)),
                (lambda block: gq_ref[block].astype(F32), (1, 2, 4)),
            )
        )
    ]

    load_gu[0].wait()
    load_gu[1].wait()
    sums[0].start()
    sums[1].start()
    load_d(1).wait()
    for c in range(chunks):
        to_core_ref[1, c] = piece(1, c).astype(BF)
        to_core(1, c).start()
    load_d(0).wait()
    load_one.wait()
    for c in range(chunks):
        one_ref[rows(c), :] += piece(0, c)

    def start_gq():
        load_x.wait()
        total = mm(d_ref[0], x_ref[0], 1, 0)
        for part in range(1, size):
            total = total + mm(d_ref[part], x_ref[part], 1, 0)
        total = total.T.astype(BF)
        for g in range(groups):
            gq_ref[g] = total[g * block_rows : (g + 1) * block_rows]
        sums[2].start()

    def store_result(i):
        at = pl.ds(i * ROWS, ROWS)
        return pltpu.make_async_copy(out_ref.at[at], result_hbm.at[at], keep.at[chunks + 1 + i])

    blocks = out_ref.shape[0] // ROWS

    def arrange_result():
        for copy in load_res:
            copy.wait()
        for copy in beside_res:
            copy.wait_recv()
        for i in range(blocks):
            out_ref[i * ROWS : (i + 1) * ROWS, :] = unpack_block(spots_ref, src_ref, i)
            store_result(i).start()

    store_over(src_ref, res_over_ref, jnp.bitwise_xor(size - 1, t))

    body = Spread(home_ref, (sends, recvs), groups, d, t)
    extra = Spread(over_ref, (s_over, r_over), groups, d, t)

    def own_copy(c):
        return pltpu.make_async_copy(own_ref.at[c, d], home_ref.at[0, d, c], keep.at[c])

    own_over = pltpu.make_async_copy(spare_ref.at[d], over_ref.at[0, d], keep.at[chunks])

    def pass_on(c):
        own_copy(c).wait()
        for k in range(groups):
            if k > 0:
                body.arrival(own_ref.at[c, 0], k, (c,), (c,)).wait_recv()
            body.across(k, (c,), (c,)).start()
            body.beside(0, k, (c,), (c,)).start()

    def pass_far(c):
        for k in range(groups):
            body.across(k, (c,), (c,)).wait_recv()
            body.beside(2, k, (c,), (c,)).start()

    for c in range(chunks):
        to_core(1, c).wait_recv()
        partial = one_ref[rows(c), :] + from_core_ref[1, c].astype(F32)
        other(c).wait_recv()
        done = (partial + other_ref[c].astype(F32)).astype(BF)
        for g in range(groups):
            own_ref[c, g] = done[g * sub : (g + 1) * sub]
        own_copy(c).start()
        for k in range(1, groups):
            body.arrival(own_ref.at[c, lax.rem(d + k, groups)], k, (c,), (c,)).start()
        if c == chunks - 1:
            last = [own_ref[c, g, sub - 16 :, :].astype(F32)[15:16] for g in range(groups)]
            for to in range(groups):
                spare = last[0] * match_ref[to]
                for g in range(1, groups):
                    spare = spare + last[g] * match_ref[g * groups + to]
                spare_ref[to] = spare.astype(BF)
            own_over.start()
            for k in range(1, groups):
                extra.arrival(spare_ref.at[lax.rem(d + k, groups)], k, (), ()).start()
        if c == 0:
            across_res.wait_recv()
            for copy in beside_res:
                copy.start()
            start_gq()
            sums[0].second()
            sums[1].second()
        else:
            pass_on(c - 1)
        if c == 1:
            sums[0].third()
            sums[1].third()
    sums[2].second()
    pass_on(chunks - 1)
    sums[2].third()
    arrange_result()
    own_over.wait()
    for k in range(groups):
        if k > 0:
            extra.arrival(spare_ref.at[0], k, (), ()).wait_recv()
        extra.across(k, (), ()).start()
        extra.beside(0, k, (), ()).start()
    gu_sum_ref[:, :wide] = sums[0].total()
    gu_sum_ref[:, wide:] = sums[1].total()
    gq_sum_ref[...] = sums[2].total()
    for c in range(chunks):
        pass_far(c)
    for k in range(groups):
        extra.across(k, (), ()).wait_recv()
        extra.beside(2, k, (), ()).start()
    across_res.wait_send()
    for copy in beside_res:
        copy.wait_send()
    for i in range(blocks):
        store_result(i).wait()
    for each in sums:
        each.finish()
    for c in range(chunks):
        to_core(0, c).wait_send()
        to_core(1, c).wait_send()
        other(c).wait_send()
    for k in range(groups):
        for c in range(chunks):
            body.beside(0, k, (c,), (c,)).wait_recv()
            body.beside(2, k, (c,), (c,)).wait_recv()
            if k > 0:
                body.arrival(own_ref.at[c, 0], k, (c,), (c,)).wait_send()
            body.across(k, (c,), (c,)).wait_send()
            body.beside(0, k, (c,), (c,)).wait_send()
            body.beside(2, k, (c,), (c,)).wait_send()
        extra.beside(0, k, (), ()).wait_recv()
        extra.beside(2, k, (), ()).wait_recv()
        if k > 0:
            extra.arrival(spare_ref.at[0], k, (), ()).wait_send()
        extra.across(k, (), ()).wait_send()
        extra.beside(0, k, (), ()).wait_send()
        extra.beside(2, k, (), ()).wait_send()


def settle(match, spots, res_over, d_qkv_t, x_all, w_t, grad_one, gu_own, gu_other, res):
    size, local, rows = d_qkv_t.shape
    _, groups, share, width = res.shape
    res = res.reshape(-1, groups, share // 16, 16, width)
    chunks = rows // BLOCK
    sub = BLOCK // groups
    part = width // groups
    wide = gu_own.shape[1]
    total_rows = size * rows
    anywhere = pl.BlockSpec(memory_space=pl.ANY)
    vmem = pl.BlockSpec(memory_space=pltpu.VMEM)
    smem = pl.BlockSpec(memory_space=pltpu.SMEM)
    dma = pltpu.SemaphoreType.DMA
    shape = jax.ShapeDtypeStruct
    buffer = pltpu.VMEM((chunks, BLOCK, width), BF)
    pair_buffer = pltpu.VMEM((2, chunks, BLOCK, width), BF)
    halving = lambda columns: [
        pltpu.VMEM((7, part, columns), BF),
        pltpu.VMEM((7, part, columns), BF),
        pltpu.VMEM((2, part, columns), F32),
    ]
    return pl.pallas_call(
        functools.partial(settle_kernel, groups, size),
        in_specs=[smem, smem, vmem] + [anywhere] * 7,
        out_specs=[anywhere, anywhere, anywhere, vmem, vmem],
        out_shape=[
            shape((size, groups, chunks, sub, width), BF),
            shape((size, groups, 1, width), BF),
            shape((total_rows, width), BF),
            shape((part, local), F32),
            shape((part, wide), F32),
        ],
        scratch_shapes=[
            pltpu.VMEM(d_qkv_t.shape, BF),
            pltpu.VMEM(x_all.shape, BF),
            pltpu.VMEM(w_t.shape, BF),
            pltpu.VMEM(grad_one.shape, F32),
            pltpu.VMEM(gu_own.shape, BF),
            pltpu.VMEM(gu_own.shape, BF),
            pltpu.VMEM((groups, size * share // 16 + 1, 16, width), BF),
            pltpu.VMEM((total_rows, width), BF),
            pair_buffer,
            pair_buffer,
            buffer,
            buffer,
            pltpu.VMEM((chunks, groups, sub, width), BF),
            pltpu.VMEM((groups, 1, width), BF),
            pltpu.VMEM((groups, part, local), BF),
            *halving(wide // 2),
            *halving(wide // 2),
            *halving(local),
            dma((11,)),
            dma((4,)),
            dma((4,)),
            dma((3, 7)),
            dma((3, 7)),
            dma((4, groups, chunks)),
            dma((4, groups, chunks)),
            dma((4, groups)),
            dma((4, groups)),
            dma((3, chunks)),
            dma((3, chunks)),
            dma((chunks + 1 + total_rows // ROWS,)),
        ],
        compiler_params=pltpu.CompilerParams(
            collective_id=1, has_side_effects=True, vmem_limit_bytes=VMEM_LIMIT
        ),
        cost_estimate=pl.CostEstimate(
            flops=4 * size * rows * local * width, bytes_accessed=150 << 20, transcendentals=0
        ),
        name="settle",
    )(match, spots, res_over, d_qkv_t, x_all, w_t, grad_one, gu_own, gu_other, res)


def local(tokens, cotangent, lengths, dealing, w_qkv, w_out, w_gu, w_down, gains, shifts):
    groups = lax.axis_size("dp")
    size = lax.axis_size("tensor")
    me = lax.axis_index("tensor")
    rows = tokens.shape[0]
    width = tokens.shape[2]
    slots = rows // groups
    share = slots // size
    own_rows = rows // size
    subs = own_rows // BLOCK
    sub = share // subs
    fused = groups == 8 and sub % 16 == 0
    i32 = jnp.int32

    ids = jnp.stack([lax.axis_index("dp"), me]).astype(i32)
    send_x, over_x, send_c, meta, table, match, spots = pack(
        lengths,
        dealing,
        ids,
        tokens.reshape(rows, width),
        cotangent.reshape(rows, width),
        groups,
        size,
    )

    def over_dp(array):
        return lax.all_to_all(array, "dp", split_axis=0, concat_axis=0, tiled=True)

    far_out, far_down = swap(w_out.T, size, 2), swap(w_down, size, 2)
    match_square = match.reshape(groups, groups)

    def fill(received, over, last):
        spare = jnp.dot(match_square.astype(BF), over, preferred_element_type=F32).astype(BF)
        hole = (jnp.sum(match_square, 1) > 0)[:, None] & (jnp.arange(share) == share - 1)[None, :]
        fix = last[:, None, None] & hole[None]
        body = jnp.where(fix[..., None], spare[None, :, None, :], received)
        body = body.reshape(-1, groups, subs, sub, width).transpose(0, 2, 1, 3, 4)
        return body.reshape(-1, own_rows, width)

    if fused:
        x_rel, over_x = route(send_x, over_x, size)
        send_c, x_rel, far_out, far_down = lax.optimization_barrier(
            (send_c, x_rel, far_out, far_down)
        )
    else:
        x_rel = jnp.stack(gather_members(over_dp(send_x)))
        relative = jnp.bitwise_xor(jnp.arange(size, dtype=i32), me)
        x_rel = fill(x_rel, over_dp(over_x)[:, 0], relative == size - 1)
    cot = over_dp(send_c)
    if not fused:
        cot = fill(cot[None, :, :share], cot[:, share], (me == size - 1)[None])[0]

    local_width = w_qkv.shape[2]
    w_qkv_t = w_qkv.transpose(1, 2, 0).reshape(3 * local_width, width)
    x_rel, near_gu = lax.optimization_barrier((x_rel, w_gu.reshape(width, -1)))
    far_gu = swap(near_gu, size, 2)
    frequency = 1000.0 ** (-(jnp.arange(HALF, dtype=F32) * 2.0) / HEAD)
    q, k, v, k_rows, v_rows, cosine, sine, x_all, x_own = project(
        meta, match, x_rel, over_x, w_qkv_t, frequency[:, None], groups, fused
    )
    o_blocks, lse = attend(meta, q, k_rows, v, groups)
    o_blocks, far_gu, cot = lax.optimization_barrier((o_blocks, far_gu, cot))

    norms = jnp.concatenate([gains.T, shifts.T], 0)
    (
        result_own,
        grad_one,
        d_heads,
        heads_own,
        normed_t,
        d_branch_t,
        d_attn_t,
        hidden,
        d_gu,
        norm_grads,
    ) = middle(
        x_own,
        match,
        cot,
        norms,
        o_blocks,
        size,
        w_out.T,
        far_out,
        near_gu,
        far_gu,
        w_down,
        far_down,
    )
    grad_args = (normed_t, d_branch_t, d_attn_t, hidden, d_gu, heads_own, norm_grads)
    if fused:
        gu_own, gu_other, pair, do_rel, home_result, over_result = grads(
            match, groups, *grad_args, d_heads, result_own
        )
        home_result = home_result.reshape(3, groups, share, width)
        gu_other = swap(gu_other, size, 2)
    else:
        sent_grads = weight_grads(1, *grad_args)
        kept_grads = weight_grads(0, *grad_args)
        pair = (kept_grads.astype(F32) + swap(sent_grads, size, 1).astype(F32)).astype(BF)
        do_rel = jnp.stack(exchange_members([d_heads[r] for r in range(size)]))

    d_qkv_t = attend_back(
        meta, q, k_rows, k, v_rows, o_blocks, do_rel, lse, cosine, sine, groups
    )
    pair = lax.psum_scatter(pair, "dp", scatter_dimension=1, tiled=True)
    def send_back(own):
        body = own.reshape(subs, groups, sub, width).transpose(1, 0, 2, 3)
        body = body.reshape(groups, share, width)
        spare = lax.dot_general(
            match_square.astype(BF),
            body[:, share - 1],
            (((0,), (0,)), ((), ())),
            preferred_element_type=F32,
        ).astype(BF)
        pair = (over_dp(body), over_dp(spare.reshape(groups, 1, width)))
        return tuple(jnp.stack(gather_members(a)) for a in pair)

    if fused:
        home_input, home_over, result, qkv_sum, gu_sum = settle(
            match,
            spots,
            over_result,
            d_qkv_t,
            x_all,
            w_qkv_t,
            grad_one,
            gu_own,
            gu_other,
            home_result,
        )
        home_input = home_input.reshape(size, groups, share, width)
        pair, home_input = lax.optimization_barrier((pair, home_input))
    else:
        back_rel, grad_qkv = project_back(meta, d_qkv_t, x_all, w_qkv_t)
        grad_qkv = grad_qkv.reshape(groups, width // groups, 3 * local_width)
        home_result = send_back(result_own)
        input_own = grad_one + reduce_members([back_rel[r] for r in range(size)])
        home_input = send_back(input_own.astype(BF))
        grad_qkv = lax.all_to_all(grad_qkv, "dp", split_axis=0, concat_axis=0, tiled=True)
        qkv_sum = jnp.sum(grad_qkv.astype(F32), 0)
    qkv_sum = qkv_sum.reshape(-1, 3, local_width)
    summed = pair[0].astype(F32) + swap(pair[1], size, 2).astype(F32)
    inner = w_down.shape[1]
    if not fused:
        gu_sum, summed = summed[:, : 2 * inner], summed[:, 2 * inner :]
    gu_sum = gu_sum.reshape(-1, 2, inner)
    down_sum = summed[:, :inner]
    out_sum = summed[:, inner : inner + local_width]
    norm_sum = summed[:, inner + local_width : inner + local_width + 4]
    norm_sum = lax.dynamic_slice_in_dim(
        norm_sum, me * (norm_sum.shape[0] // size), norm_sum.shape[0] // size, 0
    )
    if fused:
        input_grad = unpack(spots, me[None], home_input, home_over)
    else:
        row_ids = jnp.arange(rows, dtype=i32)[None, :]
        low, count, group, first = (table[i, 1:][:, None] for i in range(4))
        here = (row_ids >= low) & (row_ids < low + count)
        slot = row_ids + first - low
        home_part = jnp.minimum(slot // share, size - 1)
        flat = (jnp.bitwise_xor(home_part, me) * groups + group) * (share + 1)
        flat = jnp.sum(jnp.where(here, flat + slot - home_part * share, 0), 0)

        def arrange(home, over):
            every = jnp.concatenate([home, over], 2).reshape(-1, width)
            return jnp.take(every, flat, axis=0)

        result = arrange(*home_result)
        input_grad = arrange(*home_input)
    result = result.reshape(rows, 1, width)
    input_grad = input_grad.reshape(rows, 1, width)
    return (
        result,
        input_grad,
        qkv_sum,
        out_sum,
        gu_sum,
        down_sum,
        norm_sum[:, :2],
        norm_sum[:, 2:],
    )


def solution(mesh):
    placed = (
        P(None, "dp", None),
        P(None, "dp", None),
        P(),
        P(),
        P(None, None, "tensor"),
        P(None, "tensor"),
        P(None, None, "tensor"),
        P(None, "tensor"),
        P(),
        P(),
    )
    return jax.shard_map(
        local,
        mesh=mesh,
        in_specs=placed,
        out_specs=(
            P(None, "dp", None),
            P(None, "dp", None),
            P("dp", None, "tensor"),
            P("dp", "tensor"),
            P("dp", None, "tensor"),
            P("dp", "tensor"),
            P(("dp", "tensor"), None),
            P(("dp", "tensor"), None),
        ),
        check_vma=False,
    )
```

```python
import functools

import jax
import jax.numpy as jnp
import numpy as np
from jax import lax
from jax.experimental import pallas as pl
from jax.experimental.pallas import tpu as pltpu
from jax.sharding import PartitionSpec as P

HEAD = 64
HALF = HEAD // 2
BLOCK = 256
QUERIES = 512
PADDED = HEAD + 16
KEYS = 512
LOG_2 = 0.6931471805599453
EPSILON = 1e-05
NEGATIVE = -1000000000.0
START = -1e30
BF = jnp.bfloat16
F32 = jnp.float32
VMEM_LIMIT = 56 * 1024 * 1024


def mm(a, b, ca, cb):
    return lax.dot_general(a, b, (((ca,), (cb,)), ((), ())), preferred_element_type=F32)


HOLES = 8
ROWS = 128
WIDE = 1664
WIDE_PARTS = (896, 768)
TILE = 256


def div(value, size):
    if size & (size - 1) == 0:
        return lax.shift_right_arithmetic(value, jnp.int32(size.bit_length() - 1))
    return lax.div(value, size)


def rem(value, size):
    if size & (size - 1) == 0:
        return lax.bitwise_and(value, jnp.int32(size - 1))
    return lax.rem(value, size)


def extra_of(source, offset, length, groups):
    turned = rem(source - offset + groups, groups)
    return turned, jnp.where(turned < rem(length, groups), 1, 0)


def pack_kernel(
    groups,
    size,
    lengths,
    dealing,
    ids,
    x_ref,
    c_ref,
    send_x_ref,
    over_x_ref,
    send_c_ref,
    meta_ref,
    table_ref,
    match_ref,
    spots_ref,
    places,
):
    d = ids[0]
    t = ids[1]
    rows = x_ref.shape[0]
    slots = rows // groups
    share = slots // size
    window = (share + 31) // 16 * 16

    count = lengths.shape[0]

    def place_of(j, offset):
        places[0, j] = offset
        return offset + lengths[j]

    lax.fori_loop(0, count, place_of, jnp.int32(0), unroll=True)

    def lookup(q):
        seq = dealing[q]
        return seq, places[0, seq], lengths[seq]

    def span(offset, length):
        low = div(offset - d + groups - 1, groups)
        return low, div(offset + length - d + groups - 1, groups) - low

    def window_at(row):
        start = jnp.clip(jnp.bitwise_and(row, -16), 0, rows - window)
        return pl.ds(pl.multiple_of(start, 16), window), row - start

    def one_hot(steps, shift, wanted):
        return jnp.where((steps == shift) & wanted, 1.0, 0.0).astype(BF)

    def steps_of(count):
        shape = (count, window)
        return lax.broadcasted_iota(jnp.int32, shape, 1) - lax.broadcasted_iota(jnp.int32, shape, 0)

    steps = steps_of(share)
    spare_steps = steps_of(16)
    top = lax.broadcasted_iota(jnp.int32, (16, 1), 0) == 0
    table_ref[0, 0] = t
    slot_ids = lax.broadcasted_iota(jnp.int32, (share, 1), 0) + t * share

    @pl.loop(0, groups, unroll=4)
    def _(g):
        seq_a, off_a, len_a = lookup(2 * g)
        seq_b, off_b, len_b = lookup(2 * g + 1)
        low_a, count_a = span(off_a, len_a)
        low_b, count_b = span(off_b, len_b)
        for seq, entries in ((seq_a, (low_a, count_a, g, 0)), (seq_b, (low_b, count_b, g, count_a))):
            for i, entry in enumerate(entries):
                table_ref[i, 1 + seq] = jnp.int32(entry)
        shifted = low_b - count_a
        at_a, shift_a = window_at(low_a + t * share)
        at_b, shift_b = window_at(shifted + t * share)
        at_over, shift_over = window_at(shifted + slots)
        hot_a = one_hot(steps, shift_a, slot_ids < count_a)
        hot_b = one_hot(steps, shift_b, slot_ids >= count_a)
        hot_over = one_hot(spare_steps, shift_over, top)
        for ref, out_ref in ((x_ref, send_x_ref), (c_ref, send_c_ref)):
            picked = mm(hot_a, ref[at_a, :], 1, 0) + mm(hot_b, ref[at_b, :], 1, 0)
            out_ref[g, :share] = picked.astype(BF)
        over_x_ref[g] = mm(hot_over, x_ref[at_over, :], 1, 0)[:1].astype(BF)
        send_c_ref[g, share:] = mm(hot_over, c_ref[at_over, :], 1, 0).astype(BF)

    def spot(i, here):
        row = i * ROWS
        following = jnp.minimum(here + 1, count - 1)
        here = jnp.where(table_ref[0, 1 + following] <= row, following, here)
        after = jnp.minimum(here + 1, count - 1)
        for k, j in enumerate((here, after)):
            slot = row + table_ref[3, 1 + j] - table_ref[0, 1 + j]
            start = jnp.clip(jnp.bitwise_and(slot, -16), 0, slots - ROWS)
            spots_ref[8 * i + 3 * k] = table_ref[2, 1 + j]
            spots_ref[8 * i + 3 * k + 1] = div(start, 16)
            spots_ref[8 * i + 3 * k + 2] = slot - start
        spots_ref[8 * i + 6] = jnp.where(after > here, table_ref[0, 1 + after] - row, ROWS)
        spots_ref[8 * i + 7] = jnp.int32(0)
        return here

    lax.fori_loop(0, rows // ROWS, spot, jnp.int32(0), unroll=4)

    _, off_a, len_a = lookup(2 * d)
    _, off_b, len_b = lookup(2 * d + 1)
    off_a = rem(off_a, groups)
    off_b = rem(off_b, groups)
    meta_ref[0] = div(len_a, BLOCK)
    meta_ref[1] = div(len_a + BLOCK - 1, BLOCK)
    meta_ref[2] = t
    meta_ref[3] = off_a
    meta_ref[4] = off_b
    meta_ref[5] = len_a
    meta_ref[6] = jnp.int32(0)
    meta_ref[7] = jnp.int32(0)

    def counts(source):
        first = div(len_a, groups) + extra_of(source, off_a, len_a, groups)[1]
        second = div(len_b, groups) + extra_of(source, off_b, len_b, groups)[1]
        return first, first + second

    def clear(i, carry):
        match_ref[i] = jnp.float32(0.0)
        return carry

    lax.fori_loop(0, groups * groups, clear, 0, unroll=8)

    def sort_out(source, carry):
        holes, overs = carry
        total = counts(source)[1]
        places[1, holes] = source
        places[2, overs] = source
        meta_ref[HOLES + source] = jnp.int32(-1)
        return holes + jnp.where(total < slots, 1, 0), overs + jnp.where(total > slots, 1, 0)

    holes, _ = lax.fori_loop(0, groups, sort_out, (jnp.int32(0), jnp.int32(0)), unroll=8)

    @pl.loop(0, holes)
    def _(i):
        hole = places[1, i]
        source = places[2, i]
        match_ref[hole * groups + source] = jnp.float32(1.0)
        position = (slots - counts(source)[0]) * groups + extra_of(source, off_b, len_b, groups)[0]
        meta_ref[HOLES + hole] = position


def pack(lengths, dealing, ids, x, cotangent, groups, size):
    rows, width = x.shape
    share = rows // groups // size
    whole = lambda *shape: pl.BlockSpec(shape, lambda i, *refs: (0,) * len(shape))
    smem = pl.BlockSpec(memory_space=pltpu.SMEM)
    shapes = [(groups, share, width), (groups, 1, width), (groups, share + 16, width)]
    return pl.pallas_call(
        functools.partial(pack_kernel, groups, size),
        grid_spec=pltpu.PrefetchScalarGridSpec(
            num_scalar_prefetch=3,
            grid=(1,),
            in_specs=[whole(rows, width)] * 2,
            out_specs=[whole(*shape) for shape in shapes] + [smem] * 4,
            scratch_shapes=[pltpu.SMEM((3, max(lengths.shape[0], groups + 1)), jnp.int32)],
        ),
        out_shape=[jax.ShapeDtypeStruct(shape, BF) for shape in shapes]
        + [
            jax.ShapeDtypeStruct((HOLES + groups,), jnp.int32),
            jax.ShapeDtypeStruct((4, 1 + lengths.shape[0]), jnp.int32),
            jax.ShapeDtypeStruct((groups * groups,), F32),
            jax.ShapeDtypeStruct((rows // ROWS * 8,), jnp.int32),
        ],
        compiler_params=pltpu.CompilerParams(vmem_limit_bytes=VMEM_LIMIT),
        cost_estimate=pl.CostEstimate(flops=0, bytes_accessed=20 << 20, transcendentals=0),
        name="pack",
    )(lengths, dealing, ids, x, cotangent)


def place(row, groups):
    sub = BLOCK // groups
    inside = rem(row, BLOCK)
    return div(inside, sub), div(row, BLOCK) * sub + rem(inside, sub)


def count_first(meta, source, groups):
    turned, extra = extra_of(source, meta[3], meta[5], groups)
    return turned, div(meta[5], groups) + extra


def in_second(meta, row, groups):
    source, slot = place(row, groups)
    return jnp.where(slot < count_first(meta, source, groups)[1], 0, 1)


def positions_of(meta, row, groups, slots):
    source, slot = place(row, groups)
    turned, count = count_first(meta, source, groups)
    turned_b = rem(source - meta[4] + groups, groups)
    position = jnp.where(slot < count, slot * groups + turned, (slot - count) * groups + turned_b)
    for g in range(groups):
        fills = meta[HOLES + g]
        here = (slot == slots - 1) & (source == g) & (fills >= 0)
        position = jnp.where(here, fills, position)
    return position


def spare_row(match_ref, groups, hole, rows):
    total = rows[0] * match_ref[hole * groups]
    flag = match_ref[hole * groups]
    for source in range(1, groups):
        weight = match_ref[hole * groups + source]
        total = total + rows[source] * weight
        flag = flag + weight
    return total, flag


def project_kernel(
    groups,
    packed,
    meta,
    match_ref,
    x_in_ref,
    over_ref,
    w_ref,
    freq_ref,
    q_ref,
    k_ref,
    v_ref,
    krow_ref,
    vrow_ref,
    cos_ref,
    sin_ref,
    x_ref,
    own_ref,
):
    index = pl.program_id(0)
    parts = pl.num_programs(0)
    share, width = x_ref.shape[1:]
    heads = q_ref.shape[0] // HEAD
    local = heads * HEAD
    sub = BLOCK // groups
    if packed:
        for i in range(share // BLOCK):
            for g in range(groups):
                base = i * BLOCK + g * sub
                x_ref[0, base : base + sub, :] = x_in_ref[0, g, i * sub : (i + 1) * sub, :]

        @pl.when(index == parts - 1)
        def _():
            rows = [over_ref[g].astype(F32) for g in range(groups)]
            at_end = lax.broadcasted_iota(jnp.int32, (16, 1), 0) == 15
            for g in range(groups):
                end = share - BLOCK + (g + 1) * sub
                spare, _ = spare_row(match_ref, groups, g, rows)
                old = x_ref[0, end - 16 : end, :].astype(F32)
                new = jnp.where(at_end & (meta[HOLES + g] >= 0), spare, old)
                x_ref[0, end - 16 : end, :] = new.astype(BF)
    else:
        x_ref[...] = x_in_ref[...]

    @pl.when(index == meta[2])
    def _():
        own_ref[...] = x_ref[0]

    row = lax.broadcasted_iota(jnp.int32, (1, share), 1) + index * share
    position = positions_of(meta, row, groups, parts * share // groups)
    angles = freq_ref[...] * position.astype(F32)
    cosine = jnp.cos(angles)
    sine = jnp.sin(angles)
    cos_ref[...] = cosine
    sin_ref[...] = sine
    projected = mm(w_ref[...], x_ref[0], 1, 1)
    for part, out_ref, scale in ((0, q_ref, HEAD ** (-0.5) / LOG_2), (1, k_ref, 1.0)):
        for head in range(heads):
            base = part * local + head * HEAD
            first = projected[base : base + HALF]
            second = projected[base + HALF : base + HEAD]
            turned = jnp.concatenate(
                [first * cosine - second * sine, second * cosine + first * sine], 0
            )
            out_ref[head * HEAD : (head + 1) * HEAD, :] = (turned * scale).astype(BF)
            if part == 1:
                krow_ref[head] = turned.T.astype(BF)
    for head in range(heads):
        base = 2 * local + head * HEAD
        value = projected[base : base + HEAD]
        rest = lax.broadcasted_iota(jnp.int32, (PADDED - HEAD, share), 0) == 0
        v_ref[head * PADDED : (head + 1) * PADDED, :] = jnp.concatenate(
            [value, jnp.where(rest, 1.0, 0.0)], 0
        ).astype(BF)
        vrow_ref[head] = value.T.astype(BF)


def project(meta, match, x_rel, over, w_t, freq, groups, packed):
    parts = x_rel.shape[0]
    width = x_rel.shape[-1]
    share = x_rel.size // parts // width
    rows = parts * share
    local = w_t.shape[0] // 3
    heads = local // HEAD
    shape = jax.ShapeDtypeStruct
    columns = lambda *lead: pl.BlockSpec(lead + (share,), lambda i, meta: (0,) * len(lead) + (i,))
    tall_spec = pl.BlockSpec((heads, share, HEAD), lambda i, meta: (0, i, 0))
    whole = lambda *shape: pl.BlockSpec(shape, lambda i, meta: (0,) * len(shape))
    lead = x_rel.shape[1:]
    return pl.pallas_call(
        functools.partial(project_kernel, groups, packed),
        grid_spec=pltpu.PrefetchScalarGridSpec(
            num_scalar_prefetch=1,
            grid=(parts,),
            in_specs=[
                pl.BlockSpec(memory_space=pltpu.SMEM),
                pl.BlockSpec(
                    (1,) + lead, lambda i, meta: (jnp.bitwise_xor(i, meta[2]),) + (0,) * len(lead)
                ),
                whole(*over.shape),
                whole(3 * local, width),
                whole(HALF, 1),
            ],
            out_specs=[
                columns(local),
                columns(local),
                columns(heads * PADDED),
                tall_spec,
                tall_spec,
                columns(HALF),
                columns(HALF),
                pl.BlockSpec((1, share, width), lambda i, meta: (i, 0, 0)),
                whole(share, width),
            ],
        ),
        out_shape=[
            shape((local, rows), BF),
            shape((local, rows), BF),
            shape((heads * PADDED, rows), BF),
            shape((heads, rows, HEAD), BF),
            shape((heads, rows, HEAD), BF),
            shape((HALF, rows), F32),
            shape((HALF, rows), F32),
            shape((parts, share, width), BF),
            shape((share, width), BF),
        ],
        compiler_params=pltpu.CompilerParams(vmem_limit_bytes=VMEM_LIMIT),
        cost_estimate=pl.CostEstimate(
            flops=rows * width, bytes_accessed=1 << 20, transcendentals=0
        ),
        name="project",
    )(meta, match, x_rel, over, w_t, freq)


def visible(info, index, q_blocks, k_blocks, count):
    is_a = (index + 1) * q_blocks <= info[0]
    is_b = index * q_blocks >= info[1]
    pure = is_a | is_b
    end_a = info[0] // k_blocks
    start_b = (info[1] + k_blocks - 1) // k_blocks
    plain_low = jnp.where(is_b, start_b, 0)
    plain_high = jnp.where(is_b, count, jnp.where(is_a, end_a, 0))
    return plain_low, plain_high, jnp.where(pure, end_a, 0), jnp.where(pure, start_b, count)


def attend_kernel(groups, info, q_ref, k_ref, v_ref, o_ref, lse_ref, acc_ref):
    index = pl.program_id(0)
    heads, rows, _ = k_ref.shape
    width = q_ref.shape[1]
    tall = v_ref.shape[0] // heads
    spans_ = visible(info, index, width // BLOCK, KEYS // BLOCK, rows // KEYS)
    acc_ref[...] = jnp.zeros_like(acc_ref)
    query_ids = lax.broadcasted_iota(jnp.int32, (1, width), 1) + index * width
    key_ids = lax.broadcasted_iota(jnp.int32, (KEYS, 1), 0)
    ids = range(heads)

    def step(masked, j, tops):
        keys = pl.ds(pl.multiple_of(j * KEYS, KEYS), KEYS)
        scores = [mm(k_ref[h, keys, :], q_ref[h * HEAD : (h + 1) * HEAD, :], 1, 0) for h in ids]
        if masked:
            same = in_second(info, key_ids + j * KEYS, groups) == in_second(info, query_ids, groups)
            scores = [jnp.where(same, s, NEGATIVE) for s in scores]
        new = [jnp.maximum(tops[h], jnp.max(scores[h], 0, keepdims=True)) for h in ids]
        weights = [jnp.exp2(scores[h] - new[h]).astype(BF) for h in ids]
        shrink = [jnp.exp2(tops[h] - new[h]) for h in ids]
        sums = [mm(v_ref[h * tall : (h + 1) * tall, keys], weights[h], 1, 0) for h in ids]
        for h in ids:
            part = slice(h * tall, (h + 1) * tall)
            acc_ref[part, :] = acc_ref[part, :] * shrink[h] + sums[h]
        return tuple(new)

    tops = (jnp.full((1, width), START, F32),) * heads
    tops = lax.fori_loop(spans_[0], spans_[1], functools.partial(step, False), tops)
    tops = lax.fori_loop(spans_[2], spans_[3], functools.partial(step, True), tops)
    for h in ids:
        total = acc_ref[h * tall + HEAD : h * tall + HEAD + 1, :]
        out = (acc_ref[h * tall : h * tall + HEAD, :] / total).astype(BF)
        each = o_ref.shape[2]
        for i in range(width // each):
            o_ref[i, h * HEAD : (h + 1) * HEAD, :] = out[:, i * each : (i + 1) * each]
        lse_ref[h : h + 1, :] = tops[h] + jnp.log2(total)


def attend(info, q, k_rows, v, groups):
    local, rows = q.shape
    heads = local // HEAD
    return pl.pallas_call(
        functools.partial(attend_kernel, groups),
        grid_spec=pltpu.PrefetchScalarGridSpec(
            num_scalar_prefetch=1,
            grid=(rows // QUERIES,),
            in_specs=[
                pl.BlockSpec((local, QUERIES), lambda i, info: (0, i)),
                pl.BlockSpec((heads, rows, HEAD), lambda i, info: (0, 0, 0)),
                pl.BlockSpec(v.shape, lambda i, info: (0, 0)),
            ],
            out_specs=[
                pl.BlockSpec((QUERIES // BLOCK, local, BLOCK), lambda i, info: (i, 0, 0)),
                pl.BlockSpec((heads, QUERIES), lambda i, info: (0, i)),
            ],
            scratch_shapes=[pltpu.VMEM((v.shape[0], QUERIES), F32)],
        ),
        out_shape=[
            jax.ShapeDtypeStruct((rows // BLOCK, local, BLOCK), BF),
            jax.ShapeDtypeStruct((heads, rows), F32),
        ],
        compiler_params=pltpu.CompilerParams(vmem_limit_bytes=VMEM_LIMIT),
        cost_estimate=pl.CostEstimate(
            flops=2 * rows * rows * HEAD * heads,
            bytes_accessed=8 << 20,
            transcendentals=0,
        ),
        name="attend",
    )(info, q, k_rows, v)


def unturn(grad, cosine, sine):
    first = grad[:HALF]
    second = grad[HALF:]
    return jnp.concatenate(
        [first * cosine + second * sine, second * cosine - first * sine], 0
    ).astype(BF)


def attend_back_kernel(groups, info, q_ref, krow_ref, k_ref, vrow_ref, o_ref, *refs):
    count = QUERIES // BLOCK
    do_refs = refs[:count]
    lse_ref, cos_ref, sin_ref, out_ref, up_ref, dq_ref, dk_ref, dv_ref = refs[count:]
    index = pl.program_id(0)
    heads, rows, _ = krow_ref.shape
    width = heads * HEAD
    parts, _, share = out_ref.shape
    each = share // BLOCK
    ids = range(heads)
    part = [slice(h * HEAD, (h + 1) * HEAD) for h in ids]

    @pl.when(index == 0)
    def _():
        dk_ref[...] = jnp.zeros_like(dk_ref)
        dv_ref[...] = jnp.zeros_like(dv_ref)

    dq_ref[...] = jnp.zeros_like(dq_ref)
    query_ids = lax.broadcasted_iota(jnp.int32, (1, QUERIES), 1) + index * QUERIES
    key_ids = lax.broadcasted_iota(jnp.int32, (KEYS, 1), 0)
    deltas = []
    for i, ref in enumerate(do_refs):
        columns = slice(i * BLOCK, (i + 1) * BLOCK)
        up_ref[:, columns] = ref[0]
        terms = ref[0].astype(F32) * o_ref[i].astype(F32)
        deltas.append([jnp.sum(terms[p], 0, keepdims=True) for p in part])
    delta = [jnp.concatenate([halves[h] for halves in deltas], 1) for h in ids]
    spans_ = visible(info, index, QUERIES // BLOCK, KEYS // BLOCK, rows // KEYS)

    def step(masked, j, carry):
        keys = pl.ds(pl.multiple_of(j * KEYS, KEYS), KEYS)
        if masked:
            same = in_second(info, key_ids + j * KEYS, groups) == in_second(info, query_ids, groups)
        for h in ids:
            queries = q_ref[part[h], :]
            upstream = up_ref[part[h], :]
            scores = mm(krow_ref[h, keys, :], queries, 1, 0)
            grad_soft = mm(vrow_ref[h, keys, :], upstream, 1, 0)
            if masked:
                scores = jnp.where(same, scores, NEGATIVE)
            soft = jnp.exp2(scores - lse_ref[h : h + 1, :])
            grad_scores = (soft * (grad_soft - delta[h])).astype(BF)
            dv_ref[part[h], keys] += mm(upstream, soft.astype(BF), 1, 1)
            dk_ref[part[h], keys] += mm(queries, grad_scores, 1, 1)
            dq_ref[part[h], :] += mm(k_ref[part[h], keys], grad_scores, 1, 0)
        return carry

    lax.fori_loop(spans_[0], spans_[1], functools.partial(step, False), 0)
    lax.fori_loop(spans_[2], spans_[3], functools.partial(step, True), 0)

    for i in range(QUERIES // BLOCK):
        block = index * (QUERIES // BLOCK) + i
        columns = pl.ds(pl.multiple_of(block * BLOCK, BLOCK), BLOCK)
        inside = pl.ds(pl.multiple_of(lax.rem(block, each) * BLOCK, BLOCK), BLOCK)
        for h in ids:
            out_ref[lax.div(block, each), part[h], inside] = unturn(
                dq_ref[part[h], i * BLOCK : (i + 1) * BLOCK] * HEAD ** (-0.5),
                cos_ref[:, columns],
                sin_ref[:, columns],
            )

    @pl.when(index == pl.num_programs(0) - 1)
    def _():
        @pl.loop(0, parts)
        def _(j):
            columns = pl.ds(pl.multiple_of(j * share, share), share)
            for h in ids:
                base = width + h * HEAD
                out_ref[j, base : base + HEAD, :] = unturn(
                    dk_ref[part[h], columns] * LOG_2, cos_ref[:, columns], sin_ref[:, columns]
                )
                base = 2 * width + h * HEAD
                out_ref[j, base : base + HEAD, :] = dv_ref[part[h], columns].astype(BF)


def attend_back(info, q, k_rows, k, v_rows, o, do, lse, cosine, sine, groups):
    parts = do.shape[0]
    local, rows = q.shape
    heads = local // HEAD
    blocks = rows // BLOCK
    each = blocks // parts
    whole = lambda *shape: pl.BlockSpec(shape, lambda i, info: (0,) * len(shape))
    count = QUERIES // BLOCK

    def upstream_spec(k):
        def pick(i, info):
            block = i * count + k
            return jnp.bitwise_xor(block // each, info[2]), 0, block % each

        return pl.BlockSpec((1, local, BLOCK), pick)

    return pl.pallas_call(
        functools.partial(attend_back_kernel, groups),
        grid_spec=pltpu.PrefetchScalarGridSpec(
            num_scalar_prefetch=1,
            grid=(rows // QUERIES,),
            in_specs=[
                pl.BlockSpec((local, QUERIES), lambda i, info: (0, i)),
                whole(heads, rows, HEAD),
                whole(local, rows),
                whole(heads, rows, HEAD),
                pl.BlockSpec((count, local, BLOCK), lambda i, info: (i, 0, 0)),
                *[upstream_spec(k) for k in range(count)],
                pl.BlockSpec((heads, QUERIES), lambda i, info: (0, i)),
                whole(HALF, rows),
                whole(HALF, rows),
            ],
            out_specs=whole(parts, 3 * local, rows // parts),
            scratch_shapes=[
                pltpu.VMEM((local, QUERIES), BF),
                pltpu.VMEM((local, QUERIES), F32),
                pltpu.VMEM((local, rows), F32),
                pltpu.VMEM((local, rows), F32),
            ],
        ),
        out_shape=jax.ShapeDtypeStruct((parts, 3 * local, rows // parts), BF),
        compiler_params=pltpu.CompilerParams(vmem_limit_bytes=VMEM_LIMIT),
        cost_estimate=pl.CostEstimate(
            flops=2 * 5 * rows * rows * 256 * heads // 2,
            bytes_accessed=16 << 20,
            transcendentals=heads * rows * rows // 2,
        ),
        name="attend_back",
    )(info, q, k_rows, k, v_rows, o, *[do] * count, lse, cosine, sine)


def project_back_kernel(meta, d_ref, x_ref, w_ref, back_ref, grad_ref, acc_ref):
    index = pl.program_id(0)

    @pl.when(index == 0)
    def _():
        acc_ref[...] = jnp.zeros_like(acc_ref)

    d_t = d_ref[0]
    back_ref[0] = mm(d_t, w_ref[...], 0, 0).astype(BF)
    acc_ref[...] += mm(d_t, x_ref[0], 1, 0)

    @pl.when(index == pl.num_programs(0) - 1)
    def _():
        grad_ref[...] = acc_ref[...].T.astype(BF)


def project_back(meta, d_qkv_t, x_all, w_t):
    parts, local, share = d_qkv_t.shape
    width = w_t.shape[1]
    relative = lambda i, meta: (jnp.bitwise_xor(i, meta[2]), 0, 0)
    whole = lambda *shape: pl.BlockSpec(shape, lambda i, meta: (0,) * len(shape))
    return pl.pallas_call(
        project_back_kernel,
        grid_spec=pltpu.PrefetchScalarGridSpec(
            num_scalar_prefetch=1,
            grid=(parts,),
            in_specs=[
                pl.BlockSpec((1, local, share), lambda i, meta: (i, 0, 0)),
                pl.BlockSpec((1, share, width), lambda i, meta: (i, 0, 0)),
                whole(local, width),
            ],
            out_specs=[
                pl.BlockSpec((1, share, width), relative),
                whole(width, local),
            ],
            scratch_shapes=[pltpu.VMEM((local, width), F32)],
        ),
        out_shape=[
            jax.ShapeDtypeStruct((parts, share, width), BF),
            jax.ShapeDtypeStruct((width, local), BF),
        ],
        compiler_params=pltpu.CompilerParams(vmem_limit_bytes=VMEM_LIMIT),
        cost_estimate=pl.CostEstimate(
            flops=4 * parts * share * local * width, bytes_accessed=15 << 20, transcendentals=0
        ),
        name="project_back",
    )(meta, d_qkv_t, x_all, w_t)


MESH = pl.DeviceIdType.MESH


def greet(groups, steps, d, t):
    barrier = pltpu.get_barrier_semaphore()
    for k in range(1, groups):
        pl.semaphore_signal(
            barrier, inc=1, device_id=(lax.rem(d + k, groups), t), device_id_type=MESH
        )
    for step in steps:
        pl.semaphore_signal(
            barrier, inc=1, device_id=(d, jnp.bitwise_xor(t, step)), device_id_type=MESH
        )
    pl.semaphore_wait(barrier, groups - 1 + len(steps))


def remote(src, dst, send, recv, device):
    return pltpu.make_async_remote_copy(
        src_ref=src,
        dst_ref=dst,
        send_sem=send,
        recv_sem=recv,
        device_id=device,
        device_id_type=MESH,
    )


class Spread:
    def __init__(self, out, sems, groups, d, t):
        self.out, self.sems, self.groups, self.d, self.t = out, sems, groups, d, t

    def at(self, r, k, rest):
        return self.out.at[(r, lax.rem(self.d - k + self.groups, self.groups)) + rest]

    def arrival(self, source, k, rest, where):
        send, recv = self.sems
        to = lax.rem(self.d + k, self.groups)
        return remote(
            source, self.at(0, 0, rest), send.at[(0, k) + where], recv.at[(0, k) + where], (to, self.t)
        )

    def across(self, k, rest, where):
        send, recv = self.sems
        return remote(
            self.at(0, k, rest),
            self.at(2, k, rest),
            send.at[(2, k) + where],
            recv.at[(2, k) + where],
            (self.d, jnp.bitwise_xor(self.t, 2)),
        )

    def beside(self, r, k, rest, where):
        send, recv = self.sems
        return remote(
            self.at(r, k, rest),
            self.at(r + 1, k, rest),
            send.at[(r + 1, k) + where],
            recv.at[(r + 1, k) + where],
            (self.d, jnp.bitwise_xor(self.t, 1)),
        )


def norm_forward(resid_rows, gain_vec, shift_vec):
    row_mean = jnp.mean(resid_rows, -1, keepdims=True)
    centred = resid_rows - row_mean
    inverse = lax.rsqrt(jnp.mean(centred * centred, -1, keepdims=True) + EPSILON)
    unit_rows = centred * inverse
    return (unit_rows * gain_vec + shift_vec, unit_rows, inverse)


def norm_backward(upstream, unit_rows, inverse, gain_vec):
    scaled = upstream * gain_vec
    inner_term = (
        scaled
        - jnp.mean(scaled, -1, keepdims=True)
        - unit_rows * jnp.mean(scaled * unit_rows, -1, keepdims=True)
    )
    return (
        inner_term * inverse,
        jnp.sum(upstream * unit_rows, 0, keepdims=True),
        jnp.sum(upstream, 0, keepdims=True),
    )


def middle_kernel(size, groups, count, *refs):
    x_ref, match_ref, cot_ref, over_ref, norm_ref, blocks_ref = refs[:6]
    weights_hbm = refs[6 : 6 + count]
    (
        result_ref,
        grad_one_ref,
        d_heads_ref,
        heads_ref,
        normed_t_ref,
        d_branch_t_ref,
        d_attn_t_ref,
        hidden_ref,
        d_gu_ref,
        norm_grad_ref,
        w_out_ref,
        w_gu_ref,
        w_down_ref,
        slope_ref,
        swish_ref,
        normed_ref,
        sum_ref,
        arrived_ref,
        sems,
        sends,
        recvs,
        keep,
    ) = refs[6 + count :]
    index = pl.program_id(0)
    first = index == 0
    d = lax.axis_index("dp")
    t = lax.axis_index("tensor")
    subs, local, _ = arrived_ref.shape[1:]
    inner = w_down_ref.shape[2]
    ids = (0, 2, 1, 3)
    part = [slice(r * local, (r + 1) * local) for r in range(size)]
    core = (d, jnp.bitwise_xor(t, 1))
    targets = (lambda r: w_out_ref.at[part[r]], lambda r: w_gu_ref.at[r], lambda r: w_down_ref.at[r])

    def weight_copies(kind, r):
        target = targets[kind](r)
        pieces = [(weights_hbm[2 * kind + r // 2], target)]
        if kind == 2 and r >= 2:
            pieces = []
            for i in range(2):
                half = weights_hbm[5 + i]
                low = pl.multiple_of(lax.rem(d + i, 2) * half.shape[0], 16)
                pieces.append((half, target.at[pl.ds(low, half.shape[0])]))
        copies = []
        for i, (source, place) in enumerate(pieces):
            recv = sems.at[kind, r, i]
            if r == 1 or r == 3:
                copies.append(remote(source, place, sems.at[kind, r - 1 + size, i], recv, core))
            else:
                copies.append(pltpu.make_async_copy(source, place, recv))
        return copies

    def weight_start(kind, r):
        for copy in weight_copies(kind, r):
            copy.start()

    def weight_wait(kind, r):
        for copy in weight_copies(kind, r):
            if r % 2 == 0:
                copy.wait()
            else:
                copy.wait_recv()

    def heads_copy(r, i):
        other = jnp.bitwise_xor(t, r)
        return remote(
            blocks_ref.at[other * subs + i],
            arrived_ref.at[r, i],
            sends.at[r, i],
            recvs.at[r, i],
            (d, other),
        )

    own_copy = pltpu.make_async_copy(blocks_ref.at[pl.ds(t * subs, subs)], arrived_ref.at[0], keep)

    @pl.when(first)
    def _():
        own_copy.start()
        for r in (0, 2):
            weight_start(0, r)
        greet(1, (1, 2, 3), d, t)
        for r in (2, 3, 1):
            heads_copy(r, 0).start()
        for r in (1, 3):
            weight_start(0, r)
        for r in ids:
            for kind in (1, 2):
                weight_start(kind, r)
        own_copy.wait()
        for r in ids:
            weight_wait(0, r)

    @pl.when(first)
    def _():
        norm_grad_ref[...] = jnp.zeros_like(norm_grad_ref)

    for r in ids[1:]:
        heads_copy(r, index).wait_recv()
        heads_copy(r, index).wait_send()

    @pl.when(index < subs - 1)
    def _():
        for r in (2, 3, 1):
            heads_copy(r, index + 1).start()

    for r in ids:
        heads_ref[r] = arrived_ref[r, index]
    heads_out = jnp.concatenate([arrived_ref[r, index] for r in range(size)], 0)
    attn = mm(heads_out, w_out_ref[...], 0, 0)
    gain_one, gain_two, shift_one, shift_two = (norm_ref[i : i + 1, :] for i in range(4))
    normed_one, unit_one, inverse_one = norm_forward(
        x_ref[...].astype(F32) + attn, gain_one, shift_one
    )
    normed_ref[...] = normed_one.astype(BF)
    normed_t_ref[...] = normed_one.T.astype(BF)
    sum_ref[...] = normed_one

    @pl.loop(0, size)
    def _(i):
        r = lax.rem(i, 2) * 2 + lax.div(i, 2)
        for k in ids:

            @pl.when(first & (r == k))
            def _():
                weight_wait(1, k)
                weight_wait(2, k)

        both = mm(normed_ref[...], w_gu_ref[r], 1, 0)
        gate = both[:, :inner]
        up = both[:, inner:]
        sig = 0.5 + 0.5 * jnp.tanh(0.5 * gate)
        swish = gate * sig
        hidden = (swish * up).astype(BF)
        swish_ref[r] = swish
        slope_ref[r] = up * (sig + swish * (1.0 - sig))
        hidden_ref[r] = hidden
        sum_ref[...] += mm(hidden, w_down_ref[r], 1, 1)

    result, unit_two, inverse_two = norm_forward(sum_ref[...], gain_two, shift_two)
    result_ref[...] = result.astype(BF)
    if groups:
        sub = BLOCK // groups
        spares = [over_ref[g, 0:1, :].astype(F32) for g in range(groups)]
        in_last = jnp.where((index == subs - 1) & (t == size - 1), 1.0, 0.0)
        ends = lax.broadcasted_iota(jnp.int32, (sub, 1), 0) == sub - 1
        pieces = []
        for g in range(groups):
            piece = cot_ref[g].astype(F32)
            spare, flag = spare_row(match_ref, groups, g, spares)
            fix = jnp.where(ends, flag * in_last, 0.0)
            pieces.append(piece * (1.0 - fix) + spare * fix)
        cot = jnp.concatenate(pieces, 0)
    else:
        cot = cot_ref[...].astype(F32)
    grad_two, d_gain_two, d_shift_two = norm_backward(cot, unit_two, inverse_two, gain_two)
    normed_ref[...] = grad_two.astype(BF)
    d_branch_t_ref[...] = grad_two.T.astype(BF)
    sum_ref[...] = grad_two

    @pl.loop(0, size)
    def _(r):
        grad_hidden = mm(normed_ref[...], w_down_ref[r], 1, 0)
        d_gate = (grad_hidden * slope_ref[r]).astype(BF)
        d_up = (grad_hidden * swish_ref[r]).astype(BF)
        d_gu_ref[r, :, :inner] = d_gate
        d_gu_ref[r, :, inner:] = d_up
        sum_ref[...] += mm(jnp.concatenate([d_gate, d_up], 1), w_gu_ref[r], 1, 1)

    grad_one, d_gain_one, d_shift_one = norm_backward(
        sum_ref[...], unit_one, inverse_one, gain_one
    )
    grad_one_ref[...] = grad_one
    d_attn_t = grad_one.T.astype(BF)
    d_attn_t_ref[...] = d_attn_t
    d_heads = mm(w_out_ref[...], d_attn_t, 1, 0).astype(BF)
    for r in ids:
        d_heads_ref[r] = d_heads[part[r]]
    for i, grad in enumerate((d_gain_one, d_gain_two, d_shift_one, d_shift_two)):
        norm_grad_ref[i : i + 1, :] += grad

    @pl.when(index == subs - 1)
    def _():
        for kind in range(3):
            for r in (1, 3):
                for copy in weight_copies(kind, r):
                    copy.wait_send()


def middle(x_own, match, cot, norms, o_blocks, size, *weights):
    rows, width = x_own.shape
    local = o_blocks.shape[1]
    inner = weights[4].shape[1]
    block = pl.BlockSpec((BLOCK, width), lambda i: (i, 0))
    turned = pl.BlockSpec((width, BLOCK), lambda i: (0, i))
    anywhere = pl.BlockSpec(memory_space=pl.ANY)
    shape = jax.ShapeDtypeStruct
    groups = cot.shape[0] if cot.ndim == 3 else 0
    if groups:
        sub = BLOCK // groups
        last = cot.shape[1] // 16 - 1
        cot_specs = [
            pl.BlockSpec((groups, sub, width), lambda i: (0, i, 0)),
            pl.BlockSpec((groups, 16, width), lambda i: (0, last, 0)),
        ]
    else:
        cot_specs = [block, pl.BlockSpec((16, width), lambda i: (0, 0))]
    return pl.pallas_call(
        functools.partial(middle_kernel, size, groups, len(weights)),
        grid=(rows // BLOCK,),
        in_specs=[block, pl.BlockSpec(memory_space=pltpu.SMEM)]
        + cot_specs
        + [pl.BlockSpec(norms.shape, lambda i: (0, 0))]
        + [anywhere] * (1 + len(weights)),
        out_specs=[
            block,
            block,
            pl.BlockSpec((size, local, BLOCK), lambda i: (0, 0, i)),
            pl.BlockSpec((size, local, BLOCK), lambda i: (0, 0, i)),
            turned,
            turned,
            turned,
            pl.BlockSpec((size, BLOCK, inner), lambda i: (0, i, 0)),
            pl.BlockSpec((size, BLOCK, 2 * inner), lambda i: (0, i, 0)),
            pl.BlockSpec((8, width), lambda i: (0, 0)),
        ],
        out_shape=[
            shape((rows, width), BF),
            shape((rows, width), F32),
            shape((size, local, rows), BF),
            shape((size, local, rows), BF),
            shape((width, rows), BF),
            shape((width, rows), BF),
            shape((width, rows), BF),
            shape((size, rows, inner), BF),
            shape((size, rows, 2 * inner), BF),
            shape((8, width), F32),
        ],
        scratch_shapes=[
            pltpu.VMEM((size * local, width), BF),
            pltpu.VMEM((size, width, 2 * inner), BF),
            pltpu.VMEM((size, width, inner), BF),
            pltpu.VMEM((size, BLOCK, inner), F32),
            pltpu.VMEM((size, BLOCK, inner), F32),
            pltpu.VMEM((BLOCK, width), BF),
            pltpu.VMEM((BLOCK, width), F32),
            pltpu.VMEM((size, rows // BLOCK, local, BLOCK), BF),
            pltpu.SemaphoreType.DMA((3, 2 * size, 2)),
            pltpu.SemaphoreType.DMA((size, rows // BLOCK)),
            pltpu.SemaphoreType.DMA((size, rows // BLOCK)),
            pltpu.SemaphoreType.DMA,
        ],
        compiler_params=pltpu.CompilerParams(
            collective_id=2, has_side_effects=True, vmem_limit_bytes=VMEM_LIMIT
        ),
        cost_estimate=pl.CostEstimate(
            flops=2 * rows * width * (6 * size * inner + 2 * size * local),
            bytes_accessed=40 << 20,
            transcendentals=rows * size * inner,
        ),
        name="middle",
    )(x_own, match, cot, cot, norms, o_blocks, *weights)


def product_tiles(left_ref, right_ref, store):
    @pl.loop(0, right_ref.shape[2] // TILE)
    def _(i):
        columns = pl.ds(pl.multiple_of(i * TILE, TILE), TILE)
        store(columns, mm(left_ref[...], right_ref[0, :, columns], 1, 0))


def weight_grads_tile(
    normed_t_ref, d_branch_t_ref, d_attn_t_ref, hidden_ref, d_gu_ref, heads_ref, norm_ref, store
):
    wide = d_gu_ref.shape[2]
    local = heads_ref.shape[1]
    product_tiles(normed_t_ref, d_gu_ref, store)
    d_out = mm(d_attn_t_ref[...], heads_ref[0], 1, 1)
    norm = norm_ref[...].T
    spare = -(local + norm.shape[1]) % 128
    tail = jnp.concatenate([d_out, norm, jnp.zeros((norm.shape[0], spare), F32)], 1)
    store(pl.ds(wide, tail.shape[1]), tail)
    base = wide + tail.shape[1]

    def shifted(columns, value):
        store(pl.ds(pl.multiple_of(base + columns.start, 128), columns.size), value)

    product_tiles(d_branch_t_ref, hidden_ref, shifted)


def weight_grads_kernel(*refs):
    out_ref = refs[-1]

    def store(columns, value):
        out_ref[0, :, columns] = value.astype(BF)

    weight_grads_tile(*refs[:-1], store)


def weight_grads(odd, normed_t, d_branch_t, d_attn_t, hidden, d_gu, heads, norm_grads):
    size, rows, inner = hidden.shape
    local = heads.shape[1]
    width = normed_t.shape[0]
    wide = 3 * inner + local + norm_grads.shape[0]
    wide = (wide + 127) // 128 * 128
    flat = pl.BlockSpec((width, rows), lambda i: (0, 0))
    pick = lambda i: (2 * i + odd, 0, 0)
    return pl.pallas_call(
        weight_grads_kernel,
        grid=(size // 2,),
        in_specs=[
            flat,
            flat,
            flat,
            pl.BlockSpec((1, rows, inner), pick),
            pl.BlockSpec((1, rows, 2 * inner), pick),
            pl.BlockSpec((1, local, rows), pick),
            pl.BlockSpec(norm_grads.shape, lambda i: (0, 0)),
        ],
        out_specs=pl.BlockSpec((1, width, wide), lambda i: (i, 0, 0)),
        out_shape=jax.ShapeDtypeStruct((size // 2, width, wide), BF),
        compiler_params=pltpu.CompilerParams(vmem_limit_bytes=VMEM_LIMIT),
        cost_estimate=pl.CostEstimate(
            flops=size * rows * width * (3 * inner + local), bytes_accessed=20 << 20, transcendentals=0
        ),
        name="weight_grads",
    )(normed_t, d_branch_t, d_attn_t, hidden, d_gu, heads, norm_grads)


def grads_kernel(groups, size, match_ref, *refs):
    tile_refs = refs[:7]
    (
        d_heads_ref,
        result_ref,
        wide_own_ref,
        wide_other_ref,
        down_ref,
        do_ref,
        home_ref,
        over_ref,
        sent_ref,
        got_ref,
        own_ref,
        spare_ref,
        s_grad,
        r_grad,
        s_heads,
        r_heads,
        sends,
        recvs,
        s_over,
        r_over,
        keep,
        outs,
    ) = refs[7:]
    step = pl.program_id(0)
    d = lax.axis_index("dp")
    t = lax.axis_index("tensor")
    chunks, _, sub, width = own_ref.shape
    core = (d, jnp.bitwise_xor(t, 1))
    body = Spread(home_ref, (sends, recvs), groups, d, t)
    extra = Spread(over_ref, (s_over, r_over), groups, d, t)

    def heads_copy(r):
        return remote(
            d_heads_ref.at[r],
            do_ref.at[r],
            s_heads.at[r],
            r_heads.at[r],
            (d, jnp.bitwise_xor(t, r)),
        )

    def grad_copy(i):
        return remote(sent_ref.at[i], got_ref.at[i], s_grad.at[i], r_grad.at[i], core)

    def own_copy(c):
        return pltpu.make_async_copy(own_ref.at[c, d], home_ref.at[0, d, c], keep.at[c])

    def arrival(c, k):
        return body.arrival(own_ref.at[c, lax.rem(d + k, groups)], k, (c,), (c,))

    def pass_on(c):
        own_copy(c).wait()
        for k in range(groups):
            if k > 0:
                arrival(c, k).wait_recv()
            body.across(k, (c,), (c,)).start()

    load = pltpu.make_async_copy(result_ref, own_ref, keep.at[chunks])
    own_heads = pltpu.make_async_copy(d_heads_ref.at[0], do_ref.at[0], keep.at[chunks + 1])
    own_over = pltpu.make_async_copy(spare_ref.at[d], over_ref.at[0, d], keep.at[chunks + 2])

    @pl.when(step == 0)
    def _():
        load.start()
        own_heads.start()
        greet(groups, (1, 2, 3), d, t)
        for r in (2, 3, 1):
            heads_copy(r).start()
        load.wait()
        for c in range(chunks):
            own_copy(c).start()
            for k in range(1, groups):
                arrival(c, k).start()
        last = [own_ref[chunks - 1, g, sub - 16 :, :].astype(F32)[15:16] for g in range(groups)]
        for to in range(groups):
            spare = last[0] * match_ref[to]
            for g in range(1, groups):
                spare = spare + last[g] * match_ref[g * groups + to]
            spare_ref[to] = spare.astype(BF)
        own_over.start()
        for k in range(1, groups):
            extra.arrival(spare_ref.at[lax.rem(d + k, groups)], k, (), ()).start()

    for c in range(chunks - 1):

        @pl.when(step == c + 2)
        def _():
            pass_on(c)

    @pl.when(step < 2)
    def _():
        def store(columns, value):
            sent_ref[step, :, columns] = value.astype(BF)

        weight_grads_tile(*tile_refs, store)
        grad_copy(step).start()

    @pl.when(step >= 2)
    def _():
        grad_copy(step - 2).wait_recv()
        grad_copy(step - 2).wait_send()

        def store(columns, value):
            sent_ref[step - 2, :, columns] = (
                value + got_ref[step - 2, :, columns].astype(F32)
            ).astype(BF)

        weight_grads_tile(*tile_refs, store)

    part = down_ref.shape[2]

    def leave(i):
        copies = [(sent_ref.at[i, :, pl.ds(0, WIDE)], (wide_own_ref, wide_other_ref)[i])]
        for g in range(groups):
            rest = sent_ref.at[i, pl.ds(g * part, part), pl.ds(WIDE, down_ref.shape[3])]
            copies.append((rest, down_ref.at[g, i]))
        return [
            pltpu.make_async_copy(source, target, outs.at[i, j])
            for j, (source, target) in enumerate(copies)
        ]

    for i in range(2):

        @pl.when(step == 2 + i)
        def _():
            for copy in leave(i):
                copy.start()

    @pl.when(step == size - 1)
    def _():
        for i in range(2):
            for copy in leave(i):
                copy.wait()
        own_over.wait()
        for k in range(groups):
            if k > 0:
                extra.arrival(spare_ref.at[0], k, (), ()).wait_recv()
            extra.across(k, (), ()).start()
            extra.beside(0, k, (), ()).start()
        for k in range(groups):
            extra.across(k, (), ()).wait_recv()
            extra.beside(2, k, (), ()).start()
        own_heads.wait()
        for r in range(1, size):
            heads_copy(r).wait_recv()
            heads_copy(r).wait_send()
        own_copy(chunks - 1).wait()
        for c in range(chunks):
            for k in range(groups):
                if k > 0 and c == chunks - 1:
                    arrival(c, k).wait_recv()
                if k > 0:
                    arrival(c, k).wait_send()
                if c < chunks - 1:
                    body.across(k, (c,), (c,)).wait_recv()
                    body.across(k, (c,), (c,)).wait_send()
        for k in range(groups):
            extra.beside(0, k, (), ()).wait_recv()
            extra.beside(2, k, (), ()).wait_recv()
            if k > 0:
                extra.arrival(spare_ref.at[0], k, (), ()).wait_send()
            extra.across(k, (), ()).wait_send()
            extra.beside(0, k, (), ()).wait_send()
            extra.beside(2, k, (), ()).wait_send()


def grads(
    match, groups, normed_t, d_branch_t, d_attn_t, hidden, d_gu, heads, norm_grads, d_heads, result
):
    size, rows, inner = hidden.shape
    local = heads.shape[1]
    width = normed_t.shape[0]
    chunks = rows // BLOCK
    sub = BLOCK // groups
    total = 3 * inner + (local + norm_grads.shape[0] + 127) // 128 * 128
    part = width // groups
    whole = lambda *shape: pl.BlockSpec(shape, lambda i: (0,) * len(shape))
    pick = lambda i: (jnp.where(i < 2, 2 * i + 1, 2 * i - 4), 0, 0)
    anywhere = pl.BlockSpec(memory_space=pl.ANY)
    dma = pltpu.SemaphoreType.DMA
    return pl.pallas_call(
        functools.partial(grads_kernel, groups, size),
        grid=(size,),
        in_specs=[
            pl.BlockSpec(memory_space=pltpu.SMEM),
            whole(width, rows),
            whole(width, rows),
            whole(width, rows),
            pl.BlockSpec((1, rows, inner), pick),
            pl.BlockSpec((1, rows, 2 * inner), pick),
            pl.BlockSpec((1, local, rows), pick),
            whole(*norm_grads.shape),
            anywhere,
            anywhere,
        ],
        out_specs=[
            anywhere,
            anywhere,
            anywhere,
            anywhere,
            anywhere,
            anywhere,
        ],
        out_shape=[
            jax.ShapeDtypeStruct((width, WIDE), BF),
            jax.ShapeDtypeStruct((width, WIDE), BF),
            jax.ShapeDtypeStruct((groups, 2, part, total - WIDE), BF),
            jax.ShapeDtypeStruct(d_heads.shape, BF),
            jax.ShapeDtypeStruct((3, groups, chunks, sub, width), BF),
            jax.ShapeDtypeStruct((size, groups, 1, width), BF),
        ],
        scratch_shapes=[
            pltpu.VMEM((2, width, total), BF),
            pltpu.VMEM((2, width, total), BF),
            pltpu.VMEM((chunks, groups, sub, width), BF),
            pltpu.VMEM((groups, 1, width), BF),
            dma((2,)),
            dma((2,)),
            dma((size,)),
            dma((size,)),
            dma((3, groups, chunks)),
            dma((3, groups, chunks)),
            dma((4, groups)),
            dma((4, groups)),
            dma((chunks + 3,)),
            dma((2, groups + 1)),
        ],
        compiler_params=pltpu.CompilerParams(
            collective_id=3, has_side_effects=True, vmem_limit_bytes=VMEM_LIMIT
        ),
        cost_estimate=pl.CostEstimate(
            flops=2 * size * rows * width * (3 * inner + local),
            bytes_accessed=80 << 20,
            transcendentals=0,
        ),
        name="grads",
    )(
        match,
        normed_t,
        d_branch_t,
        d_attn_t,
        hidden,
        d_gu,
        heads,
        norm_grads,
        d_heads,
        result.reshape(chunks, groups, sub, width),
    )


def swap(array, size, step):
    return lax.ppermute(array, "tensor", [(i, i ^ step) for i in range(size)])


def gather_members(own):
    size = lax.axis_size("tensor")
    across = swap(own, size, 2)
    return [own, swap(own, size, 1), across, swap(across, size, 1)]


def exchange_members(pieces):
    size = lax.axis_size("tensor")
    return [pieces[0]] + [swap(pieces[r], size, r) for r in range(1, size)]


def reduce_members(pieces):
    size = lax.axis_size("tensor")
    near = swap(pieces[1], size, 1)
    far = swap(pieces[3], size, 1)
    other = (pieces[2].astype(F32) + far.astype(F32)).astype(BF)
    across = swap(other, size, 2)
    return pieces[0].astype(F32) + near.astype(F32) + across.astype(F32)


def unpack_block(spots_ref, src_ref, i):
    window = ROWS + 16
    shape = (ROWS, window)
    rows = lax.broadcasted_iota(jnp.int32, shape, 0)
    steps = lax.broadcasted_iota(jnp.int32, shape, 1) - rows
    bound = spots_ref[8 * i + 6]
    total = None
    for k in range(2):
        group, start, shift = (spots_ref[8 * i + 3 * k + j] for j in range(3))
        wanted = rows < bound if k == 0 else rows >= bound
        hot = jnp.where((steps == shift) & wanted, 1.0, 0.0).astype(BF)
        tiles = [src_ref[group, start + j] for j in range(window // 16)]
        part = mm(hot, jnp.concatenate(tiles, 0), 1, 0)
        total = part if k == 0 else total + part
    return total.astype(BF)


def store_over(src_ref, over_ref, last):
    top = lax.broadcasted_iota(jnp.int32, (16, 1), 0) == 0
    end = src_ref.shape[1] - 1
    for g in range(src_ref.shape[0]):
        src_ref[g, end] = jnp.where(top, over_ref[last, g].astype(F32), 0.0).astype(BF)


def unpack_kernel(
    size, spots, me, home_ref, over_ref, result_ref, out_ref, result_out_ref, src_ref, sems
):
    tiles = home_ref.shape[2]
    step = pl.program_id(0)
    each = out_ref.shape[0] // ROWS

    def load(r):
        at = pl.ds(jnp.bitwise_xor(me[0], r) * tiles, tiles)
        return pltpu.make_async_copy(home_ref.at[r], src_ref.at[:, at], sems.at[r])

    @pl.when(step == 0)
    def _():
        for r in range(size):
            load(r).start()
        store_over(src_ref, over_ref, jnp.bitwise_xor(size - 1, me[0]))
        for r in range(size):
            load(r).wait()

    for i in range(each):
        out_ref[i * ROWS : (i + 1) * ROWS, :] = unpack_block(spots, src_ref, step * each + i)
    result_out_ref[...] = result_ref[...]


def unpack(spots, me, home, over, result):
    size, groups, share, width = home.shape
    rows = size * groups * share
    home = home.reshape(size, groups, share // 16, 16, width)
    whole = lambda *shape: pl.BlockSpec(shape, lambda i, *refs: (0,) * len(shape))
    anywhere = pl.BlockSpec(memory_space=pl.ANY)
    each = 4 * ROWS
    block = pl.BlockSpec((each, width), lambda i, *refs: (i, 0))
    return pl.pallas_call(
        functools.partial(unpack_kernel, size),
        grid_spec=pltpu.PrefetchScalarGridSpec(
            num_scalar_prefetch=2,
            grid=(rows // each,),
            in_specs=[anywhere, whole(*over.shape), block],
            out_specs=[block, block],
            scratch_shapes=[
                pltpu.VMEM((groups, size * share // 16 + 1, 16, width), BF),
                pltpu.SemaphoreType.DMA((size,)),
            ],
        ),
        out_shape=[jax.ShapeDtypeStruct((rows, width), BF)] * 2,
        compiler_params=pltpu.CompilerParams(vmem_limit_bytes=VMEM_LIMIT),
        cost_estimate=pl.CostEstimate(flops=0, bytes_accessed=30 << 20, transcendentals=0),
        name="unpack",
    )(spots, me, home, over, result)


def route_kernel(groups, size, send_ref, over_ref, out_ref, over_out_ref, sends, recvs, s_over, r_over, keep):
    d = lax.axis_index("dp")
    t = lax.axis_index("tensor")
    chunks = sends.shape[2]
    count = send_ref.shape[1] // chunks
    greet(groups, (1, 2), d, t)
    spread = Spread(out_ref, (sends, recvs), groups, d, t)

    def rows(c):
        return pl.ds(c * count, count)

    def own(c):
        return pltpu.make_async_copy(
            send_ref.at[d, rows(c)], out_ref.at[0, d, rows(c)], keep.at[c]
        )

    def arrival(c, k):
        return spread.arrival(send_ref.at[lax.rem(d + k, groups), rows(c)], k, (rows(c),), (c,))

    def across(c, k):
        return spread.across(k, (rows(c),), (c,))

    def beside(r, c, k):
        return spread.beside(r, k, (rows(c),), (c,))

    def over_copy(k):
        to = lax.rem(d + k, groups)
        return remote(over_ref.at[to], over_out_ref.at[d], s_over.at[k], r_over.at[k], (to, t))

    def pass_far(c):
        for k in range(groups):
            across(c, k).wait_recv()
            beside(2, c, k).start()

    own_over = pltpu.make_async_copy(over_ref.at[d], over_out_ref.at[d], keep.at[chunks])
    for c in range(chunks):
        own(c).start()
    own_over.start()
    for c in range(chunks):
        for k in range(1, groups):
            arrival(c, k).start()
    for k in range(1, groups):
        over_copy(k).start()
    for c in range(chunks):
        own(c).wait()
        for k in range(groups):
            if k > 0:
                arrival(c, k).wait_recv()
            across(c, k).start()
            beside(0, c, k).start()
        if c > 0:
            pass_far(c - 1)
    pass_far(chunks - 1)
    own_over.wait()
    for k in range(groups):
        for c in range(chunks):
            beside(0, c, k).wait_recv()
            beside(2, c, k).wait_recv()
            if k > 0:
                arrival(c, k).wait_send()
            across(c, k).wait_send()
            beside(0, c, k).wait_send()
            beside(2, c, k).wait_send()
        if k > 0:
            over_copy(k).wait_recv()
            over_copy(k).wait_send()


def route(send, over, size):
    groups = send.shape[0]
    anywhere = pl.BlockSpec(memory_space=pl.ANY)
    return pl.pallas_call(
        functools.partial(route_kernel, groups, size),
        in_specs=[anywhere, anywhere],
        out_specs=[anywhere, anywhere],
        out_shape=[
            jax.ShapeDtypeStruct((size,) + send.shape, BF),
            jax.ShapeDtypeStruct(over.shape, BF),
        ],
        scratch_shapes=[
            pltpu.SemaphoreType.DMA((4, groups, 3)),
            pltpu.SemaphoreType.DMA((4, groups, 3)),
            pltpu.SemaphoreType.DMA((groups,)),
            pltpu.SemaphoreType.DMA((groups,)),
            pltpu.SemaphoreType.DMA((4,)),
        ],
        compiler_params=pltpu.CompilerParams(collective_id=0, has_side_effects=True),
        cost_estimate=pl.CostEstimate(flops=0, bytes_accessed=60 << 20, transcendentals=0),
        name="route",
    )(send, over)


class Halving:
    def __init__(self, fetch, links, refs, sems):
        self.fetch, self.links = fetch, links
        self.out, self.got, self.held = refs
        self.send, self.recv = sems
        self.counts = [2 ** (len(links) - 1 - step) for step in range(len(links))]
        self.first = [sum(self.counts[:step]) for step in range(len(links))]

    def term(self, side, i):
        rest = [lax.rem(lax.div(i, 2**j), 2) for j in range(len(self.links) - 1)]
        return self.fetch(side, *rest)

    def copy(self, step, i):
        at = self.first[step] + i
        return remote(
            self.out.at[at], self.got.at[at], self.send.at[at], self.recv.at[at], self.links[step][1]
        )

    def start(self):
        for i in range(self.counts[0]):
            self.out[i] = self.term(1 - self.links[0][0], jnp.int32(i)).astype(BF)
            self.copy(0, i).start()

    def advance(self, step):
        for i in range(self.counts[step - 1]):
            self.copy(step - 1, i).wait_recv()
        own = self.links[step][0]
        for keep in (False, True):
            for j in range(self.counts[step]):
                i = (own if keep else 1 - own) + 2 * j
                value = self.term(self.links[0][0], i) if step == 1 else self.held[i]
                value = value + self.got[self.first[step - 1] + i].astype(F32)
                if keep:
                    self.held[j] = value
                else:
                    self.out[self.first[step] + j] = value.astype(BF)
                    self.copy(step, j).start()

    def total(self):
        last = len(self.links) - 1
        self.copy(last, 0).wait_recv()
        return self.held[0] + self.got[self.first[last]].astype(F32)

    def finish(self):
        for step, count in enumerate(self.counts):
            for i in range(count):
                self.copy(step, i).wait_send()


def settle_kernel(
    groups,
    size,
    match_ref,
    spots_ref,
    res_over_ref,
    d_hbm,
    x_hbm,
    w_hbm,
    one_hbm,
    wide_own_hbm,
    wide_other_hbm,
    down_hbm,
    res_hbm,
    home_ref,
    over_ref,
    result_hbm,
    gq_sum_ref,
    gu_sum_ref,
    down_sum_ref,
    out_sum_ref,
    norm_sum_ref,
    d_ref,
    x_ref,
    w_ref,
    one_ref,
    wide_own_ref,
    wide_other_ref,
    down_ref,
    down_sent_ref,
    down_got_ref,
    src_ref,
    out_ref,
    to_core_ref,
    from_core_ref,
    pair_ref,
    other_ref,
    own_ref,
    spare_ref,
    gq_ref,
    gq_acc_ref,
    *refs,
):
    halving_refs = tuple(refs[3 * i : 3 * i + 3] for i in range(3))
    (
        loads,
        s_res,
        r_res,
        s_half,
        r_half,
        sends,
        recvs,
        s_over,
        r_over,
        s_sum,
        r_sum,
        keep,
    ) = refs[9:]
    d = lax.axis_index("dp")
    t = lax.axis_index("tensor")
    chunks, _, sub, width = own_ref.shape
    sent = (chunks - 1) * sub // 16
    rest = sub // 16
    core = (d, jnp.bitwise_xor(t, 1))
    chip = (d, jnp.bitwise_xor(t, 2))

    def load(source, target, i):
        return pltpu.make_async_copy(source, target, loads.at[i])

    def load_d(r):
        part = jnp.bitwise_xor(t, r)
        return load(d_hbm.at[part], d_ref.at[part], r)

    load_w = load(w_hbm, w_ref, 4)
    load_x = load(x_hbm, x_ref, 5)
    load_one = load(one_hbm, one_ref, 6)
    load_wide = (load(wide_own_hbm, wide_own_ref, 7), load(wide_other_hbm, wide_other_ref, 8))
    load_down = load(down_hbm, down_ref, 11)
    down_copy = remote(down_sent_ref, down_got_ref, s_res.at[4], r_res.at[4], chip)

    def down_sum(member):
        total = down_ref[0, member].astype(F32)
        for g in range(1, groups):
            total = total + down_ref[g, member].astype(F32)
        return total


    def in_src(r, low, count):
        base = jnp.bitwise_xor(t, r) * (sent + rest)
        return src_ref.at[:, pl.ds(base + low, count)]

    def source_of(r, low, count):
        return res_hbm.at[r, :, pl.ds(low, count)]

    res_parts = (
        (source_of(0, 0, sent + rest), in_src(0, 0, sent + rest)),
        (source_of(2, 0, sent), in_src(2, 0, sent)),
        (in_src(2, sent, rest), in_src(2, sent, rest)),
    )
    load_res = [load(source, target, 9 + i) for i, (source, target) in enumerate(res_parts[:2])]
    beside_res = [
        remote(source, target, s_res.at[i], r_res.at[i], core)
        for i, (source, target) in enumerate(res_parts)
    ]
    across_res = remote(
        source_of(0, sent, rest), in_src(0, sent, rest), s_res.at[3], r_res.at[3], chip
    )

    load_w.start()
    load_d(3).start()
    load_d(2).start()
    greet(groups, (1, 2), d, t)

    def rows(c):
        return pl.ds(pl.multiple_of(c * BLOCK, BLOCK), BLOCK)

    def piece(r, c):
        return mm(d_ref[jnp.bitwise_xor(t, r), :, rows(c)], w_ref[...], 0, 0)

    def to_core(i, c):
        return remote(
            to_core_ref.at[i, c], from_core_ref.at[i, c], s_sum.at[i, c], r_sum.at[i, c], core
        )

    def other(c):
        return remote(pair_ref.at[c], other_ref.at[c], s_sum.at[2, c], r_sum.at[2, c], chip)

    load_w.wait()
    load_d(3).wait()
    load_d(1).start()
    load_d(0).start()
    load_wide[0].start()
    load_wide[1].start()
    load_d(2).wait()

    @pl.loop(0, chunks)
    def _(c):
        to_core_ref[0, c] = piece(3, c).astype(BF)
        to_core(0, c).start()
        value = piece(2, c)
        to_core(0, c).wait_recv()
        pair_ref[c] = (value + from_core_ref[0, c].astype(F32)).astype(BF)

        @pl.when(c == 0)
        def _():
            other(0).start()

    block_rows, _, inner = gu_sum_ref.shape

    def wide_rows(part, block):
        at = pl.ds(pl.multiple_of(block * block_rows, block_rows), block_rows)
        columns = slice(part * WIDE_PARTS[0], WIDE_PARTS[0] + part * WIDE_PARTS[1])
        return wide_own_ref[at, columns].astype(F32) + wide_other_ref[at, columns].astype(F32)

    def gq_rows(y, low, high):
        return gq_ref[y + 2 * low + 4 * high].astype(F32)

    link_y, link_low, link_high = (
        (lax.rem(lax.div(d, step), 2), (jnp.bitwise_xor(d, step), t)) for step in (1, 2, 4)
    )
    sums = [
        Halving(fetch, links, halving_refs[i], (s_half.at[i], r_half.at[i]))
        for i, (fetch, links) in enumerate(
            (
                (
                    lambda y, low, high: wide_rows(0, y + 2 * low + 4 * high),
                    (link_y, link_low, link_high),
                ),
                (
                    lambda low, y, high: wide_rows(1, y + 2 * low + 4 * high),
                    (link_low, link_y, link_high),
                ),
                (gq_rows, (link_y, link_low, link_high)),
            )
        )
    ]

    load_wide[0].wait()
    load_wide[1].wait()
    load_x.start()
    load_one.start()
    load_down.start()
    for copy in load_res:
        copy.start()
    sums[0].start()
    sums[1].start()
    load_d(1).wait()

    @pl.loop(0, chunks)
    def _(c):
        to_core_ref[1, c] = piece(1, c).astype(BF)
        to_core(1, c).start()

    load_d(0).wait()
    load_one.wait()

    @pl.loop(0, chunks)
    def _(c):
        one_ref[rows(c), :] += piece(0, c)

    def start_gq():
        load_x.wait()
        gq_acc_ref[...] = jnp.zeros_like(gq_acc_ref)

        @pl.loop(0, size)
        def _(part):
            gq_acc_ref[...] += mm(d_ref[part], x_ref[part], 1, 0)

        total = gq_acc_ref[...].T.astype(BF)
        for g in range(groups):
            gq_ref[g] = total[g * block_rows : (g + 1) * block_rows]
        sums[2].start()

    def store_result(i):
        at = pl.ds(pl.multiple_of(i * ROWS, ROWS), ROWS)
        return pltpu.make_async_copy(out_ref.at[at], result_hbm.at[at], keep.at[chunks + 1 + i])

    blocks = out_ref.shape[0] // ROWS

    def arrange_result():
        for copy in load_res:
            copy.wait()
        for copy in beside_res:
            copy.wait_recv()

        @pl.loop(0, blocks)
        def _(i):
            at = pl.ds(pl.multiple_of(i * ROWS, ROWS), ROWS)
            out_ref[at, :] = unpack_block(spots_ref, src_ref, i)
            store_result(i).start()

    store_over(src_ref, res_over_ref, jnp.bitwise_xor(size - 1, t))

    body = Spread(home_ref, (sends, recvs), groups, d, t)
    extra = Spread(over_ref, (s_over, r_over), groups, d, t)

    def own_copy(c):
        return pltpu.make_async_copy(own_ref.at[c, d], home_ref.at[0, d, c], keep.at[c])

    own_over = pltpu.make_async_copy(spare_ref.at[d], over_ref.at[0, d], keep.at[chunks])

    def pass_on(c):
        own_copy(c).wait()
        for k in range(groups):
            if k > 0:
                body.arrival(own_ref.at[c, 0], k, (c,), (c,)).wait_recv()
            body.across(k, (c,), (c,)).start()
            body.beside(0, k, (c,), (c,)).start()

    def pass_far(c):
        for k in range(groups):
            body.across(k, (c,), (c,)).wait_recv()
            body.beside(2, k, (c,), (c,)).start()

    def send_home(c):
        to_core(1, c).wait_recv()
        partial = one_ref[rows(c), :] + from_core_ref[1, c].astype(F32)
        other(c).wait_recv()
        done = (partial + other_ref[c].astype(F32)).astype(BF)
        for g in range(groups):
            own_ref[c, g] = done[g * sub : (g + 1) * sub]
        own_copy(c).start()
        for k in range(1, groups):
            body.arrival(own_ref.at[c, lax.rem(d + k, groups)], k, (c,), (c,)).start()
        if c == chunks - 1:
            last = [own_ref[c, g, sub - 16 :, :].astype(F32)[15:16] for g in range(groups)]
            for to in range(groups):
                spare = last[0] * match_ref[to]
                for g in range(1, groups):
                    spare = spare + last[g] * match_ref[g * groups + to]
                spare_ref[to] = spare.astype(BF)
            own_over.start()
            for k in range(1, groups):
                extra.arrival(spare_ref.at[lax.rem(d + k, groups)], k, (), ()).start()

    other(0).wait_send()
    other(1).start()
    send_home(0)
    start_gq()
    other(1).wait_send()
    other(2).start()
    send_home(1)
    sums[0].advance(1)
    sums[1].advance(1)
    other(2).wait_send()
    pass_on(0)
    across_res.start()
    send_home(2)
    sums[0].advance(2)
    sums[1].advance(2)
    sums[2].advance(1)
    pass_on(1)
    across_res.wait_recv()
    for copy in beside_res:
        copy.start()
    load_down.wait()
    down_sent_ref[...] = down_sum(1).astype(BF)
    down_copy.start()
    pass_on(2)
    own_over.wait()
    for k in range(groups):
        if k > 0:
            extra.arrival(spare_ref.at[0], k, (), ()).wait_recv()
        extra.across(k, (), ()).start()
        extra.beside(0, k, (), ()).start()
    sums[2].advance(2)
    pass_far(0)
    pass_far(1)
    arrange_result()
    down_copy.wait_recv()
    totals = jnp.concatenate(
        [sums[0].total(), sums[1].total(), down_sum(0) + down_got_ref[...].astype(F32)], 1
    )
    gu_sum_ref[:, 0, :] = totals[:, :inner]
    gu_sum_ref[:, 1, :] = totals[:, inner : 2 * inner]
    total = sums[2].total()
    local = gq_sum_ref.shape[2]
    for i in range(3):
        gq_sum_ref[i] = total[:, i * local : (i + 1) * local]
    out_sum_ref[...] = totals[:, 2 * inner : 2 * inner + local]
    norm_sum_ref[...] = totals[:, 2 * inner + local : 2 * inner + local + norm_sum_ref.shape[1]]
    down_sum_ref[...] = totals[:, totals.shape[1] - inner :]
    pass_far(2)
    for k in range(groups):
        extra.across(k, (), ()).wait_recv()
        extra.beside(2, k, (), ()).start()
    down_copy.wait_send()
    across_res.wait_send()
    for copy in beside_res:
        copy.wait_send()

    @pl.loop(0, blocks)
    def _(i):
        store_result(i).wait()

    for each in sums:
        each.finish()
    for c in range(chunks):
        to_core(0, c).wait_send()
        to_core(1, c).wait_send()
    for k in range(groups):
        for c in range(chunks):
            body.beside(0, k, (c,), (c,)).wait_recv()
            body.beside(2, k, (c,), (c,)).wait_recv()
            if k > 0:
                body.arrival(own_ref.at[c, 0], k, (c,), (c,)).wait_send()
            body.across(k, (c,), (c,)).wait_send()
            body.beside(0, k, (c,), (c,)).wait_send()
            body.beside(2, k, (c,), (c,)).wait_send()
        extra.beside(0, k, (), ()).wait_recv()
        extra.beside(2, k, (), ()).wait_recv()
        if k > 0:
            extra.arrival(spare_ref.at[0], k, (), ()).wait_send()
        extra.across(k, (), ()).wait_send()
        extra.beside(0, k, (), ()).wait_send()
        extra.beside(2, k, (), ()).wait_send()


def settle(
    match,
    spots,
    res_over,
    d_qkv_t,
    x_all,
    w_t,
    grad_one,
    wide_own,
    wide_other,
    down,
    inner,
    res,
):
    size, local, rows = d_qkv_t.shape
    _, groups, _, sub, width = res.shape
    share = res.shape[2] * sub
    res = res.reshape(-1, groups, share // 16, 16, width)
    chunks = rows // BLOCK
    part = width // groups
    total_rows = size * rows
    anywhere = pl.BlockSpec(memory_space=pl.ANY)
    vmem = pl.BlockSpec(memory_space=pltpu.VMEM)
    smem = pl.BlockSpec(memory_space=pltpu.SMEM)
    dma = pltpu.SemaphoreType.DMA
    shape = jax.ShapeDtypeStruct
    buffer = pltpu.VMEM((chunks, BLOCK, width), BF)
    pair_buffer = pltpu.VMEM((2, chunks, BLOCK, width), BF)
    halving = lambda columns, steps: [
        pltpu.VMEM((2**steps - 1, part, columns), BF),
        pltpu.VMEM((2**steps - 1, part, columns), BF),
        pltpu.VMEM((2 ** (steps - 2), part, columns), F32),
    ]
    return pl.pallas_call(
        functools.partial(settle_kernel, groups, size),
        in_specs=[smem, smem, vmem] + [anywhere] * 8,
        out_specs=[anywhere, anywhere, anywhere] + [vmem] * 5,
        out_shape=[
            shape((size, groups, chunks, sub, width), BF),
            shape((size, groups, 1, width), BF),
            shape((total_rows, width), BF),
            shape((3, part, local // 3), F32),
            shape((part, 2, inner), F32),
            shape((part, inner), F32),
            shape((part, local // 3), F32),
            shape((part, 4), F32),
        ],
        scratch_shapes=[
            pltpu.VMEM(d_qkv_t.shape, BF),
            pltpu.VMEM(x_all.shape, BF),
            pltpu.VMEM(w_t.shape, BF),
            pltpu.VMEM(grad_one.shape, F32),
            pltpu.VMEM(wide_own.shape, BF),
            pltpu.VMEM(wide_own.shape, BF),
            pltpu.VMEM(down.shape, BF),
            pltpu.VMEM(down.shape[2:], BF),
            pltpu.VMEM(down.shape[2:], BF),
            pltpu.VMEM((groups, size * share // 16 + 1, 16, width), BF),
            pltpu.VMEM((total_rows, width), BF),
            pair_buffer,
            pair_buffer,
            buffer,
            buffer,
            pltpu.VMEM((chunks, groups, sub, width), BF),
            pltpu.VMEM((groups, 1, width), BF),
            pltpu.VMEM((groups, part, local), BF),
            pltpu.VMEM((local, width), F32),
            *halving(WIDE_PARTS[0], 3),
            *halving(WIDE_PARTS[1], 3),
            *halving(local, 3),
            dma((15,)),
            dma((5,)),
            dma((5,)),
            dma((3, 7)),
            dma((3, 7)),
            dma((4, groups, chunks)),
            dma((4, groups, chunks)),
            dma((4, groups)),
            dma((4, groups)),
            dma((3, chunks)),
            dma((3, chunks)),
            dma((chunks + 1 + total_rows // ROWS,)),
        ],
        compiler_params=pltpu.CompilerParams(
            collective_id=1, has_side_effects=True, vmem_limit_bytes=VMEM_LIMIT
        ),
        cost_estimate=pl.CostEstimate(
            flops=4 * size * rows * local * width, bytes_accessed=150 << 20, transcendentals=0
        ),
        name="settle",
    )(
        match,
        spots,
        res_over,
        d_qkv_t,
        x_all,
        w_t,
        grad_one,
        wide_own,
        wide_other,
        down,
        res,
    )


def local(tokens, cotangent, lengths, dealing, w_qkv, w_out, w_gu, w_down, gains, shifts):
    groups = lax.axis_size("dp")
    size = lax.axis_size("tensor")
    me = lax.axis_index("tensor")
    rows = tokens.shape[0]
    width = tokens.shape[2]
    slots = rows // groups
    share = slots // size
    own_rows = rows // size
    subs = own_rows // BLOCK
    sub = share // subs
    fused = groups == 8 and sub % 16 == 0
    i32 = jnp.int32

    ids = jnp.stack([lax.axis_index("dp"), me]).astype(i32)
    send_x, over_x, send_c, meta, table, match, spots = pack(
        lengths,
        dealing,
        ids,
        tokens.reshape(rows, width),
        cotangent.reshape(rows, width),
        groups,
        size,
    )

    def over_dp(array):
        return lax.all_to_all(array, "dp", split_axis=0, concat_axis=0, tiled=True)

    half = w_down.shape[0] // 2
    down_half = lax.dynamic_slice_in_dim(w_down, ids[0] % 2 * half, half, 0)
    far_out, far_down = swap(w_out.T, size, 2), swap(down_half, size, 2)
    match_square = match.reshape(groups, groups)

    def fill(received, over, last):
        spare = jnp.dot(match_square.astype(BF), over, preferred_element_type=F32).astype(BF)
        hole = (jnp.sum(match_square, 1) > 0)[:, None] & (jnp.arange(share) == share - 1)[None, :]
        fix = last[:, None, None] & hole[None]
        body = jnp.where(fix[..., None], spare[None, :, None, :], received)
        body = body.reshape(-1, groups, subs, sub, width).transpose(0, 2, 1, 3, 4)
        return body.reshape(-1, own_rows, width)

    if fused:
        x_rel, over_x = route(send_x, over_x, size)
        send_c, x_rel, far_out, far_down = lax.optimization_barrier(
            (send_c, x_rel, far_out, far_down)
        )
    else:
        x_rel = jnp.stack(gather_members(over_dp(send_x)))
        relative = jnp.bitwise_xor(jnp.arange(size, dtype=i32), me)
        x_rel = fill(x_rel, over_dp(over_x)[:, 0], relative == size - 1)
    local_width = w_qkv.shape[2]
    w_qkv_t = w_qkv.transpose(1, 2, 0).reshape(3 * local_width, width)
    x_rel, near_gu = lax.optimization_barrier((x_rel, w_gu.reshape(width, -1)))
    far_gu = swap(near_gu, size, 2)
    other_down = lax.ppermute(far_down, "dp", [(i, i ^ 1) for i in range(groups)])
    cot = over_dp(send_c)
    if not fused:
        cot = fill(cot[None, :, :share], cot[:, share], (me == size - 1)[None])[0]
    frequency = np.float32(1000.0) ** (-(np.arange(HALF, dtype=np.float32) * 2) / HEAD)
    frequency = jnp.asarray(frequency.astype(np.float32))
    q, k, v, k_rows, v_rows, cosine, sine, x_all, x_own = project(
        meta, match, x_rel, over_x, w_qkv_t, frequency[:, None], groups, fused
    )
    o_blocks, lse = attend(meta, q, k_rows, v, groups)
    o_blocks, far_gu, other_down, cot = lax.optimization_barrier(
        (o_blocks, far_gu, other_down, cot)
    )

    norms = jnp.concatenate([gains.T, shifts.T], 0)
    (
        result_own,
        grad_one,
        d_heads,
        heads_own,
        normed_t,
        d_branch_t,
        d_attn_t,
        hidden,
        d_gu,
        norm_grads,
    ) = middle(
        x_own,
        match,
        cot,
        norms,
        o_blocks,
        size,
        w_out.T,
        far_out,
        near_gu,
        far_gu,
        w_down,
        far_down,
        other_down,
    )
    grad_args = (normed_t, d_branch_t, d_attn_t, hidden, d_gu, heads_own, norm_grads)
    if fused:
        wide_own, wide_other, down, do_rel, home_result, over_result = grads(
            match, groups, *grad_args, d_heads, result_own
        )
        wide_other = swap(wide_other, size, 2)
        down = over_dp(down)
    else:
        sent_grads = weight_grads(1, *grad_args)
        kept_grads = weight_grads(0, *grad_args)
        pair = (kept_grads.astype(F32) + swap(sent_grads, size, 1).astype(F32)).astype(BF)
        do_rel = jnp.stack(exchange_members([d_heads[r] for r in range(size)]))

    d_qkv_t = attend_back(
        meta, q, k_rows, k, v_rows, o_blocks, do_rel, lse, cosine, sine, groups
    )
    def send_back(own):
        body = own.reshape(subs, groups, sub, width).transpose(1, 0, 2, 3)
        body = body.reshape(groups, share, width)
        spare = lax.dot_general(
            match_square.astype(BF),
            body[:, share - 1],
            (((0,), (0,)), ((), ())),
            preferred_element_type=F32,
        ).astype(BF)
        pair = (over_dp(body), over_dp(spare.reshape(groups, 1, width)))
        return tuple(jnp.stack(gather_members(a)) for a in pair)

    if fused:
        home_input, home_over, result, qkv_sum, gu_sum, down_sum, out_sum, norm_sum = settle(
            match,
            spots,
            over_result,
            d_qkv_t,
            x_all,
            w_qkv_t,
            grad_one,
            wide_own,
            wide_other,
            down,
            w_down.shape[1],
            home_result,
        )
        home_input = home_input.reshape(size, groups, share, width)
    else:
        back_rel, grad_qkv = project_back(meta, d_qkv_t, x_all, w_qkv_t)
        grad_qkv = grad_qkv.reshape(groups, width // groups, 3 * local_width)
        home_result = send_back(result_own)
        input_own = grad_one + reduce_members([back_rel[r] for r in range(size)])
        home_input = send_back(input_own.astype(BF))
        grad_qkv = lax.all_to_all(grad_qkv, "dp", split_axis=0, concat_axis=0, tiled=True)
        qkv_sum = jnp.sum(grad_qkv.astype(F32), 0)
        pair = lax.psum_scatter(pair, "dp", scatter_dimension=1, tiled=True)
        summed = pair[0].astype(F32) + swap(pair[1], size, 2).astype(F32)
    if fused:
        qkv_sum = qkv_sum.transpose(1, 0, 2)
    else:
        qkv_sum = qkv_sum.reshape(-1, 3, local_width)
        inner = w_down.shape[1]
        gu_sum = summed[:, : 2 * inner].reshape(-1, 2, inner)
        out_sum = summed[:, 2 * inner : 2 * inner + local_width]
        norm_sum = summed[:, 2 * inner + local_width : 2 * inner + local_width + 4]
        down_sum = summed[:, -inner:]
    norm_sum = lax.dynamic_slice_in_dim(
        norm_sum, me * (norm_sum.shape[0] // size), norm_sum.shape[0] // size, 0
    )
    if fused:
        input_grad, result = unpack(spots, me[None], home_input, home_over, result)
    else:
        row_ids = jnp.arange(rows, dtype=i32)[None, :]
        low, count, group, first = (table[i, 1:][:, None] for i in range(4))
        here = (row_ids >= low) & (row_ids < low + count)
        slot = row_ids + first - low
        home_part = jnp.minimum(slot // share, size - 1)
        flat = (jnp.bitwise_xor(home_part, me) * groups + group) * (share + 1)
        flat = jnp.sum(jnp.where(here, flat + slot - home_part * share, 0), 0)

        def arrange(home, over):
            every = jnp.concatenate([home, over], 2).reshape(-1, width)
            return jnp.take(every, flat, axis=0)

        result = arrange(*home_result)
        input_grad = arrange(*home_input)
    result = result.reshape(rows, 1, width)
    input_grad = input_grad.reshape(rows, 1, width)
    return (
        result,
        input_grad,
        qkv_sum,
        out_sum,
        gu_sum,
        down_sum,
        norm_sum[:, :2],
        norm_sum[:, 2:],
    )


def solution(mesh):
    placed = (
        P(None, "dp", None),
        P(None, "dp", None),
        P(),
        P(),
        P(None, None, "tensor"),
        P(None, "tensor"),
        P(None, None, "tensor"),
        P(None, "tensor"),
        P(),
        P(),
    )
    return jax.shard_map(
        local,
        mesh=mesh,
        in_specs=placed,
        out_specs=(
            P(None, "dp", None),
            P(None, "dp", None),
            P("dp", None, "tensor"),
            P("dp", "tensor"),
            P("dp", None, "tensor"),
            P("dp", "tensor"),
            P(("dp", "tensor"), None),
            P(("dp", "tensor"), None),
        ),
        check_vma=False,
    )
```

```python
import functools

import jax
import jax.numpy as jnp
import numpy as np
from jax import lax
from jax.experimental import pallas as pl
from jax.experimental.pallas import tpu as pltpu
from jax.sharding import PartitionSpec as P

HEAD = 64
HALF = HEAD // 2
BLOCK = 256
QUERIES = 512
PADDED = HEAD + 16
KEYS = 512
LOG_2 = 0.6931471805599453
EPSILON = 1e-05
NEGATIVE = -1000000000.0
START = -1e30
BF = jnp.bfloat16
F32 = jnp.float32
VMEM_LIMIT = 56 * 1024 * 1024


def mm(a, b, ca, cb):
    return lax.dot_general(a, b, (((ca,), (cb,)), ((), ())), preferred_element_type=F32)


HOLES = 8
ROWS = 128
WIDE = 1664
WIDE_PARTS = (896, 768)
TILE = 256


def div(value, size):
    if size & (size - 1) == 0:
        return lax.shift_right_arithmetic(value, jnp.int32(size.bit_length() - 1))
    return lax.div(value, size)


def rem(value, size):
    if size & (size - 1) == 0:
        return lax.bitwise_and(value, jnp.int32(size - 1))
    return lax.rem(value, size)


def extra_of(source, offset, length, groups):
    turned = rem(source - offset + groups, groups)
    return turned, jnp.where(turned < rem(length, groups), 1, 0)


def pack_kernel(
    groups,
    size,
    lengths,
    dealing,
    ids,
    x_ref,
    c_ref,
    send_x_ref,
    over_x_ref,
    send_c_ref,
    meta_ref,
    table_ref,
    match_ref,
    spots_ref,
    places,
):
    d = ids[0]
    t = ids[1]
    rows = x_ref.shape[0]
    slots = rows // groups
    share = slots // size
    window = (share + 31) // 16 * 16

    count = lengths.shape[0]

    def place_of(j, offset):
        places[0, j] = offset
        return offset + lengths[j]

    lax.fori_loop(0, count, place_of, jnp.int32(0), unroll=True)

    def lookup(q):
        seq = dealing[q]
        return seq, places[0, seq], lengths[seq]

    def span(offset, length):
        low = div(offset - d + groups - 1, groups)
        return low, div(offset + length - d + groups - 1, groups) - low

    def window_at(row):
        start = jnp.clip(jnp.bitwise_and(row, -16), 0, rows - window)
        return pl.ds(pl.multiple_of(start, 16), window), row - start

    def one_hot(steps, shift, wanted):
        return jnp.where((steps == shift) & wanted, 1.0, 0.0).astype(BF)

    def steps_of(count):
        shape = (count, window)
        return lax.broadcasted_iota(jnp.int32, shape, 1) - lax.broadcasted_iota(jnp.int32, shape, 0)

    steps = steps_of(share)
    spare_steps = steps_of(16)
    top = lax.broadcasted_iota(jnp.int32, (16, 1), 0) == 0
    table_ref[0, 0] = t
    slot_ids = lax.broadcasted_iota(jnp.int32, (share, 1), 0) + t * share

    @pl.loop(0, groups, unroll=4)
    def _(g):
        seq_a, off_a, len_a = lookup(2 * g)
        seq_b, off_b, len_b = lookup(2 * g + 1)
        low_a, count_a = span(off_a, len_a)
        low_b, count_b = span(off_b, len_b)
        for seq, entries in ((seq_a, (low_a, count_a, g, 0)), (seq_b, (low_b, count_b, g, count_a))):
            for i, entry in enumerate(entries):
                table_ref[i, 1 + seq] = jnp.int32(entry)
        shifted = low_b - count_a
        at_a, shift_a = window_at(low_a + t * share)
        at_b, shift_b = window_at(shifted + t * share)
        at_over, shift_over = window_at(shifted + slots)
        hot_a = one_hot(steps, shift_a, slot_ids < count_a)
        hot_b = one_hot(steps, shift_b, slot_ids >= count_a)
        hot_over = one_hot(spare_steps, shift_over, top)
        for ref, out_ref in ((x_ref, send_x_ref), (c_ref, send_c_ref)):
            picked = mm(hot_a, ref[at_a, :], 1, 0) + mm(hot_b, ref[at_b, :], 1, 0)
            out_ref[g, :share] = picked.astype(BF)
        over_x_ref[g] = mm(hot_over, x_ref[at_over, :], 1, 0)[:1].astype(BF)
        send_c_ref[g, share:] = mm(hot_over, c_ref[at_over, :], 1, 0).astype(BF)

    def spot(i, here):
        row = i * ROWS
        following = jnp.minimum(here + 1, count - 1)
        here = jnp.where(table_ref[0, 1 + following] <= row, following, here)
        after = jnp.minimum(here + 1, count - 1)
        for k, j in enumerate((here, after)):
            slot = row + table_ref[3, 1 + j] - table_ref[0, 1 + j]
            start = jnp.clip(jnp.bitwise_and(slot, -16), 0, slots - ROWS)
            spots_ref[8 * i + 3 * k] = table_ref[2, 1 + j]
            spots_ref[8 * i + 3 * k + 1] = div(start, 16)
            spots_ref[8 * i + 3 * k + 2] = slot - start
        spots_ref[8 * i + 6] = jnp.where(after > here, table_ref[0, 1 + after] - row, ROWS)
        spots_ref[8 * i + 7] = jnp.int32(0)
        return here

    lax.fori_loop(0, rows // ROWS, spot, jnp.int32(0), unroll=4)

    _, off_a, len_a = lookup(2 * d)
    _, off_b, len_b = lookup(2 * d + 1)
    off_a = rem(off_a, groups)
    off_b = rem(off_b, groups)
    meta_ref[0] = div(len_a, BLOCK)
    meta_ref[1] = div(len_a + BLOCK - 1, BLOCK)
    meta_ref[2] = t
    meta_ref[3] = off_a
    meta_ref[4] = off_b
    meta_ref[5] = len_a
    meta_ref[6] = jnp.int32(0)
    meta_ref[7] = jnp.int32(0)

    def counts(source):
        first = div(len_a, groups) + extra_of(source, off_a, len_a, groups)[1]
        second = div(len_b, groups) + extra_of(source, off_b, len_b, groups)[1]
        return first, first + second

    def clear(i, carry):
        match_ref[i] = jnp.float32(0.0)
        return carry

    lax.fori_loop(0, groups * groups, clear, 0, unroll=8)

    def sort_out(source, carry):
        holes, overs = carry
        total = counts(source)[1]
        places[1, holes] = source
        places[2, overs] = source
        meta_ref[HOLES + source] = jnp.int32(-1)
        return holes + jnp.where(total < slots, 1, 0), overs + jnp.where(total > slots, 1, 0)

    holes, _ = lax.fori_loop(0, groups, sort_out, (jnp.int32(0), jnp.int32(0)), unroll=8)

    @pl.loop(0, holes)
    def _(i):
        hole = places[1, i]
        source = places[2, i]
        match_ref[hole * groups + source] = jnp.float32(1.0)
        position = (slots - counts(source)[0]) * groups + extra_of(source, off_b, len_b, groups)[0]
        meta_ref[HOLES + hole] = position


def pack(lengths, dealing, ids, x, cotangent, groups, size):
    rows, width = x.shape
    share = rows // groups // size
    whole = lambda *shape: pl.BlockSpec(shape, lambda i, *refs: (0,) * len(shape))
    smem = pl.BlockSpec(memory_space=pltpu.SMEM)
    shapes = [(groups, share, width), (groups, 1, width), (groups, share + 16, width)]
    return pl.pallas_call(
        functools.partial(pack_kernel, groups, size),
        grid_spec=pltpu.PrefetchScalarGridSpec(
            num_scalar_prefetch=3,
            grid=(1,),
            in_specs=[whole(rows, width)] * 2,
            out_specs=[whole(*shape) for shape in shapes] + [smem] * 4,
            scratch_shapes=[pltpu.SMEM((3, max(lengths.shape[0], groups + 1)), jnp.int32)],
        ),
        out_shape=[jax.ShapeDtypeStruct(shape, BF) for shape in shapes]
        + [
            jax.ShapeDtypeStruct((HOLES + groups,), jnp.int32),
            jax.ShapeDtypeStruct((4, 1 + lengths.shape[0]), jnp.int32),
            jax.ShapeDtypeStruct((groups * groups,), F32),
            jax.ShapeDtypeStruct((rows // ROWS * 8,), jnp.int32),
        ],
        compiler_params=pltpu.CompilerParams(vmem_limit_bytes=VMEM_LIMIT),
        cost_estimate=pl.CostEstimate(flops=0, bytes_accessed=20 << 20, transcendentals=0),
        name="pack",
    )(lengths, dealing, ids, x, cotangent)


def place(row, groups):
    sub = BLOCK // groups
    inside = rem(row, BLOCK)
    return div(inside, sub), div(row, BLOCK) * sub + rem(inside, sub)


def count_first(meta, source, groups):
    turned, extra = extra_of(source, meta[3], meta[5], groups)
    return turned, div(meta[5], groups) + extra


def in_second(meta, row, groups):
    source, slot = place(row, groups)
    return jnp.where(slot < count_first(meta, source, groups)[1], 0, 1)


def positions_of(meta, row, groups, slots):
    source, slot = place(row, groups)
    turned, count = count_first(meta, source, groups)
    turned_b = rem(source - meta[4] + groups, groups)
    position = jnp.where(slot < count, slot * groups + turned, (slot - count) * groups + turned_b)
    for g in range(groups):
        fills = meta[HOLES + g]
        here = (slot == slots - 1) & (source == g) & (fills >= 0)
        position = jnp.where(here, fills, position)
    return position


def spare_row(match_ref, groups, hole, rows):
    total = rows[0] * match_ref[hole * groups]
    flag = match_ref[hole * groups]
    for source in range(1, groups):
        weight = match_ref[hole * groups + source]
        total = total + rows[source] * weight
        flag = flag + weight
    return total, flag


def project_kernel(
    groups,
    packed,
    meta,
    match_ref,
    x_in_ref,
    over_ref,
    w_ref,
    freq_ref,
    q_ref,
    k_ref,
    v_ref,
    krow_ref,
    vrow_ref,
    cos_ref,
    sin_ref,
    x_ref,
    own_ref,
):
    index = pl.program_id(0)
    parts = pl.num_programs(0)
    share, width = x_ref.shape[1:]
    heads = q_ref.shape[0] // HEAD
    local = heads * HEAD
    sub = BLOCK // groups
    if packed:
        for i in range(share // BLOCK):
            for g in range(groups):
                base = i * BLOCK + g * sub
                x_ref[0, base : base + sub, :] = x_in_ref[0, g, i * sub : (i + 1) * sub, :]

        @pl.when(index == parts - 1)
        def _():
            rows = [over_ref[g].astype(F32) for g in range(groups)]
            at_end = lax.broadcasted_iota(jnp.int32, (16, 1), 0) == 15
            for g in range(groups):
                end = share - BLOCK + (g + 1) * sub
                spare, _ = spare_row(match_ref, groups, g, rows)
                old = x_ref[0, end - 16 : end, :].astype(F32)
                new = jnp.where(at_end & (meta[HOLES + g] >= 0), spare, old)
                x_ref[0, end - 16 : end, :] = new.astype(BF)
    else:
        x_ref[...] = x_in_ref[...]

    @pl.when(index == meta[2])
    def _():
        own_ref[...] = x_ref[0]

    row = lax.broadcasted_iota(jnp.int32, (1, share), 1) + index * share
    position = positions_of(meta, row, groups, parts * share // groups)
    angles = freq_ref[...] * position.astype(F32)
    cosine = jnp.cos(angles)
    sine = jnp.sin(angles)
    cos_ref[...] = cosine
    sin_ref[...] = sine
    projected = mm(w_ref[...], x_ref[0], 1, 1)
    for part, out_ref, scale in ((0, q_ref, HEAD ** (-0.5) / LOG_2), (1, k_ref, 1.0)):
        for head in range(heads):
            base = part * local + head * HEAD
            first = projected[base : base + HALF]
            second = projected[base + HALF : base + HEAD]
            turned = jnp.concatenate(
                [first * cosine - second * sine, second * cosine + first * sine], 0
            )
            out_ref[head * HEAD : (head + 1) * HEAD, :] = (turned * scale).astype(BF)
            if part == 1:
                krow_ref[head] = turned.T.astype(BF)
    for head in range(heads):
        base = 2 * local + head * HEAD
        value = projected[base : base + HEAD]
        rest = lax.broadcasted_iota(jnp.int32, (PADDED - HEAD, share), 0) == 0
        v_ref[head * PADDED : (head + 1) * PADDED, :] = jnp.concatenate(
            [value, jnp.where(rest, 1.0, 0.0)], 0
        ).astype(BF)
        vrow_ref[head] = value.T.astype(BF)


def project(meta, match, x_rel, over, w_t, freq, groups, packed):
    parts = x_rel.shape[0]
    width = x_rel.shape[-1]
    share = x_rel.size // parts // width
    rows = parts * share
    local = w_t.shape[0] // 3
    heads = local // HEAD
    shape = jax.ShapeDtypeStruct
    columns = lambda *lead: pl.BlockSpec(lead + (share,), lambda i, meta: (0,) * len(lead) + (i,))
    tall_spec = pl.BlockSpec((heads, share, HEAD), lambda i, meta: (0, i, 0))
    whole = lambda *shape: pl.BlockSpec(shape, lambda i, meta: (0,) * len(shape))
    lead = x_rel.shape[1:]
    return pl.pallas_call(
        functools.partial(project_kernel, groups, packed),
        grid_spec=pltpu.PrefetchScalarGridSpec(
            num_scalar_prefetch=1,
            grid=(parts,),
            in_specs=[
                pl.BlockSpec(memory_space=pltpu.SMEM),
                pl.BlockSpec(
                    (1,) + lead, lambda i, meta: (jnp.bitwise_xor(i, meta[2]),) + (0,) * len(lead)
                ),
                whole(*over.shape),
                whole(3 * local, width),
                whole(HALF, 1),
            ],
            out_specs=[
                columns(local),
                columns(local),
                columns(heads * PADDED),
                tall_spec,
                tall_spec,
                columns(HALF),
                columns(HALF),
                pl.BlockSpec((1, share, width), lambda i, meta: (i, 0, 0)),
                whole(share, width),
            ],
        ),
        out_shape=[
            shape((local, rows), BF),
            shape((local, rows), BF),
            shape((heads * PADDED, rows), BF),
            shape((heads, rows, HEAD), BF),
            shape((heads, rows, HEAD), BF),
            shape((HALF, rows), F32),
            shape((HALF, rows), F32),
            shape((parts, share, width), BF),
            shape((share, width), BF),
        ],
        compiler_params=pltpu.CompilerParams(vmem_limit_bytes=VMEM_LIMIT),
        cost_estimate=pl.CostEstimate(
            flops=rows * width, bytes_accessed=1 << 20, transcendentals=0
        ),
        name="project",
    )(meta, match, x_rel, over, w_t, freq)


def visible(info, index, q_blocks, k_blocks, count):
    is_a = (index + 1) * q_blocks <= info[0]
    is_b = index * q_blocks >= info[1]
    pure = is_a | is_b
    end_a = info[0] // k_blocks
    start_b = (info[1] + k_blocks - 1) // k_blocks
    plain_low = jnp.where(is_b, start_b, 0)
    plain_high = jnp.where(is_b, count, jnp.where(is_a, end_a, 0))
    return plain_low, plain_high, jnp.where(pure, end_a, 0), jnp.where(pure, start_b, count)


def attend_kernel(groups, info, q_ref, k_ref, v_ref, o_ref, lse_ref, acc_ref):
    index = pl.program_id(0)
    heads, rows, _ = k_ref.shape
    width = q_ref.shape[1]
    tall = v_ref.shape[0] // heads
    spans_ = visible(info, index, width // BLOCK, KEYS // BLOCK, rows // KEYS)
    acc_ref[...] = jnp.zeros_like(acc_ref)
    query_ids = lax.broadcasted_iota(jnp.int32, (1, width), 1) + index * width
    key_ids = lax.broadcasted_iota(jnp.int32, (KEYS, 1), 0)
    ids = range(heads)

    def step(masked, j, tops):
        keys = pl.ds(pl.multiple_of(j * KEYS, KEYS), KEYS)
        scores = [mm(k_ref[h, keys, :], q_ref[h * HEAD : (h + 1) * HEAD, :], 1, 0) for h in ids]
        if masked:
            same = in_second(info, key_ids + j * KEYS, groups) == in_second(info, query_ids, groups)
            scores = [jnp.where(same, s, NEGATIVE) for s in scores]
        new = [jnp.maximum(tops[h], jnp.max(scores[h], 0, keepdims=True)) for h in ids]
        weights = [jnp.exp2(scores[h] - new[h]).astype(BF) for h in ids]
        shrink = [jnp.exp2(tops[h] - new[h]) for h in ids]
        sums = [mm(v_ref[h * tall : (h + 1) * tall, keys], weights[h], 1, 0) for h in ids]
        for h in ids:
            part = slice(h * tall, (h + 1) * tall)
            acc_ref[part, :] = acc_ref[part, :] * shrink[h] + sums[h]
        return tuple(new)

    tops = (jnp.full((1, width), START, F32),) * heads
    tops = lax.fori_loop(spans_[0], spans_[1], functools.partial(step, False), tops)
    tops = lax.fori_loop(spans_[2], spans_[3], functools.partial(step, True), tops)
    for h in ids:
        total = acc_ref[h * tall + HEAD : h * tall + HEAD + 1, :]
        out = (acc_ref[h * tall : h * tall + HEAD, :] / total).astype(BF)
        each = o_ref.shape[2]
        for i in range(width // each):
            o_ref[i, h * HEAD : (h + 1) * HEAD, :] = out[:, i * each : (i + 1) * each]
        lse_ref[h : h + 1, :] = tops[h] + jnp.log2(total)


def attend(info, q, k_rows, v, groups):
    local, rows = q.shape
    heads = local // HEAD
    return pl.pallas_call(
        functools.partial(attend_kernel, groups),
        grid_spec=pltpu.PrefetchScalarGridSpec(
            num_scalar_prefetch=1,
            grid=(rows // QUERIES,),
            in_specs=[
                pl.BlockSpec((local, QUERIES), lambda i, info: (0, i)),
                pl.BlockSpec((heads, rows, HEAD), lambda i, info: (0, 0, 0)),
                pl.BlockSpec(v.shape, lambda i, info: (0, 0)),
            ],
            out_specs=[
                pl.BlockSpec((QUERIES // BLOCK, local, BLOCK), lambda i, info: (i, 0, 0)),
                pl.BlockSpec((heads, QUERIES), lambda i, info: (0, i)),
            ],
            scratch_shapes=[pltpu.VMEM((v.shape[0], QUERIES), F32)],
        ),
        out_shape=[
            jax.ShapeDtypeStruct((rows // BLOCK, local, BLOCK), BF),
            jax.ShapeDtypeStruct((heads, rows), F32),
        ],
        compiler_params=pltpu.CompilerParams(vmem_limit_bytes=VMEM_LIMIT),
        cost_estimate=pl.CostEstimate(
            flops=2 * rows * rows * HEAD * heads,
            bytes_accessed=8 << 20,
            transcendentals=0,
        ),
        name="attend",
    )(info, q, k_rows, v)


def unturn(grad, cosine, sine):
    first = grad[:HALF]
    second = grad[HALF:]
    return jnp.concatenate(
        [first * cosine + second * sine, second * cosine - first * sine], 0
    ).astype(BF)


def attend_back_kernel(groups, info, q_ref, krow_ref, k_ref, vrow_ref, o_ref, *refs):
    count = QUERIES // BLOCK
    do_refs = refs[:count]
    lse_ref, cos_ref, sin_ref, out_ref, up_ref, dq_ref, dk_ref, dv_ref = refs[count:]
    index = pl.program_id(0)
    heads, rows, _ = krow_ref.shape
    width = heads * HEAD
    parts, _, share = out_ref.shape
    each = share // BLOCK
    ids = range(heads)
    part = [slice(h * HEAD, (h + 1) * HEAD) for h in ids]

    @pl.when(index == 0)
    def _():
        dk_ref[...] = jnp.zeros_like(dk_ref)
        dv_ref[...] = jnp.zeros_like(dv_ref)

    dq_ref[...] = jnp.zeros_like(dq_ref)
    query_ids = lax.broadcasted_iota(jnp.int32, (1, QUERIES), 1) + index * QUERIES
    key_ids = lax.broadcasted_iota(jnp.int32, (KEYS, 1), 0)
    deltas = []
    for i, ref in enumerate(do_refs):
        columns = slice(i * BLOCK, (i + 1) * BLOCK)
        up_ref[:, columns] = ref[0]
        terms = ref[0].astype(F32) * o_ref[i].astype(F32)
        deltas.append([jnp.sum(terms[p], 0, keepdims=True) for p in part])
    delta = [jnp.concatenate([halves[h] for halves in deltas], 1) for h in ids]
    spans_ = visible(info, index, QUERIES // BLOCK, KEYS // BLOCK, rows // KEYS)

    def step(masked, j, carry):
        keys = pl.ds(pl.multiple_of(j * KEYS, KEYS), KEYS)
        if masked:
            same = in_second(info, key_ids + j * KEYS, groups) == in_second(info, query_ids, groups)
        for h in ids:
            queries = q_ref[part[h], :]
            upstream = up_ref[part[h], :]
            scores = mm(krow_ref[h, keys, :], queries, 1, 0)
            grad_soft = mm(vrow_ref[h, keys, :], upstream, 1, 0)
            if masked:
                scores = jnp.where(same, scores, NEGATIVE)
            soft = jnp.exp2(scores - lse_ref[h : h + 1, :])
            grad_scores = (soft * (grad_soft - delta[h])).astype(BF)
            dv_ref[part[h], keys] += mm(upstream, soft.astype(BF), 1, 1)
            dk_ref[part[h], keys] += mm(queries, grad_scores, 1, 1)
            dq_ref[part[h], :] += mm(k_ref[part[h], keys], grad_scores, 1, 0)
        return carry

    lax.fori_loop(spans_[0], spans_[1], functools.partial(step, False), 0)
    lax.fori_loop(spans_[2], spans_[3], functools.partial(step, True), 0)

    for i in range(QUERIES // BLOCK):
        block = index * (QUERIES // BLOCK) + i
        columns = pl.ds(pl.multiple_of(block * BLOCK, BLOCK), BLOCK)
        inside = pl.ds(pl.multiple_of(lax.rem(block, each) * BLOCK, BLOCK), BLOCK)
        for h in ids:
            out_ref[lax.div(block, each), part[h], inside] = unturn(
                dq_ref[part[h], i * BLOCK : (i + 1) * BLOCK] * HEAD ** (-0.5),
                cos_ref[:, columns],
                sin_ref[:, columns],
            )

    @pl.when(index == pl.num_programs(0) - 1)
    def _():
        @pl.loop(0, parts)
        def _(j):
            columns = pl.ds(pl.multiple_of(j * share, share), share)
            for h in ids:
                base = width + h * HEAD
                out_ref[j, base : base + HEAD, :] = unturn(
                    dk_ref[part[h], columns] * LOG_2, cos_ref[:, columns], sin_ref[:, columns]
                )
                base = 2 * width + h * HEAD
                out_ref[j, base : base + HEAD, :] = dv_ref[part[h], columns].astype(BF)


def attend_back(info, q, k_rows, k, v_rows, o, do, lse, cosine, sine, groups):
    parts = do.shape[0]
    local, rows = q.shape
    heads = local // HEAD
    blocks = rows // BLOCK
    each = blocks // parts
    whole = lambda *shape: pl.BlockSpec(shape, lambda i, info: (0,) * len(shape))
    count = QUERIES // BLOCK

    def upstream_spec(k):
        def pick(i, info):
            block = i * count + k
            return jnp.bitwise_xor(block // each, info[2]), 0, block % each

        return pl.BlockSpec((1, local, BLOCK), pick)

    return pl.pallas_call(
        functools.partial(attend_back_kernel, groups),
        grid_spec=pltpu.PrefetchScalarGridSpec(
            num_scalar_prefetch=1,
            grid=(rows // QUERIES,),
            in_specs=[
                pl.BlockSpec((local, QUERIES), lambda i, info: (0, i)),
                whole(heads, rows, HEAD),
                whole(local, rows),
                whole(heads, rows, HEAD),
                pl.BlockSpec((count, local, BLOCK), lambda i, info: (i, 0, 0)),
                *[upstream_spec(k) for k in range(count)],
                pl.BlockSpec((heads, QUERIES), lambda i, info: (0, i)),
                whole(HALF, rows),
                whole(HALF, rows),
            ],
            out_specs=whole(parts, 3 * local, rows // parts),
            scratch_shapes=[
                pltpu.VMEM((local, QUERIES), BF),
                pltpu.VMEM((local, QUERIES), F32),
                pltpu.VMEM((local, rows), F32),
                pltpu.VMEM((local, rows), F32),
            ],
        ),
        out_shape=jax.ShapeDtypeStruct((parts, 3 * local, rows // parts), BF),
        compiler_params=pltpu.CompilerParams(vmem_limit_bytes=VMEM_LIMIT),
        cost_estimate=pl.CostEstimate(
            flops=2 * 5 * rows * rows * 256 * heads // 2,
            bytes_accessed=16 << 20,
            transcendentals=heads * rows * rows // 2,
        ),
        name="attend_back",
    )(info, q, k_rows, k, v_rows, o, *[do] * count, lse, cosine, sine)


def project_back_kernel(meta, d_ref, x_ref, w_ref, back_ref, grad_ref, acc_ref):
    index = pl.program_id(0)

    @pl.when(index == 0)
    def _():
        acc_ref[...] = jnp.zeros_like(acc_ref)

    d_t = d_ref[0]
    back_ref[0] = mm(d_t, w_ref[...], 0, 0).astype(BF)
    acc_ref[...] += mm(d_t, x_ref[0], 1, 0)

    @pl.when(index == pl.num_programs(0) - 1)
    def _():
        grad_ref[...] = acc_ref[...].T.astype(BF)


def project_back(meta, d_qkv_t, x_all, w_t):
    parts, local, share = d_qkv_t.shape
    width = w_t.shape[1]
    relative = lambda i, meta: (jnp.bitwise_xor(i, meta[2]), 0, 0)
    whole = lambda *shape: pl.BlockSpec(shape, lambda i, meta: (0,) * len(shape))
    return pl.pallas_call(
        project_back_kernel,
        grid_spec=pltpu.PrefetchScalarGridSpec(
            num_scalar_prefetch=1,
            grid=(parts,),
            in_specs=[
                pl.BlockSpec((1, local, share), lambda i, meta: (i, 0, 0)),
                pl.BlockSpec((1, share, width), lambda i, meta: (i, 0, 0)),
                whole(local, width),
            ],
            out_specs=[
                pl.BlockSpec((1, share, width), relative),
                whole(width, local),
            ],
            scratch_shapes=[pltpu.VMEM((local, width), F32)],
        ),
        out_shape=[
            jax.ShapeDtypeStruct((parts, share, width), BF),
            jax.ShapeDtypeStruct((width, local), BF),
        ],
        compiler_params=pltpu.CompilerParams(vmem_limit_bytes=VMEM_LIMIT),
        cost_estimate=pl.CostEstimate(
            flops=4 * parts * share * local * width, bytes_accessed=15 << 20, transcendentals=0
        ),
        name="project_back",
    )(meta, d_qkv_t, x_all, w_t)


MESH = pl.DeviceIdType.MESH


def greet(groups, steps, d, t):
    barrier = pltpu.get_barrier_semaphore()
    for k in range(1, groups):
        pl.semaphore_signal(
            barrier, inc=1, device_id=(lax.rem(d + k, groups), t), device_id_type=MESH
        )
    for step in steps:
        pl.semaphore_signal(
            barrier, inc=1, device_id=(d, jnp.bitwise_xor(t, step)), device_id_type=MESH
        )
    pl.semaphore_wait(barrier, groups - 1 + len(steps))


def remote(src, dst, send, recv, device):
    return pltpu.make_async_remote_copy(
        src_ref=src,
        dst_ref=dst,
        send_sem=send,
        recv_sem=recv,
        device_id=device,
        device_id_type=MESH,
    )


class Spread:
    def __init__(self, out, sems, groups, d, t):
        self.out, self.sems, self.groups, self.d, self.t = out, sems, groups, d, t

    def at(self, r, k, rest):
        return self.out.at[(r, lax.rem(self.d - k + self.groups, self.groups)) + rest]

    def arrival(self, source, k, rest, where):
        send, recv = self.sems
        to = lax.rem(self.d + k, self.groups)
        return remote(
            source, self.at(0, 0, rest), send.at[(0, k) + where], recv.at[(0, k) + where], (to, self.t)
        )

    def across(self, k, rest, where):
        send, recv = self.sems
        return remote(
            self.at(0, k, rest),
            self.at(2, k, rest),
            send.at[(2, k) + where],
            recv.at[(2, k) + where],
            (self.d, jnp.bitwise_xor(self.t, 2)),
        )

    def beside(self, r, k, rest, where):
        send, recv = self.sems
        return remote(
            self.at(r, k, rest),
            self.at(r + 1, k, rest),
            send.at[(r + 1, k) + where],
            recv.at[(r + 1, k) + where],
            (self.d, jnp.bitwise_xor(self.t, 1)),
        )


def norm_forward(resid_rows, gain_vec, shift_vec):
    row_mean = jnp.mean(resid_rows, -1, keepdims=True)
    centred = resid_rows - row_mean
    inverse = lax.rsqrt(jnp.mean(centred * centred, -1, keepdims=True) + EPSILON)
    unit_rows = centred * inverse
    return (unit_rows * gain_vec + shift_vec, unit_rows, inverse)


def norm_backward(upstream, unit_rows, inverse, gain_vec):
    scaled = upstream * gain_vec
    inner_term = (
        scaled
        - jnp.mean(scaled, -1, keepdims=True)
        - unit_rows * jnp.mean(scaled * unit_rows, -1, keepdims=True)
    )
    return (
        inner_term * inverse,
        jnp.sum(upstream * unit_rows, 0, keepdims=True),
        jnp.sum(upstream, 0, keepdims=True),
    )


def middle_kernel(size, groups, count, *refs):
    x_ref, match_ref, cot_ref, over_ref, norm_ref, blocks_ref = refs[:6]
    weights_hbm = refs[6 : 6 + count]
    (
        result_ref,
        grad_one_ref,
        d_heads_ref,
        heads_ref,
        normed_t_ref,
        d_branch_t_ref,
        d_attn_t_ref,
        hidden_ref,
        d_gu_ref,
        norm_grad_ref,
        w_out_ref,
        w_gu_ref,
        w_down_ref,
        slope_ref,
        swish_ref,
        normed_ref,
        sum_ref,
        arrived_ref,
        sems,
        sends,
        recvs,
        keep,
    ) = refs[6 + count :]
    index = pl.program_id(0)
    first = index == 0
    d = lax.axis_index("dp")
    t = lax.axis_index("tensor")
    subs, local, _ = arrived_ref.shape[1:]
    inner = w_down_ref.shape[2]
    ids = (0, 2, 1, 3)
    part = [slice(r * local, (r + 1) * local) for r in range(size)]
    core = (d, jnp.bitwise_xor(t, 1))
    targets = (lambda r: w_out_ref.at[part[r]], lambda r: w_gu_ref.at[r], lambda r: w_down_ref.at[r])

    def weight_copies(kind, r):
        target = targets[kind](r)
        pieces = [(weights_hbm[2 * kind + r // 2], target)]
        if kind == 2 and r >= 2:
            pieces = []
            for i in range(2):
                half = weights_hbm[5 + i]
                low = pl.multiple_of(lax.rem(d + i, 2) * half.shape[0], 16)
                pieces.append((half, target.at[pl.ds(low, half.shape[0])]))
        copies = []
        for i, (source, place) in enumerate(pieces):
            recv = sems.at[kind, r, i]
            if r == 1 or r == 3:
                copies.append(remote(source, place, sems.at[kind, r - 1 + size, i], recv, core))
            else:
                copies.append(pltpu.make_async_copy(source, place, recv))
        return copies

    def weight_start(kind, r):
        for copy in weight_copies(kind, r):
            copy.start()

    def weight_wait(kind, r):
        for copy in weight_copies(kind, r):
            if r % 2 == 0:
                copy.wait()
            else:
                copy.wait_recv()

    def heads_copy(r, i):
        other = jnp.bitwise_xor(t, r)
        return remote(
            blocks_ref.at[other * subs + i],
            arrived_ref.at[r, i],
            sends.at[r, i],
            recvs.at[r, i],
            (d, other),
        )

    own_copy = pltpu.make_async_copy(blocks_ref.at[pl.ds(t * subs, subs)], arrived_ref.at[0], keep)

    @pl.when(first)
    def _():
        own_copy.start()
        for r in (0, 2):
            weight_start(0, r)
        greet(1, (1, 2, 3), d, t)
        for r in (2, 3, 1):
            heads_copy(r, 0).start()
        for r in (1, 3):
            weight_start(0, r)
        for r in ids:
            for kind in (1, 2):
                weight_start(kind, r)
        own_copy.wait()
        for r in ids:
            weight_wait(0, r)

    @pl.when(first)
    def _():
        norm_grad_ref[...] = jnp.zeros_like(norm_grad_ref)

    for r in ids[1:]:
        heads_copy(r, index).wait_recv()
        heads_copy(r, index).wait_send()

    @pl.when(index < subs - 1)
    def _():
        for r in (2, 3, 1):
            heads_copy(r, index + 1).start()

    for r in ids:
        heads_ref[r] = arrived_ref[r, index]
    heads_out = jnp.concatenate([arrived_ref[r, index] for r in range(size)], 0)
    attn = mm(heads_out, w_out_ref[...], 0, 0)
    gain_one, gain_two, shift_one, shift_two = (norm_ref[i : i + 1, :] for i in range(4))
    normed_one, unit_one, inverse_one = norm_forward(
        x_ref[...].astype(F32) + attn, gain_one, shift_one
    )
    normed_ref[...] = normed_one.astype(BF)
    normed_t_ref[...] = normed_one.T.astype(BF)
    sum_ref[...] = normed_one

    @pl.loop(0, size)
    def _(i):
        r = lax.rem(i, 2) * 2 + lax.div(i, 2)
        for k in ids:

            @pl.when(first & (r == k))
            def _():
                weight_wait(1, k)
                weight_wait(2, k)

        both = mm(normed_ref[...], w_gu_ref[r], 1, 0)
        gate = both[:, :inner]
        up = both[:, inner:]
        sig = 0.5 + 0.5 * jnp.tanh(0.5 * gate)
        swish = gate * sig
        hidden = (swish * up).astype(BF)
        swish_ref[r] = swish
        slope_ref[r] = up * (sig + swish * (1.0 - sig))
        hidden_ref[r] = hidden
        sum_ref[...] += mm(hidden, w_down_ref[r], 1, 1)

    result, unit_two, inverse_two = norm_forward(sum_ref[...], gain_two, shift_two)
    result_ref[...] = result.astype(BF)
    if groups:
        sub = BLOCK // groups
        spares = [over_ref[g, 0:1, :].astype(F32) for g in range(groups)]
        in_last = jnp.where((index == subs - 1) & (t == size - 1), 1.0, 0.0)
        ends = lax.broadcasted_iota(jnp.int32, (sub, 1), 0) == sub - 1
        pieces = []
        for g in range(groups):
            piece = cot_ref[g].astype(F32)
            spare, flag = spare_row(match_ref, groups, g, spares)
            fix = jnp.where(ends, flag * in_last, 0.0)
            pieces.append(piece * (1.0 - fix) + spare * fix)
        cot = jnp.concatenate(pieces, 0)
    else:
        cot = cot_ref[...].astype(F32)
    grad_two, d_gain_two, d_shift_two = norm_backward(cot, unit_two, inverse_two, gain_two)
    normed_ref[...] = grad_two.astype(BF)
    d_branch_t_ref[...] = grad_two.T.astype(BF)
    sum_ref[...] = grad_two

    @pl.loop(0, size)
    def _(r):
        grad_hidden = mm(normed_ref[...], w_down_ref[r], 1, 0)
        d_gate = (grad_hidden * slope_ref[r]).astype(BF)
        d_up = (grad_hidden * swish_ref[r]).astype(BF)
        d_gu_ref[r, :, :inner] = d_gate
        d_gu_ref[r, :, inner:] = d_up
        sum_ref[...] += mm(jnp.concatenate([d_gate, d_up], 1), w_gu_ref[r], 1, 1)

    grad_one, d_gain_one, d_shift_one = norm_backward(
        sum_ref[...], unit_one, inverse_one, gain_one
    )
    grad_one_ref[...] = grad_one
    d_attn_t = grad_one.T.astype(BF)
    d_attn_t_ref[...] = d_attn_t
    d_heads = mm(w_out_ref[...], d_attn_t, 1, 0).astype(BF)
    for r in ids:
        d_heads_ref[r] = d_heads[part[r]]
    for i, grad in enumerate((d_gain_one, d_gain_two, d_shift_one, d_shift_two)):
        norm_grad_ref[i : i + 1, :] += grad

    @pl.when(index == subs - 1)
    def _():
        for kind in range(3):
            for r in (1, 3):
                for copy in weight_copies(kind, r):
                    copy.wait_send()


def middle(x_own, match, cot, norms, o_blocks, size, *weights):
    rows, width = x_own.shape
    local = o_blocks.shape[1]
    inner = weights[4].shape[1]
    block = pl.BlockSpec((BLOCK, width), lambda i: (i, 0))
    turned = pl.BlockSpec((width, BLOCK), lambda i: (0, i))
    anywhere = pl.BlockSpec(memory_space=pl.ANY)
    shape = jax.ShapeDtypeStruct
    groups = cot.shape[0] if cot.ndim == 3 else 0
    if groups:
        sub = BLOCK // groups
        last = cot.shape[1] // 16 - 1
        cot_specs = [
            pl.BlockSpec((groups, sub, width), lambda i: (0, i, 0)),
            pl.BlockSpec((groups, 16, width), lambda i: (0, last, 0)),
        ]
    else:
        cot_specs = [block, pl.BlockSpec((16, width), lambda i: (0, 0))]
    return pl.pallas_call(
        functools.partial(middle_kernel, size, groups, len(weights)),
        grid=(rows // BLOCK,),
        in_specs=[block, pl.BlockSpec(memory_space=pltpu.SMEM)]
        + cot_specs
        + [pl.BlockSpec(norms.shape, lambda i: (0, 0))]
        + [anywhere] * (1 + len(weights)),
        out_specs=[
            block,
            block,
            pl.BlockSpec((size, local, BLOCK), lambda i: (0, 0, i)),
            pl.BlockSpec((size, local, BLOCK), lambda i: (0, 0, i)),
            turned,
            turned,
            turned,
            pl.BlockSpec((size, BLOCK, inner), lambda i: (0, i, 0)),
            pl.BlockSpec((size, BLOCK, 2 * inner), lambda i: (0, i, 0)),
            pl.BlockSpec((8, width), lambda i: (0, 0)),
        ],
        out_shape=[
            shape((rows, width), BF),
            shape((rows, width), F32),
            shape((size, local, rows), BF),
            shape((size, local, rows), BF),
            shape((width, rows), BF),
            shape((width, rows), BF),
            shape((width, rows), BF),
            shape((size, rows, inner), BF),
            shape((size, rows, 2 * inner), BF),
            shape((8, width), F32),
        ],
        scratch_shapes=[
            pltpu.VMEM((size * local, width), BF),
            pltpu.VMEM((size, width, 2 * inner), BF),
            pltpu.VMEM((size, width, inner), BF),
            pltpu.VMEM((size, BLOCK, inner), F32),
            pltpu.VMEM((size, BLOCK, inner), F32),
            pltpu.VMEM((BLOCK, width), BF),
            pltpu.VMEM((BLOCK, width), F32),
            pltpu.VMEM((size, rows // BLOCK, local, BLOCK), BF),
            pltpu.SemaphoreType.DMA((3, 2 * size, 2)),
            pltpu.SemaphoreType.DMA((size, rows // BLOCK)),
            pltpu.SemaphoreType.DMA((size, rows // BLOCK)),
            pltpu.SemaphoreType.DMA,
        ],
        compiler_params=pltpu.CompilerParams(
            collective_id=2, has_side_effects=True, vmem_limit_bytes=VMEM_LIMIT
        ),
        cost_estimate=pl.CostEstimate(
            flops=2 * rows * width * (6 * size * inner + 2 * size * local),
            bytes_accessed=40 << 20,
            transcendentals=rows * size * inner,
        ),
        name="middle",
    )(x_own, match, cot, cot, norms, o_blocks, *weights)


def product_tiles(left_ref, right_ref, store):
    @pl.loop(0, right_ref.shape[2] // TILE)
    def _(i):
        columns = pl.ds(pl.multiple_of(i * TILE, TILE), TILE)
        store(columns, mm(left_ref[...], right_ref[0, :, columns], 1, 0))


def weight_grads_tile(
    normed_t_ref, d_branch_t_ref, d_attn_t_ref, hidden_ref, d_gu_ref, heads_ref, norm_ref, store
):
    wide = d_gu_ref.shape[2]
    local = heads_ref.shape[1]
    product_tiles(normed_t_ref, d_gu_ref, store)
    d_out = mm(d_attn_t_ref[...], heads_ref[0], 1, 1)
    norm = norm_ref[...].T
    spare = -(local + norm.shape[1]) % 128
    tail = jnp.concatenate([d_out, norm, jnp.zeros((norm.shape[0], spare), F32)], 1)
    store(pl.ds(wide, tail.shape[1]), tail)
    base = wide + tail.shape[1]

    def shifted(columns, value):
        store(pl.ds(pl.multiple_of(base + columns.start, 128), columns.size), value)

    product_tiles(d_branch_t_ref, hidden_ref, shifted)


def weight_grads_kernel(*refs):
    out_ref = refs[-1]

    def store(columns, value):
        out_ref[0, :, columns] = value.astype(BF)

    weight_grads_tile(*refs[:-1], store)


def weight_grads(odd, normed_t, d_branch_t, d_attn_t, hidden, d_gu, heads, norm_grads):
    size, rows, inner = hidden.shape
    local = heads.shape[1]
    width = normed_t.shape[0]
    wide = 3 * inner + local + norm_grads.shape[0]
    wide = (wide + 127) // 128 * 128
    flat = pl.BlockSpec((width, rows), lambda i: (0, 0))
    pick = lambda i: (2 * i + odd, 0, 0)
    return pl.pallas_call(
        weight_grads_kernel,
        grid=(size // 2,),
        in_specs=[
            flat,
            flat,
            flat,
            pl.BlockSpec((1, rows, inner), pick),
            pl.BlockSpec((1, rows, 2 * inner), pick),
            pl.BlockSpec((1, local, rows), pick),
            pl.BlockSpec(norm_grads.shape, lambda i: (0, 0)),
        ],
        out_specs=pl.BlockSpec((1, width, wide), lambda i: (i, 0, 0)),
        out_shape=jax.ShapeDtypeStruct((size // 2, width, wide), BF),
        compiler_params=pltpu.CompilerParams(vmem_limit_bytes=VMEM_LIMIT),
        cost_estimate=pl.CostEstimate(
            flops=size * rows * width * (3 * inner + local), bytes_accessed=20 << 20, transcendentals=0
        ),
        name="weight_grads",
    )(normed_t, d_branch_t, d_attn_t, hidden, d_gu, heads, norm_grads)


def grads_kernel(groups, size, match_ref, *refs):
    tile_refs = refs[:7]
    (
        d_heads_ref,
        result_ref,
        wide_own_ref,
        wide_other_ref,
        down_ref,
        do_ref,
        home_ref,
        over_ref,
        sent_ref,
        got_ref,
        own_ref,
        spare_ref,
        s_grad,
        r_grad,
        s_heads,
        r_heads,
        sends,
        recvs,
        s_over,
        r_over,
        keep,
        outs,
    ) = refs[7:]
    step = pl.program_id(0)
    d = lax.axis_index("dp")
    t = lax.axis_index("tensor")
    chunks, _, sub, width = own_ref.shape
    core = (d, jnp.bitwise_xor(t, 1))
    body = Spread(home_ref, (sends, recvs), groups, d, t)
    extra = Spread(over_ref, (s_over, r_over), groups, d, t)

    def heads_copy(r):
        return remote(
            d_heads_ref.at[r],
            do_ref.at[r],
            s_heads.at[r],
            r_heads.at[r],
            (d, jnp.bitwise_xor(t, r)),
        )

    def grad_copy(i):
        return remote(sent_ref.at[i], got_ref.at[i], s_grad.at[i], r_grad.at[i], core)

    def own_copy(c):
        return pltpu.make_async_copy(own_ref.at[c, d], home_ref.at[0, d, c], keep.at[c])

    def arrival(c, k):
        return body.arrival(own_ref.at[c, lax.rem(d + k, groups)], k, (c,), (c,))

    def pass_on(c):
        own_copy(c).wait()
        for k in range(groups):
            if k > 0:
                arrival(c, k).wait_recv()
            body.across(k, (c,), (c,)).start()

    load = pltpu.make_async_copy(result_ref, own_ref, keep.at[chunks])
    own_heads = pltpu.make_async_copy(d_heads_ref.at[0], do_ref.at[0], keep.at[chunks + 1])
    own_over = pltpu.make_async_copy(spare_ref.at[d], over_ref.at[0, d], keep.at[chunks + 2])

    @pl.when(step == 0)
    def _():
        load.start()
        own_heads.start()
        greet(groups, (1, 2, 3), d, t)
        for r in (2, 3, 1):
            heads_copy(r).start()
        load.wait()
        for c in range(chunks):
            own_copy(c).start()
            for k in range(1, groups):
                arrival(c, k).start()
        last = [own_ref[chunks - 1, g, sub - 16 :, :].astype(F32)[15:16] for g in range(groups)]
        for to in range(groups):
            spare = last[0] * match_ref[to]
            for g in range(1, groups):
                spare = spare + last[g] * match_ref[g * groups + to]
            spare_ref[to] = spare.astype(BF)
        own_over.start()
        for k in range(1, groups):
            extra.arrival(spare_ref.at[lax.rem(d + k, groups)], k, (), ()).start()

    for c in range(chunks - 1):

        @pl.when(step == c + 2)
        def _():
            pass_on(c)

    @pl.when(step < 2)
    def _():
        def store(columns, value):
            sent_ref[step, :, columns] = value.astype(BF)

        weight_grads_tile(*tile_refs, store)
        grad_copy(step).start()

    @pl.when(step >= 2)
    def _():
        grad_copy(step - 2).wait_recv()
        grad_copy(step - 2).wait_send()

        def store(columns, value):
            sent_ref[step - 2, :, columns] = (
                value + got_ref[step - 2, :, columns].astype(F32)
            ).astype(BF)

        weight_grads_tile(*tile_refs, store)

    part = down_ref.shape[2]

    def leave(i):
        copies = [(sent_ref.at[i, :, pl.ds(0, WIDE)], (wide_own_ref, wide_other_ref)[i])]
        for g in range(groups):
            rest = sent_ref.at[i, pl.ds(g * part, part), pl.ds(WIDE, down_ref.shape[3])]
            copies.append((rest, down_ref.at[g, i]))
        return [
            pltpu.make_async_copy(source, target, outs.at[i, j])
            for j, (source, target) in enumerate(copies)
        ]

    for i in range(2):

        @pl.when(step == 2 + i)
        def _():
            for copy in leave(i):
                copy.start()

    @pl.when(step == size - 1)
    def _():
        for i in range(2):
            for copy in leave(i):
                copy.wait()
        own_over.wait()
        for k in range(groups):
            if k > 0:
                extra.arrival(spare_ref.at[0], k, (), ()).wait_recv()
            extra.across(k, (), ()).start()
            extra.beside(0, k, (), ()).start()
        for k in range(groups):
            extra.across(k, (), ()).wait_recv()
            extra.beside(2, k, (), ()).start()
        own_heads.wait()
        for r in range(1, size):
            heads_copy(r).wait_recv()
            heads_copy(r).wait_send()
        own_copy(chunks - 1).wait()
        for c in range(chunks):
            for k in range(groups):
                if k > 0 and c == chunks - 1:
                    arrival(c, k).wait_recv()
                if k > 0:
                    arrival(c, k).wait_send()
                if c < chunks - 1:
                    body.across(k, (c,), (c,)).wait_recv()
                    body.across(k, (c,), (c,)).wait_send()
        for k in range(groups):
            extra.beside(0, k, (), ()).wait_recv()
            extra.beside(2, k, (), ()).wait_recv()
            if k > 0:
                extra.arrival(spare_ref.at[0], k, (), ()).wait_send()
            extra.across(k, (), ()).wait_send()
            extra.beside(0, k, (), ()).wait_send()
            extra.beside(2, k, (), ()).wait_send()


def grads(
    match, groups, normed_t, d_branch_t, d_attn_t, hidden, d_gu, heads, norm_grads, d_heads, result
):
    size, rows, inner = hidden.shape
    local = heads.shape[1]
    width = normed_t.shape[0]
    chunks = rows // BLOCK
    sub = BLOCK // groups
    total = 3 * inner + (local + norm_grads.shape[0] + 127) // 128 * 128
    part = width // groups
    whole = lambda *shape: pl.BlockSpec(shape, lambda i: (0,) * len(shape))
    pick = lambda i: (jnp.where(i < 2, 2 * i + 1, 2 * i - 4), 0, 0)
    anywhere = pl.BlockSpec(memory_space=pl.ANY)
    dma = pltpu.SemaphoreType.DMA
    return pl.pallas_call(
        functools.partial(grads_kernel, groups, size),
        grid=(size,),
        in_specs=[
            pl.BlockSpec(memory_space=pltpu.SMEM),
            whole(width, rows),
            whole(width, rows),
            whole(width, rows),
            pl.BlockSpec((1, rows, inner), pick),
            pl.BlockSpec((1, rows, 2 * inner), pick),
            pl.BlockSpec((1, local, rows), pick),
            whole(*norm_grads.shape),
            anywhere,
            anywhere,
        ],
        out_specs=[
            anywhere,
            anywhere,
            anywhere,
            anywhere,
            anywhere,
            anywhere,
        ],
        out_shape=[
            jax.ShapeDtypeStruct((width, WIDE), BF),
            jax.ShapeDtypeStruct((width, WIDE), BF),
            jax.ShapeDtypeStruct((groups, 2, part, total - WIDE), BF),
            jax.ShapeDtypeStruct(d_heads.shape, BF),
            jax.ShapeDtypeStruct((3, groups, chunks, sub, width), BF),
            jax.ShapeDtypeStruct((size, groups, 1, width), BF),
        ],
        scratch_shapes=[
            pltpu.VMEM((2, width, total), BF),
            pltpu.VMEM((2, width, total), BF),
            pltpu.VMEM((chunks, groups, sub, width), BF),
            pltpu.VMEM((groups, 1, width), BF),
            dma((2,)),
            dma((2,)),
            dma((size,)),
            dma((size,)),
            dma((3, groups, chunks)),
            dma((3, groups, chunks)),
            dma((4, groups)),
            dma((4, groups)),
            dma((chunks + 3,)),
            dma((2, groups + 1)),
        ],
        compiler_params=pltpu.CompilerParams(
            collective_id=3, has_side_effects=True, vmem_limit_bytes=VMEM_LIMIT
        ),
        cost_estimate=pl.CostEstimate(
            flops=2 * size * rows * width * (3 * inner + local),
            bytes_accessed=80 << 20,
            transcendentals=0,
        ),
        name="grads",
    )(
        match,
        normed_t,
        d_branch_t,
        d_attn_t,
        hidden,
        d_gu,
        heads,
        norm_grads,
        d_heads,
        result.reshape(chunks, groups, sub, width),
    )


def swap(array, size, step):
    return lax.ppermute(array, "tensor", [(i, i ^ step) for i in range(size)])


def gather_members(own):
    size = lax.axis_size("tensor")
    across = swap(own, size, 2)
    return [own, swap(own, size, 1), across, swap(across, size, 1)]


def exchange_members(pieces):
    size = lax.axis_size("tensor")
    return [pieces[0]] + [swap(pieces[r], size, r) for r in range(1, size)]


def reduce_members(pieces):
    size = lax.axis_size("tensor")
    near = swap(pieces[1], size, 1)
    far = swap(pieces[3], size, 1)
    other = (pieces[2].astype(F32) + far.astype(F32)).astype(BF)
    across = swap(other, size, 2)
    return pieces[0].astype(F32) + near.astype(F32) + across.astype(F32)


def unpack_block(spots_ref, src_ref, i):
    window = ROWS + 16
    shape = (ROWS, window)
    rows = lax.broadcasted_iota(jnp.int32, shape, 0)
    steps = lax.broadcasted_iota(jnp.int32, shape, 1) - rows
    bound = spots_ref[8 * i + 6]
    total = None
    for k in range(2):
        group, start, shift = (spots_ref[8 * i + 3 * k + j] for j in range(3))
        wanted = rows < bound if k == 0 else rows >= bound
        hot = jnp.where((steps == shift) & wanted, 1.0, 0.0).astype(BF)
        tiles = [src_ref[group, start + j] for j in range(window // 16)]
        part = mm(hot, jnp.concatenate(tiles, 0), 1, 0)
        total = part if k == 0 else total + part
    return total.astype(BF)


def store_over(src_ref, over_ref, last):
    top = lax.broadcasted_iota(jnp.int32, (16, 1), 0) == 0
    end = src_ref.shape[1] - 1
    for g in range(src_ref.shape[0]):
        src_ref[g, end] = jnp.where(top, over_ref[last, g].astype(F32), 0.0).astype(BF)


def unpack_kernel(
    size, spots, me, home_ref, over_ref, result_ref, out_ref, result_out_ref, src_ref, sems
):
    tiles = home_ref.shape[2]
    step = pl.program_id(0)
    each = out_ref.shape[0] // ROWS

    def load(r):
        at = pl.ds(jnp.bitwise_xor(me[0], r) * tiles, tiles)
        return pltpu.make_async_copy(home_ref.at[r], src_ref.at[:, at], sems.at[r])

    @pl.when(step == 0)
    def _():
        for r in range(size):
            load(r).start()
        store_over(src_ref, over_ref, jnp.bitwise_xor(size - 1, me[0]))
        for r in range(size):
            load(r).wait()

    for i in range(each):
        out_ref[i * ROWS : (i + 1) * ROWS, :] = unpack_block(spots, src_ref, step * each + i)
    result_out_ref[...] = result_ref[...]


def unpack(spots, me, home, over, result):
    size, groups, share, width = home.shape
    rows = size * groups * share
    home = home.reshape(size, groups, share // 16, 16, width)
    whole = lambda *shape: pl.BlockSpec(shape, lambda i, *refs: (0,) * len(shape))
    anywhere = pl.BlockSpec(memory_space=pl.ANY)
    each = 4 * ROWS
    block = pl.BlockSpec((each, width), lambda i, *refs: (i, 0))
    return pl.pallas_call(
        functools.partial(unpack_kernel, size),
        grid_spec=pltpu.PrefetchScalarGridSpec(
            num_scalar_prefetch=2,
            grid=(rows // each,),
            in_specs=[anywhere, whole(*over.shape), block],
            out_specs=[block, block],
            scratch_shapes=[
                pltpu.VMEM((groups, size * share // 16 + 1, 16, width), BF),
                pltpu.SemaphoreType.DMA((size,)),
            ],
        ),
        out_shape=[jax.ShapeDtypeStruct((rows, width), BF)] * 2,
        compiler_params=pltpu.CompilerParams(vmem_limit_bytes=VMEM_LIMIT),
        cost_estimate=pl.CostEstimate(flops=0, bytes_accessed=30 << 20, transcendentals=0),
        name="unpack",
    )(spots, me, home, over, result)


def route_kernel(groups, size, send_ref, over_ref, out_ref, over_out_ref, sends, recvs, s_over, r_over, keep):
    d = lax.axis_index("dp")
    t = lax.axis_index("tensor")
    chunks = sends.shape[2]
    count = send_ref.shape[1] // chunks
    greet(groups, (1, 2), d, t)
    spread = Spread(out_ref, (sends, recvs), groups, d, t)

    def rows(c):
        return pl.ds(c * count, count)

    def own(c):
        return pltpu.make_async_copy(
            send_ref.at[d, rows(c)], out_ref.at[0, d, rows(c)], keep.at[c]
        )

    def arrival(c, k):
        return spread.arrival(send_ref.at[lax.rem(d + k, groups), rows(c)], k, (rows(c),), (c,))

    def across(c, k):
        return spread.across(k, (rows(c),), (c,))

    def beside(r, c, k):
        return spread.beside(r, k, (rows(c),), (c,))

    def over_copy(k):
        to = lax.rem(d + k, groups)
        return remote(over_ref.at[to], over_out_ref.at[d], s_over.at[k], r_over.at[k], (to, t))

    def pass_far(c):
        for k in range(groups):
            across(c, k).wait_recv()
            beside(2, c, k).start()

    own_over = pltpu.make_async_copy(over_ref.at[d], over_out_ref.at[d], keep.at[chunks])
    for c in range(chunks):
        own(c).start()
    own_over.start()
    for c in range(chunks):
        for k in range(1, groups):
            arrival(c, k).start()
    for k in range(1, groups):
        over_copy(k).start()
    for c in range(chunks):
        own(c).wait()
        for k in range(groups):
            if k > 0:
                arrival(c, k).wait_recv()
            across(c, k).start()
            beside(0, c, k).start()
        if c > 0:
            pass_far(c - 1)
    pass_far(chunks - 1)
    own_over.wait()
    for k in range(groups):
        for c in range(chunks):
            beside(0, c, k).wait_recv()
            beside(2, c, k).wait_recv()
            if k > 0:
                arrival(c, k).wait_send()
            across(c, k).wait_send()
            beside(0, c, k).wait_send()
            beside(2, c, k).wait_send()
        if k > 0:
            over_copy(k).wait_recv()
            over_copy(k).wait_send()


def route(send, over, size):
    groups = send.shape[0]
    anywhere = pl.BlockSpec(memory_space=pl.ANY)
    return pl.pallas_call(
        functools.partial(route_kernel, groups, size),
        in_specs=[anywhere, anywhere],
        out_specs=[anywhere, anywhere],
        out_shape=[
            jax.ShapeDtypeStruct((size,) + send.shape, BF),
            jax.ShapeDtypeStruct(over.shape, BF),
        ],
        scratch_shapes=[
            pltpu.SemaphoreType.DMA((4, groups, 3)),
            pltpu.SemaphoreType.DMA((4, groups, 3)),
            pltpu.SemaphoreType.DMA((groups,)),
            pltpu.SemaphoreType.DMA((groups,)),
            pltpu.SemaphoreType.DMA((4,)),
        ],
        compiler_params=pltpu.CompilerParams(collective_id=0, has_side_effects=True),
        cost_estimate=pl.CostEstimate(flops=0, bytes_accessed=60 << 20, transcendentals=0),
        name="route",
    )(send, over)


class Halving:
    def __init__(self, fetch, links, refs, sems):
        self.fetch, self.links = fetch, links
        self.out, self.got, self.held = refs
        self.send, self.recv = sems
        self.counts = [2 ** (len(links) - 1 - step) for step in range(len(links))]
        self.first = [sum(self.counts[:step]) for step in range(len(links))]

    def term(self, side, i):
        rest = [lax.rem(lax.div(i, 2**j), 2) for j in range(len(self.links) - 1)]
        return self.fetch(side, *rest)

    def copy(self, step, i):
        at = self.first[step] + i
        return remote(
            self.out.at[at], self.got.at[at], self.send.at[at], self.recv.at[at], self.links[step][1]
        )

    def start(self):
        for i in range(self.counts[0]):
            self.out[i] = self.term(1 - self.links[0][0], jnp.int32(i)).astype(BF)
            self.copy(0, i).start()

    def advance(self, step):
        for i in range(self.counts[step - 1]):
            self.copy(step - 1, i).wait_recv()
        own = self.links[step][0]
        for keep in (False, True):
            for j in range(self.counts[step]):
                i = (own if keep else 1 - own) + 2 * j
                value = self.term(self.links[0][0], i) if step == 1 else self.held[i]
                value = value + self.got[self.first[step - 1] + i].astype(F32)
                if keep:
                    self.held[j] = value
                else:
                    self.out[self.first[step] + j] = value.astype(BF)
                    self.copy(step, j).start()

    def total(self):
        last = len(self.links) - 1
        self.copy(last, 0).wait_recv()
        return self.held[0] + self.got[self.first[last]].astype(F32)

    def finish(self):
        for step, count in enumerate(self.counts):
            for i in range(count):
                self.copy(step, i).wait_send()


def settle_kernel(
    groups,
    size,
    match_ref,
    spots_ref,
    res_over_ref,
    d_hbm,
    x_hbm,
    w_hbm,
    one_hbm,
    wide_own_hbm,
    wide_other_hbm,
    down_hbm,
    res_hbm,
    home_ref,
    over_ref,
    result_hbm,
    gq_sum_ref,
    gu_sum_ref,
    down_sum_ref,
    out_sum_ref,
    norm_sum_ref,
    d_ref,
    x_ref,
    w_ref,
    one_ref,
    wide_own_ref,
    wide_other_ref,
    down_ref,
    down_sent_ref,
    down_got_ref,
    src_ref,
    out_ref,
    to_core_ref,
    from_core_ref,
    pair_ref,
    other_ref,
    own_ref,
    spare_ref,
    gq_ref,
    gq_acc_ref,
    *refs,
):
    halving_refs = tuple(refs[3 * i : 3 * i + 3] for i in range(3))
    (
        loads,
        s_res,
        r_res,
        s_half,
        r_half,
        sends,
        recvs,
        s_over,
        r_over,
        s_sum,
        r_sum,
        keep,
    ) = refs[9:]
    d = lax.axis_index("dp")
    t = lax.axis_index("tensor")
    chunks, _, sub, width = own_ref.shape
    sent = (chunks - 1) * sub // 16
    rest = sub // 16
    core = (d, jnp.bitwise_xor(t, 1))
    chip = (d, jnp.bitwise_xor(t, 2))

    def load(source, target, i):
        return pltpu.make_async_copy(source, target, loads.at[i])

    def load_d(r):
        part = jnp.bitwise_xor(t, r)
        return load(d_hbm.at[part], d_ref.at[part], r)

    load_w = load(w_hbm, w_ref, 4)
    load_x = load(x_hbm, x_ref, 5)
    load_one = load(one_hbm, one_ref, 6)
    load_wide = (load(wide_own_hbm, wide_own_ref, 7), load(wide_other_hbm, wide_other_ref, 8))
    load_down = load(down_hbm, down_ref, 11)
    down_copy = remote(down_sent_ref, down_got_ref, s_res.at[4], r_res.at[4], chip)

    def down_sum(member):
        total = down_ref[0, member].astype(F32)
        for g in range(1, groups):
            total = total + down_ref[g, member].astype(F32)
        return total


    def in_src(r, low, count):
        base = jnp.bitwise_xor(t, r) * (sent + rest)
        return src_ref.at[:, pl.ds(base + low, count)]

    def source_of(r, low, count):
        return res_hbm.at[r, :, pl.ds(low, count)]

    res_parts = (
        (source_of(0, 0, sent + rest), in_src(0, 0, sent + rest)),
        (source_of(2, 0, sent), in_src(2, 0, sent)),
        (in_src(2, sent, rest), in_src(2, sent, rest)),
    )
    load_res = [load(source, target, 9 + i) for i, (source, target) in enumerate(res_parts[:2])]
    beside_res = [
        remote(source, target, s_res.at[i], r_res.at[i], core)
        for i, (source, target) in enumerate(res_parts)
    ]
    across_res = remote(
        source_of(0, sent, rest), in_src(0, sent, rest), s_res.at[3], r_res.at[3], chip
    )

    load_w.start()
    load_d(3).start()
    load_d(2).start()
    greet(groups, (1, 2), d, t)

    def rows(c):
        return pl.ds(pl.multiple_of(c * BLOCK, BLOCK), BLOCK)

    def piece(r, c):
        return mm(d_ref[jnp.bitwise_xor(t, r), :, rows(c)], w_ref[...], 0, 0)

    def to_core(i, c):
        return remote(
            to_core_ref.at[i, c], from_core_ref.at[i, c], s_sum.at[i, c], r_sum.at[i, c], core
        )

    def other(c):
        return remote(pair_ref.at[c], other_ref.at[c], s_sum.at[2, c], r_sum.at[2, c], chip)

    load_w.wait()
    load_d(3).wait()
    load_d(1).start()
    load_d(0).start()
    load_wide[0].start()
    load_wide[1].start()
    load_d(2).wait()

    @pl.loop(0, chunks)
    def _(c):
        to_core_ref[0, c] = piece(3, c).astype(BF)
        to_core(0, c).start()
        value = piece(2, c)
        to_core(0, c).wait_recv()
        pair_ref[c] = (value + from_core_ref[0, c].astype(F32)).astype(BF)

        @pl.when(c == 0)
        def _():
            other(0).start()

    block_rows, _, inner = gu_sum_ref.shape

    def wide_rows(part, block):
        at = pl.ds(pl.multiple_of(block * block_rows, block_rows), block_rows)
        columns = slice(part * WIDE_PARTS[0], WIDE_PARTS[0] + part * WIDE_PARTS[1])
        return wide_own_ref[at, columns].astype(F32) + wide_other_ref[at, columns].astype(F32)

    def gq_rows(y, low, high):
        return gq_ref[y + 2 * low + 4 * high].astype(F32)

    link_y, link_low, link_high = (
        (lax.rem(lax.div(d, step), 2), (jnp.bitwise_xor(d, step), t)) for step in (1, 2, 4)
    )
    sums = [
        Halving(fetch, links, halving_refs[i], (s_half.at[i], r_half.at[i]))
        for i, (fetch, links) in enumerate(
            (
                (
                    lambda y, low, high: wide_rows(0, y + 2 * low + 4 * high),
                    (link_y, link_low, link_high),
                ),
                (
                    lambda low, y, high: wide_rows(1, y + 2 * low + 4 * high),
                    (link_low, link_y, link_high),
                ),
                (gq_rows, (link_y, link_low, link_high)),
            )
        )
    ]

    load_wide[0].wait()
    load_wide[1].wait()
    load_x.start()
    load_one.start()
    load_down.start()
    for copy in load_res:
        copy.start()
    sums[0].start()
    sums[1].start()
    load_d(1).wait()

    @pl.loop(0, chunks)
    def _(c):
        to_core_ref[1, c] = piece(1, c).astype(BF)
        to_core(1, c).start()

    load_d(0).wait()
    load_one.wait()

    @pl.loop(0, chunks)
    def _(c):
        one_ref[rows(c), :] += piece(0, c)

    def start_gq():
        load_x.wait()
        gq_acc_ref[...] = jnp.zeros_like(gq_acc_ref)

        @pl.loop(0, size)
        def _(part):
            gq_acc_ref[...] += mm(d_ref[part], x_ref[part], 1, 0)

        total = gq_acc_ref[...].T.astype(BF)
        for g in range(groups):
            gq_ref[g] = total[g * block_rows : (g + 1) * block_rows]
        sums[2].start()

    def store_result(i):
        at = pl.ds(pl.multiple_of(i * ROWS, ROWS), ROWS)
        return pltpu.make_async_copy(out_ref.at[at], result_hbm.at[at], keep.at[chunks + 1 + i])

    blocks = out_ref.shape[0] // ROWS

    def arrange_result():
        for copy in load_res:
            copy.wait()
        for copy in beside_res:
            copy.wait_recv()

        @pl.loop(0, blocks)
        def _(i):
            at = pl.ds(pl.multiple_of(i * ROWS, ROWS), ROWS)
            out_ref[at, :] = unpack_block(spots_ref, src_ref, i)
            store_result(i).start()

    store_over(src_ref, res_over_ref, jnp.bitwise_xor(size - 1, t))

    body = Spread(home_ref, (sends, recvs), groups, d, t)
    extra = Spread(over_ref, (s_over, r_over), groups, d, t)

    def own_copy(c):
        return pltpu.make_async_copy(own_ref.at[c, d], home_ref.at[0, d, c], keep.at[c])

    own_over = pltpu.make_async_copy(spare_ref.at[d], over_ref.at[0, d], keep.at[chunks])

    def pass_on(c):
        own_copy(c).wait()
        for k in range(groups):
            if k > 0:
                body.arrival(own_ref.at[c, 0], k, (c,), (c,)).wait_recv()
            body.across(k, (c,), (c,)).start()
            body.beside(0, k, (c,), (c,)).start()

    def pass_far(c):
        for k in range(groups):
            body.across(k, (c,), (c,)).wait_recv()
            body.beside(2, k, (c,), (c,)).start()

    def send_home(c):
        to_core(1, c).wait_recv()
        partial = one_ref[rows(c), :] + from_core_ref[1, c].astype(F32)
        other(c).wait_recv()
        done = (partial + other_ref[c].astype(F32)).astype(BF)
        for g in range(groups):
            own_ref[c, g] = done[g * sub : (g + 1) * sub]
        own_copy(c).start()
        for k in range(1, groups):
            body.arrival(own_ref.at[c, lax.rem(d + k, groups)], k, (c,), (c,)).start()
        if c == chunks - 1:
            last = [own_ref[c, g, sub - 16 :, :].astype(F32)[15:16] for g in range(groups)]
            for to in range(groups):
                spare = last[0] * match_ref[to]
                for g in range(1, groups):
                    spare = spare + last[g] * match_ref[g * groups + to]
                spare_ref[to] = spare.astype(BF)
            own_over.start()
            for k in range(1, groups):
                extra.arrival(spare_ref.at[lax.rem(d + k, groups)], k, (), ()).start()

    other(0).wait_send()
    other(1).start()
    send_home(0)
    start_gq()
    other(1).wait_send()
    other(2).start()
    send_home(1)
    other(2).wait_send()
    pass_on(0)
    across_res.start()
    send_home(2)
    sums[0].advance(1)
    sums[1].advance(1)
    sums[2].advance(1)
    pass_on(1)
    across_res.wait_recv()
    for copy in beside_res:
        copy.start()
    load_down.wait()
    down_sent_ref[...] = down_sum(1).astype(BF)
    down_copy.start()
    pass_on(2)
    own_over.wait()
    for k in range(groups):
        if k > 0:
            extra.arrival(spare_ref.at[0], k, (), ()).wait_recv()
        extra.across(k, (), ()).start()
        extra.beside(0, k, (), ()).start()
    sums[0].advance(2)
    sums[1].advance(2)
    sums[2].advance(2)
    pass_far(0)
    pass_far(1)
    arrange_result()
    down_copy.wait_recv()
    totals = jnp.concatenate(
        [sums[0].total(), sums[1].total(), down_sum(0) + down_got_ref[...].astype(F32)], 1
    )
    gu_sum_ref[:, 0, :] = totals[:, :inner]
    gu_sum_ref[:, 1, :] = totals[:, inner : 2 * inner]
    total = sums[2].total()
    local = gq_sum_ref.shape[2]
    for i in range(3):
        gq_sum_ref[i] = total[:, i * local : (i + 1) * local]
    out_sum_ref[...] = totals[:, 2 * inner : 2 * inner + local]
    norm_sum_ref[...] = totals[:, 2 * inner + local : 2 * inner + local + norm_sum_ref.shape[1]]
    down_sum_ref[...] = totals[:, totals.shape[1] - inner :]
    pass_far(2)
    for k in range(groups):
        extra.across(k, (), ()).wait_recv()
        extra.beside(2, k, (), ()).start()
    down_copy.wait_send()
    across_res.wait_send()
    for copy in beside_res:
        copy.wait_send()

    @pl.loop(0, blocks)
    def _(i):
        store_result(i).wait()

    for each in sums:
        each.finish()
    for c in range(chunks):
        to_core(0, c).wait_send()
        to_core(1, c).wait_send()
    for k in range(groups):
        for c in range(chunks):
            body.beside(0, k, (c,), (c,)).wait_recv()
            body.beside(2, k, (c,), (c,)).wait_recv()
            if k > 0:
                body.arrival(own_ref.at[c, 0], k, (c,), (c,)).wait_send()
            body.across(k, (c,), (c,)).wait_send()
            body.beside(0, k, (c,), (c,)).wait_send()
            body.beside(2, k, (c,), (c,)).wait_send()
        extra.beside(0, k, (), ()).wait_recv()
        extra.beside(2, k, (), ()).wait_recv()
        if k > 0:
            extra.arrival(spare_ref.at[0], k, (), ()).wait_send()
        extra.across(k, (), ()).wait_send()
        extra.beside(0, k, (), ()).wait_send()
        extra.beside(2, k, (), ()).wait_send()


def settle(
    match,
    spots,
    res_over,
    d_qkv_t,
    x_all,
    w_t,
    grad_one,
    wide_own,
    wide_other,
    down,
    inner,
    res,
):
    size, local, rows = d_qkv_t.shape
    _, groups, _, sub, width = res.shape
    share = res.shape[2] * sub
    res = res.reshape(-1, groups, share // 16, 16, width)
    chunks = rows // BLOCK
    part = width // groups
    total_rows = size * rows
    anywhere = pl.BlockSpec(memory_space=pl.ANY)
    vmem = pl.BlockSpec(memory_space=pltpu.VMEM)
    smem = pl.BlockSpec(memory_space=pltpu.SMEM)
    dma = pltpu.SemaphoreType.DMA
    shape = jax.ShapeDtypeStruct
    buffer = pltpu.VMEM((chunks, BLOCK, width), BF)
    pair_buffer = pltpu.VMEM((2, chunks, BLOCK, width), BF)
    halving = lambda columns, steps: [
        pltpu.VMEM((2**steps - 1, part, columns), BF),
        pltpu.VMEM((2**steps - 1, part, columns), BF),
        pltpu.VMEM((2 ** (steps - 2), part, columns), F32),
    ]
    return pl.pallas_call(
        functools.partial(settle_kernel, groups, size),
        in_specs=[smem, smem, vmem] + [anywhere] * 8,
        out_specs=[anywhere, anywhere, anywhere] + [vmem] * 5,
        out_shape=[
            shape((size, groups, chunks, sub, width), BF),
            shape((size, groups, 1, width), BF),
            shape((total_rows, width), BF),
            shape((3, part, local // 3), F32),
            shape((part, 2, inner), F32),
            shape((part, inner), F32),
            shape((part, local // 3), F32),
            shape((part, 4), F32),
        ],
        scratch_shapes=[
            pltpu.VMEM(d_qkv_t.shape, BF),
            pltpu.VMEM(x_all.shape, BF),
            pltpu.VMEM(w_t.shape, BF),
            pltpu.VMEM(grad_one.shape, F32),
            pltpu.VMEM(wide_own.shape, BF),
            pltpu.VMEM(wide_own.shape, BF),
            pltpu.VMEM(down.shape, BF),
            pltpu.VMEM(down.shape[2:], BF),
            pltpu.VMEM(down.shape[2:], BF),
            pltpu.VMEM((groups, size * share // 16 + 1, 16, width), BF),
            pltpu.VMEM((total_rows, width), BF),
            pair_buffer,
            pair_buffer,
            buffer,
            buffer,
            pltpu.VMEM((chunks, groups, sub, width), BF),
            pltpu.VMEM((groups, 1, width), BF),
            pltpu.VMEM((groups, part, local), BF),
            pltpu.VMEM((local, width), F32),
            *halving(WIDE_PARTS[0], 3),
            *halving(WIDE_PARTS[1], 3),
            *halving(local, 3),
            dma((15,)),
            dma((5,)),
            dma((5,)),
            dma((3, 7)),
            dma((3, 7)),
            dma((4, groups, chunks)),
            dma((4, groups, chunks)),
            dma((4, groups)),
            dma((4, groups)),
            dma((3, chunks)),
            dma((3, chunks)),
            dma((chunks + 1 + total_rows // ROWS,)),
        ],
        compiler_params=pltpu.CompilerParams(
            collective_id=1, has_side_effects=True, vmem_limit_bytes=VMEM_LIMIT
        ),
        cost_estimate=pl.CostEstimate(
            flops=4 * size * rows * local * width, bytes_accessed=150 << 20, transcendentals=0
        ),
        name="settle",
    )(
        match,
        spots,
        res_over,
        d_qkv_t,
        x_all,
        w_t,
        grad_one,
        wide_own,
        wide_other,
        down,
        res,
    )


def local(tokens, cotangent, lengths, dealing, w_qkv, w_out, w_gu, w_down, gains, shifts):
    groups = lax.axis_size("dp")
    size = lax.axis_size("tensor")
    me = lax.axis_index("tensor")
    rows = tokens.shape[0]
    width = tokens.shape[2]
    slots = rows // groups
    share = slots // size
    own_rows = rows // size
    subs = own_rows // BLOCK
    sub = share // subs
    fused = groups == 8 and sub % 16 == 0
    i32 = jnp.int32

    ids = jnp.stack([lax.axis_index("dp"), me]).astype(i32)
    send_x, over_x, send_c, meta, table, match, spots = pack(
        lengths,
        dealing,
        ids,
        tokens.reshape(rows, width),
        cotangent.reshape(rows, width),
        groups,
        size,
    )

    def over_dp(array):
        return lax.all_to_all(array, "dp", split_axis=0, concat_axis=0, tiled=True)

    half = w_down.shape[0] // 2
    down_half = lax.dynamic_slice_in_dim(w_down, ids[0] % 2 * half, half, 0)
    far_out, far_down = swap(w_out.T, size, 2), swap(down_half, size, 2)
    match_square = match.reshape(groups, groups)

    def fill(received, over, last):
        spare = jnp.dot(match_square.astype(BF), over, preferred_element_type=F32).astype(BF)
        hole = (jnp.sum(match_square, 1) > 0)[:, None] & (jnp.arange(share) == share - 1)[None, :]
        fix = last[:, None, None] & hole[None]
        body = jnp.where(fix[..., None], spare[None, :, None, :], received)
        body = body.reshape(-1, groups, subs, sub, width).transpose(0, 2, 1, 3, 4)
        return body.reshape(-1, own_rows, width)

    if fused:
        x_rel, over_x = route(send_x, over_x, size)
        send_c, x_rel, far_out, far_down = lax.optimization_barrier(
            (send_c, x_rel, far_out, far_down)
        )
    else:
        x_rel = jnp.stack(gather_members(over_dp(send_x)))
        relative = jnp.bitwise_xor(jnp.arange(size, dtype=i32), me)
        x_rel = fill(x_rel, over_dp(over_x)[:, 0], relative == size - 1)
    local_width = w_qkv.shape[2]
    w_qkv_t = w_qkv.transpose(1, 2, 0).reshape(3 * local_width, width)
    x_rel, near_gu = lax.optimization_barrier((x_rel, w_gu.reshape(width, -1)))
    far_gu = swap(near_gu, size, 2)
    other_down = lax.ppermute(far_down, "dp", [(i, i ^ 1) for i in range(groups)])
    cot = over_dp(send_c)
    if not fused:
        cot = fill(cot[None, :, :share], cot[:, share], (me == size - 1)[None])[0]
    frequency = np.float32(1000.0) ** (-(np.arange(HALF, dtype=np.float32) * 2) / HEAD)
    frequency = jnp.asarray(frequency.astype(np.float32))
    q, k, v, k_rows, v_rows, cosine, sine, x_all, x_own = project(
        meta, match, x_rel, over_x, w_qkv_t, frequency[:, None], groups, fused
    )
    o_blocks, lse = attend(meta, q, k_rows, v, groups)
    o_blocks, far_gu, other_down, cot = lax.optimization_barrier(
        (o_blocks, far_gu, other_down, cot)
    )

    norms = jnp.concatenate([gains.T, shifts.T], 0)
    (
        result_own,
        grad_one,
        d_heads,
        heads_own,
        normed_t,
        d_branch_t,
        d_attn_t,
        hidden,
        d_gu,
        norm_grads,
    ) = middle(
        x_own,
        match,
        cot,
        norms,
        o_blocks,
        size,
        w_out.T,
        far_out,
        near_gu,
        far_gu,
        w_down,
        far_down,
        other_down,
    )
    grad_args = (normed_t, d_branch_t, d_attn_t, hidden, d_gu, heads_own, norm_grads)
    if fused:
        wide_own, wide_other, down, do_rel, home_result, over_result = grads(
            match, groups, *grad_args, d_heads, result_own
        )
        wide_other = swap(wide_other, size, 2)
        down = over_dp(down)
    else:
        sent_grads = weight_grads(1, *grad_args)
        kept_grads = weight_grads(0, *grad_args)
        pair = (kept_grads.astype(F32) + swap(sent_grads, size, 1).astype(F32)).astype(BF)
        do_rel = jnp.stack(exchange_members([d_heads[r] for r in range(size)]))

    d_qkv_t = attend_back(
        meta, q, k_rows, k, v_rows, o_blocks, do_rel, lse, cosine, sine, groups
    )
    def send_back(own):
        body = own.reshape(subs, groups, sub, width).transpose(1, 0, 2, 3)
        body = body.reshape(groups, share, width)
        spare = lax.dot_general(
            match_square.astype(BF),
            body[:, share - 1],
            (((0,), (0,)), ((), ())),
            preferred_element_type=F32,
        ).astype(BF)
        pair = (over_dp(body), over_dp(spare.reshape(groups, 1, width)))
        return tuple(jnp.stack(gather_members(a)) for a in pair)

    if fused:
        home_input, home_over, result, qkv_sum, gu_sum, down_sum, out_sum, norm_sum = settle(
            match,
            spots,
            over_result,
            d_qkv_t,
            x_all,
            w_qkv_t,
            grad_one,
            wide_own,
            wide_other,
            down,
            w_down.shape[1],
            home_result,
        )
        home_input = home_input.reshape(size, groups, share, width)
    else:
        back_rel, grad_qkv = project_back(meta, d_qkv_t, x_all, w_qkv_t)
        grad_qkv = grad_qkv.reshape(groups, width // groups, 3 * local_width)
        home_result = send_back(result_own)
        input_own = grad_one + reduce_members([back_rel[r] for r in range(size)])
        home_input = send_back(input_own.astype(BF))
        grad_qkv = lax.all_to_all(grad_qkv, "dp", split_axis=0, concat_axis=0, tiled=True)
        qkv_sum = jnp.sum(grad_qkv.astype(F32), 0)
        pair = lax.psum_scatter(pair, "dp", scatter_dimension=1, tiled=True)
        summed = pair[0].astype(F32) + swap(pair[1], size, 2).astype(F32)
    if fused:
        qkv_sum = qkv_sum.transpose(1, 0, 2)
    else:
        qkv_sum = qkv_sum.reshape(-1, 3, local_width)
        inner = w_down.shape[1]
        gu_sum = summed[:, : 2 * inner].reshape(-1, 2, inner)
        out_sum = summed[:, 2 * inner : 2 * inner + local_width]
        norm_sum = summed[:, 2 * inner + local_width : 2 * inner + local_width + 4]
        down_sum = summed[:, -inner:]
    norm_sum = lax.dynamic_slice_in_dim(
        norm_sum, me * (norm_sum.shape[0] // size), norm_sum.shape[0] // size, 0
    )
    if fused:
        input_grad, result = unpack(spots, me[None], home_input, home_over, result)
    else:
        row_ids = jnp.arange(rows, dtype=i32)[None, :]
        low, count, group, first = (table[i, 1:][:, None] for i in range(4))
        here = (row_ids >= low) & (row_ids < low + count)
        slot = row_ids + first - low
        home_part = jnp.minimum(slot // share, size - 1)
        flat = (jnp.bitwise_xor(home_part, me) * groups + group) * (share + 1)
        flat = jnp.sum(jnp.where(here, flat + slot - home_part * share, 0), 0)

        def arrange(home, over):
            every = jnp.concatenate([home, over], 2).reshape(-1, width)
            return jnp.take(every, flat, axis=0)

        result = arrange(*home_result)
        input_grad = arrange(*home_input)
    result = result.reshape(rows, 1, width)
    input_grad = input_grad.reshape(rows, 1, width)
    return (
        result,
        input_grad,
        qkv_sum,
        out_sum,
        gu_sum,
        down_sum,
        norm_sum[:, :2],
        norm_sum[:, 2:],
    )


def solution(mesh):
    placed = (
        P(None, "dp", None),
        P(None, "dp", None),
        P(),
        P(),
        P(None, None, "tensor"),
        P(None, "tensor"),
        P(None, None, "tensor"),
        P(None, "tensor"),
        P(),
        P(),
    )
    return jax.shard_map(
        local,
        mesh=mesh,
        in_specs=placed,
        out_specs=(
            P(None, "dp", None),
            P(None, "dp", None),
            P("dp", None, "tensor"),
            P("dp", "tensor"),
            P("dp", None, "tensor"),
            P("dp", "tensor"),
            P(("dp", "tensor"), None),
            P(("dp", "tensor"), None),
        ),
        check_vma=False,
    )
```

```python
import functools

import jax
import jax.numpy as jnp
import numpy as np
from jax import lax
from jax.experimental import pallas as pl
from jax.experimental.pallas import tpu as pltpu
from jax.sharding import PartitionSpec as P

HEAD = 64
HALF = HEAD // 2
BLOCK = 256
QUERIES = 512
PADDED = HEAD + 16
KEYS = 512
LOG_2 = 0.6931471805599453
EPSILON = 1e-05
NEGATIVE = -1000000000.0
START = -1e30
BF = jnp.bfloat16
F32 = jnp.float32
VMEM_LIMIT = 56 * 1024 * 1024


def mm(a, b, ca, cb):
    return lax.dot_general(a, b, (((ca,), (cb,)), ((), ())), preferred_element_type=F32)


HOLES = 8
ROWS = 128
WIDE = 1664
WIDE_PARTS = (896, 768)
TILE = 256


def div(value, size):
    if size & (size - 1) == 0:
        return lax.shift_right_arithmetic(value, jnp.int32(size.bit_length() - 1))
    return lax.div(value, size)


def rem(value, size):
    if size & (size - 1) == 0:
        return lax.bitwise_and(value, jnp.int32(size - 1))
    return lax.rem(value, size)


def extra_of(source, offset, length, groups):
    turned = rem(source - offset + groups, groups)
    return turned, jnp.where(turned < rem(length, groups), 1, 0)


def pack_kernel(
    groups,
    size,
    lengths,
    dealing,
    ids,
    x_ref,
    c_ref,
    send_x_ref,
    over_x_ref,
    send_c_ref,
    meta_ref,
    table_ref,
    match_ref,
    spots_ref,
    places,
):
    d = ids[0]
    t = ids[1]
    rows = x_ref.shape[0]
    slots = rows // groups
    share = slots // size
    window = (share + 31) // 16 * 16

    count = lengths.shape[0]

    def place_of(j, offset):
        places[0, j] = offset
        return offset + lengths[j]

    lax.fori_loop(0, count, place_of, jnp.int32(0), unroll=True)

    def lookup(q):
        seq = dealing[q]
        return seq, places[0, seq], lengths[seq]

    def span(offset, length):
        low = div(offset - d + groups - 1, groups)
        return low, div(offset + length - d + groups - 1, groups) - low

    def window_at(row):
        start = jnp.clip(jnp.bitwise_and(row, -16), 0, rows - window)
        return pl.ds(pl.multiple_of(start, 16), window), row - start

    def one_hot(steps, shift, wanted):
        return jnp.where((steps == shift) & wanted, 1.0, 0.0).astype(BF)

    def steps_of(count):
        shape = (count, window)
        return lax.broadcasted_iota(jnp.int32, shape, 1) - lax.broadcasted_iota(jnp.int32, shape, 0)

    steps = steps_of(share)
    spare_steps = steps_of(16)
    top = lax.broadcasted_iota(jnp.int32, (16, 1), 0) == 0
    table_ref[0, 0] = t
    slot_ids = lax.broadcasted_iota(jnp.int32, (share, 1), 0) + t * share

    @pl.loop(0, groups, unroll=4)
    def _(g):
        seq_a, off_a, len_a = lookup(2 * g)
        seq_b, off_b, len_b = lookup(2 * g + 1)
        low_a, count_a = span(off_a, len_a)
        low_b, count_b = span(off_b, len_b)
        for seq, entries in ((seq_a, (low_a, count_a, g, 0)), (seq_b, (low_b, count_b, g, count_a))):
            for i, entry in enumerate(entries):
                table_ref[i, 1 + seq] = jnp.int32(entry)
        shifted = low_b - count_a
        at_a, shift_a = window_at(low_a + t * share)
        at_b, shift_b = window_at(shifted + t * share)
        at_over, shift_over = window_at(shifted + slots)
        hot_a = one_hot(steps, shift_a, slot_ids < count_a)
        hot_b = one_hot(steps, shift_b, slot_ids >= count_a)
        hot_over = one_hot(spare_steps, shift_over, top)
        for ref, out_ref in ((x_ref, send_x_ref), (c_ref, send_c_ref)):
            picked = mm(hot_a, ref[at_a, :], 1, 0) + mm(hot_b, ref[at_b, :], 1, 0)
            out_ref[g, :share] = picked.astype(BF)
        over_x_ref[g] = mm(hot_over, x_ref[at_over, :], 1, 0)[:1].astype(BF)
        send_c_ref[g, share:] = mm(hot_over, c_ref[at_over, :], 1, 0).astype(BF)

    def spot(i, here):
        row = i * ROWS
        following = jnp.minimum(here + 1, count - 1)
        here = jnp.where(table_ref[0, 1 + following] <= row, following, here)
        after = jnp.minimum(here + 1, count - 1)
        for k, j in enumerate((here, after)):
            slot = row + table_ref[3, 1 + j] - table_ref[0, 1 + j]
            start = jnp.clip(jnp.bitwise_and(slot, -16), 0, slots - ROWS)
            spots_ref[8 * i + 3 * k] = table_ref[2, 1 + j]
            spots_ref[8 * i + 3 * k + 1] = div(start, 16)
            spots_ref[8 * i + 3 * k + 2] = slot - start
        spots_ref[8 * i + 6] = jnp.where(after > here, table_ref[0, 1 + after] - row, ROWS)
        spots_ref[8 * i + 7] = jnp.int32(0)
        return here

    lax.fori_loop(0, rows // ROWS, spot, jnp.int32(0), unroll=4)

    _, off_a, len_a = lookup(2 * d)
    _, off_b, len_b = lookup(2 * d + 1)
    off_a = rem(off_a, groups)
    off_b = rem(off_b, groups)
    meta_ref[0] = div(len_a, BLOCK)
    meta_ref[1] = div(len_a + BLOCK - 1, BLOCK)
    meta_ref[2] = t
    meta_ref[3] = off_a
    meta_ref[4] = off_b
    meta_ref[5] = len_a
    meta_ref[6] = jnp.int32(0)
    meta_ref[7] = jnp.int32(0)

    def counts(source):
        first = div(len_a, groups) + extra_of(source, off_a, len_a, groups)[1]
        second = div(len_b, groups) + extra_of(source, off_b, len_b, groups)[1]
        return first, first + second

    def clear(i, carry):
        match_ref[i] = jnp.float32(0.0)
        return carry

    lax.fori_loop(0, groups * groups, clear, 0, unroll=8)

    def sort_out(source, carry):
        holes, overs = carry
        total = counts(source)[1]
        places[1, holes] = source
        places[2, overs] = source
        meta_ref[HOLES + source] = jnp.int32(-1)
        return holes + jnp.where(total < slots, 1, 0), overs + jnp.where(total > slots, 1, 0)

    holes, _ = lax.fori_loop(0, groups, sort_out, (jnp.int32(0), jnp.int32(0)), unroll=8)

    @pl.loop(0, holes)
    def _(i):
        hole = places[1, i]
        source = places[2, i]
        match_ref[hole * groups + source] = jnp.float32(1.0)
        position = (slots - counts(source)[0]) * groups + extra_of(source, off_b, len_b, groups)[0]
        meta_ref[HOLES + hole] = position


def pack(lengths, dealing, ids, x, cotangent, groups, size):
    rows, width = x.shape
    share = rows // groups // size
    whole = lambda *shape: pl.BlockSpec(shape, lambda i, *refs: (0,) * len(shape))
    smem = pl.BlockSpec(memory_space=pltpu.SMEM)
    shapes = [(groups, share, width), (groups, 1, width), (groups, share + 16, width)]
    return pl.pallas_call(
        functools.partial(pack_kernel, groups, size),
        grid_spec=pltpu.PrefetchScalarGridSpec(
            num_scalar_prefetch=3,
            grid=(1,),
            in_specs=[whole(rows, width)] * 2,
            out_specs=[whole(*shape) for shape in shapes] + [smem] * 4,
            scratch_shapes=[pltpu.SMEM((3, max(lengths.shape[0], groups + 1)), jnp.int32)],
        ),
        out_shape=[jax.ShapeDtypeStruct(shape, BF) for shape in shapes]
        + [
            jax.ShapeDtypeStruct((HOLES + groups,), jnp.int32),
            jax.ShapeDtypeStruct((4, 1 + lengths.shape[0]), jnp.int32),
            jax.ShapeDtypeStruct((groups * groups,), F32),
            jax.ShapeDtypeStruct((rows // ROWS * 8,), jnp.int32),
        ],
        compiler_params=pltpu.CompilerParams(vmem_limit_bytes=VMEM_LIMIT),
        cost_estimate=pl.CostEstimate(flops=0, bytes_accessed=20 << 20, transcendentals=0),
        name="pack",
    )(lengths, dealing, ids, x, cotangent)


def place(row, groups):
    sub = BLOCK // groups
    inside = rem(row, BLOCK)
    return div(inside, sub), div(row, BLOCK) * sub + rem(inside, sub)


def count_first(meta, source, groups):
    turned, extra = extra_of(source, meta[3], meta[5], groups)
    return turned, div(meta[5], groups) + extra


def in_second(meta, row, groups):
    source, slot = place(row, groups)
    return jnp.where(slot < count_first(meta, source, groups)[1], 0, 1)


def positions_of(meta, row, groups, slots):
    source, slot = place(row, groups)
    turned, count = count_first(meta, source, groups)
    turned_b = rem(source - meta[4] + groups, groups)
    position = jnp.where(slot < count, slot * groups + turned, (slot - count) * groups + turned_b)
    for g in range(groups):
        fills = meta[HOLES + g]
        here = (slot == slots - 1) & (source == g) & (fills >= 0)
        position = jnp.where(here, fills, position)
    return position


def spare_row(match_ref, groups, hole, rows):
    total = rows[0] * match_ref[hole * groups]
    flag = match_ref[hole * groups]
    for source in range(1, groups):
        weight = match_ref[hole * groups + source]
        total = total + rows[source] * weight
        flag = flag + weight
    return total, flag


def project_kernel(
    groups,
    packed,
    meta,
    match_ref,
    x_in_ref,
    over_ref,
    w_ref,
    freq_ref,
    q_ref,
    k_ref,
    v_ref,
    krow_ref,
    vrow_ref,
    cos_ref,
    sin_ref,
    x_ref,
    own_ref,
):
    index = pl.program_id(0)
    parts = pl.num_programs(0)
    share, width = x_ref.shape[1:]
    heads = q_ref.shape[0] // HEAD
    local = heads * HEAD
    sub = BLOCK // groups
    if packed:
        for i in range(share // BLOCK):
            for g in range(groups):
                base = i * BLOCK + g * sub
                x_ref[0, base : base + sub, :] = x_in_ref[0, g, i * sub : (i + 1) * sub, :]

        @pl.when(index == parts - 1)
        def _():
            rows = [over_ref[g].astype(F32) for g in range(groups)]
            at_end = lax.broadcasted_iota(jnp.int32, (16, 1), 0) == 15
            for g in range(groups):
                end = share - BLOCK + (g + 1) * sub
                spare, _ = spare_row(match_ref, groups, g, rows)
                old = x_ref[0, end - 16 : end, :].astype(F32)
                new = jnp.where(at_end & (meta[HOLES + g] >= 0), spare, old)
                x_ref[0, end - 16 : end, :] = new.astype(BF)
    else:
        x_ref[...] = x_in_ref[...]

    @pl.when(index == meta[2])
    def _():
        own_ref[...] = x_ref[0]

    row = lax.broadcasted_iota(jnp.int32, (1, share), 1) + index * share
    position = positions_of(meta, row, groups, parts * share // groups)
    angles = freq_ref[...] * position.astype(F32)
    cosine = jnp.cos(angles)
    sine = jnp.sin(angles)
    cos_ref[...] = cosine
    sin_ref[...] = sine
    projected = mm(w_ref[...], x_ref[0], 1, 1)
    for part, out_ref, scale in ((0, q_ref, HEAD ** (-0.5) / LOG_2), (1, k_ref, 1.0)):
        for head in range(heads):
            base = part * local + head * HEAD
            first = projected[base : base + HALF]
            second = projected[base + HALF : base + HEAD]
            turned = jnp.concatenate(
                [first * cosine - second * sine, second * cosine + first * sine], 0
            )
            out_ref[head * HEAD : (head + 1) * HEAD, :] = (turned * scale).astype(BF)
            if part == 1:
                krow_ref[head] = turned.T.astype(BF)
    for head in range(heads):
        base = 2 * local + head * HEAD
        value = projected[base : base + HEAD]
        rest = lax.broadcasted_iota(jnp.int32, (PADDED - HEAD, share), 0) == 0
        v_ref[head * PADDED : (head + 1) * PADDED, :] = jnp.concatenate(
            [value, jnp.where(rest, 1.0, 0.0)], 0
        ).astype(BF)
        vrow_ref[head] = value.T.astype(BF)


def project(meta, match, x_rel, over, w_t, freq, groups, packed):
    parts = x_rel.shape[0]
    width = x_rel.shape[-1]
    share = x_rel.size // parts // width
    rows = parts * share
    local = w_t.shape[0] // 3
    heads = local // HEAD
    shape = jax.ShapeDtypeStruct
    columns = lambda *lead: pl.BlockSpec(lead + (share,), lambda i, meta: (0,) * len(lead) + (i,))
    tall_spec = pl.BlockSpec((heads, share, HEAD), lambda i, meta: (0, i, 0))
    whole = lambda *shape: pl.BlockSpec(shape, lambda i, meta: (0,) * len(shape))
    lead = x_rel.shape[1:]
    return pl.pallas_call(
        functools.partial(project_kernel, groups, packed),
        grid_spec=pltpu.PrefetchScalarGridSpec(
            num_scalar_prefetch=1,
            grid=(parts,),
            in_specs=[
                pl.BlockSpec(memory_space=pltpu.SMEM),
                pl.BlockSpec(
                    (1,) + lead, lambda i, meta: (jnp.bitwise_xor(i, meta[2]),) + (0,) * len(lead)
                ),
                whole(*over.shape),
                whole(3 * local, width),
                whole(HALF, 1),
            ],
            out_specs=[
                columns(local),
                columns(local),
                columns(heads * PADDED),
                tall_spec,
                tall_spec,
                columns(HALF),
                columns(HALF),
                pl.BlockSpec((1, share, width), lambda i, meta: (i, 0, 0)),
                whole(share, width),
            ],
        ),
        out_shape=[
            shape((local, rows), BF),
            shape((local, rows), BF),
            shape((heads * PADDED, rows), BF),
            shape((heads, rows, HEAD), BF),
            shape((heads, rows, HEAD), BF),
            shape((HALF, rows), F32),
            shape((HALF, rows), F32),
            shape((parts, share, width), BF),
            shape((share, width), BF),
        ],
        compiler_params=pltpu.CompilerParams(vmem_limit_bytes=VMEM_LIMIT),
        cost_estimate=pl.CostEstimate(
            flops=rows * width, bytes_accessed=1 << 20, transcendentals=0
        ),
        name="project",
    )(meta, match, x_rel, over, w_t, freq)


def visible(info, index, q_blocks, k_blocks, count):
    is_a = (index + 1) * q_blocks <= info[0]
    is_b = index * q_blocks >= info[1]
    pure = is_a | is_b
    end_a = info[0] // k_blocks
    start_b = (info[1] + k_blocks - 1) // k_blocks
    plain_low = jnp.where(is_b, start_b, 0)
    plain_high = jnp.where(is_b, count, jnp.where(is_a, end_a, 0))
    return plain_low, plain_high, jnp.where(pure, end_a, 0), jnp.where(pure, start_b, count)


def attend_kernel(groups, info, q_ref, k_ref, v_ref, o_ref, lse_ref, acc_ref):
    index = pl.program_id(0)
    heads, rows, _ = k_ref.shape
    width = q_ref.shape[1]
    tall = v_ref.shape[0] // heads
    spans_ = visible(info, index, width // BLOCK, KEYS // BLOCK, rows // KEYS)
    acc_ref[...] = jnp.zeros_like(acc_ref)
    query_ids = lax.broadcasted_iota(jnp.int32, (1, width), 1) + index * width
    key_ids = lax.broadcasted_iota(jnp.int32, (KEYS, 1), 0)
    ids = range(heads)

    def step(masked, j, tops):
        keys = pl.ds(pl.multiple_of(j * KEYS, KEYS), KEYS)
        scores = [mm(k_ref[h, keys, :], q_ref[h * HEAD : (h + 1) * HEAD, :], 1, 0) for h in ids]
        if masked:
            same = in_second(info, key_ids + j * KEYS, groups) == in_second(info, query_ids, groups)
            scores = [jnp.where(same, s, NEGATIVE) for s in scores]
        new = [jnp.maximum(tops[h], jnp.max(scores[h], 0, keepdims=True)) for h in ids]
        weights = [jnp.exp2(scores[h] - new[h]).astype(BF) for h in ids]
        shrink = [jnp.exp2(tops[h] - new[h]) for h in ids]
        sums = [mm(v_ref[h * tall : (h + 1) * tall, keys], weights[h], 1, 0) for h in ids]
        for h in ids:
            part = slice(h * tall, (h + 1) * tall)
            acc_ref[part, :] = acc_ref[part, :] * shrink[h] + sums[h]
        return tuple(new)

    tops = (jnp.full((1, width), START, F32),) * heads
    tops = lax.fori_loop(spans_[0], spans_[1], functools.partial(step, False), tops)
    tops = lax.fori_loop(spans_[2], spans_[3], functools.partial(step, True), tops)
    for h in ids:
        total = acc_ref[h * tall + HEAD : h * tall + HEAD + 1, :]
        out = (acc_ref[h * tall : h * tall + HEAD, :] / total).astype(BF)
        each = o_ref.shape[2]
        for i in range(width // each):
            o_ref[i, h * HEAD : (h + 1) * HEAD, :] = out[:, i * each : (i + 1) * each]
        lse_ref[h : h + 1, :] = tops[h] + jnp.log2(total)


def attend(info, q, k_rows, v, groups):
    local, rows = q.shape
    heads = local // HEAD
    return pl.pallas_call(
        functools.partial(attend_kernel, groups),
        grid_spec=pltpu.PrefetchScalarGridSpec(
            num_scalar_prefetch=1,
            grid=(rows // QUERIES,),
            in_specs=[
                pl.BlockSpec((local, QUERIES), lambda i, info: (0, i)),
                pl.BlockSpec((heads, rows, HEAD), lambda i, info: (0, 0, 0)),
                pl.BlockSpec(v.shape, lambda i, info: (0, 0)),
            ],
            out_specs=[
                pl.BlockSpec((QUERIES // BLOCK, local, BLOCK), lambda i, info: (i, 0, 0)),
                pl.BlockSpec((heads, QUERIES), lambda i, info: (0, i)),
            ],
            scratch_shapes=[pltpu.VMEM((v.shape[0], QUERIES), F32)],
        ),
        out_shape=[
            jax.ShapeDtypeStruct((rows // BLOCK, local, BLOCK), BF),
            jax.ShapeDtypeStruct((heads, rows), F32),
        ],
        compiler_params=pltpu.CompilerParams(vmem_limit_bytes=VMEM_LIMIT),
        cost_estimate=pl.CostEstimate(
            flops=2 * rows * rows * HEAD * heads,
            bytes_accessed=8 << 20,
            transcendentals=0,
        ),
        name="attend",
    )(info, q, k_rows, v)


def unturn(grad, cosine, sine):
    first = grad[:HALF]
    second = grad[HALF:]
    return jnp.concatenate(
        [first * cosine + second * sine, second * cosine - first * sine], 0
    ).astype(BF)


def attend_back_kernel(groups, info, q_ref, krow_ref, k_ref, vrow_ref, o_ref, *refs):
    count = QUERIES // BLOCK
    do_refs = refs[:count]
    lse_ref, cos_ref, sin_ref, out_ref, up_ref, dq_ref, dk_ref, dv_ref = refs[count:]
    index = pl.program_id(0)
    heads, rows, _ = krow_ref.shape
    width = heads * HEAD
    parts, _, share = out_ref.shape
    each = share // BLOCK
    ids = range(heads)
    part = [slice(h * HEAD, (h + 1) * HEAD) for h in ids]

    @pl.when(index == 0)
    def _():
        dk_ref[...] = jnp.zeros_like(dk_ref)
        dv_ref[...] = jnp.zeros_like(dv_ref)

    dq_ref[...] = jnp.zeros_like(dq_ref)
    query_ids = lax.broadcasted_iota(jnp.int32, (1, QUERIES), 1) + index * QUERIES
    key_ids = lax.broadcasted_iota(jnp.int32, (KEYS, 1), 0)
    deltas = []
    for i, ref in enumerate(do_refs):
        columns = slice(i * BLOCK, (i + 1) * BLOCK)
        up_ref[:, columns] = ref[0]
        terms = ref[0].astype(F32) * o_ref[i].astype(F32)
        deltas.append([jnp.sum(terms[p], 0, keepdims=True) for p in part])
    delta = [jnp.concatenate([halves[h] for halves in deltas], 1) for h in ids]
    spans_ = visible(info, index, QUERIES // BLOCK, KEYS // BLOCK, rows // KEYS)

    def step(masked, j, carry):
        keys = pl.ds(pl.multiple_of(j * KEYS, KEYS), KEYS)
        if masked:
            same = in_second(info, key_ids + j * KEYS, groups) == in_second(info, query_ids, groups)
        for h in ids:
            queries = q_ref[part[h], :]
            upstream = up_ref[part[h], :]
            scores = mm(krow_ref[h, keys, :], queries, 1, 0)
            grad_soft = mm(vrow_ref[h, keys, :], upstream, 1, 0)
            if masked:
                scores = jnp.where(same, scores, NEGATIVE)
            soft = jnp.exp2(scores - lse_ref[h : h + 1, :])
            grad_scores = (soft * (grad_soft - delta[h])).astype(BF)
            dv_ref[part[h], keys] += mm(upstream, soft.astype(BF), 1, 1)
            dk_ref[part[h], keys] += mm(queries, grad_scores, 1, 1)
            dq_ref[part[h], :] += mm(k_ref[part[h], keys], grad_scores, 1, 0)
        return carry

    lax.fori_loop(spans_[0], spans_[1], functools.partial(step, False), 0)
    lax.fori_loop(spans_[2], spans_[3], functools.partial(step, True), 0)

    for i in range(QUERIES // BLOCK):
        block = index * (QUERIES // BLOCK) + i
        columns = pl.ds(pl.multiple_of(block * BLOCK, BLOCK), BLOCK)
        inside = pl.ds(pl.multiple_of(lax.rem(block, each) * BLOCK, BLOCK), BLOCK)
        for h in ids:
            out_ref[lax.div(block, each), part[h], inside] = unturn(
                dq_ref[part[h], i * BLOCK : (i + 1) * BLOCK] * HEAD ** (-0.5),
                cos_ref[:, columns],
                sin_ref[:, columns],
            )

    @pl.when(index == pl.num_programs(0) - 1)
    def _():
        @pl.loop(0, parts)
        def _(j):
            columns = pl.ds(pl.multiple_of(j * share, share), share)
            for h in ids:
                base = width + h * HEAD
                out_ref[j, base : base + HEAD, :] = unturn(
                    dk_ref[part[h], columns] * LOG_2, cos_ref[:, columns], sin_ref[:, columns]
                )
                base = 2 * width + h * HEAD
                out_ref[j, base : base + HEAD, :] = dv_ref[part[h], columns].astype(BF)


def attend_back(info, q, k_rows, k, v_rows, o, do, lse, cosine, sine, groups):
    parts = do.shape[0]
    local, rows = q.shape
    heads = local // HEAD
    blocks = rows // BLOCK
    each = blocks // parts
    whole = lambda *shape: pl.BlockSpec(shape, lambda i, info: (0,) * len(shape))
    count = QUERIES // BLOCK

    def upstream_spec(k):
        def pick(i, info):
            block = i * count + k
            return jnp.bitwise_xor(block // each, info[2]), 0, block % each

        return pl.BlockSpec((1, local, BLOCK), pick)

    return pl.pallas_call(
        functools.partial(attend_back_kernel, groups),
        grid_spec=pltpu.PrefetchScalarGridSpec(
            num_scalar_prefetch=1,
            grid=(rows // QUERIES,),
            in_specs=[
                pl.BlockSpec((local, QUERIES), lambda i, info: (0, i)),
                whole(heads, rows, HEAD),
                whole(local, rows),
                whole(heads, rows, HEAD),
                pl.BlockSpec((count, local, BLOCK), lambda i, info: (i, 0, 0)),
                *[upstream_spec(k) for k in range(count)],
                pl.BlockSpec((heads, QUERIES), lambda i, info: (0, i)),
                whole(HALF, rows),
                whole(HALF, rows),
            ],
            out_specs=whole(parts, 3 * local, rows // parts),
            scratch_shapes=[
                pltpu.VMEM((local, QUERIES), BF),
                pltpu.VMEM((local, QUERIES), F32),
                pltpu.VMEM((local, rows), F32),
                pltpu.VMEM((local, rows), F32),
            ],
        ),
        out_shape=jax.ShapeDtypeStruct((parts, 3 * local, rows // parts), BF),
        compiler_params=pltpu.CompilerParams(vmem_limit_bytes=VMEM_LIMIT),
        cost_estimate=pl.CostEstimate(
            flops=2 * 5 * rows * rows * 256 * heads // 2,
            bytes_accessed=16 << 20,
            transcendentals=heads * rows * rows // 2,
        ),
        name="attend_back",
    )(info, q, k_rows, k, v_rows, o, *[do] * count, lse, cosine, sine)


def project_back_kernel(meta, d_ref, x_ref, w_ref, back_ref, grad_ref, acc_ref):
    index = pl.program_id(0)

    @pl.when(index == 0)
    def _():
        acc_ref[...] = jnp.zeros_like(acc_ref)

    d_t = d_ref[0]
    back_ref[0] = mm(d_t, w_ref[...], 0, 0).astype(BF)
    acc_ref[...] += mm(d_t, x_ref[0], 1, 0)

    @pl.when(index == pl.num_programs(0) - 1)
    def _():
        grad_ref[...] = acc_ref[...].T.astype(BF)


def project_back(meta, d_qkv_t, x_all, w_t):
    parts, local, share = d_qkv_t.shape
    width = w_t.shape[1]
    relative = lambda i, meta: (jnp.bitwise_xor(i, meta[2]), 0, 0)
    whole = lambda *shape: pl.BlockSpec(shape, lambda i, meta: (0,) * len(shape))
    return pl.pallas_call(
        project_back_kernel,
        grid_spec=pltpu.PrefetchScalarGridSpec(
            num_scalar_prefetch=1,
            grid=(parts,),
            in_specs=[
                pl.BlockSpec((1, local, share), lambda i, meta: (i, 0, 0)),
                pl.BlockSpec((1, share, width), lambda i, meta: (i, 0, 0)),
                whole(local, width),
            ],
            out_specs=[
                pl.BlockSpec((1, share, width), relative),
                whole(width, local),
            ],
            scratch_shapes=[pltpu.VMEM((local, width), F32)],
        ),
        out_shape=[
            jax.ShapeDtypeStruct((parts, share, width), BF),
            jax.ShapeDtypeStruct((width, local), BF),
        ],
        compiler_params=pltpu.CompilerParams(vmem_limit_bytes=VMEM_LIMIT),
        cost_estimate=pl.CostEstimate(
            flops=4 * parts * share * local * width, bytes_accessed=15 << 20, transcendentals=0
        ),
        name="project_back",
    )(meta, d_qkv_t, x_all, w_t)


MESH = pl.DeviceIdType.MESH


def greet(groups, steps, d, t):
    barrier = pltpu.get_barrier_semaphore()
    for k in range(1, groups):
        pl.semaphore_signal(
            barrier, inc=1, device_id=(lax.rem(d + k, groups), t), device_id_type=MESH
        )
    for step in steps:
        pl.semaphore_signal(
            barrier, inc=1, device_id=(d, jnp.bitwise_xor(t, step)), device_id_type=MESH
        )
    pl.semaphore_wait(barrier, groups - 1 + len(steps))


def remote(src, dst, send, recv, device):
    return pltpu.make_async_remote_copy(
        src_ref=src,
        dst_ref=dst,
        send_sem=send,
        recv_sem=recv,
        device_id=device,
        device_id_type=MESH,
    )


class Spread:
    def __init__(self, out, sems, groups, d, t):
        self.out, self.sems, self.groups, self.d, self.t = out, sems, groups, d, t

    def at(self, r, k, rest):
        return self.out.at[(r, lax.rem(self.d - k + self.groups, self.groups)) + rest]

    def arrival(self, source, k, rest, where):
        send, recv = self.sems
        to = lax.rem(self.d + k, self.groups)
        return remote(
            source, self.at(0, 0, rest), send.at[(0, k) + where], recv.at[(0, k) + where], (to, self.t)
        )

    def across(self, k, rest, where):
        send, recv = self.sems
        return remote(
            self.at(0, k, rest),
            self.at(2, k, rest),
            send.at[(2, k) + where],
            recv.at[(2, k) + where],
            (self.d, jnp.bitwise_xor(self.t, 2)),
        )

    def beside(self, r, k, rest, where):
        send, recv = self.sems
        return remote(
            self.at(r, k, rest),
            self.at(r + 1, k, rest),
            send.at[(r + 1, k) + where],
            recv.at[(r + 1, k) + where],
            (self.d, jnp.bitwise_xor(self.t, 1)),
        )


def norm_forward(resid_rows, gain_vec, shift_vec):
    row_mean = jnp.mean(resid_rows, -1, keepdims=True)
    centred = resid_rows - row_mean
    inverse = lax.rsqrt(jnp.mean(centred * centred, -1, keepdims=True) + EPSILON)
    unit_rows = centred * inverse
    return (unit_rows * gain_vec + shift_vec, unit_rows, inverse)


def norm_backward(upstream, unit_rows, inverse, gain_vec):
    scaled = upstream * gain_vec
    inner_term = (
        scaled
        - jnp.mean(scaled, -1, keepdims=True)
        - unit_rows * jnp.mean(scaled * unit_rows, -1, keepdims=True)
    )
    return (
        inner_term * inverse,
        jnp.sum(upstream * unit_rows, 0, keepdims=True),
        jnp.sum(upstream, 0, keepdims=True),
    )


def middle_kernel(size, groups, count, *refs):
    x_ref, match_ref, cot_ref, over_ref, norm_ref, blocks_ref = refs[:6]
    weights_hbm = refs[6 : 6 + count]
    (
        result_ref,
        grad_one_ref,
        d_heads_ref,
        heads_ref,
        normed_t_ref,
        d_branch_t_ref,
        d_attn_t_ref,
        hidden_ref,
        d_gu_ref,
        norm_grad_ref,
        w_out_ref,
        w_gu_ref,
        w_down_ref,
        slope_ref,
        swish_ref,
        normed_ref,
        sum_ref,
        arrived_ref,
        sems,
        sends,
        recvs,
        keep,
    ) = refs[6 + count :]
    index = pl.program_id(0)
    first = index == 0
    d = lax.axis_index("dp")
    t = lax.axis_index("tensor")
    subs, local, _ = arrived_ref.shape[1:]
    inner = w_down_ref.shape[2]
    ids = (0, 2, 1, 3)
    part = [slice(r * local, (r + 1) * local) for r in range(size)]
    core = (d, jnp.bitwise_xor(t, 1))
    targets = (lambda r: w_out_ref.at[part[r]], lambda r: w_gu_ref.at[r], lambda r: w_down_ref.at[r])

    def weight_copies(kind, r):
        target = targets[kind](r)
        pieces = [(weights_hbm[2 * kind + r // 2], target)]
        if kind == 2 and r >= 2:
            pieces = []
            for i in range(2):
                half = weights_hbm[5 + i]
                low = pl.multiple_of(lax.rem(d + i, 2) * half.shape[0], 16)
                pieces.append((half, target.at[pl.ds(low, half.shape[0])]))
        copies = []
        for i, (source, place) in enumerate(pieces):
            recv = sems.at[kind, r, i]
            if r == 1 or r == 3:
                copies.append(remote(source, place, sems.at[kind, r - 1 + size, i], recv, core))
            else:
                copies.append(pltpu.make_async_copy(source, place, recv))
        return copies

    def weight_start(kind, r):
        for copy in weight_copies(kind, r):
            copy.start()

    def weight_wait(kind, r):
        for copy in weight_copies(kind, r):
            if r % 2 == 0:
                copy.wait()
            else:
                copy.wait_recv()

    def heads_copy(r, i):
        other = jnp.bitwise_xor(t, r)
        return remote(
            blocks_ref.at[other * subs + i],
            arrived_ref.at[r, i],
            sends.at[r, i],
            recvs.at[r, i],
            (d, other),
        )

    own_copy = pltpu.make_async_copy(blocks_ref.at[pl.ds(t * subs, subs)], arrived_ref.at[0], keep)

    @pl.when(first)
    def _():
        own_copy.start()
        for r in (0, 2):
            weight_start(0, r)
        greet(1, (1, 2, 3), d, t)
        for r in (2, 3, 1):
            heads_copy(r, 0).start()
        for r in (1, 3):
            weight_start(0, r)
        for r in ids:
            for kind in (1, 2):
                weight_start(kind, r)
        own_copy.wait()
        for r in ids:
            weight_wait(0, r)

    @pl.when(first)
    def _():
        norm_grad_ref[...] = jnp.zeros_like(norm_grad_ref)

    for r in ids[1:]:
        heads_copy(r, index).wait_recv()
        heads_copy(r, index).wait_send()

    @pl.when(index < subs - 1)
    def _():
        for r in (2, 3, 1):
            heads_copy(r, index + 1).start()

    for r in ids:
        heads_ref[r] = arrived_ref[r, index]
    heads_out = jnp.concatenate([arrived_ref[r, index] for r in range(size)], 0)
    attn = mm(heads_out, w_out_ref[...], 0, 0)
    gain_one, gain_two, shift_one, shift_two = (norm_ref[i : i + 1, :] for i in range(4))
    normed_one, unit_one, inverse_one = norm_forward(
        x_ref[...].astype(F32) + attn, gain_one, shift_one
    )
    normed_ref[...] = normed_one.astype(BF)
    normed_t_ref[...] = normed_one.T.astype(BF)
    sum_ref[...] = normed_one

    @pl.loop(0, size, unroll=2)
    def _(i):
        r = lax.rem(i, 2) * 2 + lax.div(i, 2)
        for k in ids:

            @pl.when(first & (r == k))
            def _():
                weight_wait(1, k)
                weight_wait(2, k)

        both = mm(normed_ref[...], w_gu_ref[r], 1, 0)
        gate = both[:, :inner]
        up = both[:, inner:]
        sig = 0.5 + 0.5 * jnp.tanh(0.5 * gate)
        swish = gate * sig
        hidden = (swish * up).astype(BF)
        swish_ref[r] = swish
        slope_ref[r] = up * (sig + swish * (1.0 - sig))
        hidden_ref[r] = hidden
        sum_ref[...] += mm(hidden, w_down_ref[r], 1, 1)

    result, unit_two, inverse_two = norm_forward(sum_ref[...], gain_two, shift_two)
    result_ref[...] = result.astype(BF)
    if groups:
        sub = BLOCK // groups
        spares = [over_ref[g, 0:1, :].astype(F32) for g in range(groups)]
        in_last = jnp.where((index == subs - 1) & (t == size - 1), 1.0, 0.0)
        ends = lax.broadcasted_iota(jnp.int32, (sub, 1), 0) == sub - 1
        pieces = []
        for g in range(groups):
            piece = cot_ref[g].astype(F32)
            spare, flag = spare_row(match_ref, groups, g, spares)
            fix = jnp.where(ends, flag * in_last, 0.0)
            pieces.append(piece * (1.0 - fix) + spare * fix)
        cot = jnp.concatenate(pieces, 0)
    else:
        cot = cot_ref[...].astype(F32)
    grad_two, d_gain_two, d_shift_two = norm_backward(cot, unit_two, inverse_two, gain_two)
    normed_ref[...] = grad_two.astype(BF)
    d_branch_t_ref[...] = grad_two.T.astype(BF)
    sum_ref[...] = grad_two

    @pl.loop(0, size, unroll=2)
    def _(r):
        grad_hidden = mm(normed_ref[...], w_down_ref[r], 1, 0)
        d_gate = (grad_hidden * slope_ref[r]).astype(BF)
        d_up = (grad_hidden * swish_ref[r]).astype(BF)
        d_gu_ref[r, :, :inner] = d_gate
        d_gu_ref[r, :, inner:] = d_up
        sum_ref[...] += mm(jnp.concatenate([d_gate, d_up], 1), w_gu_ref[r], 1, 1)

    grad_one, d_gain_one, d_shift_one = norm_backward(
        sum_ref[...], unit_one, inverse_one, gain_one
    )
    grad_one_ref[...] = grad_one
    d_attn_t = grad_one.T.astype(BF)
    d_attn_t_ref[...] = d_attn_t
    d_heads = mm(w_out_ref[...], d_attn_t, 1, 0).astype(BF)
    for r in ids:
        d_heads_ref[r] = d_heads[part[r]]
    for i, grad in enumerate((d_gain_one, d_gain_two, d_shift_one, d_shift_two)):
        norm_grad_ref[i : i + 1, :] += grad

    @pl.when(index == subs - 1)
    def _():
        for kind in range(3):
            for r in (1, 3):
                for copy in weight_copies(kind, r):
                    copy.wait_send()


def middle(x_own, match, cot, norms, o_blocks, size, *weights):
    rows, width = x_own.shape
    local = o_blocks.shape[1]
    inner = weights[4].shape[1]
    block = pl.BlockSpec((BLOCK, width), lambda i: (i, 0))
    turned = pl.BlockSpec((width, BLOCK), lambda i: (0, i))
    anywhere = pl.BlockSpec(memory_space=pl.ANY)
    shape = jax.ShapeDtypeStruct
    groups = cot.shape[0] if cot.ndim == 3 else 0
    if groups:
        sub = BLOCK // groups
        last = cot.shape[1] // 16 - 1
        cot_specs = [
            pl.BlockSpec((groups, sub, width), lambda i: (0, i, 0)),
            pl.BlockSpec((groups, 16, width), lambda i: (0, last, 0)),
        ]
    else:
        cot_specs = [block, pl.BlockSpec((16, width), lambda i: (0, 0))]
    return pl.pallas_call(
        functools.partial(middle_kernel, size, groups, len(weights)),
        grid=(rows // BLOCK,),
        in_specs=[block, pl.BlockSpec(memory_space=pltpu.SMEM)]
        + cot_specs
        + [pl.BlockSpec(norms.shape, lambda i: (0, 0))]
        + [anywhere] * (1 + len(weights)),
        out_specs=[
            block,
            block,
            pl.BlockSpec((size, local, BLOCK), lambda i: (0, 0, i)),
            pl.BlockSpec((size, local, BLOCK), lambda i: (0, 0, i)),
            turned,
            turned,
            turned,
            pl.BlockSpec((size, BLOCK, inner), lambda i: (0, i, 0)),
            pl.BlockSpec((size, BLOCK, 2 * inner), lambda i: (0, i, 0)),
            pl.BlockSpec((8, width), lambda i: (0, 0)),
        ],
        out_shape=[
            shape((rows, width), BF),
            shape((rows, width), F32),
            shape((size, local, rows), BF),
            shape((size, local, rows), BF),
            shape((width, rows), BF),
            shape((width, rows), BF),
            shape((width, rows), BF),
            shape((size, rows, inner), BF),
            shape((size, rows, 2 * inner), BF),
            shape((8, width), F32),
        ],
        scratch_shapes=[
            pltpu.VMEM((size * local, width), BF),
            pltpu.VMEM((size, width, 2 * inner), BF),
            pltpu.VMEM((size, width, inner), BF),
            pltpu.VMEM((size, BLOCK, inner), F32),
            pltpu.VMEM((size, BLOCK, inner), F32),
            pltpu.VMEM((BLOCK, width), BF),
            pltpu.VMEM((BLOCK, width), F32),
            pltpu.VMEM((size, rows // BLOCK, local, BLOCK), BF),
            pltpu.SemaphoreType.DMA((3, 2 * size, 2)),
            pltpu.SemaphoreType.DMA((size, rows // BLOCK)),
            pltpu.SemaphoreType.DMA((size, rows // BLOCK)),
            pltpu.SemaphoreType.DMA,
        ],
        compiler_params=pltpu.CompilerParams(
            collective_id=2, has_side_effects=True, vmem_limit_bytes=VMEM_LIMIT
        ),
        cost_estimate=pl.CostEstimate(
            flops=2 * rows * width * (6 * size * inner + 2 * size * local),
            bytes_accessed=40 << 20,
            transcendentals=rows * size * inner,
        ),
        name="middle",
    )(x_own, match, cot, cot, norms, o_blocks, *weights)


def product_tiles(left_ref, right_ref, store):
    @pl.loop(0, right_ref.shape[2] // TILE)
    def _(i):
        columns = pl.ds(pl.multiple_of(i * TILE, TILE), TILE)
        store(columns, mm(left_ref[...], right_ref[0, :, columns], 1, 0))


def weight_grads_tile(
    normed_t_ref, d_branch_t_ref, d_attn_t_ref, hidden_ref, d_gu_ref, heads_ref, norm_ref, store
):
    wide = d_gu_ref.shape[2]
    local = heads_ref.shape[1]
    product_tiles(normed_t_ref, d_gu_ref, store)
    d_out = mm(d_attn_t_ref[...], heads_ref[0], 1, 1)
    norm = norm_ref[...].T
    spare = -(local + norm.shape[1]) % 128
    tail = jnp.concatenate([d_out, norm, jnp.zeros((norm.shape[0], spare), F32)], 1)
    store(pl.ds(wide, tail.shape[1]), tail)
    base = wide + tail.shape[1]

    def shifted(columns, value):
        store(pl.ds(pl.multiple_of(base + columns.start, 128), columns.size), value)

    product_tiles(d_branch_t_ref, hidden_ref, shifted)


def weight_grads_kernel(*refs):
    out_ref = refs[-1]

    def store(columns, value):
        out_ref[0, :, columns] = value.astype(BF)

    weight_grads_tile(*refs[:-1], store)


def weight_grads(odd, normed_t, d_branch_t, d_attn_t, hidden, d_gu, heads, norm_grads):
    size, rows, inner = hidden.shape
    local = heads.shape[1]
    width = normed_t.shape[0]
    wide = 3 * inner + local + norm_grads.shape[0]
    wide = (wide + 127) // 128 * 128
    flat = pl.BlockSpec((width, rows), lambda i: (0, 0))
    pick = lambda i: (2 * i + odd, 0, 0)
    return pl.pallas_call(
        weight_grads_kernel,
        grid=(size // 2,),
        in_specs=[
            flat,
            flat,
            flat,
            pl.BlockSpec((1, rows, inner), pick),
            pl.BlockSpec((1, rows, 2 * inner), pick),
            pl.BlockSpec((1, local, rows), pick),
            pl.BlockSpec(norm_grads.shape, lambda i: (0, 0)),
        ],
        out_specs=pl.BlockSpec((1, width, wide), lambda i: (i, 0, 0)),
        out_shape=jax.ShapeDtypeStruct((size // 2, width, wide), BF),
        compiler_params=pltpu.CompilerParams(vmem_limit_bytes=VMEM_LIMIT),
        cost_estimate=pl.CostEstimate(
            flops=size * rows * width * (3 * inner + local), bytes_accessed=20 << 20, transcendentals=0
        ),
        name="weight_grads",
    )(normed_t, d_branch_t, d_attn_t, hidden, d_gu, heads, norm_grads)


def grads_kernel(groups, size, match_ref, *refs):
    tile_refs = refs[:7]
    (
        d_heads_ref,
        result_ref,
        wide_own_ref,
        wide_other_ref,
        down_ref,
        do_ref,
        home_ref,
        over_ref,
        sent_ref,
        got_ref,
        own_ref,
        spare_ref,
        s_grad,
        r_grad,
        s_heads,
        r_heads,
        sends,
        recvs,
        s_over,
        r_over,
        keep,
        outs,
    ) = refs[7:]
    step = pl.program_id(0)
    d = lax.axis_index("dp")
    t = lax.axis_index("tensor")
    chunks, _, sub, width = own_ref.shape
    core = (d, jnp.bitwise_xor(t, 1))
    body = Spread(home_ref, (sends, recvs), groups, d, t)
    extra = Spread(over_ref, (s_over, r_over), groups, d, t)

    def heads_copy(r):
        return remote(
            d_heads_ref.at[r],
            do_ref.at[r],
            s_heads.at[r],
            r_heads.at[r],
            (d, jnp.bitwise_xor(t, r)),
        )

    def grad_copy(i):
        return remote(sent_ref.at[i], got_ref.at[i], s_grad.at[i], r_grad.at[i], core)

    def own_copy(c):
        return pltpu.make_async_copy(own_ref.at[c, d], home_ref.at[0, d, c], keep.at[c])

    def arrival(c, k):
        return body.arrival(own_ref.at[c, lax.rem(d + k, groups)], k, (c,), (c,))

    def pass_on(c):
        own_copy(c).wait()
        for k in range(groups):
            if k > 0:
                arrival(c, k).wait_recv()
            body.across(k, (c,), (c,)).start()

    load = pltpu.make_async_copy(result_ref, own_ref, keep.at[chunks])
    own_heads = pltpu.make_async_copy(d_heads_ref.at[0], do_ref.at[0], keep.at[chunks + 1])
    own_over = pltpu.make_async_copy(spare_ref.at[d], over_ref.at[0, d], keep.at[chunks + 2])

    @pl.when(step == 0)
    def _():
        load.start()
        own_heads.start()
        greet(groups, (1, 2, 3), d, t)
        for r in (2, 3, 1):
            heads_copy(r).start()
        load.wait()
        for c in range(chunks):
            own_copy(c).start()
            for k in range(1, groups):
                arrival(c, k).start()
        last = [own_ref[chunks - 1, g, sub - 16 :, :].astype(F32)[15:16] for g in range(groups)]
        for to in range(groups):
            spare = last[0] * match_ref[to]
            for g in range(1, groups):
                spare = spare + last[g] * match_ref[g * groups + to]
            spare_ref[to] = spare.astype(BF)
        own_over.start()
        for k in range(1, groups):
            extra.arrival(spare_ref.at[lax.rem(d + k, groups)], k, (), ()).start()

    for c in range(chunks - 1):

        @pl.when(step == c + 2)
        def _():
            pass_on(c)

    @pl.when(step < 2)
    def _():
        def store(columns, value):
            sent_ref[step, :, columns] = value.astype(BF)

        weight_grads_tile(*tile_refs, store)
        grad_copy(step).start()

    @pl.when(step >= 2)
    def _():
        grad_copy(step - 2).wait_recv()
        grad_copy(step - 2).wait_send()

        def store(columns, value):
            sent_ref[step - 2, :, columns] = (
                value + got_ref[step - 2, :, columns].astype(F32)
            ).astype(BF)

        weight_grads_tile(*tile_refs, store)

    part = down_ref.shape[2]

    def leave(i):
        copies = [(sent_ref.at[i, :, pl.ds(0, WIDE)], (wide_own_ref, wide_other_ref)[i])]
        for g in range(groups):
            rest = sent_ref.at[i, pl.ds(g * part, part), pl.ds(WIDE, down_ref.shape[3])]
            copies.append((rest, down_ref.at[g, i]))
        return [
            pltpu.make_async_copy(source, target, outs.at[i, j])
            for j, (source, target) in enumerate(copies)
        ]

    for i in range(2):

        @pl.when(step == 2 + i)
        def _():
            for copy in leave(i):
                copy.start()

    @pl.when(step == size - 1)
    def _():
        for i in range(2):
            for copy in leave(i):
                copy.wait()
        own_over.wait()
        for k in range(groups):
            if k > 0:
                extra.arrival(spare_ref.at[0], k, (), ()).wait_recv()
            extra.across(k, (), ()).start()
            extra.beside(0, k, (), ()).start()
        for k in range(groups):
            extra.across(k, (), ()).wait_recv()
            extra.beside(2, k, (), ()).start()
        own_heads.wait()
        for r in range(1, size):
            heads_copy(r).wait_recv()
            heads_copy(r).wait_send()
        own_copy(chunks - 1).wait()
        for c in range(chunks):
            for k in range(groups):
                if k > 0 and c == chunks - 1:
                    arrival(c, k).wait_recv()
                if k > 0:
                    arrival(c, k).wait_send()
                if c < chunks - 1:
                    body.across(k, (c,), (c,)).wait_recv()
                    body.across(k, (c,), (c,)).wait_send()
        for k in range(groups):
            extra.beside(0, k, (), ()).wait_recv()
            extra.beside(2, k, (), ()).wait_recv()
            if k > 0:
                extra.arrival(spare_ref.at[0], k, (), ()).wait_send()
            extra.across(k, (), ()).wait_send()
            extra.beside(0, k, (), ()).wait_send()
            extra.beside(2, k, (), ()).wait_send()


def grads(
    match, groups, normed_t, d_branch_t, d_attn_t, hidden, d_gu, heads, norm_grads, d_heads, result
):
    size, rows, inner = hidden.shape
    local = heads.shape[1]
    width = normed_t.shape[0]
    chunks = rows // BLOCK
    sub = BLOCK // groups
    total = 3 * inner + (local + norm_grads.shape[0] + 127) // 128 * 128
    part = width // groups
    whole = lambda *shape: pl.BlockSpec(shape, lambda i: (0,) * len(shape))
    pick = lambda i: (jnp.where(i < 2, 2 * i + 1, 2 * i - 4), 0, 0)
    anywhere = pl.BlockSpec(memory_space=pl.ANY)
    dma = pltpu.SemaphoreType.DMA
    return pl.pallas_call(
        functools.partial(grads_kernel, groups, size),
        grid=(size,),
        in_specs=[
            pl.BlockSpec(memory_space=pltpu.SMEM),
            whole(width, rows),
            whole(width, rows),
            whole(width, rows),
            pl.BlockSpec((1, rows, inner), pick),
            pl.BlockSpec((1, rows, 2 * inner), pick),
            pl.BlockSpec((1, local, rows), pick),
            whole(*norm_grads.shape),
            anywhere,
            anywhere,
        ],
        out_specs=[
            anywhere,
            anywhere,
            anywhere,
            anywhere,
            anywhere,
            anywhere,
        ],
        out_shape=[
            jax.ShapeDtypeStruct((width, WIDE), BF),
            jax.ShapeDtypeStruct((width, WIDE), BF),
            jax.ShapeDtypeStruct((groups, 2, part, total - WIDE), BF),
            jax.ShapeDtypeStruct(d_heads.shape, BF),
            jax.ShapeDtypeStruct((3, groups, chunks, sub, width), BF),
            jax.ShapeDtypeStruct((size, groups, 1, width), BF),
        ],
        scratch_shapes=[
            pltpu.VMEM((2, width, total), BF),
            pltpu.VMEM((2, width, total), BF),
            pltpu.VMEM((chunks, groups, sub, width), BF),
            pltpu.VMEM((groups, 1, width), BF),
            dma((2,)),
            dma((2,)),
            dma((size,)),
            dma((size,)),
            dma((3, groups, chunks)),
            dma((3, groups, chunks)),
            dma((4, groups)),
            dma((4, groups)),
            dma((chunks + 3,)),
            dma((2, groups + 1)),
        ],
        compiler_params=pltpu.CompilerParams(
            collective_id=3, has_side_effects=True, vmem_limit_bytes=VMEM_LIMIT
        ),
        cost_estimate=pl.CostEstimate(
            flops=2 * size * rows * width * (3 * inner + local),
            bytes_accessed=80 << 20,
            transcendentals=0,
        ),
        name="grads",
    )(
        match,
        normed_t,
        d_branch_t,
        d_attn_t,
        hidden,
        d_gu,
        heads,
        norm_grads,
        d_heads,
        result.reshape(chunks, groups, sub, width),
    )


def swap(array, size, step):
    return lax.ppermute(array, "tensor", [(i, i ^ step) for i in range(size)])


def gather_members(own):
    size = lax.axis_size("tensor")
    across = swap(own, size, 2)
    return [own, swap(own, size, 1), across, swap(across, size, 1)]


def exchange_members(pieces):
    size = lax.axis_size("tensor")
    return [pieces[0]] + [swap(pieces[r], size, r) for r in range(1, size)]


def reduce_members(pieces):
    size = lax.axis_size("tensor")
    near = swap(pieces[1], size, 1)
    far = swap(pieces[3], size, 1)
    other = (pieces[2].astype(F32) + far.astype(F32)).astype(BF)
    across = swap(other, size, 2)
    return pieces[0].astype(F32) + near.astype(F32) + across.astype(F32)


def unpack_block(spots_ref, src_ref, i):
    window = ROWS + 16
    shape = (ROWS, window)
    rows = lax.broadcasted_iota(jnp.int32, shape, 0)
    steps = lax.broadcasted_iota(jnp.int32, shape, 1) - rows
    bound = spots_ref[8 * i + 6]
    total = None
    for k in range(2):
        group, start, shift = (spots_ref[8 * i + 3 * k + j] for j in range(3))
        wanted = rows < bound if k == 0 else rows >= bound
        hot = jnp.where((steps == shift) & wanted, 1.0, 0.0).astype(BF)
        tiles = [src_ref[group, start + j] for j in range(window // 16)]
        part = mm(hot, jnp.concatenate(tiles, 0), 1, 0)
        total = part if k == 0 else total + part
    return total.astype(BF)


def store_over(src_ref, over_ref, last):
    top = lax.broadcasted_iota(jnp.int32, (16, 1), 0) == 0
    end = src_ref.shape[1] - 1
    for g in range(src_ref.shape[0]):
        src_ref[g, end] = jnp.where(top, over_ref[last, g].astype(F32), 0.0).astype(BF)


def unpack_kernel(
    size, spots, me, home_ref, over_ref, result_ref, out_ref, result_out_ref, src_ref, sems
):
    tiles = home_ref.shape[2]
    step = pl.program_id(0)
    each = out_ref.shape[0] // ROWS

    def load(r):
        at = pl.ds(jnp.bitwise_xor(me[0], r) * tiles, tiles)
        return pltpu.make_async_copy(home_ref.at[r], src_ref.at[:, at], sems.at[r])

    @pl.when(step == 0)
    def _():
        for r in range(size):
            load(r).start()
        store_over(src_ref, over_ref, jnp.bitwise_xor(size - 1, me[0]))
        for r in range(size):
            load(r).wait()

    for i in range(each):
        out_ref[i * ROWS : (i + 1) * ROWS, :] = unpack_block(spots, src_ref, step * each + i)
    result_out_ref[...] = result_ref[...]


def unpack(spots, me, home, over, result):
    size, groups, share, width = home.shape
    rows = size * groups * share
    home = home.reshape(size, groups, share // 16, 16, width)
    whole = lambda *shape: pl.BlockSpec(shape, lambda i, *refs: (0,) * len(shape))
    anywhere = pl.BlockSpec(memory_space=pl.ANY)
    each = 4 * ROWS
    block = pl.BlockSpec((each, width), lambda i, *refs: (i, 0))
    return pl.pallas_call(
        functools.partial(unpack_kernel, size),
        grid_spec=pltpu.PrefetchScalarGridSpec(
            num_scalar_prefetch=2,
            grid=(rows // each,),
            in_specs=[anywhere, whole(*over.shape), block],
            out_specs=[block, block],
            scratch_shapes=[
                pltpu.VMEM((groups, size * share // 16 + 1, 16, width), BF),
                pltpu.SemaphoreType.DMA((size,)),
            ],
        ),
        out_shape=[jax.ShapeDtypeStruct((rows, width), BF)] * 2,
        compiler_params=pltpu.CompilerParams(vmem_limit_bytes=VMEM_LIMIT),
        cost_estimate=pl.CostEstimate(flops=0, bytes_accessed=30 << 20, transcendentals=0),
        name="unpack",
    )(spots, me, home, over, result)


def route_kernel(groups, size, send_ref, over_ref, out_ref, over_out_ref, sends, recvs, s_over, r_over, keep):
    d = lax.axis_index("dp")
    t = lax.axis_index("tensor")
    chunks = sends.shape[2]
    count = send_ref.shape[1] // chunks
    greet(groups, (1, 2), d, t)
    spread = Spread(out_ref, (sends, recvs), groups, d, t)

    def rows(c):
        return pl.ds(c * count, count)

    def own(c):
        return pltpu.make_async_copy(
            send_ref.at[d, rows(c)], out_ref.at[0, d, rows(c)], keep.at[c]
        )

    def arrival(c, k):
        return spread.arrival(send_ref.at[lax.rem(d + k, groups), rows(c)], k, (rows(c),), (c,))

    def across(c, k):
        return spread.across(k, (rows(c),), (c,))

    def beside(r, c, k):
        return spread.beside(r, k, (rows(c),), (c,))

    def over_copy(k):
        to = lax.rem(d + k, groups)
        return remote(over_ref.at[to], over_out_ref.at[d], s_over.at[k], r_over.at[k], (to, t))

    def pass_far(c):
        for k in range(groups):
            across(c, k).wait_recv()
            beside(2, c, k).start()

    own_over = pltpu.make_async_copy(over_ref.at[d], over_out_ref.at[d], keep.at[chunks])
    for c in range(chunks):
        own(c).start()
    own_over.start()
    for c in range(chunks):
        for k in range(1, groups):
            arrival(c, k).start()
    for k in range(1, groups):
        over_copy(k).start()
    for c in range(chunks):
        own(c).wait()
        for k in range(groups):
            if k > 0:
                arrival(c, k).wait_recv()
            across(c, k).start()
            beside(0, c, k).start()
        if c > 0:
            pass_far(c - 1)
    pass_far(chunks - 1)
    own_over.wait()
    for k in range(groups):
        for c in range(chunks):
            beside(0, c, k).wait_recv()
            beside(2, c, k).wait_recv()
            if k > 0:
                arrival(c, k).wait_send()
            across(c, k).wait_send()
            beside(0, c, k).wait_send()
            beside(2, c, k).wait_send()
        if k > 0:
            over_copy(k).wait_recv()
            over_copy(k).wait_send()


def route(send, over, size):
    groups = send.shape[0]
    anywhere = pl.BlockSpec(memory_space=pl.ANY)
    return pl.pallas_call(
        functools.partial(route_kernel, groups, size),
        in_specs=[anywhere, anywhere],
        out_specs=[anywhere, anywhere],
        out_shape=[
            jax.ShapeDtypeStruct((size,) + send.shape, BF),
            jax.ShapeDtypeStruct(over.shape, BF),
        ],
        scratch_shapes=[
            pltpu.SemaphoreType.DMA((4, groups, 3)),
            pltpu.SemaphoreType.DMA((4, groups, 3)),
            pltpu.SemaphoreType.DMA((groups,)),
            pltpu.SemaphoreType.DMA((groups,)),
            pltpu.SemaphoreType.DMA((4,)),
        ],
        compiler_params=pltpu.CompilerParams(collective_id=0, has_side_effects=True),
        cost_estimate=pl.CostEstimate(flops=0, bytes_accessed=60 << 20, transcendentals=0),
        name="route",
    )(send, over)


class Halving:
    def __init__(self, fetch, links, refs, sems):
        self.fetch, self.links = fetch, links
        self.out, self.got, self.held = refs
        self.send, self.recv = sems
        self.counts = [2 ** (len(links) - 1 - step) for step in range(len(links))]
        self.first = [sum(self.counts[:step]) for step in range(len(links))]

    def term(self, side, i):
        rest = [lax.rem(lax.div(i, 2**j), 2) for j in range(len(self.links) - 1)]
        return self.fetch(side, *rest)

    def copy(self, step, i):
        at = self.first[step] + i
        return remote(
            self.out.at[at], self.got.at[at], self.send.at[at], self.recv.at[at], self.links[step][1]
        )

    def start(self):
        for i in range(self.counts[0]):
            self.out[i] = self.term(1 - self.links[0][0], jnp.int32(i)).astype(BF)
            self.copy(0, i).start()

    def advance(self, step):
        for i in range(self.counts[step - 1]):
            self.copy(step - 1, i).wait_recv()
        own = self.links[step][0]
        for keep in (False, True):
            for j in range(self.counts[step]):
                i = (own if keep else 1 - own) + 2 * j
                value = self.term(self.links[0][0], i) if step == 1 else self.held[i]
                value = value + self.got[self.first[step - 1] + i].astype(F32)
                if keep:
                    self.held[j] = value
                else:
                    self.out[self.first[step] + j] = value.astype(BF)
                    self.copy(step, j).start()

    def total(self):
        last = len(self.links) - 1
        self.copy(last, 0).wait_recv()
        return self.held[0] + self.got[self.first[last]].astype(F32)

    def finish(self):
        for step, count in enumerate(self.counts):
            for i in range(count):
                self.copy(step, i).wait_send()


def settle_kernel(
    groups,
    size,
    match_ref,
    spots_ref,
    res_over_ref,
    d_hbm,
    x_hbm,
    w_hbm,
    one_hbm,
    wide_own_hbm,
    wide_other_hbm,
    down_hbm,
    res_hbm,
    home_ref,
    over_ref,
    result_hbm,
    gq_sum_ref,
    gu_sum_ref,
    down_sum_ref,
    out_sum_ref,
    norm_sum_ref,
    d_ref,
    x_ref,
    w_ref,
    one_ref,
    wide_own_ref,
    wide_other_ref,
    down_ref,
    down_sent_ref,
    down_got_ref,
    src_ref,
    out_ref,
    to_core_ref,
    from_core_ref,
    pair_ref,
    other_ref,
    own_ref,
    spare_ref,
    gq_ref,
    gq_acc_ref,
    *refs,
):
    halving_refs = tuple(refs[3 * i : 3 * i + 3] for i in range(3))
    (
        loads,
        s_res,
        r_res,
        s_half,
        r_half,
        sends,
        recvs,
        s_over,
        r_over,
        s_sum,
        r_sum,
        keep,
    ) = refs[9:]
    d = lax.axis_index("dp")
    t = lax.axis_index("tensor")
    chunks, _, sub, width = own_ref.shape
    sent = (chunks - 1) * sub // 16
    rest = sub // 16
    core = (d, jnp.bitwise_xor(t, 1))
    chip = (d, jnp.bitwise_xor(t, 2))

    def load(source, target, i):
        return pltpu.make_async_copy(source, target, loads.at[i])

    def load_d(r):
        part = jnp.bitwise_xor(t, r)
        return load(d_hbm.at[part], d_ref.at[part], r)

    load_w = load(w_hbm, w_ref, 4)
    load_x = load(x_hbm, x_ref, 5)
    load_one = load(one_hbm, one_ref, 6)
    load_wide = (load(wide_own_hbm, wide_own_ref, 7), load(wide_other_hbm, wide_other_ref, 8))
    load_down = load(down_hbm, down_ref, 11)
    down_copy = remote(down_sent_ref, down_got_ref, s_res.at[4], r_res.at[4], chip)

    def down_sum(member):
        total = down_ref[0, member].astype(F32)
        for g in range(1, groups):
            total = total + down_ref[g, member].astype(F32)
        return total


    def in_src(r, low, count):
        base = jnp.bitwise_xor(t, r) * (sent + rest)
        return src_ref.at[:, pl.ds(base + low, count)]

    def source_of(r, low, count):
        return res_hbm.at[r, :, pl.ds(low, count)]

    res_parts = (
        (source_of(0, 0, sent + rest), in_src(0, 0, sent + rest)),
        (source_of(2, 0, sent), in_src(2, 0, sent)),
        (in_src(2, sent, rest), in_src(2, sent, rest)),
    )
    load_res = [load(source, target, 9 + i) for i, (source, target) in enumerate(res_parts[:2])]
    beside_res = [
        remote(source, target, s_res.at[i], r_res.at[i], core)
        for i, (source, target) in enumerate(res_parts)
    ]
    across_res = remote(
        source_of(0, sent, rest), in_src(0, sent, rest), s_res.at[3], r_res.at[3], chip
    )

    load_w.start()
    load_d(3).start()
    load_d(2).start()
    greet(groups, (1, 2), d, t)

    def rows(c):
        return pl.ds(pl.multiple_of(c * BLOCK, BLOCK), BLOCK)

    def piece(r, c):
        return mm(d_ref[jnp.bitwise_xor(t, r), :, rows(c)], w_ref[...], 0, 0)

    def to_core(i, c):
        return remote(
            to_core_ref.at[i, c], from_core_ref.at[i, c], s_sum.at[i, c], r_sum.at[i, c], core
        )

    def other(c):
        return remote(pair_ref.at[c], other_ref.at[c], s_sum.at[2, c], r_sum.at[2, c], chip)

    load_w.wait()
    load_d(3).wait()
    load_d(1).start()
    load_d(0).start()
    load_wide[0].start()
    load_wide[1].start()
    load_d(2).wait()

    @pl.loop(0, chunks)
    def _(c):
        to_core_ref[0, c] = piece(3, c).astype(BF)
        to_core(0, c).start()
        value = piece(2, c)
        to_core(0, c).wait_recv()
        pair_ref[c] = (value + from_core_ref[0, c].astype(F32)).astype(BF)

        @pl.when(c == 0)
        def _():
            other(0).start()

    block_rows, _, inner = gu_sum_ref.shape

    def wide_rows(part, block):
        at = pl.ds(pl.multiple_of(block * block_rows, block_rows), block_rows)
        columns = slice(part * WIDE_PARTS[0], WIDE_PARTS[0] + part * WIDE_PARTS[1])
        return wide_own_ref[at, columns].astype(F32) + wide_other_ref[at, columns].astype(F32)

    def gq_rows(y, low, high):
        return gq_ref[y + 2 * low + 4 * high].astype(F32)

    link_y, link_low, link_high = (
        (lax.rem(lax.div(d, step), 2), (jnp.bitwise_xor(d, step), t)) for step in (1, 2, 4)
    )
    sums = [
        Halving(fetch, links, halving_refs[i], (s_half.at[i], r_half.at[i]))
        for i, (fetch, links) in enumerate(
            (
                (
                    lambda y, low, high: wide_rows(0, y + 2 * low + 4 * high),
                    (link_y, link_low, link_high),
                ),
                (
                    lambda low, y, high: wide_rows(1, y + 2 * low + 4 * high),
                    (link_low, link_y, link_high),
                ),
                (gq_rows, (link_y, link_low, link_high)),
            )
        )
    ]

    load_wide[0].wait()
    load_wide[1].wait()
    load_x.start()
    load_one.start()
    load_down.start()
    for copy in load_res:
        copy.start()
    sums[0].start()
    sums[1].start()
    load_d(1).wait()

    @pl.loop(0, chunks)
    def _(c):
        to_core_ref[1, c] = piece(1, c).astype(BF)
        to_core(1, c).start()

    load_d(0).wait()
    load_one.wait()

    @pl.loop(0, chunks)
    def _(c):
        one_ref[rows(c), :] += piece(0, c)

    def start_gq():
        load_x.wait()
        gq_acc_ref[...] = jnp.zeros_like(gq_acc_ref)

        @pl.loop(0, size)
        def _(part):
            gq_acc_ref[...] += mm(d_ref[part], x_ref[part], 1, 0)

        total = gq_acc_ref[...].T.astype(BF)
        for g in range(groups):
            gq_ref[g] = total[g * block_rows : (g + 1) * block_rows]
        sums[2].start()

    def store_result(i):
        at = pl.ds(pl.multiple_of(i * ROWS, ROWS), ROWS)
        return pltpu.make_async_copy(out_ref.at[at], result_hbm.at[at], keep.at[chunks + 1 + i])

    blocks = out_ref.shape[0] // ROWS

    def arrange_result():
        for copy in load_res:
            copy.wait()
        for copy in beside_res:
            copy.wait_recv()

        @pl.loop(0, blocks)
        def _(i):
            at = pl.ds(pl.multiple_of(i * ROWS, ROWS), ROWS)
            out_ref[at, :] = unpack_block(spots_ref, src_ref, i)
            store_result(i).start()

    store_over(src_ref, res_over_ref, jnp.bitwise_xor(size - 1, t))

    body = Spread(home_ref, (sends, recvs), groups, d, t)
    extra = Spread(over_ref, (s_over, r_over), groups, d, t)

    def own_copy(c):
        return pltpu.make_async_copy(own_ref.at[c, d], home_ref.at[0, d, c], keep.at[c])

    own_over = pltpu.make_async_copy(spare_ref.at[d], over_ref.at[0, d], keep.at[chunks])

    def pass_on(c):
        own_copy(c).wait()
        for k in range(groups):
            if k > 0:
                body.arrival(own_ref.at[c, 0], k, (c,), (c,)).wait_recv()
            body.across(k, (c,), (c,)).start()
            body.beside(0, k, (c,), (c,)).start()

    def pass_far(c):
        for k in range(groups):
            body.across(k, (c,), (c,)).wait_recv()
            body.beside(2, k, (c,), (c,)).start()

    def send_home(c):
        to_core(1, c).wait_recv()
        partial = one_ref[rows(c), :] + from_core_ref[1, c].astype(F32)
        other(c).wait_recv()
        done = (partial + other_ref[c].astype(F32)).astype(BF)
        for g in range(groups):
            own_ref[c, g] = done[g * sub : (g + 1) * sub]
        own_copy(c).start()
        for k in range(1, groups):
            body.arrival(own_ref.at[c, lax.rem(d + k, groups)], k, (c,), (c,)).start()
        if c == chunks - 1:
            last = [own_ref[c, g, sub - 16 :, :].astype(F32)[15:16] for g in range(groups)]
            for to in range(groups):
                spare = last[0] * match_ref[to]
                for g in range(1, groups):
                    spare = spare + last[g] * match_ref[g * groups + to]
                spare_ref[to] = spare.astype(BF)
            own_over.start()
            for k in range(1, groups):
                extra.arrival(spare_ref.at[lax.rem(d + k, groups)], k, (), ()).start()

    other(0).wait_send()
    other(1).start()
    send_home(0)
    start_gq()
    other(1).wait_send()
    other(2).start()
    send_home(1)
    other(2).wait_send()
    pass_on(0)
    across_res.start()
    send_home(2)
    sums[0].advance(1)
    sums[1].advance(1)
    sums[2].advance(1)
    pass_on(1)
    across_res.wait_recv()
    for copy in beside_res:
        copy.start()
    load_down.wait()
    down_sent_ref[...] = down_sum(1).astype(BF)
    down_copy.start()
    pass_on(2)
    own_over.wait()
    for k in range(groups):
        if k > 0:
            extra.arrival(spare_ref.at[0], k, (), ()).wait_recv()
        extra.across(k, (), ()).start()
        extra.beside(0, k, (), ()).start()
    sums[0].advance(2)
    sums[1].advance(2)
    sums[2].advance(2)
    pass_far(0)
    pass_far(1)
    arrange_result()
    down_copy.wait_recv()
    totals = jnp.concatenate(
        [sums[0].total(), sums[1].total(), down_sum(0) + down_got_ref[...].astype(F32)], 1
    )
    gu_sum_ref[:, 0, :] = totals[:, :inner]
    gu_sum_ref[:, 1, :] = totals[:, inner : 2 * inner]
    total = sums[2].total()
    local = gq_sum_ref.shape[2]
    for i in range(3):
        gq_sum_ref[i] = total[:, i * local : (i + 1) * local]
    out_sum_ref[...] = totals[:, 2 * inner : 2 * inner + local]
    norm_sum_ref[...] = totals[:, 2 * inner + local : 2 * inner + local + norm_sum_ref.shape[1]]
    down_sum_ref[...] = totals[:, totals.shape[1] - inner :]
    pass_far(2)
    for k in range(groups):
        extra.across(k, (), ()).wait_recv()
        extra.beside(2, k, (), ()).start()
    down_copy.wait_send()
    across_res.wait_send()
    for copy in beside_res:
        copy.wait_send()

    @pl.loop(0, blocks)
    def _(i):
        store_result(i).wait()

    for each in sums:
        each.finish()
    for c in range(chunks):
        to_core(0, c).wait_send()
        to_core(1, c).wait_send()
    for k in range(groups):
        for c in range(chunks):
            body.beside(0, k, (c,), (c,)).wait_recv()
            body.beside(2, k, (c,), (c,)).wait_recv()
            if k > 0:
                body.arrival(own_ref.at[c, 0], k, (c,), (c,)).wait_send()
            body.across(k, (c,), (c,)).wait_send()
            body.beside(0, k, (c,), (c,)).wait_send()
            body.beside(2, k, (c,), (c,)).wait_send()
        extra.beside(0, k, (), ()).wait_recv()
        extra.beside(2, k, (), ()).wait_recv()
        if k > 0:
            extra.arrival(spare_ref.at[0], k, (), ()).wait_send()
        extra.across(k, (), ()).wait_send()
        extra.beside(0, k, (), ()).wait_send()
        extra.beside(2, k, (), ()).wait_send()


def settle(
    match,
    spots,
    res_over,
    d_qkv_t,
    x_all,
    w_t,
    grad_one,
    wide_own,
    wide_other,
    down,
    inner,
    res,
):
    size, local, rows = d_qkv_t.shape
    _, groups, _, sub, width = res.shape
    share = res.shape[2] * sub
    res = res.reshape(-1, groups, share // 16, 16, width)
    chunks = rows // BLOCK
    part = width // groups
    total_rows = size * rows
    anywhere = pl.BlockSpec(memory_space=pl.ANY)
    vmem = pl.BlockSpec(memory_space=pltpu.VMEM)
    smem = pl.BlockSpec(memory_space=pltpu.SMEM)
    dma = pltpu.SemaphoreType.DMA
    shape = jax.ShapeDtypeStruct
    buffer = pltpu.VMEM((chunks, BLOCK, width), BF)
    pair_buffer = pltpu.VMEM((2, chunks, BLOCK, width), BF)
    halving = lambda columns, steps: [
        pltpu.VMEM((2**steps - 1, part, columns), BF),
        pltpu.VMEM((2**steps - 1, part, columns), BF),
        pltpu.VMEM((2 ** (steps - 2), part, columns), F32),
    ]
    return pl.pallas_call(
        functools.partial(settle_kernel, groups, size),
        in_specs=[smem, smem, vmem] + [anywhere] * 8,
        out_specs=[anywhere, anywhere, anywhere] + [vmem] * 5,
        out_shape=[
            shape((size, groups, chunks, sub, width), BF),
            shape((size, groups, 1, width), BF),
            shape((total_rows, width), BF),
            shape((3, part, local // 3), F32),
            shape((part, 2, inner), F32),
            shape((part, inner), F32),
            shape((part, local // 3), F32),
            shape((part, 4), F32),
        ],
        scratch_shapes=[
            pltpu.VMEM(d_qkv_t.shape, BF),
            pltpu.VMEM(x_all.shape, BF),
            pltpu.VMEM(w_t.shape, BF),
            pltpu.VMEM(grad_one.shape, F32),
            pltpu.VMEM(wide_own.shape, BF),
            pltpu.VMEM(wide_own.shape, BF),
            pltpu.VMEM(down.shape, BF),
            pltpu.VMEM(down.shape[2:], BF),
            pltpu.VMEM(down.shape[2:], BF),
            pltpu.VMEM((groups, size * share // 16 + 1, 16, width), BF),
            pltpu.VMEM((total_rows, width), BF),
            pair_buffer,
            pair_buffer,
            buffer,
            buffer,
            pltpu.VMEM((chunks, groups, sub, width), BF),
            pltpu.VMEM((groups, 1, width), BF),
            pltpu.VMEM((groups, part, local), BF),
            pltpu.VMEM((local, width), F32),
            *halving(WIDE_PARTS[0], 3),
            *halving(WIDE_PARTS[1], 3),
            *halving(local, 3),
            dma((15,)),
            dma((5,)),
            dma((5,)),
            dma((3, 7)),
            dma((3, 7)),
            dma((4, groups, chunks)),
            dma((4, groups, chunks)),
            dma((4, groups)),
            dma((4, groups)),
            dma((3, chunks)),
            dma((3, chunks)),
            dma((chunks + 1 + total_rows // ROWS,)),
        ],
        compiler_params=pltpu.CompilerParams(
            collective_id=1, has_side_effects=True, vmem_limit_bytes=VMEM_LIMIT
        ),
        cost_estimate=pl.CostEstimate(
            flops=4 * size * rows * local * width, bytes_accessed=150 << 20, transcendentals=0
        ),
        name="settle",
    )(
        match,
        spots,
        res_over,
        d_qkv_t,
        x_all,
        w_t,
        grad_one,
        wide_own,
        wide_other,
        down,
        res,
    )


def local(tokens, cotangent, lengths, dealing, w_qkv, w_out, w_gu, w_down, gains, shifts):
    groups = lax.axis_size("dp")
    size = lax.axis_size("tensor")
    me = lax.axis_index("tensor")
    rows = tokens.shape[0]
    width = tokens.shape[2]
    slots = rows // groups
    share = slots // size
    own_rows = rows // size
    subs = own_rows // BLOCK
    sub = share // subs
    fused = groups == 8 and sub % 16 == 0
    i32 = jnp.int32

    ids = jnp.stack([lax.axis_index("dp"), me]).astype(i32)
    send_x, over_x, send_c, meta, table, match, spots = pack(
        lengths,
        dealing,
        ids,
        tokens.reshape(rows, width),
        cotangent.reshape(rows, width),
        groups,
        size,
    )

    def over_dp(array):
        return lax.all_to_all(array, "dp", split_axis=0, concat_axis=0, tiled=True)

    half = w_down.shape[0] // 2
    down_half = lax.dynamic_slice_in_dim(w_down, ids[0] % 2 * half, half, 0)
    far_out, far_down = swap(w_out.T, size, 2), swap(down_half, size, 2)
    match_square = match.reshape(groups, groups)

    def fill(received, over, last):
        spare = jnp.dot(match_square.astype(BF), over, preferred_element_type=F32).astype(BF)
        hole = (jnp.sum(match_square, 1) > 0)[:, None] & (jnp.arange(share) == share - 1)[None, :]
        fix = last[:, None, None] & hole[None]
        body = jnp.where(fix[..., None], spare[None, :, None, :], received)
        body = body.reshape(-1, groups, subs, sub, width).transpose(0, 2, 1, 3, 4)
        return body.reshape(-1, own_rows, width)

    if fused:
        x_rel, over_x = route(send_x, over_x, size)
        send_c, x_rel, far_out, far_down = lax.optimization_barrier(
            (send_c, x_rel, far_out, far_down)
        )
    else:
        x_rel = jnp.stack(gather_members(over_dp(send_x)))
        relative = jnp.bitwise_xor(jnp.arange(size, dtype=i32), me)
        x_rel = fill(x_rel, over_dp(over_x)[:, 0], relative == size - 1)
    local_width = w_qkv.shape[2]
    w_qkv_t = w_qkv.transpose(1, 2, 0).reshape(3 * local_width, width)
    x_rel, near_gu = lax.optimization_barrier((x_rel, w_gu.reshape(width, -1)))
    far_gu = swap(near_gu, size, 2)
    other_down = lax.ppermute(far_down, "dp", [(i, i ^ 1) for i in range(groups)])
    cot = over_dp(send_c)
    if not fused:
        cot = fill(cot[None, :, :share], cot[:, share], (me == size - 1)[None])[0]
    frequency = np.float32(1000.0) ** (-(np.arange(HALF, dtype=np.float32) * 2) / HEAD)
    frequency = jnp.asarray(frequency.astype(np.float32))
    q, k, v, k_rows, v_rows, cosine, sine, x_all, x_own = project(
        meta, match, x_rel, over_x, w_qkv_t, frequency[:, None], groups, fused
    )
    o_blocks, lse = attend(meta, q, k_rows, v, groups)
    o_blocks, far_gu, other_down, cot = lax.optimization_barrier(
        (o_blocks, far_gu, other_down, cot)
    )

    norms = jnp.concatenate([gains.T, shifts.T], 0)
    (
        result_own,
        grad_one,
        d_heads,
        heads_own,
        normed_t,
        d_branch_t,
        d_attn_t,
        hidden,
        d_gu,
        norm_grads,
    ) = middle(
        x_own,
        match,
        cot,
        norms,
        o_blocks,
        size,
        w_out.T,
        far_out,
        near_gu,
        far_gu,
        w_down,
        far_down,
        other_down,
    )
    grad_args = (normed_t, d_branch_t, d_attn_t, hidden, d_gu, heads_own, norm_grads)
    if fused:
        wide_own, wide_other, down, do_rel, home_result, over_result = grads(
            match, groups, *grad_args, d_heads, result_own
        )
        wide_other = swap(wide_other, size, 2)
        down = over_dp(down)
    else:
        sent_grads = weight_grads(1, *grad_args)
        kept_grads = weight_grads(0, *grad_args)
        pair = (kept_grads.astype(F32) + swap(sent_grads, size, 1).astype(F32)).astype(BF)
        do_rel = jnp.stack(exchange_members([d_heads[r] for r in range(size)]))

    d_qkv_t = attend_back(
        meta, q, k_rows, k, v_rows, o_blocks, do_rel, lse, cosine, sine, groups
    )
    def send_back(own):
        body = own.reshape(subs, groups, sub, width).transpose(1, 0, 2, 3)
        body = body.reshape(groups, share, width)
        spare = lax.dot_general(
            match_square.astype(BF),
            body[:, share - 1],
            (((0,), (0,)), ((), ())),
            preferred_element_type=F32,
        ).astype(BF)
        pair = (over_dp(body), over_dp(spare.reshape(groups, 1, width)))
        return tuple(jnp.stack(gather_members(a)) for a in pair)

    if fused:
        home_input, home_over, result, qkv_sum, gu_sum, down_sum, out_sum, norm_sum = settle(
            match,
            spots,
            over_result,
            d_qkv_t,
            x_all,
            w_qkv_t,
            grad_one,
            wide_own,
            wide_other,
            down,
            w_down.shape[1],
            home_result,
        )
        home_input = home_input.reshape(size, groups, share, width)
    else:
        back_rel, grad_qkv = project_back(meta, d_qkv_t, x_all, w_qkv_t)
        grad_qkv = grad_qkv.reshape(groups, width // groups, 3 * local_width)
        home_result = send_back(result_own)
        input_own = grad_one + reduce_members([back_rel[r] for r in range(size)])
        home_input = send_back(input_own.astype(BF))
        grad_qkv = lax.all_to_all(grad_qkv, "dp", split_axis=0, concat_axis=0, tiled=True)
        qkv_sum = jnp.sum(grad_qkv.astype(F32), 0)
        pair = lax.psum_scatter(pair, "dp", scatter_dimension=1, tiled=True)
        summed = pair[0].astype(F32) + swap(pair[1], size, 2).astype(F32)
    if fused:
        qkv_sum = qkv_sum.transpose(1, 0, 2)
    else:
        qkv_sum = qkv_sum.reshape(-1, 3, local_width)
        inner = w_down.shape[1]
        gu_sum = summed[:, : 2 * inner].reshape(-1, 2, inner)
        out_sum = summed[:, 2 * inner : 2 * inner + local_width]
        norm_sum = summed[:, 2 * inner + local_width : 2 * inner + local_width + 4]
        down_sum = summed[:, -inner:]
    norm_sum = lax.dynamic_slice_in_dim(
        norm_sum, me * (norm_sum.shape[0] // size), norm_sum.shape[0] // size, 0
    )
    if fused:
        input_grad, result = unpack(spots, me[None], home_input, home_over, result)
    else:
        row_ids = jnp.arange(rows, dtype=i32)[None, :]
        low, count, group, first = (table[i, 1:][:, None] for i in range(4))
        here = (row_ids >= low) & (row_ids < low + count)
        slot = row_ids + first - low
        home_part = jnp.minimum(slot // share, size - 1)
        flat = (jnp.bitwise_xor(home_part, me) * groups + group) * (share + 1)
        flat = jnp.sum(jnp.where(here, flat + slot - home_part * share, 0), 0)

        def arrange(home, over):
            every = jnp.concatenate([home, over], 2).reshape(-1, width)
            return jnp.take(every, flat, axis=0)

        result = arrange(*home_result)
        input_grad = arrange(*home_input)
    result = result.reshape(rows, 1, width)
    input_grad = input_grad.reshape(rows, 1, width)
    return (
        result,
        input_grad,
        qkv_sum,
        out_sum,
        gu_sum,
        down_sum,
        norm_sum[:, :2],
        norm_sum[:, 2:],
    )


def solution(mesh):
    placed = (
        P(None, "dp", None),
        P(None, "dp", None),
        P(),
        P(),
        P(None, None, "tensor"),
        P(None, "tensor"),
        P(None, None, "tensor"),
        P(None, "tensor"),
        P(),
        P(),
    )
    return jax.shard_map(
        local,
        mesh=mesh,
        in_specs=placed,
        out_specs=(
            P(None, "dp", None),
            P(None, "dp", None),
            P("dp", None, "tensor"),
            P("dp", "tensor"),
            P("dp", None, "tensor"),
            P("dp", "tensor"),
            P(("dp", "tensor"), None),
            P(("dp", "tensor"), None),
        ),
        check_vma=False,
    )
```
